32 devices in a mesh: dp: 8 (over z, x), ctx: 2 (over y), tensor: 2 (over core).
Axes of the slice: x: 2, y: 2, z: 4, core: 2. Of those that a mesh axis runs over, the one named last changes fastest.
Arguments:
- tokens: bfloat16 [16384, 768], P(('dp', 'ctx')), may hold values from -6 to 6
- lengths: int32 [8, 4], P('dp'), may hold values from 1 to 2045, as said below
- gain_one: bfloat16 [768], P('dp'), may hold values from 0.5 to 1.5
- w_qkv: bfloat16 [3, 768, 768], P(None, 'dp', 'tensor'), may hold values from -0.21875 to 0.21875
- w_out: bfloat16 [768, 768], P('tensor', 'dp'), may hold values from -0.625 to 0.625
- gain_two: bfloat16 [768], P('dp'), may hold values from 0.5 to 1.5
- w_in: bfloat16 [2, 768, 1152], P(None, 'dp', 'tensor'), may hold values from -0.21875 to 0.21875
- w_down: bfloat16 [1152, 768], P('tensor', 'dp'), may hold values from -0.25 to 0.25
- cotangent: bfloat16 [16384, 768], P(('dp', 'ctx')), may hold values from -6 to 6
Outputs:
- mixed: bfloat16 [16384, 768], P(('dp', 'ctx'))
- token_grad: float32 [16384, 768], P(('dp', 'ctx'))
- grad_gain_one: float32 [768], P('dp')
- grad_qkv: float32 [3, 768, 768], P(None, 'dp', 'tensor')
- grad_out: float32 [768, 768], P('tensor', 'dp')
- grad_gain_two: float32 [768], P('dp')
- grad_in: float32 [2, 768, 1152], P(None, 'dp', 'tensor')
- grad_down: float32 [1152, 768], P('tensor', 'dp')
The draws below stay inside these ranges and needn't reach their ends.
Inputs may be any that keep to these rules, and one draw needn't show every extreme that they name: Each group's 4 lengths sum to 2048; one of them, at a place drawn from the seed, is 1025 or more; in one group, drawn from the seed, all other lengths are 1.
All inputs are finite; a program needn't handle non-finite values.
Results may differ from the reference program's by a relative error of at most 0.02.
Values may be sent and summed in bfloat16 or wider, within the bound.
No kernel may reach another device: no remote copies, remote signals or barrier semaphores. Data moves between devices by JAX's collectives and lax.ppermute only.
A program may use at most 256 MiB of HBM per device.

```python
import math
import jax
import jax.numpy as jnp
from jax import lax

D = 768
HEADS = 12
FF = 1152
HEAD = 64
WINDOW = 128
NSEQ = 4
GROUP = 2048
ROWS_DEV = 1024
GROUPS = 8
TOKENS = 16384


def draw_lengths(key, part):
    key = jax.random.fold_in(key, 7)
    first_key, second_key, third_key = jax.random.split(key, 3)
    ceiling = (ROWS_DEV - 1) // (NSEQ - 1)
    short = jax.random.randint(first_key, (GROUPS, NSEQ), 1, ceiling + 1)
    picked = jax.random.randint(third_key, (1, 1), 0, GROUPS)
    tight = jnp.arange(GROUPS, dtype=jnp.int32)[:, None] == picked
    short = jnp.where(tight, 1, short)
    chosen = jax.random.randint(second_key, (GROUPS, 1), 0, NSEQ)
    marked = jnp.arange(NSEQ, dtype=jnp.int32)[None, :] == chosen
    others = jnp.sum(jnp.where(marked, 0, short), axis=1, keepdims=True)
    return jnp.where(marked, GROUP - others, short).astype(jnp.int32)


def shard_levels(own_key, extent, shards, least, top_value):
    level = 1.0
    for dim, shards_of in shards:
        heights = jax.random.uniform(jax.random.fold_in(jax.random.fold_in(own_key, 6), dim), (shards_of,), jnp.float32, least / len(shards), top_value / len(shards))
        level = level * jnp.repeat(jnp.exp(heights), extent[dim] // shards_of).reshape((-1,) + (1,) * (len(extent) - 1 - dim))
    return level


def gaussian(key, shape, width, bound, pieces=(), kind=jnp.bfloat16):
    array = width * jax.random.normal(key, shape, jnp.float32)
    if pieces:
        array = array * shard_levels(key, shape, pieces, -0.22, 0.18)
    return jnp.clip(array, -bound, bound).astype(kind)


def setup_inputs(seed: int = 0) -> dict:
    seeds = jax.random.split(jax.random.key(seed), 10)
    return {
        "tokens": gaussian(seeds[0], (TOKENS, D), 1.0, 6.0, ((0, 16),)),
        "lengths": draw_lengths(jax.random.fold_in(seeds[9], 71), 0),
        "gain_one": jnp.clip(1.0 + 0.1 * jax.random.normal(seeds[2], (D,), jnp.float32), 0.5, 1.5).astype(jnp.bfloat16),
        "w_qkv": gaussian(seeds[3], (3, D, D), D ** -0.5, 0.21875, ((1, 8), (2, 2))),
        "w_out": gaussian(seeds[4], (D, D), (D // 8) ** -0.5, 0.625, ((0, 2), (1, 8))),
        "gain_two": jnp.clip(1.0 + 0.1 * jax.random.normal(seeds[5], (D,), jnp.float32), 0.5, 1.5).astype(jnp.bfloat16),
        "w_in": gaussian(seeds[6], (2, D, FF), D ** -0.5, 0.21875, ((1, 8), (2, 2))),
        "w_down": gaussian(seeds[7], (FF, D), (FF // 2) ** -0.5, 0.25, ((0, 2), (1, 8))),
        "cotangent": gaussian(seeds[8], (TOKENS, D), 1.0, 6.0, ((0, 16),)),
    }


highest = lax.Precision.HIGHEST
norm_eps = 1e-05

@jax.custom_vjp
def low(v):
    return lax.optimization_barrier(v.astype(jnp.bfloat16)).astype(jnp.float32)

@jax.custom_vjp
def low_back(v):
    return v

def low_keep(v):
    return (low(v), None)

def low_pass(kept, grad):
    return (grad,)

def back_keep(v):
    return (v, None)

def back_low(kept, grad):
    return (low(grad),)
low.defvjp(low_keep, low_pass)
low_back.defvjp(back_keep, back_low)

def layer_norm(values, gain):
    centered = values - lax.optimization_barrier(jnp.mean(values, axis=-1, keepdims=True))
    spread = lax.optimization_barrier(jnp.mean(centered * centered, axis=-1, keepdims=True))
    return centered * lax.rsqrt(spread + norm_eps) * gain

def rotate(values, cosine, sine):
    middle = values.shape[-1] // 2
    turned = jnp.concatenate([-values[..., middle:], values[..., :middle]], axis=-1)
    return values * cosine + turned * sine

def angle_tables(position):
    number = (jnp.arange(HEAD, dtype=jnp.int32) % (HEAD // 2)).astype(jnp.float32)
    freq = jnp.exp(number * (-2.0 * math.log(10000.0) / HEAD))
    angle = position.astype(jnp.float32)[:, None] * freq[None, :]
    return (jnp.cos(angle)[:, None, :], jnp.sin(angle)[:, None, :])

def row_tables(lengths):
    ends = jnp.cumsum(lengths, axis=1).astype(jnp.int32)
    starts = (ends - lengths).astype(jnp.int32)
    rows = jnp.arange(GROUP, dtype=jnp.int32)
    inside = (rows[None, :, None] >= starts[:, None, :]) & (rows[None, :, None] < ends[:, None, :])
    labels = jnp.arange(NSEQ, dtype=jnp.int32)
    seq = lax.optimization_barrier(jnp.sum(jnp.where(inside, labels[None, None, :], 0), axis=2)).astype(jnp.int32)
    begin = lax.optimization_barrier(jnp.sum(jnp.where(inside, starts[:, None, :], 0), axis=2)).astype(jnp.int32)
    owner = seq + NSEQ * jnp.arange(GROUPS, dtype=jnp.int32)[:, None]
    return (owner.reshape(-1), (rows[None, :] - begin).reshape(-1))

def attend(query, key, value, owner):
    rows = query.shape[0]
    step = 512 if rows % 512 == 0 else 128
    half = WINDOW // 2
    pad = ((half, half), (0, 0), (0, 0))
    key_pad = jnp.pad(key, pad)
    value_pad = jnp.pad(value, pad)
    owner_pad = jnp.pad(owner, (half, half), constant_values=-1)
    near = jnp.abs(jnp.arange(step, dtype=jnp.int32)[:, None] + half - jnp.arange(step + 2 * half, dtype=jnp.int32)[None, :]) <= half

    def one_block(start):
        query_blk = lax.dynamic_slice_in_dim(query, start, step, 0)
        key_blk = lax.dynamic_slice_in_dim(key_pad, start, step + 2 * half, 0)
        value_blk = lax.dynamic_slice_in_dim(value_pad, start, step + 2 * half, 0)
        mine = lax.dynamic_slice_in_dim(owner, start, step, 0)
        other = lax.dynamic_slice_in_dim(owner_pad, start, step + 2 * half, 0)
        allowed = near & (mine[:, None] == other[None, :])
        raw = low_back(jnp.einsum('qhd,khd->hqk', query_blk, key_blk, precision=highest) * HEAD ** (-0.5))
        scores = jnp.where(allowed[None], raw, -1e+30)
        peak = lax.optimization_barrier(jnp.max(scores, axis=-1, keepdims=True))
        weights = jnp.exp(scores - peak)
        shares = weights / lax.optimization_barrier(jnp.sum(weights, axis=-1, keepdims=True))
        return jnp.einsum('hqk,khd->qhd', low(shares), value_blk, precision=highest)
    starts = jnp.arange(rows // step, dtype=jnp.int32) * step
    blocks = lax.map(jax.checkpoint(one_block), starts)
    return blocks.reshape(rows, query.shape[1], query.shape[2])

def forward(tokens, gain_one, w_qkv, w_out, gain_two, w_in, w_down, owner, cosine, sine):
    rows = tokens.shape[0]
    split = (rows, HEADS, HEAD)
    first = low(layer_norm(tokens, gain_one))
    query = low(rotate(low_back(jnp.dot(first, w_qkv[0], precision=highest)).reshape(split), cosine, sine))
    key = low(rotate(low_back(jnp.dot(first, w_qkv[1], precision=highest)).reshape(split), cosine, sine))
    value = low_back(low(jnp.dot(first, w_qkv[2], precision=highest))).reshape(split)
    attended = low_back(low(attend(query, key, value, owner).reshape(rows, D)))
    middle = tokens + low_back(jnp.dot(attended, w_out, precision=highest))
    second = low(layer_norm(middle, gain_two))
    gate = low_back(jnp.dot(second, w_in[0], precision=highest))
    upper = low_back(jnp.dot(second, w_in[1], precision=highest))
    hidden = low(jax.nn.gelu(gate, approximate=False) * upper)
    return middle + low_back(jnp.dot(hidden, w_down, precision=highest))

def reference(tokens, lengths, gain_one, w_qkv, w_out, gain_two, w_in, w_down, cotangent):
    owner, position = row_tables(lengths)
    cosine, sine = angle_tables(position)
    inputs = (tokens.astype(jnp.float32), gain_one.astype(jnp.float32), w_qkv.astype(jnp.float32), w_out.astype(jnp.float32), gain_two.astype(jnp.float32), w_in.astype(jnp.float32), w_down.astype(jnp.float32))

    def run(tokens_f, gain_one_f, w_qkv_f, w_out_f, gain_two_f, w_in_f, w_down_f):
        return forward(tokens_f, gain_one_f, w_qkv_f, w_out_f, gain_two_f, w_in_f, w_down_f, owner, cosine, sine)
    mixed, pullback = jax.vjp(run, *inputs)
    grads = pullback(cotangent.astype(jnp.float32))
    return (mixed.astype(jnp.bfloat16), grads[0], grads[1], grads[2], grads[3], grads[4], grads[5], grads[6])
```

```python
import functools
import math

import jax
import jax.numpy as jnp
from jax import lax
from jax.experimental import pallas as pl
from jax.experimental.pallas import tpu as pltpu
from jax.sharding import PartitionSpec as P

HEAD = 64
WINDOW = 128
NSEQ = 4
HALF = WINDOW // 2
BLOCK = 128
LANES = 128
KEYS = BLOCK + WINDOW

norm_eps = 1e-05
f32 = jnp.float32
bf16 = jnp.bfloat16

NN = (((1,), (0,)), ((), ()))
NT = (((1,), (1,)), ((), ()))
TN = (((0,), (0,)), ((), ()))


def dot(a, b, dims=NN):
    return lax.dot_general(a, b, dims, preferred_element_type=f32)


def step_of(rows, most):
    best = LANES
    for size in range(LANES, most + 1, LANES):
        if rows % size == 0:
            best = size
    return best


def call(kernel, out_shape, args, flops, name, scalars=()):
    vmem = pl.BlockSpec(memory_space=pltpu.VMEM)
    smem = pl.BlockSpec(memory_space=pltpu.SMEM)
    moved = sum(x.size * x.dtype.itemsize for x in (*args, *out_shape))
    return pl.pallas_call(
        kernel[0],
        out_shape=out_shape,
        in_specs=[smem] * len(scalars) + [vmem] * len(args),
        out_specs=[vmem] * len(out_shape),
        scratch_shapes=kernel[1],
        compiler_params=pltpu.CompilerParams(vmem_limit_bytes=56 * 2**20),
        cost_estimate=pl.CostEstimate(flops=flops, bytes_accessed=moved, transcendentals=0),
        name=name,
    )(*scalars, *args)


def shape(dims, dtype):
    return jax.ShapeDtypeStruct(dims, dtype)


def normed(values):
    centered = values - jnp.mean(values, axis=-1, keepdims=True)
    spread = jnp.mean(centered * centered, axis=-1, keepdims=True)
    scale = lax.rsqrt(spread + norm_eps)
    return centered * scale, scale


def norm_back(grad, gain, hat, scale):
    inner = grad * gain
    one = jnp.mean(inner, axis=-1, keepdims=True)
    two = jnp.mean(inner * hat, axis=-1, keepdims=True)
    return scale * (inner - one - hat * two)


def turned(values, low):
    return jnp.where(low, pltpu.roll(values, LANES - HEAD // 2, 1), pltpu.roll(values, HEAD // 2, 1))


def halves(values):
    even = (lax.broadcasted_iota(jnp.int32, (1, LANES), 1) < HEAD).astype(f32).astype(bf16)
    return jnp.concatenate([values * even, values * (1 - even)], axis=0)


def joined(values):
    return jnp.concatenate([values[:HEAD, :BLOCK], values[HEAD:, BLOCK:]], axis=0).T


def stack_weight(src, index, dst):
    parts, _, depth, _ = src.shape
    for part in range(parts):
        dst[part * depth : (part + 1) * depth, :] = src[part, index]


def loop(count, body):
    def run(index, carry):
        body(index)
        return carry

    lax.fori_loop(0, count, run, 0)


def attend_kernel(
    bounds, tokens, before, after, gain, weights, cosine, sine,
    first, query, key, value, shares, attended, branch,
    wide, out_t,
):
    rows, width = tokens.shape
    extent, local = key.shape
    pairs = local // LANES
    for number in range(3):
        stack_weight(weights, number, wide.at[number])
    stack_weight(weights, 3, out_t)
    gains = gain[...]

    def norm_rows(src, dst, size):
        hat, _ = normed(src.astype(f32))
        first[pl.ds(dst, size), :] = (hat * gains).astype(bf16)

    norm_rows(before[...], 0, HALF)
    norm_rows(after[...], rows + HALF, HALF)

    def norm_step(index):
        at = pl.multiple_of(index * BLOCK, BLOCK)
        norm_rows(tokens[pl.ds(at, BLOCK), :], at + HALF, BLOCK)

    loop(rows // BLOCK, norm_step)
    low = lax.broadcasted_iota(jnp.int32, (1, LANES), 1) % HEAD < HEAD // 2

    def rotated(src, at, size, dst, place, scale):
        co, si = cosine[pl.ds(at, size), :], sine[pl.ds(at, size), :]
        for pair in range(pairs):
            lanes = slice(pair * LANES, (pair + 1) * LANES)
            part = src[:, lanes]
            dst[pl.ds(place, size), lanes] = ((part * co + turned(part, low) * si) * scale).astype(bf16)

    chunk = step_of(extent, 384)

    def key_step(index):
        at = pl.multiple_of(index * chunk, chunk)
        part = first[pl.ds(at, chunk), :]
        rotated(dot(part, wide[1]), at, chunk, key, at, 1.0)
        value[pl.ds(at, chunk), :] = dot(part, wide[2]).astype(bf16)

    loop(extent // chunk, key_step)
    size = step_of(rows, 256)

    def query_step(index):
        at = pl.multiple_of(index * size, size)
        start = pl.multiple_of(at + HALF, HALF)
        rotated(dot(first[pl.ds(start, size), :], wide[0]), start, size, query, at, HEAD**-0.5)

    loop(rows // size, query_step)
    key_at = lax.broadcasted_iota(jnp.int32, (KEYS, KEYS), 0)
    lane_at = lax.broadcasted_iota(jnp.int32, (1, KEYS), 1) % BLOCK

    def attend_step(index):
        at = pl.multiple_of(index * BLOCK, BLOCK)
        origin = bounds[NSEQ] + at - HALF
        own = lane_at + (origin + HALF)
        begin = jnp.zeros_like(own)
        end = jnp.zeros_like(own) + bounds[NSEQ - 1]
        for number in range(NSEQ - 1):
            begin = jnp.where(own >= bounds[number], bounds[number], begin)
        for number in reversed(range(NSEQ - 1)):
            end = jnp.where(own < bounds[number], bounds[number], end)
        least = jnp.maximum(lane_at, begin - origin)
        most = jnp.minimum(lane_at + WINDOW, end - 1 - origin)
        bias = jnp.where((key_at >= least) & (key_at <= most), 0.0, -1e30)
        for pair in range(pairs):
            lanes = slice(pair * LANES, (pair + 1) * LANES)
            both = halves(query[pl.ds(at, BLOCK), lanes])
            scores = dot(key[pl.ds(at, KEYS), lanes], both, NT) + bias
            weight = jnp.exp(scores - jnp.max(scores, axis=0, keepdims=True))
            part = (weight * (1.0 / jnp.sum(weight, axis=0, keepdims=True))).astype(bf16)
            shares[index * pairs + pair] = part
            mixed = dot(value[pl.ds(at, KEYS), lanes], part, TN)
            attended[pl.ds(at, BLOCK), lanes] = joined(mixed).astype(bf16)

    loop(rows // BLOCK, attend_step)

    def out_step(index):
        at = pl.multiple_of(index * size, size)
        branch[pl.ds(at, size), :] = dot(attended[pl.ds(at, size), :], out_t[...], NT).astype(bf16)

    loop(rows // size, out_step)


def feed_kernel(
    tokens, own, other, gain, weights, cotangent,
    middle, second, hidden, grad_gate, grad_upper, partial,
    gate_w, upper_w, down_t,
):
    rows, width = tokens.shape
    stack_weight(weights, 0, gate_w)
    stack_weight(weights, 1, upper_w)
    stack_weight(weights, 2, down_t)
    gains = gain[...]
    size = step_of(rows, 256)

    def step(index):
        at = pl.multiple_of(index * size, size)
        here = pl.ds(at, size)
        mid = tokens[here, :].astype(f32) + (own[here, :].astype(f32) + other[here, :].astype(f32))
        middle[here, :] = mid
        hat, _ = normed(mid)
        low = (hat * gains).astype(bf16)
        second[here, :] = low
        gate = dot(low, gate_w[...])
        upper = dot(low, upper_w[...])
        grad = dot(cotangent[here, :], down_t[...])
        share = 0.5 * (1.0 + lax.erf(gate * (0.5**0.5)))
        smooth = gate * share
        slope = share + gate * (jnp.exp(gate * gate * -0.5) * ((2.0 * math.pi) ** -0.5))
        hidden[here, :] = (smooth * upper).astype(bf16)
        gate_low = (grad * upper * slope).astype(bf16)
        upper_low = (grad * smooth).astype(bf16)
        grad_gate[here, :] = gate_low
        grad_upper[here, :] = upper_low
        partial[here, :] = (dot(gate_low, gate_w[...], NT) + dot(upper_low, upper_w[...], NT)).astype(bf16)

    loop(rows // size, step)


def weight_kernel(second, hidden, grad_gate, grad_upper, cotangent, weights, feed, grads, down_t, total):
    rows, width = second.shape
    stack_weight(weights, 2, down_t)
    size = step_of(rows, 256)

    def step(index):
        here = pl.ds(pl.multiple_of(index * size, size), size)
        feed[here, :] = dot(hidden[here, :], down_t[...], NT).astype(bf16)

    loop(rows // size, step)
    scatter_grads(second, grad_gate, grads, 0, total)
    scatter_grads(second, grad_upper, grads, 1, total)
    scatter_grads(cotangent, hidden, grads, 2, total)


def scatter_grads(left, right, grads, number, total):
    width = left.shape[-1]
    parts, _, depth, _ = grads.shape
    for start in range(0, width, 2 * LANES):
        total[start : start + 2 * LANES, :] = dot(left[:, start : start + 2 * LANES], right[...], TN).astype(bf16)
    for part in range(parts):
        grads[part, number] = total[part * depth : (part + 1) * depth, :]


def back_kernel(
    middle, own, other, gain, cotangent, weights, first, query, key, value, shares, attended, cosine, sine,
    grad_middle, grad_proj, grads, gain_grad,
    out_t, low_mid, grad_att, grad_key, grad_value, total,
):
    rows, width = middle.shape
    extent, local = key.shape
    pairs = local // LANES
    stack_weight(weights, 3, out_t)
    gains = gain[...]
    size = step_of(rows, 256)
    gain_grad[...] = jnp.zeros_like(gain_grad)

    def norm_step(index):
        here = pl.ds(pl.multiple_of(index * size, size), size)
        hat, scale = normed(middle[here, :])
        grad = own[here, :].astype(f32) + other[here, :].astype(f32)
        gain_grad[...] += jnp.sum(grad * hat, axis=0, keepdims=True)
        mid = cotangent[here, :].astype(f32) + norm_back(grad, gains, hat, scale)
        grad_middle[here, :] = mid
        mid_low = mid.astype(bf16)
        low_mid[here, :] = mid_low
        grad_att[here, :] = dot(mid_low, out_t[...]).astype(bf16)

    loop(rows // size, norm_step)
    grad_key[...] = jnp.zeros_like(grad_key)
    grad_value[...] = jnp.zeros_like(grad_value)
    low = lax.broadcasted_iota(jnp.int32, (1, LANES), 1) % HEAD < HEAD // 2
    zero = jnp.zeros((HALF, local), bf16)
    grad_proj[:HALF, :local] = zero
    grad_proj[rows + HALF :, :local] = zero

    def attend_step(index):
        at = pl.multiple_of(index * BLOCK, BLOCK)
        start = pl.multiple_of(at + HALF, HALF)
        co, si = cosine[pl.ds(start, BLOCK), :], sine[pl.ds(start, BLOCK), :]
        for pair in range(pairs):
            lanes = slice(pair * LANES, (pair + 1) * LANES)
            both = halves(query[pl.ds(at, BLOCK), lanes])
            grad = halves(grad_att[pl.ds(at, BLOCK), lanes])
            keys = key[pl.ds(at, KEYS), lanes]
            part = shares[index * pairs + pair]
            wide = part.astype(f32)
            grad_shares = dot(value[pl.ds(at, KEYS), lanes], grad, NT)
            delta = jnp.sum(wide * grad_shares, axis=0, keepdims=True)
            raw = (wide * (grad_shares - delta)).astype(bf16)
            grad_key[pl.ds(at, KEYS), lanes] += dot(raw, both)
            grad_value[pl.ds(at, KEYS), lanes] += dot(part, grad)
            grad_query = joined(dot(keys, raw, TN)) * HEAD**-0.5
            grad_proj[pl.ds(start, BLOCK), lanes] = (grad_query * co - turned(grad_query, low) * si).astype(bf16)

    loop(rows // BLOCK, attend_step)

    def turn_step(index):
        at = pl.multiple_of(index * BLOCK, BLOCK)
        here = pl.ds(at, BLOCK)
        co, si = cosine[here, :], sine[here, :]
        for pair in range(pairs):
            lanes = slice(pair * LANES, (pair + 1) * LANES)
            part = grad_key[here, lanes]
            turn = slice(local + pair * LANES, local + (pair + 1) * LANES)
            grad_proj[here, turn] = (part * co - turned(part, low) * si).astype(bf16)
        grad_proj[here, 2 * local :] = grad_value[here, :].astype(bf16)

    loop(extent // BLOCK, turn_step)
    for number in range(3):
        scatter_grads(first, grad_proj.at[:, number * local : (number + 1) * local], grads, number, total)
    scatter_grads(low_mid, attended, grads, 3, total)


def first_kernel(grad_proj, weights, tokens, before, after, partial, front, behind, gain_grad, wide):
    rows, width = tokens.shape
    extent = grad_proj.shape[0]
    local = weights.shape[-1]
    for number in range(3):
        stack_weight(weights, number, wide.at[:, number * local : (number + 1) * local])
    gain_grad[...] = jnp.zeros_like(gain_grad)

    def part(at, values, size):
        grad = dot(grad_proj[pl.ds(at, size), :], wide[...], NT)
        hat, _ = normed(values.astype(f32))
        gain_grad[...] += jnp.sum(grad * hat, axis=0, keepdims=True)
        return grad.astype(bf16)

    front[...] = part(0, before[...], HALF)
    behind[...] = part(rows + HALF, after[...], HALF)
    size = step_of(rows, 256)

    def step(index):
        at = pl.multiple_of(index * size, size)
        here = pl.ds(at, size)
        partial[here, :] = part(pl.multiple_of(at + HALF, HALF), tokens[here, :], size)

    loop(rows // size, step)


def final_kernel(tokens, gain, grad_middle, own, other, middle, feed_own, feed_other, *rest):
    edges, (mixed, token_grad) = rest[:4], rest[4:]
    rows, width = tokens.shape
    gains = gain[...]
    size = BLOCK

    def back(here, values, grad):
        hat, scale = normed(values)
        return norm_back(grad, gains, hat, scale)

    def step(index):
        here = pl.ds(pl.multiple_of(index * size, size), size)
        grad = own[here, :].astype(f32) + other[here, :].astype(f32)
        token_grad[here, :] = grad_middle[here, :] + back(here, tokens[here, :].astype(f32), grad)
        feed = feed_own[here, :].astype(f32) + feed_other[here, :].astype(f32)
        mixed[here, :] = (middle[here, :] + feed).astype(bf16)

    loop(rows // size, step)
    for start, one, two in ((0, edges[0], edges[1]), (rows - HALF, edges[2], edges[3])):
        here = pl.ds(start, HALF)
        grad = one[...].astype(f32) + two[...].astype(f32)
        token_grad[here, :] += back(here, tokens[here, :].astype(f32), grad)


def edge(array, by, cross):
    devices, cores = lax.axis_size("ctx"), lax.axis_size("tensor")
    pairs = []
    for i in range(devices):
        if 0 <= i + by < devices:
            for c in range(cores):
                pairs.append((i * cores + c, (i + by) * cores + (c + cross) % cores))
    return lax.ppermute(array, ("ctx", "tensor"), pairs)


def swap(array):
    return lax.ppermute(array, "tensor", [(0, 1), (1, 0)])


def tables(lengths, rows):
    place = lax.axis_index("ctx") * rows
    ends = jnp.cumsum(lengths[0])
    starts = ends - lengths[0]
    span = place + jnp.arange(-HALF, rows + HALF, dtype=jnp.int32)
    inside = (span[:, None] >= starts[None, :]) & (span[:, None] < ends[None, :])
    position = span - jnp.sum(jnp.where(inside, starts[None, :], 0), axis=1)
    number = (jnp.arange(HEAD, dtype=jnp.int32) % (HEAD // 2)).astype(f32)
    freq = jnp.exp(number * (-2.0 * math.log(10000.0) / HEAD))
    angle = position.astype(f32)[:, None] * freq[None, :]
    cosine, sine = jnp.cos(angle), jnp.sin(angle)
    sine = jnp.where(jnp.arange(HEAD)[None, :] < HEAD // 2, -sine, sine)
    bounds = jnp.concatenate([ends, place[None]]).astype(jnp.int32)
    return jnp.tile(cosine, (1, 2)), jnp.tile(sine, (1, 2)), bounds


def body(tokens, lengths, gain_one, w_qkv, w_out, gain_two, w_in, w_down, cotangent):
    rows, width = tokens.shape
    local, units = w_out.shape[0], w_down.shape[0]
    pairs, blocks, extent = local // LANES, rows // BLOCK, rows + WINDOW
    groups = lax.axis_size("dp")
    gains = lax.all_gather(jnp.stack([gain_one, gain_two]), "dp", axis=0, tiled=False)
    mine_one = jnp.concatenate([w_qkv, w_out.T[None]])
    mine_two = jnp.concatenate([w_in, w_down.T[None]])
    weights_one = lax.all_gather(mine_one, "dp", axis=0, tiled=False)
    weights_two = lax.all_gather(mine_two, "dp", axis=0, tiled=False)
    norm_one = gains[:, 0].reshape(1, width).astype(f32)
    norm_two = gains[:, 1].reshape(1, width).astype(f32)
    before = edge(tokens[rows - HALF :], 1, 0)
    after = edge(tokens[:HALF], -1, 0)
    cosine, sine, bounds = tables(lengths, rows)

    first, query, key, value, shares, attended, branch = call(
        (attend_kernel, [pltpu.VMEM((3, width, local), bf16), pltpu.VMEM((width, local), bf16)]),
        [
            shape((extent, width), bf16),
            shape((rows, local), bf16),
            shape((extent, local), bf16),
            shape((extent, local), bf16),
            shape((blocks * pairs, KEYS, KEYS), bf16),
            shape((rows, local), bf16),
            shape((rows, width), bf16),
        ],
        (tokens, before, after, norm_one, weights_one, cosine, sine),
        2 * rows * width * local * 5,
        "project_and_attend",
        (bounds,),
    )
    branch_other = swap(branch)
    plain = [pltpu.VMEM((width, units), bf16)] * 3
    middle, second, hidden, grad_gate, grad_upper, partial = call(
        (feed_kernel, plain),
        [
            shape((rows, width), f32),
            shape((rows, width), bf16),
            shape((rows, units), bf16),
            shape((rows, units), bf16),
            shape((rows, units), bf16),
            shape((rows, width), bf16),
        ],
        (tokens, branch, branch_other, norm_two, weights_two, cotangent),
        2 * rows * width * units * 5,
        "feed_forward_and_back",
    )
    partial_other = swap(partial)
    feed, grads_two = call(
        (weight_kernel, [pltpu.VMEM((width, units), bf16)] * 2),
        [shape((rows, width), bf16), shape((groups, 3, width // groups, units), bf16)],
        (second, hidden, grad_gate, grad_upper, cotangent, weights_two),
        2 * rows * width * units * 4,
        "feed_weight_grads",
    )
    feed_other = swap(feed)
    grad_middle, grad_proj, grads_one, grad_gain_two = call(
        (
            back_kernel,
            [
                pltpu.VMEM((width, local), bf16),
                pltpu.VMEM((rows, width), bf16),
                pltpu.VMEM((rows, local), bf16),
                pltpu.VMEM((extent, local), f32),
                pltpu.VMEM((extent, local), f32),
                pltpu.VMEM((width, local), bf16),
            ],
        ),
        [
            shape((rows, width), f32),
            shape((extent, 3 * local), bf16),
            shape((groups, 4, width // groups, local), bf16),
            shape((1, width), f32),
        ],
        (
            middle, partial, partial_other, norm_two, cotangent, weights_one, first, query, key, value, shares,
            attended, cosine, sine,
        ),
        2 * rows * width * local * 6,
        "attention_back",
    )
    first_part, front, behind, grad_gain_one = call(
        (first_kernel, [pltpu.VMEM((width, 3 * local), bf16)]),
        [
            shape((rows, width), bf16),
            shape((HALF, width), bf16),
            shape((HALF, width), bf16),
            shape((1, width), f32),
        ],
        (grad_proj, weights_one, tokens, before, after),
        2 * rows * width * local * 3,
        "first_grad",
    )
    first_other = swap(first_part)
    edges = [edge(behind, 1, 0), edge(behind, 1, 1), edge(front, -1, 0), edge(front, -1, 1)]
    mixed, token_grad = call(
        (final_kernel, []),
        [shape((rows, width), bf16), shape((rows, width), f32)],
        (tokens, norm_one, grad_middle, first_part, first_other, middle, feed, feed_other, *edges),
        rows * width * 20,
        "token_grad",
    )

    def reduced(grads):
        part = lax.psum_scatter(grads, "dp", scatter_dimension=0, tiled=False)
        return lax.psum(part, "ctx")

    two = reduced(grads_two).astype(f32)
    one = reduced(grads_one).astype(f32)
    gain_grads = jnp.stack([grad_gain_one.reshape(groups, -1), grad_gain_two.reshape(groups, -1)], axis=1)
    both = lax.psum_scatter(gain_grads, "dp", scatter_dimension=0, tiled=False)
    gain_one_grad = lax.psum(both[0], ("ctx", "tensor"))
    gain_two_grad = lax.psum(both[1], "ctx")
    return (mixed, token_grad, gain_one_grad, one[:3], one[3].T, gain_two_grad, two[:2], two[2].T)


def solution(mesh):
    in_specs = (
        P(("dp", "ctx"), None),
        P("dp", None),
        P("dp"),
        P(None, "dp", "tensor"),
        P("tensor", "dp"),
        P("dp"),
        P(None, "dp", "tensor"),
        P("tensor", "dp"),
        P(("dp", "ctx"), None),
    )
    out_specs = (
        P(("dp", "ctx"), None),
        P(("dp", "ctx"), None),
        P("dp"),
        P(None, "dp", "tensor"),
        P("tensor", "dp"),
        P("dp"),
        P(None, "dp", "tensor"),
        P("tensor", "dp"),
    )
    return jax.shard_map(body, mesh=mesh, in_specs=in_specs, out_specs=out_specs, check_vma=False)
```

```python
import functools
import math

import jax
import jax.numpy as jnp
from jax import lax
from jax.experimental import pallas as pl
from jax.experimental.pallas import tpu as pltpu
from jax.sharding import PartitionSpec as P

HEAD = 64
WINDOW = 128
NSEQ = 4
HALF = WINDOW // 2
PAD = 16
BLOCK = 128
LANES = 128
KEYS = BLOCK + WINDOW

norm_eps = 1e-05
f32 = jnp.float32
bf16 = jnp.bfloat16

NN = (((1,), (0,)), ((), ()))
NT = (((1,), (1,)), ((), ()))
TN = (((0,), (0,)), ((), ()))


def dot(a, b, dims=NN):
    return lax.dot_general(a, b, dims, preferred_element_type=f32)


def step_of(rows, most):
    best = LANES
    for size in range(LANES, most + 1, LANES):
        if rows % size == 0:
            best = size
    return best


def call(kernel, out_shape, args, flops, name, scalars=()):
    vmem = pl.BlockSpec(memory_space=pltpu.VMEM)
    smem = pl.BlockSpec(memory_space=pltpu.SMEM)
    moved = sum(x.size * x.dtype.itemsize for x in (*args, *out_shape))
    held = sum(math.prod(x.shape) * jnp.dtype(x.dtype).itemsize for x in kernel[1])
    limit = min(56 * 2**20, (moved + held) * 9 // 8 + 8 * 2**20)
    return pl.pallas_call(
        kernel[0],
        out_shape=out_shape,
        in_specs=[smem] * len(scalars) + [vmem] * len(args),
        out_specs=[vmem] * len(out_shape),
        scratch_shapes=kernel[1],
        compiler_params=pltpu.CompilerParams(vmem_limit_bytes=limit),
        cost_estimate=pl.CostEstimate(flops=flops, bytes_accessed=moved, transcendentals=0),
        name=name,
    )(*scalars, *args)


def shape(dims, dtype):
    return jax.ShapeDtypeStruct(dims, dtype)


def normed(values):
    centered = values - jnp.mean(values, axis=-1, keepdims=True)
    spread = jnp.mean(centered * centered, axis=-1, keepdims=True)
    scale = lax.rsqrt(spread + norm_eps)
    return centered * scale, scale


def norm_back(grad, gain, hat, scale):
    inner = grad * gain
    one = jnp.mean(inner, axis=-1, keepdims=True)
    two = jnp.mean(inner * hat, axis=-1, keepdims=True)
    return scale * (inner - one - hat * two)


def turned(values, low):
    return jnp.where(low, pltpu.roll(values, LANES - HEAD // 2, 1), pltpu.roll(values, HEAD // 2, 1))


def halves(values):
    even = (lax.broadcasted_iota(jnp.int32, (1, LANES), 1) < HEAD).astype(f32).astype(bf16)
    return jnp.concatenate([values * even, values * (1 - even)], axis=0)


def joined(values):
    return jnp.concatenate([values[:HEAD, :BLOCK], values[HEAD:, BLOCK:]], axis=0).T


def stack_weight(src, index, dst):
    parts, _, depth, _ = src.shape
    for part in range(parts):
        dst[part * depth : (part + 1) * depth, :] = src[part, index]


def loop(count, body):
    def run(index, carry):
        body(index)
        return carry

    lax.fori_loop(0, count, run, 0)


def attend_kernel(
    bounds, slots, tokens, before, after, cosine, sine, *rest
):
    pieces, (wide, gain, first, query, key, value, shares, attended, branch) = rest[:-9], rest[-9:]
    rows, width = tokens.shape
    extent, local = key.shape
    pairs = local // LANES
    groups = len(pieces)
    depth = width // groups
    lane = lax.broadcasted_iota(jnp.int32, (LANES, width), 1) - lax.broadcasted_iota(jnp.int32, (LANES, width), 0)
    gain_sum = jnp.zeros((PAD, width), f32)
    for number, piece in enumerate(pieces):
        place = pl.multiple_of(slots[number] * depth, depth)
        for part in range(4):
            wide[pl.ds(place, depth), part * local : (part + 1) * local] = piece[part * depth : (part + 1) * depth, :]
        spread = jnp.where(lane == place, 1.0, 0.0).astype(bf16)
        gain_sum += dot(piece[4 * depth :, :LANES], spread)
    gain[...] = gain_sum
    gains = gain_sum[:1]
    query_w, key_w, value_w, out_t = (wide.at[:, part * local : (part + 1) * local] for part in range(4))

    def norm_rows(src, dst, size):
        hat, _ = normed(src.astype(f32))
        first[pl.ds(dst, size), :] = (hat * gains).astype(bf16)

    norm_rows(before[...], 0, HALF)
    norm_rows(after[...], rows + HALF, HALF)

    def norm_step(index):
        at = pl.multiple_of(index * BLOCK, BLOCK)
        norm_rows(tokens[pl.ds(at, BLOCK), :], at + HALF, BLOCK)

    loop(rows // BLOCK, norm_step)
    low = lax.broadcasted_iota(jnp.int32, (1, LANES), 1) % HEAD < HEAD // 2

    def rotated(src, at, size, dst, place, scale):
        co, si = cosine[pl.ds(at, size), :], sine[pl.ds(at, size), :]
        for pair in range(pairs):
            lanes = slice(pair * LANES, (pair + 1) * LANES)
            part = src[:, lanes]
            dst[pl.ds(place, size), lanes] = ((part * co + turned(part, low) * si) * scale).astype(bf16)

    chunk = step_of(extent, 384)

    def key_step(index):
        at = pl.multiple_of(index * chunk, chunk)
        part = first[pl.ds(at, chunk), :]
        rotated(dot(part, key_w[...]), at, chunk, key, at, 1.0)
        value[pl.ds(at, chunk), :] = dot(part, value_w[...]).astype(bf16)

    loop(extent // chunk, key_step)
    size = step_of(rows, 256)

    def query_step(index):
        at = pl.multiple_of(index * size, size)
        start = pl.multiple_of(at + HALF, HALF)
        rotated(dot(first[pl.ds(start, size), :], query_w[...]), start, size, query, at, HEAD**-0.5)

    loop(rows // size, query_step)
    key_at = lax.broadcasted_iota(jnp.int32, (KEYS, KEYS), 0)
    lane_at = lax.broadcasted_iota(jnp.int32, (1, KEYS), 1) % BLOCK

    def attend_step(index):
        at = pl.multiple_of(index * BLOCK, BLOCK)
        origin = bounds[NSEQ] + at - HALF
        own = lane_at + (origin + HALF)
        begin = jnp.zeros_like(own)
        end = jnp.zeros_like(own) + bounds[NSEQ - 1]
        for number in range(NSEQ - 1):
            begin = jnp.where(own >= bounds[number], bounds[number], begin)
        for number in reversed(range(NSEQ - 1)):
            end = jnp.where(own < bounds[number], bounds[number], end)
        least = jnp.maximum(lane_at, begin - origin)
        most = jnp.minimum(lane_at + WINDOW, end - 1 - origin)
        bias = jnp.where((key_at >= least) & (key_at <= most), 0.0, -1e30)
        for pair in range(pairs):
            lanes = slice(pair * LANES, (pair + 1) * LANES)
            both = halves(query[pl.ds(at, BLOCK), lanes])
            scores = dot(key[pl.ds(at, KEYS), lanes], both, NT) + bias
            weight = jnp.exp(scores - jnp.max(scores, axis=0, keepdims=True))
            part = (weight * (1.0 / jnp.sum(weight, axis=0, keepdims=True))).astype(bf16)
            shares[index * pairs + pair] = part
            mixed = dot(value[pl.ds(at, KEYS), lanes], part, TN)
            attended[pl.ds(at, BLOCK), lanes] = joined(mixed).astype(bf16)

    loop(rows // BLOCK, attend_step)

    def out_step(index):
        at = pl.multiple_of(index * size, size)
        branch[pl.ds(at, size), :] = dot(attended[pl.ds(at, size), :], out_t[...], NT).astype(bf16)

    loop(rows // size, out_step)


def feed_kernel(
    tokens, own, other, gain, weights, cotangent,
    middle, second, hidden, grad_gate, grad_upper, partial,
    gate_w, upper_w, down_t,
):
    rows, width = tokens.shape
    stack_weight(weights, 0, gate_w)
    stack_weight(weights, 1, upper_w)
    stack_weight(weights, 2, down_t)
    gains = gain[1:2, :]
    size = step_of(rows, 256)

    def step(index):
        at = pl.multiple_of(index * size, size)
        here = pl.ds(at, size)
        mid = tokens[here, :].astype(f32) + (own[here, :].astype(f32) + other[here, :].astype(f32))
        middle[here, :] = mid
        hat, _ = normed(mid)
        low = (hat * gains).astype(bf16)
        second[here, :] = low
        gate = dot(low, gate_w[...])
        upper = dot(low, upper_w[...])
        grad = dot(cotangent[here, :], down_t[...])
        share = 0.5 * (1.0 + lax.erf(gate * (0.5**0.5)))
        smooth = gate * share
        slope = share + gate * (jnp.exp(gate * gate * -0.5) * ((2.0 * math.pi) ** -0.5))
        hidden[here, :] = (smooth * upper).astype(bf16)
        gate_low = (grad * upper * slope).astype(bf16)
        upper_low = (grad * smooth).astype(bf16)
        grad_gate[here, :] = gate_low
        grad_upper[here, :] = upper_low
        partial[here, :] = (dot(gate_low, gate_w[...], NT) + dot(upper_low, upper_w[...], NT)).astype(bf16)

    loop(rows // size, step)


def weight_kernel(second, hidden, grad_gate, grad_upper, cotangent, weights, feed, grads, down_t, total):
    rows, width = second.shape
    stack_weight(weights, 2, down_t)
    size = step_of(rows, 256)

    def step(index):
        here = pl.ds(pl.multiple_of(index * size, size), size)
        feed[here, :] = dot(hidden[here, :], down_t[...], NT).astype(bf16)

    loop(rows // size, step)
    scatter_grads(second, grad_gate, grads, 0, total)
    scatter_grads(second, grad_upper, grads, 1, total)
    scatter_grads(cotangent, hidden, grads, 2, total)


def scatter_grads(left, right, grads, number, total, slots=None):
    width = left.shape[-1]
    parts, _, depth, _ = grads.shape
    for start in range(0, width, 2 * LANES):
        total[start : start + 2 * LANES, :] = dot(left[:, start : start + 2 * LANES], right[...], TN).astype(bf16)
    for part in range(parts):
        place = part * depth if slots is None else pl.multiple_of(slots[part] * depth, depth)
        grads[part, number] = total[pl.ds(place, depth), :]


def back_kernel(
    slots, middle, own, other, gain, cotangent, wide, first, query, key, value, shares, attended, cosine, sine,
    grad_middle, grad_proj, grads,
    low_mid, grad_att, grad_key, grad_value, total,
):
    rows, width = middle.shape
    extent, local = key.shape
    pairs = local // LANES
    out_t = wide.at[:, 3 * local :]
    gains = gain[1:2, :]
    size = step_of(rows, 256)

    def norm_step(index):
        here = pl.ds(pl.multiple_of(index * size, size), size)
        hat, scale = normed(middle[here, :])
        grad = own[here, :].astype(f32) + other[here, :].astype(f32)
        mid = cotangent[here, :].astype(f32) + norm_back(grad, gains, hat, scale)
        grad_middle[here, :] = mid
        mid_low = mid.astype(bf16)
        low_mid[here, :] = mid_low
        grad_att[here, :] = dot(mid_low, out_t[...]).astype(bf16)

    loop(rows // size, norm_step)
    grad_key[...] = jnp.zeros_like(grad_key)
    grad_value[...] = jnp.zeros_like(grad_value)
    low = lax.broadcasted_iota(jnp.int32, (1, LANES), 1) % HEAD < HEAD // 2
    zero = jnp.zeros((HALF, local), bf16)
    grad_proj[:HALF, :local] = zero
    grad_proj[rows + HALF :, :local] = zero

    def attend_step(index):
        at = pl.multiple_of(index * BLOCK, BLOCK)
        start = pl.multiple_of(at + HALF, HALF)
        co, si = cosine[pl.ds(start, BLOCK), :], sine[pl.ds(start, BLOCK), :]
        for pair in range(pairs):
            lanes = slice(pair * LANES, (pair + 1) * LANES)
            both = halves(query[pl.ds(at, BLOCK), lanes])
            grad = halves(grad_att[pl.ds(at, BLOCK), lanes])
            keys = key[pl.ds(at, KEYS), lanes]
            part = shares[index * pairs + pair]
            wide = part.astype(f32)
            grad_shares = dot(value[pl.ds(at, KEYS), lanes], grad, NT)
            delta = jnp.sum(wide * grad_shares, axis=0, keepdims=True)
            raw = (wide * (grad_shares - delta)).astype(bf16)
            grad_key[pl.ds(at, KEYS), lanes] += dot(raw, both)
            grad_value[pl.ds(at, KEYS), lanes] += dot(part, grad)
            grad_query = joined(dot(keys, raw, TN)) * HEAD**-0.5
            grad_proj[pl.ds(start, BLOCK), lanes] = (grad_query * co - turned(grad_query, low) * si).astype(bf16)

    loop(rows // BLOCK, attend_step)

    def turn_step(index):
        at = pl.multiple_of(index * BLOCK, BLOCK)
        here = pl.ds(at, BLOCK)
        co, si = cosine[here, :], sine[here, :]
        for pair in range(pairs):
            lanes = slice(pair * LANES, (pair + 1) * LANES)
            part = grad_key[here, lanes]
            turn = slice(local + pair * LANES, local + (pair + 1) * LANES)
            grad_proj[here, turn] = (part * co - turned(part, low) * si).astype(bf16)
        grad_proj[here, 2 * local :] = grad_value[here, :].astype(bf16)

    loop(extent // BLOCK, turn_step)
    for number in range(3):
        part = grad_proj.at[:, number * local : (number + 1) * local]
        scatter_grads(first, part, grads, number, total, slots)
    scatter_grads(low_mid, attended, grads, 3, total, slots)


def first_kernel(grad_proj, wide, partial):
    extent, inner = grad_proj.shape
    size = step_of(extent, 384)

    def step(index):
        here = pl.ds(pl.multiple_of(index * size, size), size)
        partial[here, :] = dot(grad_proj[here, :], wide[:, :inner], NT).astype(bf16)

    loop(extent // size, step)


def final_kernel(tokens, gain, grad_middle, own, other, before, after, middle, feed_own, feed_other, mixed, token_grad):
    rows, width = tokens.shape
    gains = gain[:1, :]
    size = BLOCK

    def back(here, grad):
        hat, scale = normed(tokens[here, :].astype(f32))
        return norm_back(grad, gains, hat, scale)

    def step(index):
        at = pl.multiple_of(index * size, size)
        here, wider = pl.ds(at, size), pl.ds(pl.multiple_of(at + HALF, HALF), size)
        grad = own[wider, :].astype(f32) + other[wider, :].astype(f32)
        token_grad[here, :] = grad_middle[here, :] + back(here, grad)
        feed = feed_own[here, :].astype(f32) + feed_other[here, :].astype(f32)
        mixed[here, :] = (middle[here, :] + feed).astype(bf16)

    loop(rows // size, step)
    for start, edge in ((0, before), (rows - HALF, after)):
        here = pl.ds(start, HALF)
        token_grad[here, :] += back(here, edge[...].astype(f32))


def exchange(initial, last):
    devices, spot = lax.axis_size("ctx"), lax.axis_index("ctx")
    if devices == 2:
        got = lax.ppermute(jnp.where(spot == 0, last, initial), "ctx", [(0, 1), (1, 0)])
        none = jnp.zeros_like(got)
        return jnp.where(spot == 1, got, none), jnp.where(spot == 0, got, none)
    up = [(i, i + 1) for i in range(devices - 1)]
    return lax.ppermute(last, "ctx", up), lax.ppermute(initial, "ctx", [(j, i) for i, j in up])


def swap(array, axis="tensor"):
    return lax.ppermute(array, axis, [(0, 1), (1, 0)])


def over_ctx(array):
    if lax.axis_size("ctx") == 2:
        return array.astype(f32) + swap(array, "ctx").astype(f32)
    return lax.psum(array, "ctx").astype(f32)


def ring():
    count = lax.axis_size("dp")
    order = [2 * i for i in range(count // 2)] + [2 * i + 1 for i in reversed(range(count // 2))]
    ahead = [(order[i], order[(i + 1) % count]) for i in range(count)]
    back = [(j, i) for i, j in ahead]
    index = lax.axis_index("dp")
    spot = jnp.where(index % 2 == 0, index // 2, count - 1 - index // 2)
    place = (spot + jnp.arange(count, dtype=jnp.int32)) % count
    slots = jnp.where(place < count // 2, 2 * place, 2 * (count - 1 - place) + 1)
    return count, ahead, back, slots.astype(jnp.int32)


def ring_gather(mine):
    count, ahead, back, _ = ring()
    middle = count // 2
    half = mine.shape[0] // 2
    pieces = {0: mine}
    one = two = mine
    for hop in range(1, middle):
        one, two = lax.ppermute(one, "dp", ahead), lax.ppermute(two, "dp", back)
        pieces[count - hop], pieces[hop] = one, two
    pieces[middle] = jnp.concatenate(
        [lax.ppermute(one[:half], "dp", ahead), lax.ppermute(two[half:], "dp", back)]
    )
    return [pieces[i] for i in range(count)]


def ring_scatter(parts):
    count, ahead, back, _ = ring()
    middle = count // 2
    half = parts.shape[1] // 2
    one = lax.ppermute(parts[middle, :half], "dp", ahead)
    two = lax.ppermute(parts[middle, half:], "dp", back)
    none = jnp.zeros_like(one)
    one, two = jnp.concatenate([one, none]), jnp.concatenate([none, two])
    for hop in range(middle - 1, 0, -1):
        one = lax.ppermute(parts[hop] + one, "dp", ahead)
        two = lax.ppermute(parts[count - hop] + two, "dp", back)
    return (parts[0].astype(f32) + one.astype(f32) + two.astype(f32)).astype(bf16)


def tables(lengths, rows):
    place = lax.axis_index("ctx") * rows
    ends = jnp.cumsum(lengths[0])
    starts = ends - lengths[0]
    span = place + jnp.arange(-HALF, rows + HALF, dtype=jnp.int32)
    inside = (span[:, None] >= starts[None, :]) & (span[:, None] < ends[None, :])
    position = span - jnp.sum(jnp.where(inside, starts[None, :], 0), axis=1)
    number = (jnp.arange(HEAD, dtype=jnp.int32) % (HEAD // 2)).astype(f32)
    freq = jnp.exp(number * (-2.0 * math.log(10000.0) / HEAD))
    angle = position.astype(f32)[:, None] * freq[None, :]
    cosine, sine = jnp.cos(angle), jnp.sin(angle)
    sine = jnp.where(jnp.arange(HEAD)[None, :] < HEAD // 2, -sine, sine)
    bounds = jnp.concatenate([ends, place[None]]).astype(jnp.int32)
    return jnp.tile(cosine, (1, 2)), jnp.tile(sine, (1, 2)), bounds


def body(tokens, lengths, gain_one, w_qkv, w_out, gain_two, w_in, w_down, cotangent):
    rows, width = tokens.shape
    local, units = w_out.shape[0], w_down.shape[0]
    pairs, blocks, extent = local // LANES, rows // BLOCK, rows + WINDOW
    groups = lax.axis_size("dp")
    depth = width // groups
    gains = jnp.pad(jnp.stack([gain_one, gain_two]), ((0, PAD - 2), (0, local - depth)))
    mine_one = jnp.concatenate([w_qkv.reshape(3 * depth, local), w_out.T, gains])
    mine_two = jnp.concatenate([w_in, w_down.T[None]])
    pieces = ring_gather(mine_one)
    slots = ring()[-1]
    weights_two = lax.all_gather(mine_two, "dp", axis=0, tiled=False)
    before, after = exchange(tokens[:HALF], tokens[rows - HALF :])
    cosine, sine, bounds = tables(lengths, rows)

    wide, gain, first, query, key, value, shares, attended, branch = call(
        (attend_kernel, []),
        [
            shape((width, 4 * local), bf16),
            shape((PAD, width), f32),
            shape((extent, width), bf16),
            shape((rows, local), bf16),
            shape((extent, local), bf16),
            shape((extent, local), bf16),
            shape((blocks * pairs, KEYS, KEYS), bf16),
            shape((rows, local), bf16),
            shape((rows, width), bf16),
        ],
        (tokens, before, after, cosine, sine, *pieces),
        2 * rows * width * local * 5,
        "project_and_attend",
        (bounds, slots),
    )
    branch_other = swap(branch)
    plain = [pltpu.VMEM((width, units), bf16)] * 3
    middle, second, hidden, grad_gate, grad_upper, partial = call(
        (feed_kernel, plain),
        [
            shape((rows, width), f32),
            shape((rows, width), bf16),
            shape((rows, units), bf16),
            shape((rows, units), bf16),
            shape((rows, units), bf16),
            shape((rows, width), bf16),
        ],
        (tokens, branch, branch_other, gain, weights_two, cotangent),
        2 * rows * width * units * 5,
        "feed_forward_and_back",
    )
    partial_other = swap(partial)
    feed, grads_two = call(
        (weight_kernel, [pltpu.VMEM((width, units), bf16)] * 2),
        [shape((rows, width), bf16), shape((groups, 3, width // groups, units), bf16)],
        (second, hidden, grad_gate, grad_upper, cotangent, weights_two),
        2 * rows * width * units * 4,
        "feed_weight_grads",
    )
    feed_other = swap(feed)
    grad_middle, grad_proj, grads_one = call(
        (
            back_kernel,
            [
                pltpu.VMEM((rows, width), bf16),
                pltpu.VMEM((rows, local), bf16),
                pltpu.VMEM((extent, local), f32),
                pltpu.VMEM((extent, local), f32),
                pltpu.VMEM((width, local), bf16),
            ],
        ),
        [
            shape((rows, width), f32),
            shape((extent, 3 * local), bf16),
            shape((groups, 4, depth, local), bf16),
        ],
        (
            middle, partial, partial_other, gain, cotangent, wide, first, query, key, value, shares, attended,
            cosine, sine,
        ),
        2 * rows * width * local * 6,
        "attention_back",
        (slots,),
    )
    one = over_ctx(ring_scatter(grads_one.reshape(groups, 4 * depth, local))).reshape(4, depth, local)
    two = over_ctx(lax.psum_scatter(grads_two, "dp", scatter_dimension=0, tiled=False))
    first_part, = call(
        (first_kernel, []),
        [shape((extent, width), bf16)],
        (grad_proj, wide),
        2 * rows * width * local * 3,
        "first_grad",
    )
    first_other = swap(first_part)

    def edge_sum(at):
        here = slice(at, at + HALF)
        return (first_part[here].astype(f32) + first_other[here].astype(f32)).astype(bf16)

    from_before, from_after = exchange(edge_sum(0), edge_sum(rows + HALF))
    mixed, token_grad = call(
        (final_kernel, []),
        [shape((rows, width), bf16), shape((rows, width), f32)],
        (
            tokens, gain, grad_middle, first_part, first_other, from_before, from_after, middle, feed, feed_other,
        ),
        rows * width * 20,
        "token_grad",
    )
    gain_one_grad = jnp.sum(one[:3] * w_qkv.astype(f32), axis=(0, 2)) / gain_one.astype(f32)
    gain_two_grad = jnp.sum(two[:2] * w_in.astype(f32), axis=(0, 2)) / gain_two.astype(f32)
    both = jnp.stack([gain_one_grad, gain_two_grad])
    both = both + swap(both)
    return (mixed, token_grad, both[0], one[:3], one[3].T, both[1], two[:2], two[2].T)


def solution(mesh):
    in_specs = (
        P(("dp", "ctx"), None),
        P("dp", None),
        P("dp"),
        P(None, "dp", "tensor"),
        P("tensor", "dp"),
        P("dp"),
        P(None, "dp", "tensor"),
        P("tensor", "dp"),
        P(("dp", "ctx"), None),
    )
    out_specs = (
        P(("dp", "ctx"), None),
        P(("dp", "ctx"), None),
        P("dp"),
        P(None, "dp", "tensor"),
        P("tensor", "dp"),
        P("dp"),
        P(None, "dp", "tensor"),
        P("tensor", "dp"),
    )
    return jax.shard_map(body, mesh=mesh, in_specs=in_specs, out_specs=out_specs, check_vma=False)
```

```python
import functools
import math

import jax
import jax.numpy as jnp
from jax import lax
from jax.experimental import pallas as pl
from jax.experimental.pallas import tpu as pltpu
from jax.sharding import PartitionSpec as P

HEAD = 64
WINDOW = 128
NSEQ = 4
HALF = WINDOW // 2
PAD = 16
BLOCK = 128
LANES = 128
KEYS = BLOCK + WINDOW

norm_eps = 1e-05
f32 = jnp.float32
bf16 = jnp.bfloat16

NN = (((1,), (0,)), ((), ()))
NT = (((1,), (1,)), ((), ()))
TN = (((0,), (0,)), ((), ()))


def dot(a, b, dims=NN):
    return lax.dot_general(a, b, dims, preferred_element_type=f32)


def step_of(rows, most):
    best = LANES
    for size in range(LANES, most + 1, LANES):
        if rows % size == 0:
            best = size
    return best


def call(kernel, out_shape, args, flops, name, scalars=()):
    vmem = pl.BlockSpec(memory_space=pltpu.VMEM)
    smem = pl.BlockSpec(memory_space=pltpu.SMEM)
    moved = sum(x.size * x.dtype.itemsize for x in (*args, *out_shape))
    held = sum(math.prod(x.shape) * jnp.dtype(x.dtype).itemsize for x in kernel[1])
    limit = min(56 * 2**20, moved + held + 6 * 2**20)
    return pl.pallas_call(
        kernel[0],
        out_shape=out_shape,
        in_specs=[smem] * len(scalars) + [vmem] * len(args),
        out_specs=[vmem] * len(out_shape),
        scratch_shapes=kernel[1],
        compiler_params=pltpu.CompilerParams(vmem_limit_bytes=limit),
        cost_estimate=pl.CostEstimate(flops=flops, bytes_accessed=moved, transcendentals=0),
        name=name,
    )(*scalars, *args)


def shape(dims, dtype):
    return jax.ShapeDtypeStruct(dims, dtype)


def normed(values):
    centered = values - jnp.mean(values, axis=-1, keepdims=True)
    spread = jnp.mean(centered * centered, axis=-1, keepdims=True)
    scale = lax.rsqrt(spread + norm_eps)
    return centered * scale, scale


def norm_back(grad, gain, hat, scale):
    inner = grad * gain
    one = jnp.mean(inner, axis=-1, keepdims=True)
    two = jnp.mean(inner * hat, axis=-1, keepdims=True)
    return scale * (inner - one - hat * two)


def turned(values, low):
    return jnp.where(low, pltpu.roll(values, LANES - HEAD // 2, 1), pltpu.roll(values, HEAD // 2, 1))


def halves(values):
    even = (lax.broadcasted_iota(jnp.int32, (1, LANES), 1) < HEAD).astype(f32).astype(bf16)
    return jnp.concatenate([values * even, values * (1 - even)], axis=0)


def joined(values):
    return jnp.concatenate([values[:HEAD, :BLOCK], values[HEAD:, BLOCK:]], axis=0).T


def loop(count, body):
    def run(index, carry):
        body(index)
        return carry

    lax.fori_loop(0, count, run, 0)


def project_kernel(slots, tokens, before, after, cosine, sine, *rest):
    pieces, (wide, gain, first, query, key, value) = rest[:-6], rest[-6:]
    rows, width = tokens.shape
    extent, local = key.shape
    pairs = local // LANES
    groups = len(pieces)
    depth = width // groups
    lane = lax.broadcasted_iota(jnp.int32, (LANES, width), 1) - lax.broadcasted_iota(jnp.int32, (LANES, width), 0)
    gain_sum = jnp.zeros((PAD, width), f32)
    for number, piece in enumerate(pieces):
        place = pl.multiple_of(slots[number] * depth, depth)
        for part in range(4):
            wide[pl.ds(place, depth), part * local : (part + 1) * local] = piece[part * depth : (part + 1) * depth, :]
        spread = jnp.where(lane == place, 1.0, 0.0).astype(bf16)
        gain_sum += dot(piece[4 * depth :, :LANES], spread)
    gain[...] = gain_sum
    gains = gain_sum[:1]
    query_w, key_w, value_w = (wide.at[:, part * local : (part + 1) * local] for part in range(3))

    def norm_rows(src, dst, size):
        hat, _ = normed(src.astype(f32))
        first[pl.ds(dst, size), :] = (hat * gains).astype(bf16)

    norm_rows(before[...], 0, HALF)
    norm_rows(after[...], rows + HALF, HALF)

    def norm_step(index):
        at = pl.multiple_of(index * BLOCK, BLOCK)
        norm_rows(tokens[pl.ds(at, BLOCK), :], at + HALF, BLOCK)

    loop(rows // BLOCK, norm_step)
    low = lax.broadcasted_iota(jnp.int32, (1, LANES), 1) % HEAD < HEAD // 2

    def rotated(src, at, size, dst, place, scale):
        co, si = cosine[pl.ds(at, size), :], sine[pl.ds(at, size), :]
        for pair in range(pairs):
            lanes = slice(pair * LANES, (pair + 1) * LANES)
            part = src[:, lanes]
            dst[pl.ds(place, size), lanes] = ((part * co + turned(part, low) * si) * scale).astype(bf16)

    chunk = step_of(extent, 384)

    def key_step(index):
        at = pl.multiple_of(index * chunk, chunk)
        part = first[pl.ds(at, chunk), :]
        rotated(dot(part, key_w[...]), at, chunk, key, at, 1.0)
        value[pl.ds(at, chunk), :] = dot(part, value_w[...]).astype(bf16)

    loop(extent // chunk, key_step)
    size = step_of(rows, 256)

    def query_step(index):
        at = pl.multiple_of(index * size, size)
        start = pl.multiple_of(at + HALF, HALF)
        rotated(dot(first[pl.ds(start, size), :], query_w[...]), start, size, query, at, HEAD**-0.5)

    loop(rows // size, query_step)


def attend_kernel(bounds, query, key, value, wide, shares, attended, branch):
    rows, local = query.shape
    pairs = local // LANES
    out_t = wide.at[:, 3 * local :]
    size = step_of(rows, 256)
    key_at = lax.broadcasted_iota(jnp.int32, (KEYS, KEYS), 0)
    lane_at = lax.broadcasted_iota(jnp.int32, (1, KEYS), 1) % BLOCK

    def attend_step(index):
        at = pl.multiple_of(index * BLOCK, BLOCK)
        origin = bounds[NSEQ] + at - HALF
        own = lane_at + (origin + HALF)
        begin = jnp.zeros_like(own)
        end = jnp.zeros_like(own) + bounds[NSEQ - 1]
        for number in range(NSEQ - 1):
            begin = jnp.where(own >= bounds[number], bounds[number], begin)
        for number in reversed(range(NSEQ - 1)):
            end = jnp.where(own < bounds[number], bounds[number], end)
        least = jnp.maximum(lane_at, begin - origin)
        most = jnp.minimum(lane_at + WINDOW, end - 1 - origin)
        bias = jnp.where((key_at >= least) & (key_at <= most), 0.0, -1e30)
        for pair in range(pairs):
            lanes = slice(pair * LANES, (pair + 1) * LANES)
            both = halves(query[pl.ds(at, BLOCK), lanes])
            scores = dot(key[pl.ds(at, KEYS), lanes], both, NT) + bias
            weight = jnp.exp(scores - jnp.max(scores, axis=0, keepdims=True))
            part = (weight * (1.0 / jnp.sum(weight, axis=0, keepdims=True))).astype(bf16)
            shares[index * pairs + pair] = part
            mixed = dot(value[pl.ds(at, KEYS), lanes], part, TN)
            attended[pl.ds(at, BLOCK), lanes] = joined(mixed).astype(bf16)

    loop(rows // BLOCK, attend_step)

    def out_step(index):
        at = pl.multiple_of(index * size, size)
        branch[pl.ds(at, size), :] = dot(attended[pl.ds(at, size), :], out_t[...], NT).astype(bf16)

    loop(rows // size, out_step)


def feed_kernel(slots, tokens, own, other, gain, cotangent, *rest):
    pieces, rest = rest[:-9], rest[-9:]
    middle, second, hidden, grad_gate, grad_upper, partial, down_t, gate_w, upper_w = rest
    rows, width = tokens.shape
    depth = width // len(pieces)
    for number, piece in enumerate(pieces):
        place = pl.ds(pl.multiple_of(slots[number] * depth, depth), depth)
        for part, whole in enumerate((gate_w, upper_w, down_t)):
            whole[place, :] = piece[part * depth : (part + 1) * depth, :]
    gains = gain[1:2, :]
    size = step_of(rows, 256)

    def step(index):
        at = pl.multiple_of(index * size, size)
        here = pl.ds(at, size)
        mid = tokens[here, :].astype(f32) + (own[here, :].astype(f32) + other[here, :].astype(f32))
        middle[here, :] = mid
        hat, _ = normed(mid)
        low = (hat * gains).astype(bf16)
        second[here, :] = low
        gate = dot(low, gate_w[...])
        upper = dot(low, upper_w[...])
        grad = dot(cotangent[here, :], down_t[...])
        share = 0.5 * (1.0 + lax.erf(gate * (0.5**0.5)))
        smooth = gate * share
        slope = share + gate * (jnp.exp(gate * gate * -0.5) * ((2.0 * math.pi) ** -0.5))
        hidden[here, :] = (smooth * upper).astype(bf16)
        gate_low = (grad * upper * slope).astype(bf16)
        upper_low = (grad * smooth).astype(bf16)
        grad_gate[here, :] = gate_low
        grad_upper[here, :] = upper_low
        partial[here, :] = (dot(gate_low, gate_w[...], NT) + dot(upper_low, upper_w[...], NT)).astype(bf16)

    loop(rows // size, step)


def weight_kernel(slots, second, hidden, grad_gate, grad_upper, cotangent, down_t, feed, grads, total):
    rows, width = second.shape
    size = step_of(rows, 256)

    def step(index):
        here = pl.ds(pl.multiple_of(index * size, size), size)
        feed[here, :] = dot(hidden[here, :], down_t[...], NT).astype(bf16)

    loop(rows // size, step)
    scatter_grads(second, grad_gate, grads, 0, total, slots)
    scatter_grads(second, grad_upper, grads, 1, total, slots)
    scatter_grads(cotangent, hidden, grads, 2, total, slots)


def scatter_grads(left, right, grads, number, total, slots):
    width = left.shape[-1]
    parts = grads.shape[0]
    depth = width // parts
    for start in range(0, width, 2 * LANES):
        total[start : start + 2 * LANES, :] = dot(left[:, start : start + 2 * LANES], right[...], TN).astype(bf16)
    for part in range(parts):
        place = pl.ds(pl.multiple_of(slots[part] * depth, depth), depth)
        grads[part, number * depth : (number + 1) * depth, :] = total[place, :]


def middle_kernel(middle, own, other, gain, cotangent, wide, grad_middle, low_mid, grad_att):
    rows, width = middle.shape
    local = grad_att.shape[1]
    out_t = wide.at[:, 3 * local :]
    gains = gain[1:2, :]
    size = step_of(rows, 256)

    def norm_step(index):
        here = pl.ds(pl.multiple_of(index * size, size), size)
        hat, scale = normed(middle[here, :])
        grad = own[here, :].astype(f32) + other[here, :].astype(f32)
        mid = cotangent[here, :].astype(f32) + norm_back(grad, gains, hat, scale)
        grad_middle[here, :] = mid
        mid_low = mid.astype(bf16)
        low_mid[here, :] = mid_low
        grad_att[here, :] = dot(mid_low, out_t[...]).astype(bf16)

    loop(rows // size, norm_step)


def back_kernel(query, key, value, shares, grad_att, cosine, sine, grad_proj, grad_key, grad_value):
    rows, local = query.shape
    extent = key.shape[0]
    pairs = local // LANES
    grad_key[...] = jnp.zeros_like(grad_key)
    grad_value[...] = jnp.zeros_like(grad_value)
    low = lax.broadcasted_iota(jnp.int32, (1, LANES), 1) % HEAD < HEAD // 2
    zero = jnp.zeros((HALF, local), bf16)
    grad_proj[:HALF, :local] = zero
    grad_proj[rows + HALF :, :local] = zero

    def attend_step(index):
        at = pl.multiple_of(index * BLOCK, BLOCK)
        start = pl.multiple_of(at + HALF, HALF)
        co, si = cosine[pl.ds(start, BLOCK), :], sine[pl.ds(start, BLOCK), :]
        for pair in range(pairs):
            lanes = slice(pair * LANES, (pair + 1) * LANES)
            both = halves(query[pl.ds(at, BLOCK), lanes])
            grad = halves(grad_att[pl.ds(at, BLOCK), lanes])
            keys = key[pl.ds(at, KEYS), lanes]
            part = shares[index * pairs + pair]
            wide = part.astype(f32)
            grad_shares = dot(value[pl.ds(at, KEYS), lanes], grad, NT)
            delta = jnp.sum(wide * grad_shares, axis=0, keepdims=True)
            raw = (wide * (grad_shares - delta)).astype(bf16)
            grad_key[pl.ds(at, KEYS), lanes] += dot(raw, both)
            grad_value[pl.ds(at, KEYS), lanes] += dot(part, grad)
            grad_query = joined(dot(keys, raw, TN)) * HEAD**-0.5
            grad_proj[pl.ds(start, BLOCK), lanes] = (grad_query * co - turned(grad_query, low) * si).astype(bf16)

    loop(rows // BLOCK, attend_step)

    def turn_step(index):
        at = pl.multiple_of(index * BLOCK, BLOCK)
        here = pl.ds(at, BLOCK)
        co, si = cosine[here, :], sine[here, :]
        for pair in range(pairs):
            lanes = slice(pair * LANES, (pair + 1) * LANES)
            part = grad_key[here, lanes]
            turn = slice(local + pair * LANES, local + (pair + 1) * LANES)
            grad_proj[here, turn] = (part * co - turned(part, low) * si).astype(bf16)
        grad_proj[here, 2 * local :] = grad_value[here, :].astype(bf16)

    loop(extent // BLOCK, turn_step)


def grad_kernel(slots, first, grad_proj, low_mid, attended, grads, total):
    local = attended.shape[1]
    for number in range(3):
        part = grad_proj.at[:, number * local : (number + 1) * local]
        scatter_grads(first, part, grads, number, total, slots)
    scatter_grads(low_mid, attended, grads, 3, total, slots)


def first_kernel(grad_proj, wide, partial):
    extent, inner = grad_proj.shape
    size = step_of(extent, 384)

    def step(index):
        here = pl.ds(pl.multiple_of(index * size, size), size)
        partial[here, :] = dot(grad_proj[here, :], wide[:, :inner], NT).astype(bf16)

    loop(extent // size, step)


def final_kernel(tokens, gain, grad_middle, own, other, before, after, middle, feed_own, feed_other, mixed, token_grad):
    rows, width = tokens.shape
    gains = gain[:1, :]
    size = BLOCK

    def back(here, grad):
        hat, scale = normed(tokens[here, :].astype(f32))
        return norm_back(grad, gains, hat, scale)

    def step(index):
        at = pl.multiple_of(index * size, size)
        here, wider = pl.ds(at, size), pl.ds(pl.multiple_of(at + HALF, HALF), size)
        grad = own[wider, :].astype(f32) + other[wider, :].astype(f32)
        token_grad[here, :] = grad_middle[here, :] + back(here, grad)
        feed = feed_own[here, :].astype(f32) + feed_other[here, :].astype(f32)
        mixed[here, :] = (middle[here, :] + feed).astype(bf16)

    loop(rows // size, step)
    for start, edge in ((0, before), (rows - HALF, after)):
        here = pl.ds(start, HALF)
        token_grad[here, :] += back(here, edge[...].astype(f32))


def exchange(initial, last):
    devices, spot = lax.axis_size("ctx"), lax.axis_index("ctx")
    if devices == 2:
        got = lax.ppermute(jnp.where(spot == 0, last, initial), "ctx", [(0, 1), (1, 0)])
        none = jnp.zeros_like(got)
        return jnp.where(spot == 1, got, none), jnp.where(spot == 0, got, none)
    up = [(i, i + 1) for i in range(devices - 1)]
    return lax.ppermute(last, "ctx", up), lax.ppermute(initial, "ctx", [(j, i) for i, j in up])


def swap(array, axis="tensor"):
    return lax.ppermute(array, axis, [(0, 1), (1, 0)])


def over_ctx(array):
    if lax.axis_size("ctx") == 2:
        return array.astype(f32) + swap(array, "ctx").astype(f32)
    return lax.psum(array, "ctx").astype(f32)


def ring():
    count = lax.axis_size("dp")
    order = [2 * i for i in range(count // 2)] + [2 * i + 1 for i in reversed(range(count // 2))]
    ahead = [(order[i], order[(i + 1) % count]) for i in range(count)]
    back = [(j, i) for i, j in ahead]
    index = lax.axis_index("dp")
    spot = jnp.where(index % 2 == 0, index // 2, count - 1 - index // 2)
    place = (spot + jnp.arange(count, dtype=jnp.int32)) % count
    slots = jnp.where(place < count // 2, 2 * place, 2 * (count - 1 - place) + 1)
    return count, ahead, back, slots.astype(jnp.int32)


def tied(values, others):
    held = lax.optimization_barrier((tuple(values), tuple(others)))
    return held[0]


def locked(values, chain):
    held = lax.optimization_barrier((tuple(values), tuple(chain.state)))
    chain.state = held[1]
    return held[0]


class RingGather:
    def __init__(self, mine):
        self.count, self.ahead, self.back, _ = ring()
        self.pieces = {0: mine}
        self.state = (mine, mine)
        self.hops = 0

    def hop(self):
        self.hops += 1
        one, two = self.state
        middle = self.count // 2
        half = one.shape[0] // 2
        if self.hops == middle:
            one, two = one[:half], two[half:]
        one, two = lax.ppermute(one, "dp", self.ahead), lax.ppermute(two, "dp", self.back)
        self.state = (one, two)
        if self.hops == middle:
            self.pieces[middle] = jnp.concatenate([one, two])
        else:
            self.pieces[self.count - self.hops], self.pieces[self.hops] = one, two

    def finish(self):
        while self.hops < self.count // 2:
            self.hop()
        return [self.pieces[i] for i in range(self.count)]


class RingScatter:
    def __init__(self, parts):
        self.count, self.ahead, self.back, _ = ring()
        self.parts = parts
        self.hops = 0
        self.state = ()

    def hop(self):
        middle = self.count // 2
        parts = self.parts
        half = parts.shape[1] // 2
        if self.hops == 0:
            one, two = parts[middle, :half], parts[middle, half:]
        else:
            one, two = self.state
            if self.hops == 1:
                none = jnp.zeros_like(one)
                one, two = jnp.concatenate([one, none]), jnp.concatenate([none, two])
            at = middle - self.hops
            one, two = parts[at] + one, parts[self.count - at] + two
        self.state = (lax.ppermute(one, "dp", self.ahead), lax.ppermute(two, "dp", self.back))
        self.hops += 1

    def finish(self):
        while self.hops < self.count // 2:
            self.hop()
        one, two = self.state
        return (self.parts[0].astype(f32) + one.astype(f32) + two.astype(f32)).astype(bf16)


def tables(lengths, rows):
    place = lax.axis_index("ctx") * rows
    ends = jnp.cumsum(lengths[0])
    starts = ends - lengths[0]
    span = place + jnp.arange(-HALF, rows + HALF, dtype=jnp.int32)
    inside = (span[:, None] >= starts[None, :]) & (span[:, None] < ends[None, :])
    position = span - jnp.sum(jnp.where(inside, starts[None, :], 0), axis=1)
    number = (jnp.arange(HEAD, dtype=jnp.int32) % (HEAD // 2)).astype(f32)
    freq = jnp.exp(number * (-2.0 * math.log(10000.0) / HEAD))
    angle = position.astype(f32)[:, None] * freq[None, :]
    cosine, sine = jnp.cos(angle), jnp.sin(angle)
    sine = jnp.where(jnp.arange(HEAD)[None, :] < HEAD // 2, -sine, sine)
    bounds = jnp.concatenate([ends, place[None]]).astype(jnp.int32)
    return jnp.tile(cosine, (1, 2)), jnp.tile(sine, (1, 2)), bounds


def body(tokens, lengths, gain_one, w_qkv, w_out, gain_two, w_in, w_down, cotangent):
    rows, width = tokens.shape
    local, units = w_out.shape[0], w_down.shape[0]
    pairs, blocks, extent = local // LANES, rows // BLOCK, rows + WINDOW
    groups = lax.axis_size("dp")
    depth = width // groups
    gains = jnp.pad(jnp.stack([gain_one, gain_two]), ((0, PAD - 2), (0, local - depth)))
    mine_one = jnp.concatenate([w_qkv.reshape(3 * depth, local), w_out.T, gains])
    mine_two = jnp.concatenate([w_in.reshape(2 * depth, units), w_down.T])
    pieces = RingGather(mine_one).finish()
    slots = ring()[-1]
    later = RingGather(tied([mine_two], pieces)[0])
    later.hop()
    before, after = exchange(tokens[:HALF], tokens[rows - HALF :])
    cosine, sine, bounds = tables(lengths, rows)

    wide, gain, first, query, key, value = call(
        (project_kernel, []),
        [
            shape((width, 4 * local), bf16),
            shape((PAD, width), f32),
            shape((extent, width), bf16),
            shape((rows, local), bf16),
            shape((extent, local), bf16),
            shape((extent, local), bf16),
        ],
        (tokens, before, after, cosine, sine, *pieces),
        2 * rows * width * local * 5,
        "project",
        (slots,),
    )
    query, key, value = tied([query, key, value], later.state)
    later.hop()
    shares, attended, branch = call(
        (attend_kernel, []),
        [
            shape((blocks * pairs, KEYS, KEYS), bf16),
            shape((rows, local), bf16),
            shape((rows, width), bf16),
        ],
        (query, key, value, wide),
        2 * rows * width * local * 10,
        "attend",
        (bounds,),
    )
    branch, = tied([branch], later.state)
    branch_other = swap(branch)
    pieces_two = later.finish()
    middle, second, hidden, grad_gate, grad_upper, partial, down_t = call(
        (feed_kernel, [pltpu.VMEM((width, units), bf16)] * 2),
        [
            shape((rows, width), f32),
            shape((rows, width), bf16),
            shape((rows, units), bf16),
            shape((rows, units), bf16),
            shape((rows, units), bf16),
            shape((rows, width), bf16),
            shape((width, units), bf16),
        ],
        (tokens, branch, branch_other, gain, cotangent, *pieces_two),
        2 * rows * width * units * 8,
        "feed_forward_and_back",
        (slots,),
    )
    partial_other = swap(partial)
    feed, grads_two = call(
        (weight_kernel, [pltpu.VMEM((width, units), bf16)]),
        [shape((rows, width), bf16), shape((groups, 3 * depth, units), bf16)],
        (second, hidden, grad_gate, grad_upper, cotangent, down_t),
        2 * rows * width * units * 5,
        "feed_weight_grads",
        (slots,),
    )
    feed_other = swap(feed)
    sums_two = RingScatter(grads_two)
    sums_two.hop()
    grad_middle, low_mid, grad_att = call(
        (middle_kernel, []),
        [shape((rows, width), f32), shape((rows, width), bf16), shape((rows, local), bf16)],
        (middle, partial, partial_other, gain, cotangent, wide),
        2 * rows * width * local * 4,
        "middle_grad",
    )
    grad_att, = locked([grad_att], sums_two)
    sums_two.hop()
    grad_proj, = call(
        (back_kernel, [pltpu.VMEM((extent, local), f32)] * 2),
        [shape((extent, 3 * local), bf16)],
        (query, key, value, shares, grad_att, cosine, sine),
        2 * rows * width * local * 15,
        "attention_back",
    )
    grad_proj, = locked([grad_proj], sums_two)
    sums_two.hop()
    grads_one, = call(
        (grad_kernel, [pltpu.VMEM((width, local), bf16)]),
        [shape((groups, 4 * depth, local), bf16)],
        (first, grad_proj, low_mid, attended),
        2 * rows * width * local * 5,
        "attention_weight_grads",
        (slots,),
    )
    sums_two.state = tied(sums_two.state, [grads_one])
    one = over_ctx(RingScatter(grads_one).finish()).reshape(4, depth, local)
    two = over_ctx(sums_two.finish()).reshape(3, depth, units)
    first_part, = call(
        (first_kernel, []),
        [shape((extent, width), bf16)],
        (grad_proj, wide),
        2 * rows * width * local * 3,
        "first_grad",
    )
    first_other = swap(first_part)

    def edge_sum(at):
        here = slice(at, at + HALF)
        return (first_part[here].astype(f32) + first_other[here].astype(f32)).astype(bf16)

    from_before, from_after = exchange(edge_sum(0), edge_sum(rows + HALF))
    mixed, token_grad = call(
        (final_kernel, []),
        [shape((rows, width), bf16), shape((rows, width), f32)],
        (
            tokens, gain, grad_middle, first_part, first_other, from_before, from_after, middle, feed, feed_other,
        ),
        rows * width * 20,
        "token_grad",
    )
    gain_one_grad = jnp.sum(one[:3] * w_qkv.astype(f32), axis=(0, 2)) / gain_one.astype(f32)
    gain_two_grad = jnp.sum(two[:2] * w_in.astype(f32), axis=(0, 2)) / gain_two.astype(f32)
    both = jnp.stack([gain_one_grad, gain_two_grad])
    both = both + swap(both)
    return (mixed, token_grad, both[0], one[:3], one[3].T, both[1], two[:2], two[2].T)


def solution(mesh):
    in_specs = (
        P(("dp", "ctx"), None),
        P("dp", None),
        P("dp"),
        P(None, "dp", "tensor"),
        P("tensor", "dp"),
        P("dp"),
        P(None, "dp", "tensor"),
        P("tensor", "dp"),
        P(("dp", "ctx"), None),
    )
    out_specs = (
        P(("dp", "ctx"), None),
        P(("dp", "ctx"), None),
        P("dp"),
        P(None, "dp", "tensor"),
        P("tensor", "dp"),
        P("dp"),
        P(None, "dp", "tensor"),
        P("tensor", "dp"),
    )
    return jax.shard_map(body, mesh=mesh, in_specs=in_specs, out_specs=out_specs, check_vma=False)
```

```python
import functools
import math

import jax
import jax.numpy as jnp
from jax import lax
from jax.experimental import pallas as pl
from jax.experimental.pallas import tpu as pltpu
from jax.sharding import PartitionSpec as P

HEAD = 64
WINDOW = 128
NSEQ = 4
HALF = WINDOW // 2
PAD = 16
BLOCK = 128
LANES = 128
KEYS = BLOCK + WINDOW

norm_eps = 1e-05
f32 = jnp.float32
bf16 = jnp.bfloat16

NN = (((1,), (0,)), ((), ()))
NT = (((1,), (1,)), ((), ()))
TN = (((0,), (0,)), ((), ()))


def dot(a, b, dims=NN):
    return lax.dot_general(a, b, dims, preferred_element_type=f32)


def step_of(rows, most):
    best = LANES
    for size in range(LANES, most + 1, LANES):
        if rows % size == 0:
            best = size
    return best


def call(kernel, out_shape, args, flops, name, scalars=(), scratch=(), raw=()):
    vmem = pl.BlockSpec(memory_space=pltpu.VMEM)
    smem = pl.BlockSpec(memory_space=pltpu.SMEM)
    anywhere = pl.BlockSpec(memory_space=pl.ANY)
    moved = sum(x.size * x.dtype.itemsize for x in (*args, *out_shape))
    held = sum(math.prod(x.shape) * jnp.dtype(x.dtype).itemsize for x in scratch if x.dtype in (f32, bf16))
    limit = min(56 * 2**20, moved + held + 6 * 2**20)
    return pl.pallas_call(
        kernel,
        out_shape=out_shape,
        in_specs=[smem] * len(scalars) + [vmem] * len(args) + [anywhere] * len(raw),
        out_specs=[vmem] * len(out_shape),
        scratch_shapes=scratch,
        compiler_params=pltpu.CompilerParams(vmem_limit_bytes=limit),
        cost_estimate=pl.CostEstimate(flops=flops, bytes_accessed=moved, transcendentals=0),
        name=name,
    )(*scalars, *args, *raw)


def shape(dims, dtype):
    return jax.ShapeDtypeStruct(dims, dtype)


def normed(values):
    centered = values - jnp.mean(values, axis=-1, keepdims=True)
    spread = jnp.mean(centered * centered, axis=-1, keepdims=True)
    scale = lax.rsqrt(spread + norm_eps)
    return centered * scale, scale


def norm_back(grad, gain, hat, scale):
    inner = grad * gain
    one = jnp.mean(inner, axis=-1, keepdims=True)
    two = jnp.mean(inner * hat, axis=-1, keepdims=True)
    return scale * (inner - one - hat * two)


def turned(values, low):
    return jnp.where(low, pltpu.roll(values, LANES - HEAD // 2, 1), pltpu.roll(values, HEAD // 2, 1))


def halves(values):
    even = (lax.broadcasted_iota(jnp.int32, (1, LANES), 1) < HEAD).astype(f32).astype(bf16)
    return jnp.concatenate([values * even, values * (1 - even)], axis=0)


def joined(values):
    return jnp.concatenate([values[:HEAD, :BLOCK], values[HEAD:, BLOCK:]], axis=0).T


def loop(count, body):
    def run(index, carry):
        body(index)
        return carry

    lax.fori_loop(0, count, run, 0)


def fetch(copies, sems):
    started = []
    for number, (source, target) in enumerate(copies):
        copy = pltpu.make_async_copy(source, target, sems.at[number])
        copy.start()
        started.append(copy)
    for copy in started:
        copy.wait()


def norm_kernel(tokens, before, after, hat):
    rows, width = tokens.shape

    def norm_rows(src, dst, size):
        hat[pl.ds(dst, size), :] = normed(src.astype(f32))[0]

    norm_rows(before[...], 0, HALF)
    norm_rows(after[...], rows + HALF, HALF)

    def norm_step(index):
        at = pl.multiple_of(index * BLOCK, BLOCK)
        norm_rows(tokens[pl.ds(at, BLOCK), :], pl.multiple_of(at + HALF, HALF), BLOCK)

    loop(rows // BLOCK, norm_step)


def project_kernel(plan, slots, thirds, hat, cosine, sine, *rest):
    pieces, (wide, gain, first, query, key, value, gain_held, sems) = rest[:-8], rest[-8:]
    extent, local = key.shape
    rows = query.shape[0]
    width = hat.shape[1]
    pairs = local // LANES
    groups = len(plan)
    depth = width // groups
    part = wide.shape[1] // 3
    copies = []
    for number, sources in enumerate(plan):
        place = pl.ds(pl.multiple_of(slots[number] * depth, depth), depth)
        for third, (piece, row) in enumerate(sources[:3]):
            lanes = pl.ds(pl.multiple_of(thirds[third] * part, LANES), part)
            copies.append((pieces[piece].at[row : row + depth, :], wide.at[place, lanes]))
        piece, row = sources[3]
        copies.append((pieces[piece].at[row : row + PAD, :], gain_held.at[number]))
    fetch(copies, sems)
    lane = lax.broadcasted_iota(jnp.int32, (LANES, width), 1) - lax.broadcasted_iota(jnp.int32, (LANES, width), 0)
    gain_sum = jnp.zeros((PAD, width), f32)
    for number in range(groups):
        spread = jnp.where(lane == slots[number] * depth, 1.0, 0.0).astype(bf16)
        gain_sum += dot(gain_held[number][:, :LANES], spread)
    gain[...] = gain_sum
    gains = gain_sum[:1]
    query_w, key_w, value_w = (wide.at[:, at * local : (at + 1) * local] for at in range(3))
    low = lax.broadcasted_iota(jnp.int32, (1, LANES), 1) % HEAD < HEAD // 2

    def rotated(src, at, size, dst, place, scale):
        co, si = cosine[pl.ds(at, size), :], sine[pl.ds(at, size), :]
        for pair in range(pairs):
            lanes = slice(pair * LANES, (pair + 1) * LANES)
            value = src[:, lanes]
            dst[pl.ds(place, size), lanes] = ((value * co + turned(value, low) * si) * scale).astype(bf16)

    chunk = step_of(extent, 384)

    def key_step(index):
        at = pl.multiple_of(index * chunk, chunk)
        here = pl.ds(at, chunk)
        part = (hat[here, :] * gains).astype(bf16)
        first[here, :] = part
        rotated(dot(part, key_w[...]), at, chunk, key, at, 1.0)
        value[here, :] = dot(part, value_w[...]).astype(bf16)

    loop(extent // chunk, key_step)
    size = step_of(rows, 256)

    def query_step(index):
        at = pl.multiple_of(index * size, size)
        start = pl.multiple_of(at + HALF, HALF)
        rotated(dot(first[pl.ds(start, size), :], query_w[...]), start, size, query, at, HEAD**-0.5)

    loop(rows // size, query_step)


def attend_kernel(pair, bounds, query, key, value, shares, attended):
    rows = query.shape[0]
    lanes = slice(pair * LANES, (pair + 1) * LANES)
    key_at = lax.broadcasted_iota(jnp.int32, (KEYS, KEYS), 0)
    lane_at = lax.broadcasted_iota(jnp.int32, (1, KEYS), 1) % BLOCK

    def attend_step(index):
        at = pl.multiple_of(index * BLOCK, BLOCK)
        origin = bounds[NSEQ] + at - HALF
        own = lane_at + (origin + HALF)
        begin = jnp.zeros_like(own)
        end = jnp.zeros_like(own) + bounds[NSEQ - 1]
        for number in range(NSEQ - 1):
            begin = jnp.where(own >= bounds[number], bounds[number], begin)
        for number in reversed(range(NSEQ - 1)):
            end = jnp.where(own < bounds[number], bounds[number], end)
        least = jnp.maximum(lane_at, begin - origin)
        most = jnp.minimum(lane_at + WINDOW, end - 1 - origin)
        both = halves(query[pl.ds(at, BLOCK), lanes])
        raw = dot(key[pl.ds(at, KEYS), lanes], both, NT)
        scores = jnp.where((key_at >= least) & (key_at <= most), raw, -1e30)
        weight = jnp.exp(scores - jnp.max(scores, axis=0, keepdims=True))
        part = (weight * (1.0 / jnp.sum(weight, axis=0, keepdims=True))).astype(bf16)
        shares[index] = part
        mixed = dot(value[pl.ds(at, KEYS), lanes], part, TN)
        attended[pl.ds(at, BLOCK), :] = joined(mixed).astype(bf16)

    unrolled(rows // BLOCK, attend_step)


def unrolled(count, body, most=4):
    size = max(step for step in range(1, most + 1) if count % step == 0)

    def run(index):
        for step in range(size):
            body(index * size + step)

    loop(count // size, run)


def out_kernel(wide, *rest):
    parts, (attended, branch) = rest[:-2], rest[-2:]
    rows, local = attended.shape
    out_t = wide.at[:, 3 * local :]
    size = step_of(rows, 256)
    for pair, part in enumerate(parts):
        attended[:, pair * LANES : (pair + 1) * LANES] = part[...]

    def out_step(index):
        here = pl.ds(pl.multiple_of(index * size, size), size)
        branch[here, :] = dot(attended[here, :], out_t[...], NT).astype(bf16)

    loop(rows // size, out_step)


def feed_kernel(plan, slots, thirds, tokens, own, other, gain, cotangent, *rest):
    pieces, rest = rest[:-8], rest[-8:]
    middle, second, hidden, grad_gate, grad_upper, partial, whole, sems = rest
    rows, width = tokens.shape
    depth = width // len(plan)
    copies = []
    for number, sources in enumerate(plan):
        place = pl.ds(pl.multiple_of(slots[number] * depth, depth), depth)
        for third, (piece, row) in enumerate(sources):
            copies.append((pieces[piece].at[row : row + depth, :], whole.at[thirds[third], place, :]))
    fetch(copies, sems)
    gate_w, upper_w, down_t = (whole.at[number] for number in range(3))
    gains = gain[1:2, :]
    size = step_of(rows, 256)

    def step(index):
        at = pl.multiple_of(index * size, size)
        here = pl.ds(at, size)
        mid = tokens[here, :].astype(f32) + (own[here, :].astype(f32) + other[here, :].astype(f32))
        middle[here, :] = mid
        hat, _ = normed(mid)
        low = (hat * gains).astype(bf16)
        second[here, :] = low
        gate = dot(low, gate_w[...])
        upper = dot(low, upper_w[...])
        grad = dot(cotangent[here, :], down_t[...])
        share = 0.5 * (1.0 + lax.erf(gate * (0.5**0.5)))
        smooth = gate * share
        slope = share + gate * (jnp.exp(gate * gate * -0.5) * ((2.0 * math.pi) ** -0.5))
        hidden[here, :] = (smooth * upper).astype(bf16)
        gate_low = (grad * upper * slope).astype(bf16)
        upper_low = (grad * smooth).astype(bf16)
        grad_gate[here, :] = gate_low
        grad_upper[here, :] = upper_low
        partial[here, :] = (dot(gate_low, gate_w[...], NT) + dot(upper_low, upper_w[...], NT)).astype(bf16)

    loop(rows // size, step)


def weight_kernel(slots, thirds, second, hidden, grad_gate, grad_upper, cotangent, whole, feed, *rest):
    outs, total = rest[:-1], rest[-1]
    rows, width = second.shape
    size = step_of(rows, 256)
    step_rows = step_of(width, 256)
    for number, (left, right) in enumerate(((second, grad_gate), (second, grad_upper), (cotangent, hidden))):
        for start in range(0, width, step_rows):
            here = slice(start, start + step_rows)
            total[number, here, :] = dot(left[:, here], right[...], TN).astype(bf16)
    spread_out(outs, slots, lambda third, place: total[thirds[third], place, :])

    def step(index):
        here = pl.ds(pl.multiple_of(index * size, size), size)
        feed[here, :] = dot(hidden[here, :], whole[2], NT).astype(bf16)

    loop(rows // size, step)


def hop_order(count):
    middle = count // 2
    order = [middle]
    for hop in range(middle - 1, 0, -1):
        order += [hop, count - hop]
    return order + [0]


def spread_out(outs, slots, block):
    ring_one, ring_two, rest, *others = outs
    ringed = rest.shape[1]
    depth = rest.shape[2]
    order = hop_order(rest.shape[0] + 1)
    spot = 0
    lengths = [other.shape[0] for other in others]
    for number, slot in enumerate(order):
        place = pl.ds(pl.multiple_of(slots[slot] * depth, depth), depth)
        if number == 0:
            for third in range(ringed - 1):
                ring_one[third] = block(third, place)
            ring_two[0] = block(ringed - 1, place)
        else:
            for third in range(ringed):
                rest[number - 1, third] = block(third, place)
        if others:
            where = number - sum(lengths[:spot])
            others[spot][where] = block(2, place)
            if where + 1 == lengths[spot]:
                spot += 1


def spread_shapes(count, ringed, depth, size):
    shapes = [(ringed - 1, depth, size), (1, depth, size), (count - 1, ringed, depth, size)]
    if ringed == 2:
        shapes += [(1, depth, size)] + [(2, depth, size)] * (count // 2 - 1) + [(1, depth, size)]
    return [shape(dims, bf16) for dims in shapes]


def middle_kernel(middle, own, other, gain, cotangent, wide, grad_middle, low_mid, grad_att):
    rows, width = middle.shape
    local = grad_att.shape[1]
    out_t = wide.at[:, 3 * local :]
    gains = gain[1:2, :]
    size = step_of(rows, 256)

    def norm_step(index):
        here = pl.ds(pl.multiple_of(index * size, size), size)
        hat, scale = normed(middle[here, :])
        grad = own[here, :].astype(f32) + other[here, :].astype(f32)
        mid = cotangent[here, :].astype(f32) + norm_back(grad, gains, hat, scale)
        grad_middle[here, :] = mid
        mid_low = mid.astype(bf16)
        low_mid[here, :] = mid_low
        grad_att[here, :] = dot(mid_low, out_t[...]).astype(bf16)

    loop(rows // size, norm_step)


def back_kernel(pair, query, key, value, shares, grad_att, cosine, sine, grad_proj, grad_key, grad_value):
    rows = query.shape[0]
    extent = key.shape[0]
    lanes = slice(pair * LANES, (pair + 1) * LANES)
    grad_key[...] = jnp.zeros_like(grad_key)
    grad_value[...] = jnp.zeros_like(grad_value)
    low = lax.broadcasted_iota(jnp.int32, (1, LANES), 1) % HEAD < HEAD // 2
    zero = jnp.zeros((HALF, LANES), bf16)
    grad_proj[:HALF, :LANES] = zero
    grad_proj[rows + HALF :, :LANES] = zero

    def attend_step(index):
        at = pl.multiple_of(index * BLOCK, BLOCK)
        start = pl.multiple_of(at + HALF, HALF)
        co, si = cosine[pl.ds(start, BLOCK), :], sine[pl.ds(start, BLOCK), :]
        both = halves(query[pl.ds(at, BLOCK), lanes])
        grad = halves(grad_att[pl.ds(at, BLOCK), lanes])
        keys = key[pl.ds(at, KEYS), lanes]
        part = shares[index]
        wide = part.astype(f32)
        grad_shares = dot(value[pl.ds(at, KEYS), lanes], grad, NT)
        delta = jnp.sum(wide * grad_shares, axis=0, keepdims=True)
        raw = (wide * (grad_shares - delta)).astype(bf16)
        grad_query = joined(dot(keys, raw, TN)) * HEAD**-0.5
        grad_proj[pl.ds(start, BLOCK), :LANES] = (grad_query * co - turned(grad_query, low) * si).astype(bf16)
        grad_key[pl.ds(at, KEYS), :] += dot(raw, both)
        grad_value[pl.ds(at, KEYS), :] += dot(part, grad)

    unrolled(rows // BLOCK, attend_step)

    def turn_step(index):
        here = pl.ds(pl.multiple_of(index * BLOCK, BLOCK), BLOCK)
        part = grad_key[here, :]
        turn = part * cosine[here, :] - turned(part, low) * sine[here, :]
        grad_proj[here, LANES : 2 * LANES] = turn.astype(bf16)
        grad_proj[here, 2 * LANES :] = grad_value[here, :].astype(bf16)

    loop(extent // BLOCK, turn_step)


def grad_kernel(pairs, slots, thirds, first, low_mid, attended, *rest):
    parts, grad_proj, outs, total = rest[:pairs], rest[pairs], rest[pairs + 1 : -1], rest[-1]
    local = attended.shape[1]
    width = first.shape[1]
    size = total.shape[1] // 3
    for pair, part in enumerate(parts):
        for number in range(3):
            lanes = slice(number * local + pair * LANES, number * local + (pair + 1) * LANES)
            grad_proj[:, lanes] = part[:, number * LANES : (number + 1) * LANES]
    step_rows = step_of(width, 256)
    for start in range(0, width, step_rows):
        here = slice(start, start + step_rows)
        for number in range(3):
            lanes = slice(number * local, (number + 1) * local)
            total[here, lanes] = dot(first[:, here], grad_proj[:, lanes], TN).astype(bf16)
        total[here, 3 * local :] = dot(low_mid[:, here], attended[...], TN).astype(bf16)

    def block(third, place):
        return total[place, pl.ds(pl.multiple_of(thirds[third] * size, LANES), size)]

    spread_out(outs, slots, block)


def first_kernel(grad_proj, wide, partial):
    extent, inner = grad_proj.shape
    size = step_of(extent, 384)

    def step(index):
        here = pl.ds(pl.multiple_of(index * size, size), size)
        partial[here, :] = dot(grad_proj[here, :], wide[:, :inner], NT).astype(bf16)

    loop(extent // size, step)


def final_kernel(tokens, gain, grad_middle, own, other, before, after, middle, feed_own, feed_other, mixed, token_grad):
    rows, width = tokens.shape
    gains = gain[:1, :]
    size = BLOCK

    def back(here, grad):
        hat, scale = normed(tokens[here, :].astype(f32))
        return norm_back(grad, gains, hat, scale)

    def step(index):
        at = pl.multiple_of(index * size, size)
        here, wider = pl.ds(at, size), pl.ds(pl.multiple_of(at + HALF, HALF), size)
        grad = own[wider, :].astype(f32) + other[wider, :].astype(f32)
        token_grad[here, :] = grad_middle[here, :] + back(here, grad)
        feed = feed_own[here, :].astype(f32) + feed_other[here, :].astype(f32)
        mixed[here, :] = (middle[here, :] + feed).astype(bf16)

    loop(rows // size, step)
    for start, edge in ((0, before), (rows - HALF, after)):
        here = pl.ds(start, HALF)
        token_grad[here, :] += back(here, edge[...].astype(f32))


def exchange(initial, last):
    devices, spot = lax.axis_size("ctx"), lax.axis_index("ctx")
    if devices == 2:
        got = lax.ppermute(jnp.where(spot == 0, last, initial), "ctx", [(0, 1), (1, 0)])
        none = jnp.zeros_like(got)
        return jnp.where(spot == 1, got, none), jnp.where(spot == 0, got, none)
    up = [(i, i + 1) for i in range(devices - 1)]
    return lax.ppermute(last, "ctx", up), lax.ppermute(initial, "ctx", [(j, i) for i, j in up])


def swap(array, axis="tensor"):
    return lax.ppermute(array, axis, [(0, 1), (1, 0)])


def ring():
    count = lax.axis_size("dp")
    order = [2 * i for i in range(count // 2)] + [2 * i + 1 for i in reversed(range(count // 2))]
    ahead = [(order[i], order[(i + 1) % count]) for i in range(count)]
    back = [(j, i) for i, j in ahead]
    index = lax.axis_index("dp")
    spot = jnp.where(index % 2 == 0, index // 2, count - 1 - index // 2)
    place = (spot + jnp.arange(count, dtype=jnp.int32)) % count
    slots = jnp.where(place < count // 2, 2 * place, 2 * (count - 1 - place) + 1)
    return count, ahead, back, slots.astype(jnp.int32)


def tied(values, others):
    held = lax.optimization_barrier((tuple(values), tuple(others)))
    return held[0]


def locked(values, chain):
    held = lax.optimization_barrier((tuple(values), tuple(chain.state)))
    chain.state = held[1]
    return held[0]


def third_places():
    if lax.axis_size("ctx") == 2:
        spot = lax.axis_index("ctx")
        return jnp.stack([2 * spot, jnp.ones_like(spot), 2 - 2 * spot]).astype(jnp.int32)
    return jnp.arange(3, dtype=jnp.int32)


class RingGather:
    def __init__(self, blocks, extra=None):
        self.count, self.ahead, self.back, _ = ring()
        self.depth = blocks[0].shape[0]
        self.split = lax.axis_size("ctx") == 2
        if self.split:
            low = lax.axis_index("ctx") == 0
            mine, other = jnp.where(low, blocks[0], blocks[2]), jnp.where(low, blocks[2], blocks[0])
            ringed = [mine, blocks[1]]
        else:
            ringed = list(blocks)
        self.ringed = len(ringed)
        whole = jnp.concatenate(ringed + ([] if extra is None else [extra]))
        self.pieces = {0: (whole,)}
        self.others = {0: other} if self.split else {}
        self.state = (whole, whole)
        self.hops = 0

    def side(self):
        if not self.split or self.hops == 0:
            return
        one, two = self.state
        depth = self.depth
        if self.hops == self.count // 2:
            self.others[self.hops] = swap(one, "ctx")
        else:
            self.others[self.count - self.hops] = swap(one[:depth], "ctx")
            self.others[self.hops] = swap(two[:depth], "ctx")

    def hop(self):
        one, two = self.state
        middle = self.count // 2
        if self.hops + 1 == middle:
            cut = (self.ringed - 1) * self.depth
            one, two = one[:cut], two[cut:]
        ahead, behind = lax.ppermute(one, "dp", self.ahead), lax.ppermute(two, "dp", self.back)
        self.side()
        self.hops += 1
        one, two = lax.optimization_barrier((ahead, behind))
        self.state = (one, two)
        if self.hops == middle:
            self.pieces[middle] = (one, two)
        else:
            self.pieces[self.count - self.hops], self.pieces[self.hops] = (one,), (two,)

    def finish(self, extra):
        while self.hops < self.count // 2:
            self.hop()
        self.side()
        arrays, plan = [], []
        for slot in range(self.count):
            base, row, sources = len(arrays), 0, []
            held = self.pieces[slot]
            arrays += held
            for third in range(self.ringed):
                if len(held) == 2 and third == self.ringed - 1:
                    base, row = base + 1, 0
                sources.append((base, row))
                row += self.depth
            if self.split:
                sources.append((len(arrays), 0))
                arrays.append(self.others[slot])
            if extra:
                sources.append((base, row))
            plan.append(tuple(sources))
        return tuple(plan), arrays


class RingScatter:
    def __init__(self, outs):
        self.count, self.ahead, self.back, _ = ring()
        self.start = outs[:2]
        self.parts = outs[2]
        self.others = outs[3:]
        self.split = len(self.others) > 0
        self.sides = []
        self.hops = 0
        self.state = ()
        self.side()

    def side(self):
        if self.split and len(self.sides) < len(self.others):
            self.sides.append(swap(self.others[len(self.sides)], "ctx"))

    def summed(self, at, extra):
        part = self.parts[at]
        if extra is not None:
            part = part + jnp.concatenate([extra[None], jnp.zeros_like(part[1:])])
        return part

    def hop(self):
        if self.hops == 0:
            one, two = self.start
            if self.split:
                one = one + self.sides[0]
        else:
            one, two = self.state
            if self.hops == 1:
                one = jnp.concatenate([one, jnp.zeros_like(two)])
                two = jnp.concatenate([jnp.zeros_like(one[:-1]), two])
            at = 2 * self.hops - 2
            first, second = self.sides[self.hops] if self.split else (None, None)
            one, two = self.summed(at, first) + one, self.summed(at + 1, second) + two
        one, two = lax.ppermute(one, "dp", self.ahead), lax.ppermute(two, "dp", self.back)
        self.side()
        self.state = lax.optimization_barrier((one, two))
        self.hops += 1

    def finish(self):
        while self.hops < self.count // 2:
            self.hop()
        one, two = self.state
        last = self.sides[-1][0] if self.split else None
        total = (self.summed(self.count - 2, last).astype(f32) + one.astype(f32) + two.astype(f32)).astype(bf16)
        if not self.split:
            return lax.psum(total, "ctx").astype(f32)
        got = swap(total, "ctx").astype(f32)
        total = total.astype(f32)
        low = lax.axis_index("ctx") == 0
        shared = total[1] + got[1]
        return jnp.stack([jnp.where(low, total[0], got[0]), shared, jnp.where(low, got[0], total[0])])


def tables(lengths, rows):
    place = lax.axis_index("ctx") * rows
    ends = jnp.cumsum(lengths[0])
    starts = ends - lengths[0]
    span = place + jnp.arange(-HALF, rows + HALF, dtype=jnp.int32)
    inside = (span[:, None] >= starts[None, :]) & (span[:, None] < ends[None, :])
    position = span - jnp.sum(jnp.where(inside, starts[None, :], 0), axis=1)
    number = (jnp.arange(HEAD, dtype=jnp.int32) % (HEAD // 2)).astype(f32)
    freq = jnp.exp(number * (-2.0 * math.log(10000.0) / HEAD))
    angle = position.astype(f32)[:, None] * freq[None, :]
    cosine, sine = jnp.cos(angle), jnp.sin(angle)
    sine = jnp.where(jnp.arange(HEAD)[None, :] < HEAD // 2, -sine, sine)
    bounds = jnp.concatenate([ends, place[None]]).astype(jnp.int32)
    return jnp.tile(cosine, (1, 2)), jnp.tile(sine, (1, 2)), bounds


def body(tokens, lengths, gain_one, w_qkv, w_out, gain_two, w_in, w_down, cotangent):
    rows, width = tokens.shape
    local, units = w_out.shape[0], w_down.shape[0]
    pairs, blocks, extent = local // LANES, rows // BLOCK, rows + WINDOW
    groups = lax.axis_size("dp")
    depth = width // groups
    size = 4 * local // 3
    gains = jnp.pad(jnp.stack([gain_one, gain_two]), ((0, PAD - 2), (0, size - depth)))
    joint = jnp.concatenate([w_qkv[0], w_qkv[1], w_qkv[2], w_out.T], axis=1)
    now = RingGather([joint[:, at * size : (at + 1) * size] for at in range(3)], gains)
    now.hop()
    before, after = exchange(tokens[:HALF], tokens[rows - HALF :])
    slots, thirds = ring()[-1], third_places()
    cosine, sine, bounds = tables(lengths, rows)
    hat, = call(
        norm_kernel, [shape((extent, width), f32)], (tokens, before, after), rows * width * 2000, "first_norm"
    )
    while now.hops < groups // 2:
        now.hop()
    blocks_two = tied([w_in[0], w_in[1], w_down.T], now.state)
    later = RingGather(blocks_two)
    later.hop()
    plan, pieces = now.finish(True)
    wide, gain, first, query, key, value = call(
        functools.partial(project_kernel, plan),
        [
            shape((width, 4 * local), bf16),
            shape((PAD, width), f32),
            shape((extent, width), bf16),
            shape((rows, local), bf16),
            shape((extent, local), bf16),
            shape((extent, local), bf16),
        ],
        (hat, cosine, sine),
        2 * rows * width * local * 8,
        "project",
        (slots, thirds),
        [pltpu.VMEM((groups, PAD, size), bf16), pltpu.SemaphoreType.DMA((4 * groups,))],
        pieces,
    )
    shares, attended_parts = [], []
    for pair in range(pairs):
        if pair in (0, pairs - 1):
            query, key, value = locked([query, key, value], later)
            later.hop()
        part, attended = call(
            functools.partial(attend_kernel, pair),
            [shape((blocks, KEYS, KEYS), bf16), shape((rows, LANES), bf16)],
            (query, key, value),
            2 * rows * width * local * 5,
            "attend",
            (bounds,),
        )
        shares.append(part)
        attended_parts.append(attended)
    attended, branch = call(
        out_kernel,
        [shape((rows, local), bf16), shape((rows, width), bf16)],
        (wide, *attended_parts),
        2 * rows * width * local * 2,
        "attention_out",
    )
    branch, = locked([branch], later)
    branch_other = swap(branch)
    plan, pieces = later.finish(False)
    middle, second, hidden, grad_gate, grad_upper, partial, whole = call(
        functools.partial(feed_kernel, plan),
        [
            shape((rows, width), f32),
            shape((rows, width), bf16),
            shape((rows, units), bf16),
            shape((rows, units), bf16),
            shape((rows, units), bf16),
            shape((rows, width), bf16),
            shape((3, width, units), bf16),
        ],
        (tokens, branch, branch_other, gain, cotangent),
        2 * rows * width * units * 8,
        "feed_forward_and_back",
        (slots, thirds),
        [pltpu.SemaphoreType.DMA((3 * groups,))],
        pieces,
    )
    partial_other = swap(partial)
    ringed = now.ringed
    feed, *grads_two = call(
        weight_kernel,
        [shape((rows, width), bf16)] + spread_shapes(groups, ringed, depth, units),
        (second, hidden, grad_gate, grad_upper, cotangent, whole),
        2 * rows * width * units * 5,
        "feed_weight_grads",
        (slots, thirds),
        [pltpu.VMEM((3, width, units), bf16)],
    )
    feed_other = swap(feed)
    sums_two = RingScatter(grads_two)
    grad_middle, low_mid, grad_att = call(
        middle_kernel,
        [shape((rows, width), f32), shape((rows, width), bf16), shape((rows, local), bf16)],
        (middle, partial, partial_other, gain, cotangent, wide),
        2 * rows * width * local * 4,
        "middle_grad",
    )
    sums_two.state = sums_two.sides if sums_two.split else ()
    grad_att, = tied([grad_att], sums_two.state)
    sums_two.hop()
    grad_parts = []
    for pair in range(pairs):
        if pair:
            grad_att, = locked([grad_att, *grad_parts], sums_two)[:1]
            sums_two.hop()
        grad_part, = call(
            functools.partial(back_kernel, pair),
            [shape((extent, 3 * LANES), bf16)],
            (query, key, value, shares[pair], grad_att, cosine, sine),
            2 * rows * width * local * 5,
            "attention_back",
            (),
            [pltpu.VMEM((extent, LANES), f32)] * 2,
        )
        grad_parts.append(grad_part)
    grad_parts = locked(grad_parts, sums_two)
    sums_two.hop()
    grad_proj, *grads_one = call(
        functools.partial(grad_kernel, pairs),
        [shape((extent, 3 * local), bf16)] + spread_shapes(groups, ringed, depth, size),
        (first, low_mid, attended, *grad_parts),
        2 * rows * width * local * 6,
        "attention_weight_grads",
        (slots, thirds),
        [pltpu.VMEM((width, 4 * local), bf16)],
    )
    sums_two.state = tied(sums_two.state, grads_one)
    sums_one = RingScatter(grads_one)
    one = sums_one.finish()
    two = sums_two.finish()
    first_part, = call(
        first_kernel,
        [shape((extent, width), bf16)],
        (grad_proj, wide),
        2 * rows * width * local * 3,
        "first_grad",
    )
    first_other = swap(first_part)

    def edge_sum(at):
        here = slice(at, at + HALF)
        return (first_part[here].astype(f32) + first_other[here].astype(f32)).astype(bf16)

    from_before, from_after = exchange(edge_sum(0), edge_sum(rows + HALF))
    mixed, token_grad = call(
        final_kernel,
        [shape((rows, width), bf16), shape((rows, width), f32)],
        (tokens, gain, grad_middle, first_part, first_other, from_before, from_after, middle, feed, feed_other),
        rows * width * 2000,
        "token_grad",
    )
    joint_grad = jnp.concatenate([one[0], one[1], one[2]], axis=1)
    grad_qkv = [joint_grad[:, at * local : (at + 1) * local] for at in range(4)]
    qkv = jnp.stack(grad_qkv[:3])
    gain_one_grad = jnp.sum(qkv * w_qkv.astype(f32), axis=(0, 2)) / gain_one.astype(f32)
    gain_two_grad = jnp.sum(two[:2] * w_in.astype(f32), axis=(0, 2)) / gain_two.astype(f32)
    both = jnp.stack([gain_one_grad, gain_two_grad])
    both = both + swap(both)
    return (mixed, token_grad, both[0], qkv, grad_qkv[3].T, both[1], two[:2], two[2].T)


def solution(mesh):
    in_specs = (
        P(("dp", "ctx"), None),
        P("dp", None),
        P("dp"),
        P(None, "dp", "tensor"),
        P("tensor", "dp"),
        P("dp"),
        P(None, "dp", "tensor"),
        P("tensor", "dp"),
        P(("dp", "ctx"), None),
    )
    out_specs = (
        P(("dp", "ctx"), None),
        P(("dp", "ctx"), None),
        P("dp"),
        P(None, "dp", "tensor"),
        P("tensor", "dp"),
        P("dp"),
        P(None, "dp", "tensor"),
        P("tensor", "dp"),
    )
    return jax.shard_map(body, mesh=mesh, in_specs=in_specs, out_specs=out_specs, check_vma=False)
```

```python
import functools
import math

import jax
import jax.numpy as jnp
from jax import lax
from jax.experimental import pallas as pl
from jax.experimental.pallas import tpu as pltpu
from jax.sharding import PartitionSpec as P

HEAD = 64
WINDOW = 128
NSEQ = 4
HALF = WINDOW // 2
PAD = 16
BLOCK = 128
LANES = 128
KEYS = BLOCK + WINDOW

norm_eps = 1e-05
f32 = jnp.float32
bf16 = jnp.bfloat16

NN = (((1,), (0,)), ((), ()))
NT = (((1,), (1,)), ((), ()))
TN = (((0,), (0,)), ((), ()))


def dot(a, b, dims=NN):
    return lax.dot_general(a, b, dims, preferred_element_type=f32)


def step_of(rows, most):
    best = LANES
    for size in range(LANES, most + 1, LANES):
        if rows % size == 0:
            best = size
    return best


def call(kernel, out_shape, args, flops, name, scalars=(), scratch=(), raw=()):
    vmem = pl.BlockSpec(memory_space=pltpu.VMEM)
    smem = pl.BlockSpec(memory_space=pltpu.SMEM)
    anywhere = pl.BlockSpec(memory_space=pl.ANY)
    moved = sum(x.size * x.dtype.itemsize for x in (*args, *out_shape))
    held = sum(math.prod(x.shape) * jnp.dtype(x.dtype).itemsize for x in scratch if x.dtype in (f32, bf16))
    limit = min(56 * 2**20, moved // 3 + held + 4 * 2**20)
    return pl.pallas_call(
        kernel,
        out_shape=out_shape,
        in_specs=[smem] * len(scalars) + [vmem] * len(args) + [anywhere] * len(raw),
        out_specs=[vmem] * len(out_shape),
        scratch_shapes=scratch,
        compiler_params=pltpu.CompilerParams(vmem_limit_bytes=limit),
        cost_estimate=pl.CostEstimate(flops=flops, bytes_accessed=moved, transcendentals=0),
        name=name,
    )(*scalars, *args, *raw)


def shape(dims, dtype):
    return jax.ShapeDtypeStruct(dims, dtype)


def normed(values):
    centered = values - jnp.mean(values, axis=-1, keepdims=True)
    spread = jnp.mean(centered * centered, axis=-1, keepdims=True)
    scale = lax.rsqrt(spread + norm_eps)
    return centered * scale, scale


def norm_back(grad, gain, hat, scale):
    inner = grad * gain
    one = jnp.mean(inner, axis=-1, keepdims=True)
    two = jnp.mean(inner * hat, axis=-1, keepdims=True)
    return scale * (inner - one - hat * two)


def turned(values, low):
    return jnp.where(low, pltpu.roll(values, LANES - HEAD // 2, 1), pltpu.roll(values, HEAD // 2, 1))


def halves(values):
    even = (lax.broadcasted_iota(jnp.int32, (1, LANES), 1) < HEAD).astype(f32).astype(bf16)
    return jnp.concatenate([values * even, values * (1 - even)], axis=0)


def joined(values):
    return jnp.concatenate([values[:HEAD, :BLOCK], values[HEAD:, BLOCK:]], axis=0).T


def loop(count, body):
    def run(index, carry):
        body(index)
        return carry

    lax.fori_loop(0, count, run, 0)


def fetch(copies, sems):
    started = []
    for number, (source, target) in enumerate(copies):
        copy = pltpu.make_async_copy(source, target, sems.at[number])
        copy.start()
        started.append(copy)
    for copy in started:
        copy.wait()


def norm_kernel(tokens, before, after, hat):
    rows, width = tokens.shape

    def norm_rows(src, dst, size):
        hat[pl.ds(dst, size), :] = normed(src.astype(f32))[0]

    norm_rows(before[...], 0, HALF)
    norm_rows(after[...], rows + HALF, HALF)

    def norm_step(index):
        at = pl.multiple_of(index * BLOCK, BLOCK)
        norm_rows(tokens[pl.ds(at, BLOCK), :], pl.multiple_of(at + HALF, HALF), BLOCK)

    loop(rows // BLOCK, norm_step)


def piece_plan(count, sizes, break_at):
    plan, used = [], 0
    for slot in range(count):
        row, sources = 0, []
        for number, size in enumerate(sizes):
            if slot == count // 2 and number == break_at:
                used, row = used + 1, 0
            sources.append((used, row))
            row += size
        plan.append(tuple(sources))
        used += 1
    return plan


def project_kernel(slots, hat, cosine, sine, *rest):
    pieces, (wide, gain, first, query, key, value, gain_held, sems) = rest[:-8], rest[-8:]
    extent, local = key.shape
    rows = query.shape[0]
    width = hat.shape[1]
    pairs = local // LANES
    groups = gain_held.shape[0]
    depth = width // groups
    plan = piece_plan(groups, [depth] * 4 + [PAD], 2)
    copies = []
    for number, sources in enumerate(plan):
        place = pl.ds(pl.multiple_of(slots[number] * depth, depth), depth)
        for part, (piece, row) in enumerate(sources[:4]):
            lanes = slice(part * local, (part + 1) * local)
            copies.append((pieces[piece].at[row : row + depth, :], wide.at[place, lanes]))
        piece, row = sources[4]
        copies.append((pieces[piece].at[row : row + PAD, :], gain_held.at[number]))
    fetch(copies, sems)
    lane = lax.broadcasted_iota(jnp.int32, (LANES, width), 1) - lax.broadcasted_iota(jnp.int32, (LANES, width), 0)
    gain_sum = jnp.zeros((PAD, width), f32)
    for number in range(groups):
        spread = jnp.where(lane == slots[number] * depth, 1.0, 0.0).astype(bf16)
        gain_sum += dot(gain_held[number][:, :LANES], spread)
    gain[...] = gain_sum
    gains = gain_sum[:1]
    query_w, key_w, value_w = (wide.at[:, at * local : (at + 1) * local] for at in range(3))
    low = lax.broadcasted_iota(jnp.int32, (1, LANES), 1) % HEAD < HEAD // 2

    def rotated(src, at, size, dst, place, scale):
        co, si = cosine[pl.ds(at, size), :], sine[pl.ds(at, size), :]
        for pair in range(pairs):
            lanes = slice(pair * LANES, (pair + 1) * LANES)
            value = src[:, lanes]
            dst[pl.ds(place, size), lanes] = ((value * co + turned(value, low) * si) * scale).astype(bf16)

    chunk = step_of(extent, 384)

    def key_step(index):
        at = pl.multiple_of(index * chunk, chunk)
        here = pl.ds(at, chunk)
        part = (hat[here, :] * gains).astype(bf16)
        first[here, :] = part
        rotated(dot(part, key_w[...]), at, chunk, key, at, 1.0)
        value[here, :] = dot(part, value_w[...]).astype(bf16)

    loop(extent // chunk, key_step)
    size = step_of(rows, 256)

    def query_step(index):
        at = pl.multiple_of(index * size, size)
        start = pl.multiple_of(at + HALF, HALF)
        rotated(dot(first[pl.ds(start, size), :], query_w[...]), start, size, query, at, HEAD**-0.5)

    loop(rows // size, query_step)


def attend_kernel(bounds, query, key, value, wide, shares, attended, branch):
    rows, local = query.shape
    pairs = local // LANES
    key_at = lax.broadcasted_iota(jnp.int32, (KEYS, KEYS), 0)
    lane_at = lax.broadcasted_iota(jnp.int32, (1, KEYS), 1) % BLOCK

    def attend_step(index):
        at = pl.multiple_of(index * BLOCK, BLOCK)
        origin = bounds[NSEQ] + at - HALF
        own = lane_at + (origin + HALF)
        begin = jnp.zeros_like(own)
        end = jnp.zeros_like(own) + bounds[NSEQ - 1]
        for number in range(NSEQ - 1):
            begin = jnp.where(own >= bounds[number], bounds[number], begin)
        for number in reversed(range(NSEQ - 1)):
            end = jnp.where(own < bounds[number], bounds[number], end)
        least = jnp.maximum(lane_at, begin - origin)
        most = jnp.minimum(lane_at + WINDOW, end - 1 - origin)
        allowed = (key_at >= least) & (key_at <= most)
        for pair in range(pairs):
            lanes = slice(pair * LANES, (pair + 1) * LANES)
            both = halves(query[pl.ds(at, BLOCK), lanes])
            scores = jnp.where(allowed, dot(key[pl.ds(at, KEYS), lanes], both, NT), -1e30)
            weight = jnp.exp(scores - jnp.max(scores, axis=0, keepdims=True))
            part = (weight * (1.0 / jnp.sum(weight, axis=0, keepdims=True))).astype(bf16)
            shares[index * pairs + pair] = part
            mixed = dot(value[pl.ds(at, KEYS), lanes], part, TN)
            attended[pl.ds(at, BLOCK), lanes] = joined(mixed).astype(bf16)

    loop(rows // BLOCK, attend_step)
    out_t = wide.at[:, 3 * local :]
    size = step_of(rows, 256)

    def out_step(index):
        here = pl.ds(pl.multiple_of(index * size, size), size)
        branch[here, :] = dot(attended[here, :], out_t[...], NT).astype(bf16)

    loop(rows // size, out_step)


def feed_kernel(slots, parts_at, tokens, own, other, gain, cotangent, *rest):
    pieces, rest = rest[:-8], rest[-8:]
    middle, second, hidden, grad_gate, grad_upper, partial, whole, sems = rest
    rows, width = tokens.shape
    groups = slots.shape[0]
    depth = width // groups
    sides = len(pieces) // groups
    size = depth // sides
    copies = []
    for number in range(groups):
        for side in range(sides):
            start = slots[number] * depth + parts_at[side] * size
            place = pl.ds(pl.multiple_of(start, size), size)
            copies.append((pieces[number * sides + side], whole.at[:, place, :]))
    fetch(copies, sems)
    gate_w, upper_w, down_t = (whole.at[number] for number in range(3))
    gains = gain[1:2, :]
    size = step_of(rows, 256)

    def step(index):
        at = pl.multiple_of(index * size, size)
        here = pl.ds(at, size)
        mid = tokens[here, :].astype(f32) + (own[here, :].astype(f32) + other[here, :].astype(f32))
        middle[here, :] = mid
        hat, _ = normed(mid)
        low = (hat * gains).astype(bf16)
        second[here, :] = low
        gate = dot(low, gate_w[...])
        upper = dot(low, upper_w[...])
        grad = dot(cotangent[here, :], down_t[...])
        share = 0.5 * (1.0 + lax.erf(gate * (0.5**0.5)))
        smooth = gate * share
        slope = share + gate * (jnp.exp(gate * gate * -0.5) * ((2.0 * math.pi) ** -0.5))
        hidden[here, :] = (smooth * upper).astype(bf16)
        gate_low = (grad * upper * slope).astype(bf16)
        upper_low = (grad * smooth).astype(bf16)
        grad_gate[here, :] = gate_low
        grad_upper[here, :] = upper_low
        partial[here, :] = (dot(gate_low, gate_w[...], NT) + dot(upper_low, upper_w[...], NT)).astype(bf16)

    loop(rows // size, step)


def feed_out_kernel(hidden, whole, feed):
    rows = hidden.shape[0]
    size = step_of(rows, 256)

    def step(index):
        here = pl.ds(pl.multiple_of(index * size, size), size)
        feed[here, :] = dot(hidden[here, :], whole[2], NT).astype(bf16)

    loop(rows // size, step)


def weight_kernel(slots, parts_at, second, hidden, grad_gate, grad_upper, cotangent, *rest):
    outs, total = rest[:-1], rest[-1]
    rows, width = second.shape
    step_rows = step_of(width, 256)
    for number, (left, right) in enumerate(((second, grad_gate), (second, grad_upper), (cotangent, hidden))):
        for start in range(0, width, step_rows):
            here = slice(start, start + step_rows)
            total[number, here, :] = dot(left[:, here], right[...], TN).astype(bf16)
    size = outs[0].shape[2]
    for number, slot in enumerate(hop_order(outs[0].shape[0])):
        for side, out in enumerate(outs):
            start = slots[slot] * (size * len(outs)) + parts_at[side] * size
            out[number] = total[:, pl.ds(pl.multiple_of(start, size), size), :]


def hop_order(count):
    middle = count // 2
    order = [middle]
    for hop in range(middle - 1, 0, -1):
        order += [hop, count - hop]
    return order + [0]


def middle_kernel(middle, own, other, gain, cotangent, wide, grad_middle, low_mid, grad_att):
    rows, width = middle.shape
    local = grad_att.shape[1]
    out_t = wide.at[:, 3 * local :]
    gains = gain[1:2, :]
    size = step_of(rows, 256)

    def norm_step(index):
        here = pl.ds(pl.multiple_of(index * size, size), size)
        hat, scale = normed(middle[here, :])
        grad = own[here, :].astype(f32) + other[here, :].astype(f32)
        mid = cotangent[here, :].astype(f32) + norm_back(grad, gains, hat, scale)
        grad_middle[here, :] = mid
        mid_low = mid.astype(bf16)
        low_mid[here, :] = mid_low
        grad_att[here, :] = dot(mid_low, out_t[...]).astype(bf16)

    loop(rows // size, norm_step)


def back_kernel(query, key, value, shares, grad_att, cosine, sine, grad_proj, grad_key, grad_value):
    rows, local = query.shape
    extent = key.shape[0]
    pairs = local // LANES
    grad_key[...] = jnp.zeros_like(grad_key)
    grad_value[...] = jnp.zeros_like(grad_value)
    low = lax.broadcasted_iota(jnp.int32, (1, LANES), 1) % HEAD < HEAD // 2
    zero = jnp.zeros((HALF, local), bf16)
    grad_proj[:HALF, :local] = zero
    grad_proj[rows + HALF :, :local] = zero

    def attend_step(index):
        at = pl.multiple_of(index * BLOCK, BLOCK)
        start = pl.multiple_of(at + HALF, HALF)
        co, si = cosine[pl.ds(start, BLOCK), :], sine[pl.ds(start, BLOCK), :]
        found = []
        for pair in range(pairs):
            lanes = slice(pair * LANES, (pair + 1) * LANES)
            both = halves(query[pl.ds(at, BLOCK), lanes])
            grad = halves(grad_att[pl.ds(at, BLOCK), lanes])
            keys = key[pl.ds(at, KEYS), lanes]
            part = shares[index * pairs + pair]
            wide = part.astype(f32)
            grad_shares = dot(value[pl.ds(at, KEYS), lanes], grad, NT)
            delta = jnp.sum(wide * grad_shares, axis=0, keepdims=True)
            raw = (wide * (grad_shares - delta)).astype(bf16)
            grad_query = joined(dot(keys, raw, TN)) * HEAD**-0.5
            turn = (grad_query * co - turned(grad_query, low) * si).astype(bf16)
            found.append((lanes, turn, dot(raw, both), dot(part, grad)))
        for lanes, turn, key_part, value_part in found:
            grad_proj[pl.ds(start, BLOCK), lanes] = turn
            grad_key[pl.ds(at, KEYS), lanes] += key_part
            grad_value[pl.ds(at, KEYS), lanes] += value_part

    loop(rows // BLOCK, attend_step)

    def turn_step(index):
        here = pl.ds(pl.multiple_of(index * BLOCK, BLOCK), BLOCK)
        co, si = cosine[here, :], sine[here, :]
        for pair in range(pairs):
            lanes = slice(pair * LANES, (pair + 1) * LANES)
            part = grad_key[here, lanes]
            turn = slice(local + pair * LANES, local + (pair + 1) * LANES)
            grad_proj[here, turn] = (part * co - turned(part, low) * si).astype(bf16)
        grad_proj[here, 2 * local :] = grad_value[here, :].astype(bf16)

    loop(extent // BLOCK, turn_step)


def grad_kernel(slots, first, grad_proj, low_mid, attended, grads, total):
    local = attended.shape[1]
    width = first.shape[1]
    depth = grads.shape[2]
    step_rows = step_of(width, 256)
    for start in range(0, width, step_rows):
        here = slice(start, start + step_rows)
        for number in range(3):
            lanes = slice(number * local, (number + 1) * local)
            total[number, here, :] = dot(first[:, here], grad_proj[:, lanes], TN).astype(bf16)
        total[3, here, :] = dot(low_mid[:, here], attended[...], TN).astype(bf16)
    for number, slot in enumerate(hop_order(grads.shape[0])):
        grads[number] = total[:, pl.ds(pl.multiple_of(slots[slot] * depth, depth), depth), :]


def first_kernel(grad_proj, wide, partial):
    extent, inner = grad_proj.shape
    size = step_of(extent, 384)

    def step(index):
        here = pl.ds(pl.multiple_of(index * size, size), size)
        partial[here, :] = dot(grad_proj[here, :], wide[:, :inner], NT).astype(bf16)

    loop(extent // size, step)


def final_kernel(tokens, gain, grad_middle, own, other, before, after, middle, feed_own, feed_other, mixed, token_grad):
    rows, width = tokens.shape
    gains = gain[:1, :]
    size = BLOCK

    def back(here, grad):
        hat, scale = normed(tokens[here, :].astype(f32))
        return norm_back(grad, gains, hat, scale)

    def step(index):
        at = pl.multiple_of(index * size, size)
        here, wider = pl.ds(at, size), pl.ds(pl.multiple_of(at + HALF, HALF), size)
        grad = own[wider, :].astype(f32) + other[wider, :].astype(f32)
        token_grad[here, :] = grad_middle[here, :] + back(here, grad)
        feed = feed_own[here, :].astype(f32) + feed_other[here, :].astype(f32)
        mixed[here, :] = (middle[here, :] + feed).astype(bf16)

    loop(rows // size, step)
    for start, edge in ((0, before), (rows - HALF, after)):
        here = pl.ds(start, HALF)
        token_grad[here, :] += back(here, edge[...].astype(f32))


def exchange(initial, last):
    devices, spot = lax.axis_size("ctx"), lax.axis_index("ctx")
    if devices == 2:
        got = lax.ppermute(jnp.where(spot == 0, last, initial), "ctx", [(0, 1), (1, 0)])
        none = jnp.zeros_like(got)
        return jnp.where(spot == 1, got, none), jnp.where(spot == 0, got, none)
    up = [(i, i + 1) for i in range(devices - 1)]
    return lax.ppermute(last, "ctx", up), lax.ppermute(initial, "ctx", [(j, i) for i, j in up])


def swap(array, axis="tensor"):
    return lax.ppermute(array, axis, [(0, 1), (1, 0)])


def ring():
    count = lax.axis_size("dp")
    order = [2 * i for i in range(count // 2)] + [2 * i + 1 for i in reversed(range(count // 2))]
    ahead = [(order[i], order[(i + 1) % count]) for i in range(count)]
    back = [(j, i) for i, j in ahead]
    index = lax.axis_index("dp")
    spot = jnp.where(index % 2 == 0, index // 2, count - 1 - index // 2)
    place = (spot + jnp.arange(count, dtype=jnp.int32)) % count
    slots = jnp.where(place < count // 2, 2 * place, 2 * (count - 1 - place) + 1)
    return count, ahead, back, slots.astype(jnp.int32)


def tied(values, others):
    held = lax.optimization_barrier((tuple(values), tuple(others)))
    return held[0]


class RingGather:
    def __init__(self, block, cut):
        self.count, self.ahead, self.back, _ = ring()
        self.cut = cut
        self.pieces = {0: (block,)}
        self.state = (block, block)
        self.hops = 0

    def hop(self):
        one, two = self.state
        middle = self.count // 2
        if self.hops + 1 == middle:
            one, two = one[: self.cut], two[self.cut :]
        one, two = lax.ppermute(one, "dp", self.ahead), lax.ppermute(two, "dp", self.back)
        self.hops += 1
        one, two = lax.optimization_barrier((one, two))
        self.state = (one, two)
        if self.hops == middle:
            self.pieces[middle] = (one, two)
        else:
            self.pieces[self.count - self.hops], self.pieces[self.hops] = (one,), (two,)

    def after(self, others):
        self.state = tied(self.state, others)


class RingScatter:
    def __init__(self, parts, axis):
        self.count, self.ahead, self.back, _ = ring()
        self.parts = parts
        self.axis = axis
        self.hops = 0
        self.state = ()

    def part(self, at):
        total = self.parts[0][at]
        for part in self.parts[1:]:
            total = total + part[at]
        return total

    def hop(self):
        if self.hops == 0:
            one, two = jnp.split(self.part(0), 2, axis=self.axis)
        else:
            one, two = self.state
            if self.hops == 1:
                none = jnp.zeros_like(one)
                one = jnp.concatenate([one, none], axis=self.axis)
                two = jnp.concatenate([none, two], axis=self.axis)
            at = 2 * self.hops - 1
            one, two = self.part(at) + one, self.part(at + 1) + two
        one, two = lax.ppermute(one, "dp", self.ahead), lax.ppermute(two, "dp", self.back)
        self.state = lax.optimization_barrier((one, two))
        self.hops += 1

    def after(self, others):
        self.state = tied(self.state, others)

    def total(self):
        one, two = self.state
        return (self.part(self.count - 1).astype(f32) + one.astype(f32) + two.astype(f32)).astype(bf16)


def tables(lengths, rows):
    place = lax.axis_index("ctx") * rows
    ends = jnp.cumsum(lengths[0])
    starts = ends - lengths[0]
    span = place + jnp.arange(-HALF, rows + HALF, dtype=jnp.int32)
    inside = (span[:, None] >= starts[None, :]) & (span[:, None] < ends[None, :])
    position = span - jnp.sum(jnp.where(inside, starts[None, :], 0), axis=1)
    lane = jnp.arange(LANES, dtype=jnp.int32)
    number = (lane % (HEAD // 2)).astype(f32)
    freq = jnp.exp(number * (-2.0 * math.log(10000.0) / HEAD))
    angle = position.astype(f32)[:, None] * freq[None, :]
    sine = jnp.sin(angle)
    sine = jnp.where((lane % HEAD < HEAD // 2)[None, :], -sine, sine)
    bounds = jnp.concatenate([ends, place[None]]).astype(jnp.int32)
    return jnp.cos(angle), sine, bounds


def body(tokens, lengths, gain_one, w_qkv, w_out, gain_two, w_in, w_down, cotangent):
    rows, width = tokens.shape
    local, units = w_out.shape[0], w_down.shape[0]
    pairs, blocks, extent = local // LANES, rows // BLOCK, rows + WINDOW
    groups = lax.axis_size("dp")
    depth = width // groups
    middle_hop = groups // 2
    split = lax.axis_size("ctx") == 2
    spot = lax.axis_index("ctx")
    low = spot == 0
    gains = jnp.pad(jnp.stack([gain_one, gain_two]), ((0, PAD - 2), (0, local - depth)))
    mine_one = jnp.concatenate([w_qkv.reshape(3 * depth, local), w_out.T, gains])
    now = RingGather(mine_one, 2 * depth)
    now.hop()
    before, after = exchange(tokens[:HALF], tokens[rows - HALF :])
    slots = ring()[-1]
    mine_two = jnp.concatenate([w_in, w_down.T[None]])
    if split:
        sides = [mine_two[:, : depth // 2], mine_two[:, depth // 2 :]]
        mine_two, other_two = jnp.where(low, sides[0], sides[1]), jnp.where(low, sides[1], sides[0])
        parts_at = jnp.stack([spot, 1 - spot]).astype(jnp.int32)
    else:
        parts_at = jnp.zeros((1,), jnp.int32)
    later = RingGather(tied([mine_two], now.state)[0], 1)
    now.hop()
    later.hop()
    cosine, sine, bounds = tables(lengths, rows)
    later.after(now.state)
    while now.hops < middle_hop:
        now.hop()
        later.hop()
        later.after(now.state)
    while later.hops < middle_hop:
        later.hop()
    hat, = call(
        norm_kernel, [shape((extent, width), f32)], (tokens, before, after), rows * width * 2000, "first_norm"
    )
    pieces = [piece for slot in range(groups) for piece in now.pieces[slot]]
    wide, gain, first, query, key, value = call(
        project_kernel,
        [
            shape((width, 4 * local), bf16),
            shape((PAD, width), f32),
            shape((extent, width), bf16),
            shape((rows, local), bf16),
            shape((extent, local), bf16),
            shape((extent, local), bf16),
        ],
        (hat, cosine, sine),
        2 * rows * width * local * 8,
        "project",
        (slots,),
        [pltpu.VMEM((groups, PAD, local), bf16), pltpu.SemaphoreType.DMA((5 * groups,))],
        pieces,
    )
    held = {slot: later.pieces[slot][0] for slot in range(groups) if slot != middle_hop}
    held[middle_hop] = jnp.concatenate(later.pieces[middle_hop])
    if split:
        early = [slot for hop in range(1, middle_hop // 2 + 1) for slot in (hop, groups - hop)]
        late = [slot for slot in range(1, groups) if slot not in early]
        others = {0: other_two}
        for batch in (early, late):
            got = swap(jnp.stack([held[slot] for slot in batch]), "ctx")
            if batch is early:
                query, key, value = tied([query, key, value], [got])
            for number, slot in enumerate(batch):
                others[slot] = got[number]
        query, key, value = tied([query, key, value], later.state)
        pieces = [piece for slot in range(groups) for piece in (held[slot], others[slot])]
    else:
        got = held[middle_hop]
        pieces = [held[slot] for slot in range(groups)]
    shares, attended, branch = call(
        attend_kernel,
        [
            shape((blocks * pairs, KEYS, KEYS), bf16),
            shape((rows, local), bf16),
            shape((rows, width), bf16),
        ],
        (query, key, value, wide),
        2 * rows * width * local * 16,
        "attend",
        (bounds,),
    )
    branch, = tied([branch], [got])
    branch_other = swap(branch)
    middle, second, hidden, grad_gate, grad_upper, partial, whole = call(
        feed_kernel,
        [
            shape((rows, width), f32),
            shape((rows, width), bf16),
            shape((rows, units), bf16),
            shape((rows, units), bf16),
            shape((rows, units), bf16),
            shape((rows, width), bf16),
            shape((3, width, units), bf16),
        ],
        (tokens, branch, branch_other, gain, cotangent),
        2 * rows * width * units * 8,
        "feed_forward_and_back",
        (slots, parts_at),
        [pltpu.SemaphoreType.DMA((len(pieces),))],
        pieces,
    )
    partial_other = swap(partial)
    ways = 2 if split else 1
    grads_two = call(
        weight_kernel,
        [shape((groups, 3, depth // ways, units), bf16)] * ways,
        (second, hidden, grad_gate, grad_upper, cotangent),
        2 * rows * width * units * 5,
        "feed_weight_grads",
        (slots, parts_at),
        [pltpu.VMEM((3, width, units), bf16)],
    )
    if split:
        grads_two = [grads_two[0], swap(grads_two[1], "ctx")]
    feed, = call(
        feed_out_kernel,
        [shape((rows, width), bf16)],
        (hidden, whole),
        2 * rows * width * units,
        "feed_out",
    )
    feed_other = swap(feed)
    grad_middle, low_mid, grad_att = call(
        middle_kernel,
        [shape((rows, width), f32), shape((rows, width), bf16), shape((rows, local), bf16)],
        (middle, partial, partial_other, gain, cotangent, wide),
        2 * rows * width * local * 4,
        "middle_grad",
    )
    grad_proj, = call(
        back_kernel,
        [shape((extent, 3 * local), bf16)],
        (query, key, value, shares, grad_att, cosine, sine),
        2 * rows * width * local * 16,
        "attention_back",
        (),
        [pltpu.VMEM((extent, local), f32)] * 2,
    )
    grads_one, = call(
        grad_kernel,
        [shape((groups, 4, depth, local), bf16)],
        (first, grad_proj, low_mid, attended),
        2 * rows * width * local * 6,
        "attention_weight_grads",
        (slots,),
        [pltpu.VMEM((4, width, local), bf16)],
    )
    sums_one = RingScatter([grads_one], 0)
    sums_one.hop()
    sums_two = RingScatter(tied(grads_two, sums_one.state), 1)
    sums_two.hop()
    first_part, = call(
        first_kernel,
        [shape((extent, width), bf16)],
        (tied([grad_proj], [grads_one])[0], wide),
        2 * rows * width * local * 3,
        "first_grad",
    )
    first_other = swap(first_part)

    def edge_sum(at):
        here = slice(at, at + HALF)
        return (first_part[here].astype(f32) + first_other[here].astype(f32)).astype(bf16)

    sums_one.after([first_part, feed])
    while sums_one.hops < middle_hop - 1:
        sums_one.hop()
        sums_two.after(sums_one.state)
        sums_two.hop()
    from_before, from_after = exchange(edge_sum(0), edge_sum(rows + HALF))
    sums_one.after([from_before, from_after])
    sums_one.hop()
    sums_two.after(sums_one.state)
    sums_two.hop()
    mixed, token_grad = call(
        final_kernel,
        [shape((rows, width), bf16), shape((rows, width), f32)],
        (tokens, gain, grad_middle, first_part, first_other, from_before, from_after, middle, feed, feed_other),
        rows * width * 2000,
        "token_grad",
    )
    one, two = tied([sums_one.total()], [mixed, token_grad])[0], sums_two.total()
    if split:
        one = one.astype(f32) + swap(one, "ctx").astype(f32)
        got = swap(two, "ctx")
        two = jnp.concatenate([jnp.where(low, two, got), jnp.where(low, got, two)], axis=1).astype(f32)
    else:
        one, two = lax.psum(one, "ctx").astype(f32), lax.psum(two, "ctx").astype(f32)
    gain_one_grad = jnp.sum(one[:3] * w_qkv.astype(f32), axis=(0, 2)) / gain_one.astype(f32)
    gain_two_grad = jnp.sum(two[:2] * w_in.astype(f32), axis=(0, 2)) / gain_two.astype(f32)
    both = jnp.stack([gain_one_grad, gain_two_grad])
    both = both + swap(both)
    return (mixed, token_grad, both[0], one[:3], one[3].T, both[1], two[:2], two[2].T)


def solution(mesh):
    in_specs = (
        P(("dp", "ctx"), None),
        P("dp", None),
        P("dp"),
        P(None, "dp", "tensor"),
        P("tensor", "dp"),
        P("dp"),
        P(None, "dp", "tensor"),
        P("tensor", "dp"),
        P(("dp", "ctx"), None),
    )
    out_specs = (
        P(("dp", "ctx"), None),
        P(("dp", "ctx"), None),
        P("dp"),
        P(None, "dp", "tensor"),
        P("tensor", "dp"),
        P("dp"),
        P(None, "dp", "tensor"),
        P("tensor", "dp"),
    )
    return jax.shard_map(body, mesh=mesh, in_specs=in_specs, out_specs=out_specs, check_vma=False)
```

```python
import functools
import math

import jax
import jax.numpy as jnp
from jax import lax
from jax.experimental import pallas as pl
from jax.experimental.pallas import tpu as pltpu
from jax.sharding import PartitionSpec as P

HEAD = 64
WINDOW = 128
NSEQ = 4
HALF = WINDOW // 2
PAD = 16
BLOCK = 128
LANES = 128
KEYS = BLOCK + WINDOW

norm_eps = 1e-05
f32 = jnp.float32
bf16 = jnp.bfloat16

NN = (((1,), (0,)), ((), ()))
NT = (((1,), (1,)), ((), ()))
TN = (((0,), (0,)), ((), ()))


def dot(a, b, dims=NN):
    return lax.dot_general(a, b, dims, preferred_element_type=f32)


def step_of(rows, most):
    best = LANES
    for size in range(LANES, most + 1, LANES):
        if rows % size == 0:
            best = size
    return best


def call(kernel, out_shape, args, flops, name, scalars=(), scratch=(), raw=(), raw_out=()):
    vmem = pl.BlockSpec(memory_space=pltpu.VMEM)
    smem = pl.BlockSpec(memory_space=pltpu.SMEM)
    anywhere = pl.BlockSpec(memory_space=pl.ANY)
    moved = sum(x.size * x.dtype.itemsize for x in (*args, *out_shape))
    held = sum(math.prod(x.shape) * jnp.dtype(x.dtype).itemsize for x in scratch if x.dtype in (f32, bf16))
    limit = min(56 * 2**20, moved // 2 + held + 4 * 2**20)
    return pl.pallas_call(
        kernel,
        out_shape=[*out_shape, *raw_out],
        in_specs=[smem] * len(scalars) + [vmem] * len(args) + [anywhere] * len(raw),
        out_specs=[vmem] * len(out_shape) + [pl.BlockSpec(memory_space=pltpu.HBM)] * len(raw_out),
        scratch_shapes=scratch,
        compiler_params=pltpu.CompilerParams(vmem_limit_bytes=limit),
        cost_estimate=pl.CostEstimate(flops=flops, bytes_accessed=moved, transcendentals=0),
        name=name,
    )(*scalars, *args, *raw)


def shape(dims, dtype):
    return jax.ShapeDtypeStruct(dims, dtype)


def normed(values):
    centered = values - jnp.mean(values, axis=-1, keepdims=True)
    spread = jnp.mean(centered * centered, axis=-1, keepdims=True)
    scale = lax.rsqrt(spread + norm_eps)
    return centered * scale, scale


def norm_back(grad, gain, hat, scale):
    inner = grad * gain
    one = jnp.mean(inner, axis=-1, keepdims=True)
    two = jnp.mean(inner * hat, axis=-1, keepdims=True)
    return scale * (inner - one - hat * two)


def turned(values, low):
    return jnp.where(low, pltpu.roll(values, LANES - HEAD // 2, 1), pltpu.roll(values, HEAD // 2, 1))


def halves(values):
    even = (lax.broadcasted_iota(jnp.int32, (1, LANES), 1) < HEAD).astype(f32).astype(bf16)
    return jnp.concatenate([values * even, values * (1 - even)], axis=0)


def joined(values):
    return jnp.concatenate([values[:HEAD, :BLOCK], values[HEAD:, BLOCK:]], axis=0).T


def loop(count, body):
    def run(index, carry):
        body(index)
        return carry

    lax.fori_loop(0, count, run, 0)


def begin(copies, sems):
    started = []
    for number, (source, target) in enumerate(copies):
        copy = pltpu.make_async_copy(source, target, sems.at[number])
        copy.start()
        started.append(copy)
    return started


def end(started):
    for copy in started:
        copy.wait()


def norm_kernel(tokens, before, after, hat):
    rows, width = tokens.shape

    def norm_rows(src, dst, size):
        hat[pl.ds(dst, size), :] = normed(src.astype(f32))[0]

    norm_rows(before[...], 0, HALF)
    norm_rows(after[...], rows + HALF, HALF)

    def norm_step(index):
        at = pl.multiple_of(index * BLOCK, BLOCK)
        norm_rows(tokens[pl.ds(at, BLOCK), :], pl.multiple_of(at + HALF, HALF), BLOCK)

    loop(rows // BLOCK, norm_step)


def piece_plan(count, sizes, break_at):
    plan, used = [], 0
    for slot in range(count):
        row, sources = 0, []
        for number, size in enumerate(sizes):
            if slot == count // 2 and number == break_at:
                used, row = used + 1, 0
            sources.append((used, row))
            row += size
        plan.append(tuple(sources))
        used += 1
    return plan


def project_kernel(slots, hat, cosine, sine, *rest):
    pieces, (wide, gain, first, query, key, value, gain_held, sems) = rest[:-8], rest[-8:]
    extent, local = key.shape
    rows = query.shape[0]
    width = hat.shape[1]
    pairs = local // LANES
    groups = gain_held.shape[0]
    depth = width // groups
    plan = piece_plan(groups, [depth] * 4 + [PAD], 2)
    copies = []
    for number, sources in enumerate(plan):
        place = pl.ds(pl.multiple_of(slots[number] * depth, depth), depth)
        for part, (piece, row) in enumerate(sources[:4]):
            lanes = slice(part * local, (part + 1) * local)
            copies.append((pieces[piece].at[row : row + depth, :], wide.at[place, lanes]))
        piece, row = sources[4]
        copies.append((pieces[piece].at[row : row + PAD, :], gain_held.at[number]))
    end(begin(copies, sems))
    lane = lax.broadcasted_iota(jnp.int32, (LANES, width), 1) - lax.broadcasted_iota(jnp.int32, (LANES, width), 0)
    gain_sum = jnp.zeros((PAD, width), f32)
    for number in range(groups):
        spread = jnp.where(lane == slots[number] * depth, 1.0, 0.0).astype(bf16)
        gain_sum += dot(gain_held[number][:, :LANES], spread)
    gain[...] = gain_sum
    gains = gain_sum[:1]
    query_w, key_w, value_w = (wide.at[:, at * local : (at + 1) * local] for at in range(3))
    low = lax.broadcasted_iota(jnp.int32, (1, LANES), 1) % HEAD < HEAD // 2

    def rotated(src, at, size, dst, place, scale):
        co, si = cosine[pl.ds(at, size), :], sine[pl.ds(at, size), :]
        for pair in range(pairs):
            lanes = slice(pair * LANES, (pair + 1) * LANES)
            value = src[:, lanes]
            dst[pl.ds(place, size), lanes] = ((value * co + turned(value, low) * si) * scale).astype(bf16)

    chunk = step_of(extent, 384)

    def key_step(index):
        at = pl.multiple_of(index * chunk, chunk)
        here = pl.ds(at, chunk)
        part = (hat[here, :] * gains).astype(bf16)
        first[here, :] = part
        rotated(dot(part, key_w[...]), at, chunk, key, at, 1.0)
        value[here, :] = dot(part, value_w[...]).astype(bf16)

    loop(extent // chunk, key_step)
    size = step_of(rows, 256)

    def query_step(index):
        at = pl.multiple_of(index * size, size)
        start = pl.multiple_of(at + HALF, HALF)
        rotated(dot(first[pl.ds(start, size), :], query_w[...]), start, size, query, at, HEAD**-0.5)

    loop(rows // size, query_step)


def attend_kernel(chosen, last, bounds, query, key, value, *rest):
    if last:
        wide, first, done, attended, branch, *kept, held, sems = rest
        shares, kept = kept[0], kept[1:]
    else:
        attended, shares, held, sems = rest
    rows, local = query.shape
    count = len(chosen)
    started = []
    if last:
        started = begin(list(zip((first, query, key, value), kept)), sems.at[2 * count :])
        attended[...] = done[...]
    key_at = lax.broadcasted_iota(jnp.int32, (KEYS, KEYS), 0)
    lane_at = lax.broadcasted_iota(jnp.int32, (1, KEYS), 1) % BLOCK

    def out_copy(index, number, side):
        return pltpu.make_async_copy(
            held.at[side, number], shares.at[index * count + number], sems.at[side * count + number]
        )

    def attend_step(index, side, old):
        at = pl.multiple_of(index * BLOCK, BLOCK)
        origin = bounds[NSEQ] + at - HALF
        own = lane_at + (origin + HALF)
        begin_at = jnp.zeros_like(own)
        end_at = jnp.zeros_like(own) + bounds[NSEQ - 1]
        for number in range(NSEQ - 1):
            begin_at = jnp.where(own >= bounds[number], bounds[number], begin_at)
        for number in reversed(range(NSEQ - 1)):
            end_at = jnp.where(own < bounds[number], bounds[number], end_at)
        least = jnp.maximum(lane_at, begin_at - origin)
        most = jnp.minimum(lane_at + WINDOW, end_at - 1 - origin)
        allowed = (key_at >= least) & (key_at <= most)
        for number, pair in enumerate(chosen):
            lanes = slice(pair * LANES, (pair + 1) * LANES)
            both = halves(query[pl.ds(at, BLOCK), lanes])
            scores = jnp.where(allowed, dot(key[pl.ds(at, KEYS), lanes], both, NT), -1e30)
            weight = jnp.exp(scores - jnp.max(scores, axis=0, keepdims=True))
            part = (weight * (1.0 / jnp.sum(weight, axis=0, keepdims=True))).astype(bf16)
            if old is not None:
                out_copy(old, number, side).wait()
            held[side, number] = part
            out_copy(index, number, side).start()
            mixed = dot(value[pl.ds(at, KEYS), lanes], part, TN)
            attended[pl.ds(at, BLOCK), lanes] = joined(mixed).astype(bf16)

    steps = rows // BLOCK
    attend_step(0, 0, None)
    attend_step(1, 1, None)

    def two_steps(index):
        for side in range(2):
            attend_step(2 * index + 2 + side, side, 2 * index + side)

    loop(steps // 2 - 1, two_steps)
    for side in range(2):
        for number in range(count):
            out_copy(steps - 2 + side, number, side).wait()
    end(started)
    if not last:
        return
    out_t = wide.at[:, 3 * local :]
    size = step_of(rows, 256)

    def out_step(index):
        here = pl.ds(pl.multiple_of(index * size, size), size)
        branch[here, :] = dot(attended[here, :], out_t[...], NT).astype(bf16)

    loop(rows // size, out_step)


def feed_kernel(slots, tokens, own, other, gain, cotangent, *rest):
    pieces, rest = rest[:-8], rest[-8:]
    middle, second, hidden, grad_gate, grad_upper, partial, whole, sems = rest
    rows, width = tokens.shape
    groups = slots.shape[0]
    depth = width // groups
    copies = []
    for number, sources in enumerate(piece_plan(groups, [depth] * 3, 1)):
        place = pl.ds(pl.multiple_of(slots[number] * depth, depth), depth)
        for part, (piece, row) in enumerate(sources):
            copies.append((pieces[piece].at[row : row + depth, :], whole.at[part, place, :]))
    started = begin(copies, sems)
    gate_w, upper_w, down_t = (whole.at[number] for number in range(3))
    gains = gain[1:2, :]
    size = step_of(rows, 256)

    def norm_step(index):
        here = pl.ds(pl.multiple_of(index * size, size), size)
        mid = tokens[here, :].astype(f32) + (own[here, :].astype(f32) + other[here, :].astype(f32))
        middle[here, :] = mid
        second[here, :] = (normed(mid)[0] * gains).astype(bf16)

    loop(rows // size, norm_step)
    end(started)

    def step(index):
        here = pl.ds(pl.multiple_of(index * size, size), size)
        low = second[here, :]
        gate = dot(low, gate_w[...])
        upper = dot(low, upper_w[...])
        grad = dot(cotangent[here, :], down_t[...])
        share = 0.5 * (1.0 + lax.erf(gate * (0.5**0.5)))
        smooth = gate * share
        slope = share + gate * (jnp.exp(gate * gate * -0.5) * ((2.0 * math.pi) ** -0.5))
        hidden[here, :] = (smooth * upper).astype(bf16)
        gate_low = (grad * upper * slope).astype(bf16)
        upper_low = (grad * smooth).astype(bf16)
        grad_gate[here, :] = gate_low
        grad_upper[here, :] = upper_low
        partial[here, :] = (dot(gate_low, gate_w[...], NT) + dot(upper_low, upper_w[...], NT)).astype(bf16)

    loop(rows // size, step)


def feed_out_kernel(hidden, whole, feed):
    rows = hidden.shape[0]
    size = step_of(rows, 256)

    def step(index):
        here = pl.ds(pl.multiple_of(index * size, size), size)
        feed[here, :] = dot(hidden[here, :], whole[2], NT).astype(bf16)

    loop(rows // size, step)


def weight_kernel(slots, second, hidden, grad_gate, grad_upper, cotangent, grads, total):
    rows, width = second.shape
    step_rows = step_of(width, 256)
    for number, (left, right) in enumerate(((second, grad_gate), (second, grad_upper), (cotangent, hidden))):
        for start in range(0, width, step_rows):
            here = slice(start, start + step_rows)
            total[number, here, :] = dot(left[:, here], right[...], TN).astype(bf16)
    depth = grads.shape[2]
    for number, slot in enumerate(hop_order(grads.shape[0])):
        grads[number] = total[:, pl.ds(pl.multiple_of(slots[slot] * depth, depth), depth), :]


def hop_order(count):
    middle = count // 2
    order = [middle]
    for hop in range(middle - 1, 0, -1):
        order += [hop, count - hop]
    return order + [0]


def middle_kernel(middle, own, other, gain, cotangent, wide, grad_middle, low_mid, grad_att):
    rows, width = middle.shape
    local = grad_att.shape[1]
    out_t = wide.at[:, 3 * local :]
    gains = gain[1:2, :]
    size = step_of(rows, 256)

    def norm_step(index):
        here = pl.ds(pl.multiple_of(index * size, size), size)
        hat, scale = normed(middle[here, :])
        grad = own[here, :].astype(f32) + other[here, :].astype(f32)
        mid = cotangent[here, :].astype(f32) + norm_back(grad, gains, hat, scale)
        grad_middle[here, :] = mid
        mid_low = mid.astype(bf16)
        low_mid[here, :] = mid_low
        grad_att[here, :] = dot(mid_low, out_t[...]).astype(bf16)

    loop(rows // size, norm_step)


def back_kernel(chosen, query, key, value, shares, grad_att, cosine, sine, *rest):
    parts, (grad_key, grad_value) = rest[:-2], rest[-2:]
    rows = query.shape[0]
    extent = key.shape[0]
    count = len(chosen)
    grad_key[...] = jnp.zeros_like(grad_key)
    grad_value[...] = jnp.zeros_like(grad_value)
    low = lax.broadcasted_iota(jnp.int32, (1, LANES), 1) % HEAD < HEAD // 2
    zero = jnp.zeros((HALF, LANES), bf16)
    for part in parts:
        part[:HALF, :LANES] = zero
        part[rows + HALF :, :LANES] = zero

    def attend_step(index):
        at = pl.multiple_of(index * BLOCK, BLOCK)
        start = pl.multiple_of(at + HALF, HALF)
        co, si = cosine[pl.ds(start, BLOCK), :], sine[pl.ds(start, BLOCK), :]
        for number, pair in enumerate(chosen):
            lanes = slice(pair * LANES, (pair + 1) * LANES)
            here = slice(number * LANES, (number + 1) * LANES)
            both = halves(query[pl.ds(at, BLOCK), lanes])
            grad = halves(grad_att[pl.ds(at, BLOCK), lanes])
            keys = key[pl.ds(at, KEYS), lanes]
            part = shares[index * count + number]
            wide = part.astype(f32)
            grad_shares = dot(value[pl.ds(at, KEYS), lanes], grad, NT)
            delta = jnp.sum(wide * grad_shares, axis=0, keepdims=True)
            raw = (wide * (grad_shares - delta)).astype(bf16)
            grad_query = joined(dot(keys, raw, TN)) * HEAD**-0.5
            turn = (grad_query * co - turned(grad_query, low) * si).astype(bf16)
            parts[number][pl.ds(start, BLOCK), :LANES] = turn
            grad_key[pl.ds(at, KEYS), here] += dot(raw, both)
            grad_value[pl.ds(at, KEYS), here] += dot(part, grad)

    loop(rows // BLOCK, attend_step)

    def turn_step(index):
        here = pl.ds(pl.multiple_of(index * BLOCK, BLOCK), BLOCK)
        co, si = cosine[here, :], sine[here, :]
        for number, out in enumerate(parts):
            lanes = slice(number * LANES, (number + 1) * LANES)
            part = grad_key[here, lanes]
            out[here, LANES : 2 * LANES] = (part * co - turned(part, low) * si).astype(bf16)
            out[here, 2 * LANES :] = grad_value[here, lanes].astype(bf16)

    loop(extent // BLOCK, turn_step)


def grad_kernel(slots, first, low_mid, attended, *rest):
    parts, (grad_proj, grads_a, grads_b, total) = rest[:-4], rest[-4:]
    local = attended.shape[1]
    width = first.shape[1]
    depth = grads_a.shape[2]
    for pair, part in enumerate(parts):
        for number in range(3):
            lanes = slice(number * local + pair * LANES, number * local + (pair + 1) * LANES)
            grad_proj[:, lanes] = part[:, number * LANES : (number + 1) * LANES]
    step_rows = step_of(width, 256)
    for start in range(0, width, step_rows):
        here = slice(start, start + step_rows)
        for number in range(3):
            lanes = slice(number * local, (number + 1) * local)
            total[number, here, :] = dot(first[:, here], grad_proj[:, lanes], TN).astype(bf16)
        total[3, here, :] = dot(low_mid[:, here], attended[...], TN).astype(bf16)
    for number, slot in enumerate(hop_order(grads_a.shape[0])):
        place = pl.ds(pl.multiple_of(slots[slot] * depth, depth), depth)
        grads_a[number] = total[:2, place, :]
        grads_b[number] = total[2:, place, :]


def first_kernel(grad_proj, wide, partial):
    extent, inner = grad_proj.shape
    size = step_of(extent, 384)

    def step(index):
        here = pl.ds(pl.multiple_of(index * size, size), size)
        partial[here, :] = dot(grad_proj[here, :], wide[:, :inner], NT).astype(bf16)

    loop(extent // size, step)


def final_kernel(tokens, gain, grad_middle, own, other, before, after, middle, feed_own, feed_other, mixed, token_grad):
    rows, width = tokens.shape
    gains = gain[:1, :]
    size = BLOCK

    def back(here, grad):
        hat, scale = normed(tokens[here, :].astype(f32))
        return norm_back(grad, gains, hat, scale)

    def step(index):
        at = pl.multiple_of(index * size, size)
        here, wider = pl.ds(at, size), pl.ds(pl.multiple_of(at + HALF, HALF), size)
        grad = own[wider, :].astype(f32) + other[wider, :].astype(f32)
        token_grad[here, :] = grad_middle[here, :] + back(here, grad)
        feed = feed_own[here, :].astype(f32) + feed_other[here, :].astype(f32)
        mixed[here, :] = (middle[here, :] + feed).astype(bf16)

    loop(rows // size, step)
    for start, edge in ((0, before), (rows - HALF, after)):
        here = pl.ds(start, HALF)
        token_grad[here, :] += back(here, edge[...].astype(f32))


def exchange(initial, last):
    devices, spot = lax.axis_size("ctx"), lax.axis_index("ctx")
    if devices == 2:
        got = lax.ppermute(jnp.where(spot == 0, last, initial), "ctx", [(0, 1), (1, 0)])
        none = jnp.zeros_like(got)
        return jnp.where(spot == 1, got, none), jnp.where(spot == 0, got, none)
    up = [(i, i + 1) for i in range(devices - 1)]
    return lax.ppermute(last, "ctx", up), lax.ppermute(initial, "ctx", [(j, i) for i, j in up])


def over_ctx(array):
    if lax.axis_size("ctx") == 2:
        return array.astype(f32) + swap(array, "ctx").astype(f32)
    return lax.psum(array, "ctx").astype(f32)


def swap(array, axis="tensor"):
    return lax.ppermute(array, axis, [(0, 1), (1, 0)])


def ring():
    count = lax.axis_size("dp")
    order = [2 * i for i in range(count // 2)] + [2 * i + 1 for i in reversed(range(count // 2))]
    ahead = [(order[i], order[(i + 1) % count]) for i in range(count)]
    back = [(j, i) for i, j in ahead]
    index = lax.axis_index("dp")
    spot = jnp.where(index % 2 == 0, index // 2, count - 1 - index // 2)
    place = (spot + jnp.arange(count, dtype=jnp.int32)) % count
    slots = jnp.where(place < count // 2, 2 * place, 2 * (count - 1 - place) + 1)
    return count, ahead, back, slots.astype(jnp.int32)


def tied(values, others):
    held = lax.optimization_barrier((tuple(values), tuple(others)))
    return held[0]


def locked(values, chain):
    held = lax.optimization_barrier((tuple(values), tuple(chain.state)))
    chain.state = held[1]
    return held[0]


class RingGather:
    def __init__(self, block, cut):
        self.count, self.ahead, self.back, _ = ring()
        self.cut = cut
        self.pieces = {0: (block,)}
        self.state = (block, block)
        self.hops = 0

    def hop(self):
        one, two = self.state
        middle = self.count // 2
        if self.hops + 1 == middle:
            one, two = one[: self.cut], two[self.cut :]
        one, two = lax.ppermute(one, "dp", self.ahead), lax.ppermute(two, "dp", self.back)
        self.hops += 1
        one, two = lax.optimization_barrier((one, two))
        self.state = (one, two)
        if self.hops == middle:
            self.pieces[middle] = (one, two)
        else:
            self.pieces[self.count - self.hops], self.pieces[self.hops] = (one,), (two,)

    def after(self, others):
        self.state = tied(self.state, others)


class RingScatter:
    def __init__(self, parts, axis):
        self.count, self.ahead, self.back, _ = ring()
        self.parts = parts
        self.axis = axis
        self.hops = 0
        self.state = ()

    def part(self, at):
        total = self.parts[0][at]
        for part in self.parts[1:]:
            total = total + part[at]
        return total

    def hop(self):
        if self.hops == 0:
            one, two = jnp.split(self.part(0), 2, axis=self.axis)
        else:
            one, two = self.state
            if self.hops == 1:
                none = jnp.zeros_like(one)
                one = jnp.concatenate([one, none], axis=self.axis)
                two = jnp.concatenate([none, two], axis=self.axis)
            at = 2 * self.hops - 1
            one, two = self.part(at) + one, self.part(at + 1) + two
        one, two = lax.ppermute(one, "dp", self.ahead), lax.ppermute(two, "dp", self.back)
        self.state = lax.optimization_barrier((one, two))
        self.hops += 1

    def after(self, others):
        self.state = tied(self.state, others)

    def total(self):
        one, two = self.state
        return (self.part(self.count - 1).astype(f32) + one.astype(f32) + two.astype(f32)).astype(bf16)


def tables(lengths, rows):
    place = lax.axis_index("ctx") * rows
    ends = jnp.cumsum(lengths[0])
    starts = ends - lengths[0]
    span = place + jnp.arange(-HALF, rows + HALF, dtype=jnp.int32)
    inside = (span[:, None] >= starts[None, :]) & (span[:, None] < ends[None, :])
    position = span - jnp.sum(jnp.where(inside, starts[None, :], 0), axis=1)
    lane = jnp.arange(LANES, dtype=jnp.int32)
    number = (lane % (HEAD // 2)).astype(f32)
    freq = jnp.exp(number * (-2.0 * math.log(10000.0) / HEAD))
    angle = position.astype(f32)[:, None] * freq[None, :]
    sine = jnp.sin(angle)
    sine = jnp.where((lane % HEAD < HEAD // 2)[None, :], -sine, sine)
    bounds = jnp.concatenate([ends, place[None]]).astype(jnp.int32)
    return jnp.cos(angle), sine, bounds


def body(tokens, lengths, gain_one, w_qkv, w_out, gain_two, w_in, w_down, cotangent):
    rows, width = tokens.shape
    local, units = w_out.shape[0], w_down.shape[0]
    pairs, blocks, extent = local // LANES, rows // BLOCK, rows + WINDOW
    groups = lax.axis_size("dp")
    depth = width // groups
    middle_hop = groups // 2
    gains = jnp.pad(jnp.stack([gain_one, gain_two]), ((0, PAD - 2), (0, local - depth)))
    mine_one = jnp.concatenate([w_qkv.reshape(3 * depth, local), w_out.T, gains])
    now = RingGather(mine_one, 2 * depth)
    now.hop()
    before, after = exchange(tokens[:HALF], tokens[rows - HALF :])
    slots = ring()[-1]
    cosine, sine, bounds = tables(lengths, rows)
    while now.hops < middle_hop:
        now.hop()
    mine_two = jnp.concatenate([w_in.reshape(2 * depth, units), w_down.T])
    later = RingGather(tied([mine_two], now.state)[0], depth)
    later.hop()
    hat, = call(
        norm_kernel, [shape((extent, width), f32)], (tokens, before, after), rows * width * 2000, "first_norm"
    )
    pieces = [piece for slot in range(groups) for piece in now.pieces[slot]]
    wide, gain, first, query, key, value = call(
        project_kernel,
        [
            shape((width, 4 * local), bf16),
            shape((PAD, width), f32),
            shape((extent, width), bf16),
            shape((rows, local), bf16),
            shape((extent, local), bf16),
            shape((extent, local), bf16),
        ],
        (hat, cosine, sine),
        2 * rows * width * local * 8,
        "project",
        (slots,),
        [pltpu.VMEM((groups, PAD, local), bf16), pltpu.SemaphoreType.DMA((5 * groups,))],
        pieces,
    )
    early, late = tuple(range(pairs - 1)), (pairs - 1,)

    def share_shapes(chosen):
        return (
            shape((blocks * len(chosen), KEYS, KEYS), bf16),
            [pltpu.VMEM((2, len(chosen), KEYS, KEYS), bf16), pltpu.SemaphoreType.DMA((2 * len(chosen) + 4,))],
        )

    query, key, value = tied([query, key, value], later.state)
    later.hop()
    out, scratch = share_shapes(early)
    attended, shares_early = call(
        functools.partial(attend_kernel, early, False),
        [shape((rows, local), bf16)],
        (query, key, value),
        2 * rows * width * local * 10,
        "attend",
        (bounds,),
        scratch,
        (),
        [out],
    )
    attended, = locked([attended], later)
    later.hop()
    out, scratch = share_shapes(late)
    attended, branch, shares_late, first, query, key, value = call(
        functools.partial(attend_kernel, late, True),
        [shape((rows, local), bf16), shape((rows, width), bf16)],
        (query, key, value, wide, first, attended),
        2 * rows * width * local * 7,
        "attend",
        (bounds,),
        scratch,
        (),
        [out] + [shape(x.shape, bf16) for x in (first, query, key, value)],
    )
    branch_other = swap(branch)
    later.after([branch])
    while later.hops < middle_hop:
        later.hop()
    pieces = [piece for slot in range(groups) for piece in later.pieces[slot]]
    middle, second, hidden, grad_gate, grad_upper, partial, whole = call(
        feed_kernel,
        [
            shape((rows, width), f32),
            shape((rows, width), bf16),
            shape((rows, units), bf16),
            shape((rows, units), bf16),
            shape((rows, units), bf16),
            shape((rows, width), bf16),
            shape((3, width, units), bf16),
        ],
        (tokens, branch, branch_other, gain, cotangent),
        2 * rows * width * units * 8,
        "feed_forward_and_back",
        (slots,),
        [pltpu.SemaphoreType.DMA((3 * groups,))],
        pieces,
    )
    partial_other = swap(partial)
    grads_two, = call(
        weight_kernel,
        [shape((groups, 3, depth, units), bf16)],
        (second, hidden, grad_gate, grad_upper, cotangent),
        2 * rows * width * units * 5,
        "feed_weight_grads",
        (slots,),
        [pltpu.VMEM((3, width, units), bf16)],
    )
    sums_two = RingScatter([grads_two], 1)
    sums_two.hop()
    grad_middle, low_mid, grad_att = call(
        middle_kernel,
        [shape((rows, width), f32), shape((rows, width), bf16), shape((rows, local), bf16)],
        (middle, partial, partial_other, gain, cotangent, wide),
        2 * rows * width * local * 4,
        "middle_grad",
    )
    grad_att, = locked([grad_att], sums_two)
    sums_two.hop()
    grad_parts = []
    for chosen, shares in ((early, shares_early), (late, shares_late)):
        if grad_parts:
            grad_att, *grad_parts = locked([grad_att, *grad_parts], sums_two)
            sums_two.hop()
        grad_parts += call(
            functools.partial(back_kernel, chosen),
            [shape((extent, 3 * LANES), bf16)] * len(chosen),
            (query, key, value, shares, grad_att, cosine, sine),
            2 * rows * width * local * 5 * len(chosen),
            "attention_back",
            (),
            [pltpu.VMEM((extent, len(chosen) * LANES), f32)] * 2,
        )
    feed, = call(
        feed_out_kernel,
        [shape((rows, width), bf16)],
        (tied([hidden], grad_parts[: len(early)])[0], whole),
        2 * rows * width * units,
        "feed_out",
    )
    feed_other = swap(feed)
    grad_parts = tied(grad_parts, [feed, *sums_two.state])
    grad_proj, *grads_one = call(
        grad_kernel,
        [shape((extent, 3 * local), bf16)] + [shape((groups, 2, depth, local), bf16)] * 2,
        (first, low_mid, attended, *grad_parts),
        2 * rows * width * local * 6,
        "attention_weight_grads",
        (slots,),
        [pltpu.VMEM((4, width, local), bf16)],
    )
    sums_one = [RingScatter([part], 0) for part in grads_one]
    sums_one[0].hop()
    sums_one[1].hop()
    sums_two.after(sums_one[0].state)
    while sums_two.hops < middle_hop:
        sums_two.hop()
    first_part, = call(
        first_kernel,
        [shape((extent, width), bf16)],
        (tied([grad_proj], grads_one)[0], wide),
        2 * rows * width * local * 3,
        "first_grad",
    )
    first_other = swap(first_part)

    def edge_sum(at):
        here = slice(at, at + HALF)
        return (first_part[here].astype(f32) + first_other[here].astype(f32)).astype(bf16)

    for chain in sums_one:
        chain.after([first_part, feed])
    while sums_one[0].hops < middle_hop - 1:
        for chain in sums_one:
            chain.hop()
    from_before, from_after = exchange(edge_sum(0), edge_sum(rows + HALF))
    for chain in sums_one:
        chain.after([from_before, from_after])
        chain.hop()
    mixed, token_grad = call(
        final_kernel,
        [shape((rows, width), bf16), shape((rows, width), f32)],
        (tokens, gain, grad_middle, first_part, first_other, from_before, from_after, middle, feed, feed_other),
        rows * width * 2000,
        "token_grad",
    )
    two = over_ctx(sums_two.total())
    one = [over_ctx(sums_one[0].total()), over_ctx(sums_one[1].total())]
    one = jnp.concatenate(one)
    gain_one_grad = jnp.sum(one[:3] * w_qkv.astype(f32), axis=(0, 2)) / gain_one.astype(f32)
    gain_two_grad = jnp.sum(two[:2] * w_in.astype(f32), axis=(0, 2)) / gain_two.astype(f32)
    both = jnp.stack([gain_one_grad, gain_two_grad])
    both = both + swap(both)
    return (mixed, token_grad, both[0], one[:3], one[3].T, both[1], two[:2], two[2].T)


def solution(mesh):
    in_specs = (
        P(("dp", "ctx"), None),
        P("dp", None),
        P("dp"),
        P(None, "dp", "tensor"),
        P("tensor", "dp"),
        P("dp"),
        P(None, "dp", "tensor"),
        P("tensor", "dp"),
        P(("dp", "ctx"), None),
    )
    out_specs = (
        P(("dp", "ctx"), None),
        P(("dp", "ctx"), None),
        P("dp"),
        P(None, "dp", "tensor"),
        P("tensor", "dp"),
        P("dp"),
        P(None, "dp", "tensor"),
        P("tensor", "dp"),
    )
    return jax.shard_map(body, mesh=mesh, in_specs=in_specs, out_specs=out_specs, check_vma=False)
```

```python
import functools
import math

import jax
import jax.numpy as jnp
from jax import lax
from jax.experimental import pallas as pl
from jax.experimental.pallas import tpu as pltpu
from jax.sharding import PartitionSpec as P

HEAD = 64
WINDOW = 128
NSEQ = 4
HALF = WINDOW // 2
PAD = 16
BLOCK = 128
LANES = 128
KEYS = BLOCK + WINDOW

norm_eps = 1e-05
f32 = jnp.float32
bf16 = jnp.bfloat16

NN = (((1,), (0,)), ((), ()))
NT = (((1,), (1,)), ((), ()))
TN = (((0,), (0,)), ((), ()))


def dot(a, b, dims=NN):
    return lax.dot_general(a, b, dims, preferred_element_type=f32)


def step_of(rows, most):
    best = LANES
    for size in range(LANES, most + 1, LANES):
        if rows % size == 0:
            best = size
    return best


def call(kernel, out_shape, args, flops, name, scalars=(), scratch=()):
    vmem = pl.BlockSpec(memory_space=pltpu.VMEM)
    smem = pl.BlockSpec(memory_space=pltpu.SMEM)
    moved = sum(x.size * x.dtype.itemsize for x in (*args, *out_shape))
    held = sum(math.prod(x.shape) * jnp.dtype(x.dtype).itemsize for x in scratch if x.dtype in (f32, bf16))
    limit = min(56 * 2**20, moved // 2 + held + 4 * 2**20)
    return pl.pallas_call(
        kernel,
        out_shape=out_shape,
        in_specs=[smem] * len(scalars) + [vmem] * len(args),
        out_specs=[vmem] * len(out_shape),
        scratch_shapes=scratch,
        compiler_params=pltpu.CompilerParams(vmem_limit_bytes=limit),
        cost_estimate=pl.CostEstimate(flops=flops, bytes_accessed=moved, transcendentals=0),
        name=name,
    )(*scalars, *args)


def shape(dims, dtype):
    return jax.ShapeDtypeStruct(dims, dtype)


def normed(values):
    centered = values - jnp.mean(values, axis=-1, keepdims=True)
    spread = jnp.mean(centered * centered, axis=-1, keepdims=True)
    scale = lax.rsqrt(spread + norm_eps)
    return centered * scale, scale


def norm_back(grad, gain, hat, scale):
    inner = grad * gain
    one = jnp.mean(inner, axis=-1, keepdims=True)
    two = jnp.mean(inner * hat, axis=-1, keepdims=True)
    return scale * (inner - one - hat * two)


def turned(values, low):
    return jnp.where(low, pltpu.roll(values, LANES - HEAD // 2, 1), pltpu.roll(values, HEAD // 2, 1))


def halves(values):
    even = (lax.broadcasted_iota(jnp.int32, (1, LANES), 1) < HEAD).astype(f32).astype(bf16)
    return jnp.concatenate([values * even, values * (1 - even)], axis=0)


def joined(values):
    return jnp.concatenate([values[:HEAD, :BLOCK], values[HEAD:, BLOCK:]], axis=0).T


def loop(count, body):
    def run(index, carry):
        body(index)
        return carry

    lax.fori_loop(0, count, run, 0)


def norm_kernel(tokens, before, after, hat):
    rows, width = tokens.shape

    def norm_rows(src, dst, size):
        hat[pl.ds(dst, size), :] = normed(src.astype(f32))[0]

    norm_rows(before[...], 0, HALF)
    norm_rows(after[...], rows + HALF, HALF)

    def norm_step(index):
        at = pl.multiple_of(index * BLOCK, BLOCK)
        norm_rows(tokens[pl.ds(at, BLOCK), :], pl.multiple_of(at + HALF, HALF), BLOCK)

    loop(rows // BLOCK, norm_step)


def piece_plan(count, sizes, break_at):
    plan, used = [], 0
    for slot in range(count):
        row, sources = 0, []
        for number, size in enumerate(sizes):
            if slot == count // 2 and number == break_at:
                used, row = used + 1, 0
            sources.append((used, row))
            row += size
        plan.append(tuple(sources))
        used += 1
    return plan


def project_kernel(slots, hat, cosine, sine, *rest):
    pieces, (wide, gain, first, query, key, value) = rest[:-6], rest[-6:]
    extent, local = key.shape
    rows = query.shape[0]
    width = hat.shape[1]
    pairs = local // LANES
    groups = slots.shape[0]
    depth = width // groups
    plan = piece_plan(groups, [depth] * 4 + [PAD], 2)
    lane = lax.broadcasted_iota(jnp.int32, (LANES, width), 1) - lax.broadcasted_iota(jnp.int32, (LANES, width), 0)
    gain_sum = jnp.zeros((PAD, width), f32)
    for number, sources in enumerate(plan):
        start = pl.multiple_of(slots[number] * depth, depth)
        for part, (piece, row) in enumerate(sources[:4]):
            lanes = slice(part * local, (part + 1) * local)
            wide[pl.ds(start, depth), lanes] = pieces[piece][row : row + depth, :]
        piece, row = sources[4]
        spread = jnp.where(lane == start, 1.0, 0.0).astype(bf16)
        gain_sum += dot(pieces[piece][row : row + PAD, :LANES], spread)
    gain[...] = gain_sum
    gains = gain_sum[:1]
    query_w, key_w, value_w = (wide.at[:, at * local : (at + 1) * local] for at in range(3))
    low = lax.broadcasted_iota(jnp.int32, (1, LANES), 1) % HEAD < HEAD // 2

    def rotated(src, at, size, dst, place, scale):
        co, si = cosine[pl.ds(at, size), :], sine[pl.ds(at, size), :]
        for pair in range(pairs):
            lanes = slice(pair * LANES, (pair + 1) * LANES)
            value = src[:, lanes]
            dst[pl.ds(place, size), lanes] = ((value * co + turned(value, low) * si) * scale).astype(bf16)

    chunk = step_of(extent, 384)

    def key_step(index):
        at = pl.multiple_of(index * chunk, chunk)
        here = pl.ds(at, chunk)
        part = (hat[here, :] * gains).astype(bf16)
        first[here, :] = part
        rotated(dot(part, key_w[...]), at, chunk, key, at, 1.0)
        value[here, :] = dot(part, value_w[...]).astype(bf16)

    loop(extent // chunk, key_step)
    size = step_of(rows, 256)

    def query_step(index):
        at = pl.multiple_of(index * size, size)
        start = pl.multiple_of(at + HALF, HALF)
        rotated(dot(first[pl.ds(start, size), :], query_w[...]), start, size, query, at, HEAD**-0.5)

    loop(rows // size, query_step)


def attend_kernel(bounds, query, key, value, wide, shares, attended, branch):
    rows, local = query.shape
    pairs = local // LANES
    key_at = lax.broadcasted_iota(jnp.int32, (KEYS, KEYS), 0)
    lane_at = lax.broadcasted_iota(jnp.int32, (1, KEYS), 1) % BLOCK

    def attend_step(index):
        at = pl.multiple_of(index * BLOCK, BLOCK)
        origin = bounds[NSEQ] + at - HALF
        own = lane_at + (origin + HALF)
        begin = jnp.zeros_like(own)
        end = jnp.zeros_like(own) + bounds[NSEQ - 1]
        for number in range(NSEQ - 1):
            begin = jnp.where(own >= bounds[number], bounds[number], begin)
        for number in reversed(range(NSEQ - 1)):
            end = jnp.where(own < bounds[number], bounds[number], end)
        least = jnp.maximum(lane_at, begin - origin)
        most = jnp.minimum(lane_at + WINDOW, end - 1 - origin)
        allowed = (key_at >= least) & (key_at <= most)
        for pair in range(pairs):
            lanes = slice(pair * LANES, (pair + 1) * LANES)
            both = halves(query[pl.ds(at, BLOCK), lanes])
            scores = jnp.where(allowed, dot(key[pl.ds(at, KEYS), lanes], both, NT), -1e30)
            weight = jnp.exp(scores - jnp.max(scores, axis=0, keepdims=True))
            part = (weight * (1.0 / jnp.sum(weight, axis=0, keepdims=True))).astype(bf16)
            shares[index * pairs + pair] = part
            mixed = dot(value[pl.ds(at, KEYS), lanes], part, TN)
            attended[pl.ds(at, BLOCK), lanes] = joined(mixed).astype(bf16)

    loop(rows // BLOCK, attend_step)
    out_t = wide.at[:, 3 * local :]
    size = step_of(rows, 256)

    def out_step(index):
        here = pl.ds(pl.multiple_of(index * size, size), size)
        branch[here, :] = dot(attended[here, :], out_t[...], NT).astype(bf16)

    loop(rows // size, out_step)


def feed_kernel(plan, slots, parts_at, tokens, own, other, gain, cotangent, *rest):
    pieces, rest = rest[:-7], rest[-7:]
    middle, second, hidden, grad_gate, grad_upper, partial, whole = rest
    rows, width = tokens.shape
    depth = width // slots.shape[0]
    size = depth // (1 + max(side for _, side, _, _, _ in plan))
    for slot, side, part, piece, at in plan:
        start = slots[slot] * depth + parts_at[side] * size
        whole[part, pl.ds(pl.multiple_of(start, size), size), :] = pieces[piece][at]
    gate_w, upper_w, down_t = (whole.at[number] for number in range(3))
    gains = gain[1:2, :]
    size = step_of(rows, 256)

    def step(index):
        at = pl.multiple_of(index * size, size)
        here = pl.ds(at, size)
        mid = tokens[here, :].astype(f32) + (own[here, :].astype(f32) + other[here, :].astype(f32))
        middle[here, :] = mid
        hat, _ = normed(mid)
        low = (hat * gains).astype(bf16)
        second[here, :] = low
        gate = dot(low, gate_w[...])
        upper = dot(low, upper_w[...])
        grad = dot(cotangent[here, :], down_t[...])
        share = 0.5 * (1.0 + lax.erf(gate * (0.5**0.5)))
        smooth = gate * share
        slope = share + gate * (jnp.exp(gate * gate * -0.5) * ((2.0 * math.pi) ** -0.5))
        hidden[here, :] = (smooth * upper).astype(bf16)
        gate_low = (grad * upper * slope).astype(bf16)
        upper_low = (grad * smooth).astype(bf16)
        grad_gate[here, :] = gate_low
        grad_upper[here, :] = upper_low
        partial[here, :] = (dot(gate_low, gate_w[...], NT) + dot(upper_low, upper_w[...], NT)).astype(bf16)

    loop(rows // size, step)


def feed_out_kernel(hidden, whole, feed):
    rows = hidden.shape[0]
    size = step_of(rows, 256)

    def step(index):
        here = pl.ds(pl.multiple_of(index * size, size), size)
        feed[here, :] = dot(hidden[here, :], whole[2], NT).astype(bf16)

    loop(rows // size, step)


def weight_kernel(slots, parts_at, second, hidden, grad_gate, grad_upper, cotangent, *rest):
    outs, total = rest[:-1], rest[-1]
    rows, width = second.shape
    step_rows = step_of(width, 256)
    for number, (left, right) in enumerate(((second, grad_gate), (second, grad_upper), (cotangent, hidden))):
        for start in range(0, width, step_rows):
            here = slice(start, start + step_rows)
            total[number, here, :] = dot(left[:, here], right[...], TN).astype(bf16)
    size = outs[0].shape[2]
    for number, slot in enumerate(hop_order(outs[0].shape[0])):
        for side, out in enumerate(outs):
            start = slots[slot] * (size * len(outs)) + parts_at[side] * size
            out[number] = total[:, pl.ds(pl.multiple_of(start, size), size), :]


def hop_order(count):
    middle = count // 2
    order = [middle]
    for hop in range(middle - 1, 0, -1):
        order += [hop, count - hop]
    return order + [0]


def middle_kernel(middle, own, other, gain, cotangent, wide, grad_middle, low_mid, grad_att):
    rows, width = middle.shape
    local = grad_att.shape[1]
    out_t = wide.at[:, 3 * local :]
    gains = gain[1:2, :]
    size = step_of(rows, 256)

    def norm_step(index):
        here = pl.ds(pl.multiple_of(index * size, size), size)
        hat, scale = normed(middle[here, :])
        grad = own[here, :].astype(f32) + other[here, :].astype(f32)
        mid = cotangent[here, :].astype(f32) + norm_back(grad, gains, hat, scale)
        grad_middle[here, :] = mid
        mid_low = mid.astype(bf16)
        low_mid[here, :] = mid_low
        grad_att[here, :] = dot(mid_low, out_t[...]).astype(bf16)

    loop(rows // size, norm_step)


def back_kernel(query, key, value, shares, grad_att, cosine, sine, grad_proj, grad_key, grad_value):
    rows, local = query.shape
    extent = key.shape[0]
    pairs = local // LANES
    grad_key[...] = jnp.zeros_like(grad_key)
    grad_value[...] = jnp.zeros_like(grad_value)
    low = lax.broadcasted_iota(jnp.int32, (1, LANES), 1) % HEAD < HEAD // 2
    zero = jnp.zeros((HALF, local), bf16)
    grad_proj[:HALF, :local] = zero
    grad_proj[rows + HALF :, :local] = zero

    def attend_step(index):
        at = pl.multiple_of(index * BLOCK, BLOCK)
        start = pl.multiple_of(at + HALF, HALF)
        co, si = cosine[pl.ds(start, BLOCK), :], sine[pl.ds(start, BLOCK), :]
        found = []
        for pair in range(pairs):
            lanes = slice(pair * LANES, (pair + 1) * LANES)
            both = halves(query[pl.ds(at, BLOCK), lanes])
            grad = halves(grad_att[pl.ds(at, BLOCK), lanes])
            keys = key[pl.ds(at, KEYS), lanes]
            part = shares[index * pairs + pair]
            wide = part.astype(f32)
            grad_shares = dot(value[pl.ds(at, KEYS), lanes], grad, NT)
            delta = jnp.sum(wide * grad_shares, axis=0, keepdims=True)
            raw = (wide * (grad_shares - delta)).astype(bf16)
            grad_query = joined(dot(keys, raw, TN)) * HEAD**-0.5
            turn = (grad_query * co - turned(grad_query, low) * si).astype(bf16)
            found.append((lanes, turn, dot(raw, both), dot(part, grad)))
        for lanes, turn, key_part, value_part in found:
            grad_proj[pl.ds(start, BLOCK), lanes] = turn
            grad_key[pl.ds(at, KEYS), lanes] += key_part
            grad_value[pl.ds(at, KEYS), lanes] += value_part

    loop(rows // BLOCK, attend_step)

    def turn_step(index):
        here = pl.ds(pl.multiple_of(index * BLOCK, BLOCK), BLOCK)
        co, si = cosine[here, :], sine[here, :]
        for pair in range(pairs):
            lanes = slice(pair * LANES, (pair + 1) * LANES)
            part = grad_key[here, lanes]
            turn = slice(local + pair * LANES, local + (pair + 1) * LANES)
            grad_proj[here, turn] = (part * co - turned(part, low) * si).astype(bf16)
        grad_proj[here, 2 * local :] = grad_value[here, :].astype(bf16)

    loop(extent // BLOCK, turn_step)


def grad_kernel(slots, first, grad_proj, low_mid, attended, grads, total):
    local = attended.shape[1]
    width = first.shape[1]
    depth = grads.shape[2]
    step_rows = step_of(width, 256)
    for start in range(0, width, step_rows):
        here = slice(start, start + step_rows)
        for number in range(3):
            lanes = slice(number * local, (number + 1) * local)
            total[number, here, :] = dot(first[:, here], grad_proj[:, lanes], TN).astype(bf16)
        total[3, here, :] = dot(low_mid[:, here], attended[...], TN).astype(bf16)
    for number, slot in enumerate(hop_order(grads.shape[0])):
        grads[number] = total[:, pl.ds(pl.multiple_of(slots[slot] * depth, depth), depth), :]


def first_kernel(grad_proj, wide, partial):
    extent, inner = grad_proj.shape
    size = step_of(extent, 384)

    def step(index):
        here = pl.ds(pl.multiple_of(index * size, size), size)
        partial[here, :] = dot(grad_proj[here, :], wide[:, :inner], NT).astype(bf16)

    loop(extent // size, step)


def final_kernel(tokens, gain, grad_middle, own, other, before, after, middle, feed_own, feed_other, mixed, token_grad):
    rows, width = tokens.shape
    gains = gain[:1, :]
    size = BLOCK

    def back(here, grad):
        hat, scale = normed(tokens[here, :].astype(f32))
        return norm_back(grad, gains, hat, scale)

    def step(index):
        at = pl.multiple_of(index * size, size)
        here, wider = pl.ds(at, size), pl.ds(pl.multiple_of(at + HALF, HALF), size)
        grad = own[wider, :].astype(f32) + other[wider, :].astype(f32)
        token_grad[here, :] = grad_middle[here, :] + back(here, grad)
        feed = feed_own[here, :].astype(f32) + feed_other[here, :].astype(f32)
        mixed[here, :] = (middle[here, :] + feed).astype(bf16)

    loop(rows // size, step)
    for start, edge in ((0, before), (rows - HALF, after)):
        here = pl.ds(start, HALF)
        token_grad[here, :] += back(here, edge[...].astype(f32))


def exchange(initial, last):
    devices, spot = lax.axis_size("ctx"), lax.axis_index("ctx")
    if devices == 2:
        got = lax.ppermute(jnp.where(spot == 0, last, initial), "ctx", [(0, 1), (1, 0)])
        none = jnp.zeros_like(got)
        return jnp.where(spot == 1, got, none), jnp.where(spot == 0, got, none)
    up = [(i, i + 1) for i in range(devices - 1)]
    return lax.ppermute(last, "ctx", up), lax.ppermute(initial, "ctx", [(j, i) for i, j in up])


def swap(array, axis="tensor"):
    return lax.ppermute(array, axis, [(0, 1), (1, 0)])


def ring():
    count = lax.axis_size("dp")
    order = [2 * i for i in range(count // 2)] + [2 * i + 1 for i in reversed(range(count // 2))]
    ahead = [(order[i], order[(i + 1) % count]) for i in range(count)]
    back = [(j, i) for i, j in ahead]
    index = lax.axis_index("dp")
    spot = jnp.where(index % 2 == 0, index // 2, count - 1 - index // 2)
    place = (spot + jnp.arange(count, dtype=jnp.int32)) % count
    slots = jnp.where(place < count // 2, 2 * place, 2 * (count - 1 - place) + 1)
    return count, ahead, back, slots.astype(jnp.int32)


def tied(values, others):
    held = lax.optimization_barrier((tuple(values), tuple(others)))
    return held[0]


class RingGather:
    def __init__(self, block, cut):
        self.count, self.ahead, self.back, _ = ring()
        self.cut = cut
        self.pieces = {0: (block,)}
        self.state = (block, block)
        self.hops = 0

    def hop(self):
        one, two = self.state
        middle = self.count // 2
        if self.hops + 1 == middle:
            one, two = one[: self.cut], two[self.cut :]
        one, two = lax.ppermute(one, "dp", self.ahead), lax.ppermute(two, "dp", self.back)
        self.hops += 1
        one, two = lax.optimization_barrier((one, two))
        self.state = (one, two)
        if self.hops == middle:
            self.pieces[middle] = (one, two)
        else:
            self.pieces[self.count - self.hops], self.pieces[self.hops] = (one,), (two,)

    def after(self, others):
        self.state = tied(self.state, others)


class RingScatter:
    def __init__(self, parts, axis):
        self.count, self.ahead, self.back, _ = ring()
        self.parts = parts
        self.axis = axis
        self.hops = 0
        self.state = ()

    def part(self, at):
        total = self.parts[0][at]
        for part in self.parts[1:]:
            total = total + part[at]
        return total

    def hop(self):
        if self.hops == 0:
            one, two = jnp.split(self.part(0), 2, axis=self.axis)
        else:
            one, two = self.state
            if self.hops == 1:
                none = jnp.zeros_like(one)
                one = jnp.concatenate([one, none], axis=self.axis)
                two = jnp.concatenate([none, two], axis=self.axis)
            at = 2 * self.hops - 1
            one, two = self.part(at) + one, self.part(at + 1) + two
        one, two = lax.ppermute(one, "dp", self.ahead), lax.ppermute(two, "dp", self.back)
        self.state = lax.optimization_barrier((one, two))
        self.hops += 1

    def after(self, others):
        self.state = tied(self.state, others)

    def total(self):
        one, two = self.state
        return (self.part(self.count - 1).astype(f32) + one.astype(f32) + two.astype(f32)).astype(bf16)


def tables(lengths, rows):
    place = lax.axis_index("ctx") * rows
    ends = jnp.cumsum(lengths[0])
    starts = ends - lengths[0]
    span = place + jnp.arange(-HALF, rows + HALF, dtype=jnp.int32)
    inside = (span[:, None] >= starts[None, :]) & (span[:, None] < ends[None, :])
    position = span - jnp.sum(jnp.where(inside, starts[None, :], 0), axis=1)
    lane = jnp.arange(LANES, dtype=jnp.int32)
    number = (lane % (HEAD // 2)).astype(f32)
    freq = jnp.exp(number * (-2.0 * math.log(10000.0) / HEAD))
    angle = position.astype(f32)[:, None] * freq[None, :]
    sine = jnp.sin(angle)
    sine = jnp.where((lane % HEAD < HEAD // 2)[None, :], -sine, sine)
    bounds = jnp.concatenate([ends, place[None]]).astype(jnp.int32)
    return jnp.cos(angle), sine, bounds


def body(tokens, lengths, gain_one, w_qkv, w_out, gain_two, w_in, w_down, cotangent):
    rows, width = tokens.shape
    local, units = w_out.shape[0], w_down.shape[0]
    pairs, blocks, extent = local // LANES, rows // BLOCK, rows + WINDOW
    groups = lax.axis_size("dp")
    depth = width // groups
    middle_hop = groups // 2
    split = lax.axis_size("ctx") == 2
    spot = lax.axis_index("ctx")
    low = spot == 0
    gains = jnp.pad(jnp.stack([gain_one, gain_two]), ((0, PAD - 2), (0, local - depth)))
    mine_one = jnp.concatenate([w_qkv.reshape(3 * depth, local), w_out.T, gains])
    now = RingGather(mine_one, 2 * depth)
    now.hop()
    before, after = exchange(tokens[:HALF], tokens[rows - HALF :])
    slots = ring()[-1]
    mine_two = jnp.concatenate([w_in, w_down.T[None]])
    if split:
        sides = [mine_two[:, : depth // 2], mine_two[:, depth // 2 :]]
        mine_two, other_two = jnp.where(low, sides[0], sides[1]), jnp.where(low, sides[1], sides[0])
        parts_at = jnp.stack([spot, 1 - spot]).astype(jnp.int32)
    else:
        parts_at = jnp.zeros((1,), jnp.int32)
    now.hop()
    cosine, sine, bounds = tables(lengths, rows)
    later = RingGather(tied([mine_two], now.state)[0], 1)
    while now.hops < middle_hop:
        if now.hops > 2:
            later.after(now.state)
        later.hop()
        now.hop()
    hat, = call(
        norm_kernel, [shape((extent, width), f32)], (tokens, before, after), rows * width * 2000, "first_norm"
    )
    pieces = [piece for slot in range(groups) for piece in now.pieces[slot]]
    wide, gain, first, query, key, value = call(
        project_kernel,
        [
            shape((width, 4 * local), bf16),
            shape((PAD, width), f32),
            shape((extent, width), bf16),
            shape((rows, local), bf16),
            shape((extent, local), bf16),
            shape((extent, local), bf16),
        ],
        (hat, cosine, sine, *pieces),
        2 * rows * width * local * 8,
        "project",
        (slots,),
    )
    later.after(now.state)
    batches, others = [], []

    def trade(slots_now):
        batches.append(slots_now)
        others.append(swap(jnp.stack([later.pieces[slot][0] for slot in slots_now]), "ctx"))

    if split:
        trade([groups - 1, 1])
    later.hop()
    query, key, value = tied([query, key, value], [*later.state, *others])
    if split:
        trade([slot for slot in later.pieces if slot not in (0, 1, groups - 1)])
    while later.hops < middle_hop:
        later.hop()
    shares, attended, branch = call(
        attend_kernel,
        [
            shape((blocks * pairs, KEYS, KEYS), bf16),
            shape((rows, local), bf16),
            shape((rows, width), bf16),
        ],
        (query, key, value, wide),
        2 * rows * width * local * 16,
        "attend",
        (bounds,),
    )
    branch, *later.state = tied([branch, *later.state], others)
    branch_other = swap(branch)
    plan, pieces = [], []
    for slot in range(groups):
        part = 0
        for piece in later.pieces[slot]:
            for at in range(piece.shape[0]):
                plan.append((slot, 0, part, len(pieces), at))
                part += 1
            pieces.append(piece)
    if split:
        batches.append([middle_hop])
        others.append(swap(jnp.concatenate(later.state), "ctx")[None])
        batches.append([0])
        others.append(other_two[None])
        for batch, other in zip(batches, others):
            for number, slot in enumerate(batch):
                plan += [(slot, 1, part, len(pieces), (number, part)) for part in range(3)]
            pieces.append(other)
    middle, second, hidden, grad_gate, grad_upper, partial, whole = call(
        functools.partial(feed_kernel, tuple(plan)),
        [
            shape((rows, width), f32),
            shape((rows, width), bf16),
            shape((rows, units), bf16),
            shape((rows, units), bf16),
            shape((rows, units), bf16),
            shape((rows, width), bf16),
            shape((3, width, units), bf16),
        ],
        (tokens, branch, branch_other, gain, cotangent, *pieces),
        2 * rows * width * units * 8,
        "feed_forward_and_back",
        (slots, parts_at),
    )
    partial_other = swap(partial)
    ways = 2 if split else 1
    grads_two = call(
        weight_kernel,
        [shape((groups, 3, depth // ways, units), bf16)] * ways,
        (second, hidden, grad_gate, grad_upper, cotangent),
        2 * rows * width * units * 5,
        "feed_weight_grads",
        (slots, parts_at),
        [pltpu.VMEM((3, width, units), bf16)],
    )
    if split:
        grads_two = [grads_two[0], swap(grads_two[1], "ctx")]
    middle, = tied([middle], grads_two[:1])
    grad_middle, low_mid, grad_att = call(
        middle_kernel,
        [shape((rows, width), f32), shape((rows, width), bf16), shape((rows, local), bf16)],
        (middle, partial, partial_other, gain, cotangent, wide),
        2 * rows * width * local * 4,
        "middle_grad",
    )
    grad_proj, = call(
        back_kernel,
        [shape((extent, 3 * local), bf16)],
        (query, key, value, shares, grad_att, cosine, sine),
        2 * rows * width * local * 16,
        "attention_back",
        (),
        [pltpu.VMEM((extent, local), f32)] * 2,
    )
    grads_one, = call(
        grad_kernel,
        [shape((groups, 4, depth, local), bf16)],
        (first, grad_proj, low_mid, attended),
        2 * rows * width * local * 6,
        "attention_weight_grads",
        (slots,),
        [pltpu.VMEM((4, width, local), bf16)],
    )
    sums_one = RingScatter([grads_one], 0)
    sums_one.hop()
    sums_two = RingScatter(tied(grads_two, sums_one.state), 1)
    sums_two.hop()
    feed, = call(
        feed_out_kernel,
        [shape((rows, width), bf16)],
        (tied([hidden], [grads_one])[0], whole),
        2 * rows * width * units,
        "feed_out",
    )
    feed_other = swap(feed)
    first_part, = call(
        first_kernel,
        [shape((extent, width), bf16)],
        (tied([grad_proj], sums_one.state)[0], wide),
        2 * rows * width * local * 3,
        "first_grad",
    )
    first_other = swap(first_part)

    def edge_sum(at):
        here = slice(at, at + HALF)
        return (first_part[here].astype(f32) + first_other[here].astype(f32)).astype(bf16)

    while sums_one.hops < middle_hop - 2:
        sums_one.hop()
        sums_two.after(sums_one.state)
        sums_two.hop()
    from_before, from_after = exchange(edge_sum(0), edge_sum(rows + HALF))
    sums_one.after([from_before, from_after])
    sums_one.hop()
    sums_two.after(sums_one.state)
    sums_two.hop()
    tokens, = tied([tokens], sums_one.state)
    sums_one.hop()
    sums_two.hop()
    mixed, token_grad = call(
        final_kernel,
        [shape((rows, width), bf16), shape((rows, width), f32)],
        (tokens, gain, grad_middle, first_part, first_other, from_before, from_after, middle, feed, feed_other),
        rows * width * 2000,
        "token_grad",
    )
    one, two = tied([sums_one.total()], [mixed, token_grad])[0], sums_two.total()
    if split:
        one = one.astype(f32) + swap(one, "ctx").astype(f32)
        got = swap(two, "ctx")
        two = jnp.concatenate([jnp.where(low, two, got), jnp.where(low, got, two)], axis=1).astype(f32)
    else:
        one, two = lax.psum(one, "ctx").astype(f32), lax.psum(two, "ctx").astype(f32)
    gain_one_grad = jnp.sum(one[:3] * w_qkv.astype(f32), axis=(0, 2)) / gain_one.astype(f32)
    gain_two_grad = jnp.sum(two[:2] * w_in.astype(f32), axis=(0, 2)) / gain_two.astype(f32)
    both = jnp.stack([gain_one_grad, gain_two_grad])
    both = both + swap(both)
    return (mixed, token_grad, both[0], one[:3], one[3].T, both[1], two[:2], two[2].T)


def solution(mesh):
    in_specs = (
        P(("dp", "ctx"), None),
        P("dp", None),
        P("dp"),
        P(None, "dp", "tensor"),
        P("tensor", "dp"),
        P("dp"),
        P(None, "dp", "tensor"),
        P("tensor", "dp"),
        P(("dp", "ctx"), None),
    )
    out_specs = (
        P(("dp", "ctx"), None),
        P(("dp", "ctx"), None),
        P("dp"),
        P(None, "dp", "tensor"),
        P("tensor", "dp"),
        P("dp"),
        P(None, "dp", "tensor"),
        P("tensor", "dp"),
    )
    return jax.shard_map(body, mesh=mesh, in_specs=in_specs, out_specs=out_specs, check_vma=False)
```

```python
import functools
import math

import jax
import jax.numpy as jnp
from jax import lax
from jax.experimental import pallas as pl
from jax.experimental.pallas import tpu as pltpu
from jax.sharding import PartitionSpec as P

HEAD = 64
WINDOW = 128
NSEQ = 4
HALF = WINDOW // 2
PAD = 16
SPARE = 6
BLOCK = 128
LANES = 128
KEYS = BLOCK + WINDOW

norm_eps = 1e-05
f32 = jnp.float32
bf16 = jnp.bfloat16

NN = (((1,), (0,)), ((), ()))
NT = (((1,), (1,)), ((), ()))
TN = (((0,), (0,)), ((), ()))


def dot(a, b, dims=NN):
    return lax.dot_general(a, b, dims, preferred_element_type=f32)


def step_of(rows, most):
    best = LANES
    for size in range(LANES, most + 1, LANES):
        if rows % size == 0:
            best = size
    return best


def call(kernel, out_shape, args, flops, name, scalars=(), scratch=()):
    vmem = pl.BlockSpec(memory_space=pltpu.VMEM)
    smem = pl.BlockSpec(memory_space=pltpu.SMEM)
    moved = sum(x.size * x.dtype.itemsize for x in (*args, *out_shape))
    held = sum(math.prod(x.shape) * jnp.dtype(x.dtype).itemsize for x in scratch if x.dtype in (f32, bf16))
    limit = held + SPARE * 2**20
    return pl.pallas_call(
        kernel,
        out_shape=out_shape,
        in_specs=[smem] * len(scalars) + [vmem] * len(args),
        out_specs=[vmem] * len(out_shape),
        scratch_shapes=scratch,
        compiler_params=pltpu.CompilerParams(vmem_limit_bytes=limit),
        cost_estimate=pl.CostEstimate(flops=flops, bytes_accessed=moved, transcendentals=0),
        name=name,
    )(*scalars, *args)


def shape(dims, dtype):
    return jax.ShapeDtypeStruct(dims, dtype)


def normed(values):
    centered = values - jnp.mean(values, axis=-1, keepdims=True)
    spread = jnp.mean(centered * centered, axis=-1, keepdims=True)
    scale = lax.rsqrt(spread + norm_eps)
    return centered * scale, scale


def norm_back(grad, gain, hat, scale):
    inner = grad * gain
    one = jnp.mean(inner, axis=-1, keepdims=True)
    two = jnp.mean(inner * hat, axis=-1, keepdims=True)
    return scale * (inner - one - hat * two)


def turned(values, low):
    return jnp.where(low, pltpu.roll(values, LANES - HEAD // 2, 1), pltpu.roll(values, HEAD // 2, 1))


def halves(values):
    even = (lax.broadcasted_iota(jnp.int32, (1, LANES), 1) < HEAD).astype(f32).astype(bf16)
    return jnp.concatenate([values * even, values * (1 - even)], axis=0)


def joined(values):
    return jnp.concatenate([values[:HEAD, :BLOCK], values[HEAD:, BLOCK:]], axis=0).T


def loop(count, body):
    def run(index, carry):
        body(index)
        return carry

    lax.fori_loop(0, count, run, 0)


def norm_kernel(tokens, before, after, hat):
    rows, width = tokens.shape

    def norm_rows(src, dst, size):
        hat[pl.ds(dst, size), :] = normed(src.astype(f32))[0]

    norm_rows(before[...], 0, HALF)
    norm_rows(after[...], rows + HALF, HALF)

    def norm_step(index):
        at = pl.multiple_of(index * BLOCK, BLOCK)
        norm_rows(tokens[pl.ds(at, BLOCK), :], pl.multiple_of(at + HALF, HALF), BLOCK)

    loop(rows // BLOCK, norm_step)


def piece_plan(count, sizes, break_at):
    plan, used = [], 0
    for slot in range(count):
        row, sources = 0, []
        for number, size in enumerate(sizes):
            if slot == count // 2 and number == break_at:
                used, row = used + 1, 0
            sources.append((used, row))
            row += size
        plan.append(tuple(sources))
        used += 1
    return plan


def project_kernel(slots, hat, cosine, sine, *rest):
    pieces, (wide, gain, first, query, key, value) = rest[:-6], rest[-6:]
    extent, local = key.shape
    rows = query.shape[0]
    width = hat.shape[1]
    pairs = local // LANES
    groups = slots.shape[0]
    depth = width // groups
    plan = piece_plan(groups, [depth] * 4 + [PAD], 2)
    lane = lax.broadcasted_iota(jnp.int32, (LANES, width), 1) - lax.broadcasted_iota(jnp.int32, (LANES, width), 0)
    gain_sum = jnp.zeros((PAD, width), f32)
    for number, sources in enumerate(plan):
        start = pl.multiple_of(slots[number] * depth, depth)
        for part, (piece, row) in enumerate(sources[:4]):
            lanes = slice(part * local, (part + 1) * local)
            wide[pl.ds(start, depth), lanes] = pieces[piece][row : row + depth, :]
        piece, row = sources[4]
        spread = jnp.where(lane == start, 1.0, 0.0).astype(bf16)
        gain_sum += dot(pieces[piece][row : row + PAD, :LANES], spread)
    gain[...] = gain_sum
    gains = gain_sum[:1]
    query_w, key_w, value_w = (wide.at[:, at * local : (at + 1) * local] for at in range(3))
    low = lax.broadcasted_iota(jnp.int32, (1, LANES), 1) % HEAD < HEAD // 2

    def rotated(src, at, size, dst, place, scale):
        co, si = cosine[pl.ds(at, size), :], sine[pl.ds(at, size), :]
        for pair in range(pairs):
            lanes = slice(pair * LANES, (pair + 1) * LANES)
            value = src[:, lanes]
            dst[pl.ds(place, size), lanes] = ((value * co + turned(value, low) * si) * scale).astype(bf16)

    chunk = step_of(extent, 384)

    def key_step(index):
        at = pl.multiple_of(index * chunk, chunk)
        here = pl.ds(at, chunk)
        part = (hat[here, :] * gains).astype(bf16)
        first[here, :] = part
        rotated(dot(part, key_w[...]), at, chunk, key, at, 1.0)
        value[here, :] = dot(part, value_w[...]).astype(bf16)

    loop(extent // chunk, key_step)
    size = step_of(rows, 256)

    def query_step(index):
        at = pl.multiple_of(index * size, size)
        start = pl.multiple_of(at + HALF, HALF)
        rotated(dot(first[pl.ds(start, size), :], query_w[...]), start, size, query, at, HEAD**-0.5)

    loop(rows // size, query_step)


def attend_kernel(chosen, last, bounds, query, key, value, *rest):
    if last:
        wide, done, shares, attended, branch = rest
        attended[...] = done[...]
    else:
        shares, attended = rest
    rows, local = query.shape
    count = len(chosen)
    key_at = lax.broadcasted_iota(jnp.int32, (KEYS, KEYS), 0)
    lane_at = lax.broadcasted_iota(jnp.int32, (1, KEYS), 1) % BLOCK

    def attend_step(index):
        at = pl.multiple_of(index * BLOCK, BLOCK)
        origin = bounds[NSEQ] + at - HALF
        own = lane_at + (origin + HALF)
        begin = jnp.zeros_like(own)
        end = jnp.zeros_like(own) + bounds[NSEQ - 1]
        for number in range(NSEQ - 1):
            begin = jnp.where(own >= bounds[number], bounds[number], begin)
        for number in reversed(range(NSEQ - 1)):
            end = jnp.where(own < bounds[number], bounds[number], end)
        least = jnp.maximum(lane_at, begin - origin)
        most = jnp.minimum(lane_at + WINDOW, end - 1 - origin)
        allowed = (key_at >= least) & (key_at <= most)
        for number, pair in enumerate(chosen):
            lanes = slice(pair * LANES, (pair + 1) * LANES)
            both = halves(query[pl.ds(at, BLOCK), lanes])
            scores = jnp.where(allowed, dot(key[pl.ds(at, KEYS), lanes], both, NT), -1e30)
            weight = jnp.exp(scores - jnp.max(scores, axis=0, keepdims=True))
            part = (weight * (1.0 / jnp.sum(weight, axis=0, keepdims=True))).astype(bf16)
            shares[index * count + number] = part
            mixed = dot(value[pl.ds(at, KEYS), lanes], part, TN)
            attended[pl.ds(at, BLOCK), lanes] = joined(mixed).astype(bf16)

    loop(rows // BLOCK, attend_step)
    if not last:
        return
    out_t = wide.at[:, 3 * local :]
    size = step_of(rows, 256)

    def out_step(index):
        here = pl.ds(pl.multiple_of(index * size, size), size)
        branch[here, :] = dot(attended[here, :], out_t[...], NT).astype(bf16)

    loop(rows // size, out_step)


def feed_kernel(slots, tokens, own, other, gain, cotangent, *rest):
    pieces, rest = rest[:-7], rest[-7:]
    middle, second, hidden, grad_gate, grad_upper, partial, whole = rest
    rows, width = tokens.shape
    groups = slots.shape[0]
    depth = width // groups
    for number, sources in enumerate(piece_plan(groups, [depth] * 3, 1)):
        place = pl.ds(pl.multiple_of(slots[number] * depth, depth), depth)
        for part, (piece, row) in enumerate(sources):
            whole[part, place, :] = pieces[piece][row : row + depth, :]
    gate_w, upper_w, down_t = (whole.at[number] for number in range(3))
    gains = gain[1:2, :]
    size = step_of(rows, 256)

    def step(index):
        here = pl.ds(pl.multiple_of(index * size, size), size)
        mid = tokens[here, :].astype(f32) + (own[here, :].astype(f32) + other[here, :].astype(f32))
        middle[here, :] = mid
        low = (normed(mid)[0] * gains).astype(bf16)
        second[here, :] = low
        gate = dot(low, gate_w[...])
        upper = dot(low, upper_w[...])
        grad = dot(cotangent[here, :], down_t[...])
        share = 0.5 * (1.0 + lax.erf(gate * (0.5**0.5)))
        smooth = gate * share
        slope = share + gate * (jnp.exp(gate * gate * -0.5) * ((2.0 * math.pi) ** -0.5))
        hidden[here, :] = (smooth * upper).astype(bf16)
        gate_low = (grad * upper * slope).astype(bf16)
        upper_low = (grad * smooth).astype(bf16)
        grad_gate[here, :] = gate_low
        grad_upper[here, :] = upper_low
        partial[here, :] = (dot(gate_low, gate_w[...], NT) + dot(upper_low, upper_w[...], NT)).astype(bf16)

    loop(rows // size, step)


def feed_out_kernel(hidden, whole, feed):
    rows = hidden.shape[0]
    size = step_of(rows, 256)

    def step(index):
        here = pl.ds(pl.multiple_of(index * size, size), size)
        feed[here, :] = dot(hidden[here, :], whole[2], NT).astype(bf16)

    loop(rows // size, step)


def weight_kernel(slots, second, hidden, grad_gate, grad_upper, cotangent, grads, total):
    rows, width = second.shape
    step_rows = step_of(width, 256)
    for number, (left, right) in enumerate(((second, grad_gate), (second, grad_upper), (cotangent, hidden))):
        for start in range(0, width, step_rows):
            here = slice(start, start + step_rows)
            total[number, here, :] = dot(left[:, here], right[...], TN).astype(bf16)
    depth = grads.shape[2]
    for number, slot in enumerate(hop_order(grads.shape[0])):
        grads[number] = total[:, pl.ds(pl.multiple_of(slots[slot] * depth, depth), depth), :]


def hop_order(count):
    middle = count // 2
    order = [middle]
    for hop in range(middle - 1, 0, -1):
        order += [hop, count - hop]
    return order + [0]


def middle_kernel(middle, own, other, gain, cotangent, wide, grad_middle, low_mid, grad_att):
    rows, width = middle.shape
    local = grad_att.shape[1]
    out_t = wide.at[:, 3 * local :]
    gains = gain[1:2, :]
    size = step_of(rows, 256)

    def norm_step(index):
        here = pl.ds(pl.multiple_of(index * size, size), size)
        hat, scale = normed(middle[here, :])
        grad = own[here, :].astype(f32) + other[here, :].astype(f32)
        mid = cotangent[here, :].astype(f32) + norm_back(grad, gains, hat, scale)
        grad_middle[here, :] = mid
        mid_low = mid.astype(bf16)
        low_mid[here, :] = mid_low
        grad_att[here, :] = dot(mid_low, out_t[...]).astype(bf16)

    loop(rows // size, norm_step)


def back_kernel(chosen, query, key, value, grad_att, cosine, sine, *rest):
    held, parts, (grad_key, grad_value) = rest[: len(chosen)], rest[len(chosen) : -2], rest[-2:]
    rows = query.shape[0]
    extent = key.shape[0]
    flat = [(part, number, len(group)) for part, group in zip(held, chosen) for number in range(len(group))]
    grad_key[...] = jnp.zeros_like(grad_key)
    grad_value[...] = jnp.zeros_like(grad_value)
    low = lax.broadcasted_iota(jnp.int32, (1, LANES), 1) % HEAD < HEAD // 2
    zero = jnp.zeros((HALF, LANES), bf16)
    for part in parts:
        part[:HALF, :LANES] = zero
        part[rows + HALF :, :LANES] = zero

    def attend_step(index):
        at = pl.multiple_of(index * BLOCK, BLOCK)
        start = pl.multiple_of(at + HALF, HALF)
        co, si = cosine[pl.ds(start, BLOCK), :], sine[pl.ds(start, BLOCK), :]
        for number, (shares, spot, count) in enumerate(flat):
            lanes = slice(number * LANES, (number + 1) * LANES)
            both = halves(query[pl.ds(at, BLOCK), lanes])
            grad = halves(grad_att[pl.ds(at, BLOCK), lanes])
            keys = key[pl.ds(at, KEYS), lanes]
            part = shares[index * count + spot]
            wide = part.astype(f32)
            grad_shares = dot(value[pl.ds(at, KEYS), lanes], grad, NT)
            delta = jnp.sum(wide * grad_shares, axis=0, keepdims=True)
            raw = (wide * (grad_shares - delta)).astype(bf16)
            grad_query = joined(dot(keys, raw, TN)) * HEAD**-0.5
            turn = (grad_query * co - turned(grad_query, low) * si).astype(bf16)
            parts[number][pl.ds(start, BLOCK), :LANES] = turn
            grad_key[pl.ds(at, KEYS), lanes] += dot(raw, both)
            grad_value[pl.ds(at, KEYS), lanes] += dot(part, grad)

    loop(rows // BLOCK, attend_step)

    def turn_step(index):
        here = pl.ds(pl.multiple_of(index * BLOCK, BLOCK), BLOCK)
        co, si = cosine[here, :], sine[here, :]
        for number, out in enumerate(parts):
            lanes = slice(number * LANES, (number + 1) * LANES)
            part = grad_key[here, lanes]
            out[here, LANES : 2 * LANES] = (part * co - turned(part, low) * si).astype(bf16)
            out[here, 2 * LANES :] = grad_value[here, lanes].astype(bf16)

    loop(extent // BLOCK, turn_step)


def grad_kernel(slots, first, low_mid, attended, *rest):
    parts, (grad_proj, grads_a, grads_b, total) = rest[:-4], rest[-4:]
    local = attended.shape[1]
    width = first.shape[1]
    depth = grads_a.shape[2]
    for pair, part in enumerate(parts):
        for number in range(3):
            lanes = slice(number * local + pair * LANES, number * local + (pair + 1) * LANES)
            grad_proj[:, lanes] = part[:, number * LANES : (number + 1) * LANES]
    step_rows = step_of(width, 256)
    for start in range(0, width, step_rows):
        here = slice(start, start + step_rows)
        for number in range(3):
            lanes = slice(number * local, (number + 1) * local)
            total[number, here, :] = dot(first[:, here], grad_proj[:, lanes], TN).astype(bf16)
        total[3, here, :] = dot(low_mid[:, here], attended[...], TN).astype(bf16)
    for number, slot in enumerate(hop_order(grads_a.shape[0])):
        place = pl.ds(pl.multiple_of(slots[slot] * depth, depth), depth)
        grads_a[number] = total[:2, place, :]
        grads_b[number] = total[2:, place, :]


def first_kernel(grad_proj, wide, partial):
    extent, inner = grad_proj.shape
    size = step_of(extent, 384)

    def step(index):
        here = pl.ds(pl.multiple_of(index * size, size), size)
        partial[here, :] = dot(grad_proj[here, :], wide[:, :inner], NT).astype(bf16)

    loop(extent // size, step)


def final_kernel(tokens, gain, grad_middle, own, other, before, after, middle, feed_own, feed_other, mixed, token_grad):
    rows, width = tokens.shape
    gains = gain[:1, :]
    size = BLOCK

    def back(here, grad):
        hat, scale = normed(tokens[here, :].astype(f32))
        return norm_back(grad, gains, hat, scale)

    def step(index):
        at = pl.multiple_of(index * size, size)
        here, wider = pl.ds(at, size), pl.ds(pl.multiple_of(at + HALF, HALF), size)
        grad = own[wider, :].astype(f32) + other[wider, :].astype(f32)
        token_grad[here, :] = grad_middle[here, :] + back(here, grad)
        feed = feed_own[here, :].astype(f32) + feed_other[here, :].astype(f32)
        mixed[here, :] = (middle[here, :] + feed).astype(bf16)

    loop(rows // size, step)
    for start, edge in ((0, before), (rows - HALF, after)):
        here = pl.ds(start, HALF)
        token_grad[here, :] += back(here, edge[...].astype(f32))


def exchange(initial, last):
    devices, spot = lax.axis_size("ctx"), lax.axis_index("ctx")
    if devices == 2:
        got = lax.ppermute(jnp.where(spot == 0, last, initial), "ctx", [(0, 1), (1, 0)])
        none = jnp.zeros_like(got)
        return jnp.where(spot == 1, got, none), jnp.where(spot == 0, got, none)
    up = [(i, i + 1) for i in range(devices - 1)]
    return lax.ppermute(last, "ctx", up), lax.ppermute(initial, "ctx", [(j, i) for i, j in up])


def over_ctx(array):
    if lax.axis_size("ctx") == 2:
        return array.astype(f32) + swap(array, "ctx").astype(f32)
    return lax.psum(array, "ctx").astype(f32)


def swap(array, axis="tensor"):
    return lax.ppermute(array, axis, [(0, 1), (1, 0)])


def ring():
    count = lax.axis_size("dp")
    order = [2 * i for i in range(count // 2)] + [2 * i + 1 for i in reversed(range(count // 2))]
    ahead = [(order[i], order[(i + 1) % count]) for i in range(count)]
    back = [(j, i) for i, j in ahead]
    index = lax.axis_index("dp")
    spot = jnp.where(index % 2 == 0, index // 2, count - 1 - index // 2)
    place = (spot + jnp.arange(count, dtype=jnp.int32)) % count
    slots = jnp.where(place < count // 2, 2 * place, 2 * (count - 1 - place) + 1)
    return count, ahead, back, slots.astype(jnp.int32)


def tied(values, others):
    held = lax.optimization_barrier((tuple(values), tuple(others)))
    return held[0]


def locked(values, chain):
    held = lax.optimization_barrier((tuple(values), tuple(chain.state)))
    chain.state = held[1]
    return held[0]


class RingGather:
    def __init__(self, block, cut):
        self.count, self.ahead, self.back, _ = ring()
        self.cut = cut
        self.pieces = {0: (block,)}
        self.state = (block, block)
        self.hops = 0

    def hop(self):
        one, two = self.state
        middle = self.count // 2
        if self.hops + 1 == middle:
            one, two = one[: self.cut], two[self.cut :]
        one, two = lax.ppermute(one, "dp", self.ahead), lax.ppermute(two, "dp", self.back)
        self.hops += 1
        one, two = lax.optimization_barrier((one, two))
        self.state = (one, two)
        if self.hops == middle:
            self.pieces[middle] = (one, two)
        else:
            self.pieces[self.count - self.hops], self.pieces[self.hops] = (one,), (two,)

    def after(self, others):
        self.state = tied(self.state, others)


class RingScatter:
    def __init__(self, parts, axis):
        self.count, self.ahead, self.back, _ = ring()
        self.parts = parts
        self.axis = axis
        self.hops = 0
        self.state = ()

    def part(self, at):
        total = self.parts[0][at]
        for part in self.parts[1:]:
            total = total + part[at]
        return total

    def hop(self):
        if self.hops == 0:
            one, two = jnp.split(self.part(0), 2, axis=self.axis)
        else:
            one, two = self.state
            if self.hops == 1:
                none = jnp.zeros_like(one)
                one = jnp.concatenate([one, none], axis=self.axis)
                two = jnp.concatenate([none, two], axis=self.axis)
            at = 2 * self.hops - 1
            one, two = self.part(at) + one, self.part(at + 1) + two
        one, two = lax.ppermute(one, "dp", self.ahead), lax.ppermute(two, "dp", self.back)
        self.state = lax.optimization_barrier((one, two))
        self.hops += 1

    def after(self, others):
        self.state = tied(self.state, others)

    def total(self):
        one, two = self.state
        return (self.part(self.count - 1).astype(f32) + one.astype(f32) + two.astype(f32)).astype(bf16)


def tables(lengths, rows):
    place = lax.axis_index("ctx") * rows
    ends = jnp.cumsum(lengths[0])
    starts = ends - lengths[0]
    span = place + jnp.arange(-HALF, rows + HALF, dtype=jnp.int32)
    inside = (span[:, None] >= starts[None, :]) & (span[:, None] < ends[None, :])
    position = span - jnp.sum(jnp.where(inside, starts[None, :], 0), axis=1)
    lane = jnp.arange(LANES, dtype=jnp.int32)
    number = (lane % (HEAD // 2)).astype(f32)
    freq = jnp.exp(number * (-2.0 * math.log(10000.0) / HEAD))
    angle = position.astype(f32)[:, None] * freq[None, :]
    sine = jnp.sin(angle)
    sine = jnp.where((lane % HEAD < HEAD // 2)[None, :], -sine, sine)
    bounds = jnp.concatenate([ends, place[None]]).astype(jnp.int32)
    return jnp.cos(angle), sine, bounds


def body(tokens, lengths, gain_one, w_qkv, w_out, gain_two, w_in, w_down, cotangent):
    rows, width = tokens.shape
    local, units = w_out.shape[0], w_down.shape[0]
    pairs, blocks, extent = local // LANES, rows // BLOCK, rows + WINDOW
    groups = lax.axis_size("dp")
    depth = width // groups
    middle_hop = groups // 2
    gains = jnp.pad(jnp.stack([gain_one, gain_two]), ((0, PAD - 2), (0, local - depth)))
    mine_one = jnp.concatenate([w_qkv.reshape(3 * depth, local), w_out.T, gains])
    now = RingGather(mine_one, 2 * depth)
    now.hop()
    before, after = exchange(tokens[:HALF], tokens[rows - HALF :])
    slots = ring()[-1]
    cosine, sine, bounds = tables(lengths, rows)
    while now.hops < middle_hop:
        now.hop()
    mine_two = jnp.concatenate([w_in.reshape(2 * depth, units), w_down.T])
    later = RingGather(tied([mine_two], now.state)[0], depth)
    later.hop()
    hat, = call(
        norm_kernel, [shape((extent, width), f32)], (tokens, before, after), rows * width * 2000, "first_norm"
    )
    pieces = [piece for slot in range(groups) for piece in now.pieces[slot]]
    wide, gain, first, query, key, value = call(
        project_kernel,
        [
            shape((width, 4 * local), bf16),
            shape((PAD, width), f32),
            shape((extent, width), bf16),
            shape((rows, local), bf16),
            shape((extent, local), bf16),
            shape((extent, local), bf16),
        ],
        (hat, cosine, sine, *pieces),
        2 * rows * width * local * 8,
        "project",
        (slots,),
    )
    early, late = tuple(range(pairs - 1)), (pairs - 1,)

    query, key, value = tied([query, key, value], later.state)
    later.hop()
    shares_early, attended = call(
        functools.partial(attend_kernel, early, False),
        [shape((blocks * len(early), KEYS, KEYS), bf16), shape((rows, local), bf16)],
        (query, key, value),
        2 * rows * width * local * 10,
        "attend",
        (bounds,),
    )
    attended, = locked([attended], later)
    later.hop()
    shares_late, attended, branch = call(
        functools.partial(attend_kernel, late, True),
        [
            shape((blocks * len(late), KEYS, KEYS), bf16),
            shape((rows, local), bf16),
            shape((rows, width), bf16),
        ],
        (query, key, value, wide, attended),
        2 * rows * width * local * 7,
        "attend",
        (bounds,),
    )
    branch_other = swap(branch)
    later.after([branch])
    while later.hops < middle_hop:
        later.hop()
    pieces = [piece for slot in range(groups) for piece in later.pieces[slot]]
    middle, second, hidden, grad_gate, grad_upper, partial, whole = call(
        feed_kernel,
        [
            shape((rows, width), f32),
            shape((rows, width), bf16),
            shape((rows, units), bf16),
            shape((rows, units), bf16),
            shape((rows, units), bf16),
            shape((rows, width), bf16),
            shape((3, width, units), bf16),
        ],
        (tokens, branch, branch_other, gain, cotangent, *pieces),
        2 * rows * width * units * 8,
        "feed_forward_and_back",
        (slots,),
    )
    partial_other = swap(partial)
    grads_two, = call(
        weight_kernel,
        [shape((groups, 3, depth, units), bf16)],
        (second, hidden, grad_gate, grad_upper, cotangent),
        2 * rows * width * units * 5,
        "feed_weight_grads",
        (slots,),
        [pltpu.VMEM((3, width, units), bf16)],
    )
    grads_two, = tied([grads_two], [partial_other])
    sums_two = RingScatter([grads_two], 1)
    sums_two.hop()
    grad_middle, low_mid, grad_att = call(
        middle_kernel,
        [shape((rows, width), f32), shape((rows, width), bf16), shape((rows, local), bf16)],
        (middle, partial, partial_other, gain, cotangent, wide),
        2 * rows * width * local * 4,
        "middle_grad",
    )
    grad_att, = locked([grad_att], sums_two)
    sums_two.hop()
    grad_parts = call(
        functools.partial(back_kernel, (early, late)),
        [shape((extent, 3 * LANES), bf16)] * pairs,
        (query, key, value, grad_att, cosine, sine, shares_early, shares_late),
        2 * rows * width * local * 15,
        "attention_back",
        (),
        [pltpu.VMEM((extent, local), f32)] * 2,
    )
    grad_parts = locked(grad_parts, sums_two)
    sums_two.hop()
    grad_proj, *grads_one = call(
        grad_kernel,
        [shape((extent, 3 * local), bf16)] + [shape((groups, 2, depth, local), bf16)] * 2,
        (first, low_mid, attended, *grad_parts),
        2 * rows * width * local * 6,
        "attention_weight_grads",
        (slots,),
        [pltpu.VMEM((4, width, local), bf16)],
    )
    feed, = call(
        feed_out_kernel,
        [shape((rows, width), bf16)],
        (tied([hidden], grads_one)[0], whole),
        2 * rows * width * units,
        "feed_out",
    )
    feed_other = swap(feed)
    first_part, = call(
        first_kernel,
        [shape((extent, width), bf16)],
        (grad_proj, wide),
        2 * rows * width * local * 3,
        "first_grad",
    )
    first_other = swap(first_part)
    grads_one = tied(grads_one, [*sums_two.state, feed, first_part])
    sums_one = [RingScatter([part], 0) for part in grads_one]
    sums_one[0].hop()
    sums_one[1].hop()
    while sums_two.hops < middle_hop:
        sums_two.hop()

    def edge_sum(at):
        here = slice(at, at + HALF)
        return (first_part[here].astype(f32) + first_other[here].astype(f32)).astype(bf16)

    from_before, from_after = exchange(edge_sum(0), edge_sum(rows + HALF))
    for chain in sums_one:
        chain.after([from_before, from_after])
    while sums_one[0].hops < middle_hop - 1:
        for chain in sums_one:
            chain.hop()
    tokens, = tied([tokens], sums_one[0].state)
    for chain in sums_one:
        chain.hop()
    mixed, token_grad = call(
        final_kernel,
        [shape((rows, width), bf16), shape((rows, width), f32)],
        (tokens, gain, grad_middle, first_part, first_other, from_before, from_after, middle, feed, feed_other),
        rows * width * 2000,
        "token_grad",
    )
    two = over_ctx(sums_two.total())
    one = tied([chain.total() for chain in sums_one], [mixed, token_grad])
    one = jnp.concatenate([over_ctx(part) for part in one])
    gain_one_grad = jnp.sum(one[:3] * w_qkv.astype(f32), axis=(0, 2)) / gain_one.astype(f32)
    gain_two_grad = jnp.sum(two[:2] * w_in.astype(f32), axis=(0, 2)) / gain_two.astype(f32)
    both = jnp.stack([gain_one_grad, gain_two_grad])
    both = both + swap(both)
    return (mixed, token_grad, both[0], one[:3], one[3].T, both[1], two[:2], two[2].T)


def solution(mesh):
    in_specs = (
        P(("dp", "ctx"), None),
        P("dp", None),
        P("dp"),
        P(None, "dp", "tensor"),
        P("tensor", "dp"),
        P("dp"),
        P(None, "dp", "tensor"),
        P("tensor", "dp"),
        P(("dp", "ctx"), None),
    )
    out_specs = (
        P(("dp", "ctx"), None),
        P(("dp", "ctx"), None),
        P("dp"),
        P(None, "dp", "tensor"),
        P("tensor", "dp"),
        P("dp"),
        P(None, "dp", "tensor"),
        P("tensor", "dp"),
    )
    return jax.shard_map(body, mesh=mesh, in_specs=in_specs, out_specs=out_specs, check_vma=False)
```

```python
import functools
import math

import jax
import jax.numpy as jnp
from jax import lax
from jax.experimental import pallas as pl
from jax.experimental.pallas import tpu as pltpu
from jax.sharding import PartitionSpec as P

HEAD = 64
WINDOW = 128
NSEQ = 4
HALF = WINDOW // 2
PAD = 16
SPARE = 6
SHARE = 8
BLOCK = 128
LANES = 128
KEYS = BLOCK + WINDOW

norm_eps = 1e-05
f32 = jnp.float32
bf16 = jnp.bfloat16

NN = (((1,), (0,)), ((), ()))
NT = (((1,), (1,)), ((), ()))
TN = (((0,), (0,)), ((), ()))


def dot(a, b, dims=NN):
    return lax.dot_general(a, b, dims, preferred_element_type=f32)


def step_of(rows, most):
    best = LANES
    for size in range(LANES, most + 1, LANES):
        if rows % size == 0:
            best = size
    return best


def call(kernel, out_shape, args, flops, name, scalars=(), scratch=()):
    vmem = pl.BlockSpec(memory_space=pltpu.VMEM)
    smem = pl.BlockSpec(memory_space=pltpu.SMEM)
    moved = sum(x.size * x.dtype.itemsize for x in (*args, *out_shape))
    held = sum(math.prod(x.shape) * jnp.dtype(x.dtype).itemsize for x in scratch if x.dtype in (f32, bf16))
    limit = held + SPARE * 2**20
    return pl.pallas_call(
        kernel,
        out_shape=out_shape,
        in_specs=[smem] * len(scalars) + [vmem] * len(args),
        out_specs=[vmem] * len(out_shape),
        scratch_shapes=scratch,
        compiler_params=pltpu.CompilerParams(vmem_limit_bytes=limit),
        cost_estimate=pl.CostEstimate(flops=flops // SHARE, bytes_accessed=moved // SHARE, transcendentals=0),
        name=name,
    )(*scalars, *args)


def shape(dims, dtype):
    return jax.ShapeDtypeStruct(dims, dtype)


def normed(values):
    centered = values - jnp.mean(values, axis=-1, keepdims=True)
    spread = jnp.mean(centered * centered, axis=-1, keepdims=True)
    scale = lax.rsqrt(spread + norm_eps)
    return centered * scale, scale


def norm_back(grad, gain, hat, scale):
    inner = grad * gain
    one = jnp.mean(inner, axis=-1, keepdims=True)
    two = jnp.mean(inner * hat, axis=-1, keepdims=True)
    return scale * (inner - one - hat * two)


def turned(values, low):
    return jnp.where(low, pltpu.roll(values, LANES - HEAD // 2, 1), pltpu.roll(values, HEAD // 2, 1))


def halves(values):
    even = (lax.broadcasted_iota(jnp.int32, (1, LANES), 1) < HEAD).astype(f32).astype(bf16)
    return jnp.concatenate([values * even, values * (1 - even)], axis=0)


def joined(values):
    return jnp.concatenate([values[:HEAD, :BLOCK], values[HEAD:, BLOCK:]], axis=0).T


def loop(count, body):
    def run(index, carry):
        body(index)
        return carry

    lax.fori_loop(0, count, run, 0)


def norm_kernel(tokens, before, after, hat):
    rows, width = tokens.shape

    def norm_rows(src, dst, size):
        hat[pl.ds(dst, size), :] = normed(src.astype(f32))[0]

    norm_rows(before[...], 0, HALF)
    norm_rows(after[...], rows + HALF, HALF)

    def norm_step(index):
        at = pl.multiple_of(index * BLOCK, BLOCK)
        norm_rows(tokens[pl.ds(at, BLOCK), :], pl.multiple_of(at + HALF, HALF), BLOCK)

    loop(rows // BLOCK, norm_step)


def piece_plan(count, sizes, break_at):
    plan, used = [], 0
    for slot in range(count):
        row, sources = 0, []
        for number, size in enumerate(sizes):
            if slot == count // 2 and number == break_at:
                used, row = used + 1, 0
            sources.append((used, row))
            row += size
        plan.append(tuple(sources))
        used += 1
    return plan


def project_kernel(slots, hat, cosine, sine, *rest):
    pieces, (wide, gain, first, query, key, value) = rest[:-6], rest[-6:]
    extent, local = key.shape
    rows = query.shape[0]
    width = hat.shape[1]
    pairs = local // LANES
    groups = slots.shape[0]
    depth = width // groups
    half = piece_plan(groups, [depth] * 2, 1)
    later = piece_plan(groups, [depth] * 2 + [PAD], 1)
    shift = groups + 1
    plan = [one + tuple((piece + shift, row) for piece, row in two) for one, two in zip(half, later)]
    lane = lax.broadcasted_iota(jnp.int32, (LANES, width), 1) - lax.broadcasted_iota(jnp.int32, (LANES, width), 0)
    gain_sum = jnp.zeros((PAD, width), f32)
    for number, sources in enumerate(plan):
        start = pl.multiple_of(slots[number] * depth, depth)
        for part, (piece, row) in enumerate(sources[:4]):
            lanes = slice(part * local, (part + 1) * local)
            wide[pl.ds(start, depth), lanes] = pieces[piece][row : row + depth, :]
        piece, row = sources[4]
        spread = jnp.where(lane == start, 1.0, 0.0).astype(bf16)
        gain_sum += dot(pieces[piece][row : row + PAD, :LANES], spread)
    gain[...] = gain_sum
    gains = gain_sum[:1]
    query_w, key_w, value_w = (wide.at[:, at * local : (at + 1) * local] for at in range(3))
    low = lax.broadcasted_iota(jnp.int32, (1, LANES), 1) % HEAD < HEAD // 2

    def rotated(src, at, size, dst, place, scale):
        co, si = cosine[pl.ds(at, size), :], sine[pl.ds(at, size), :]
        for pair in range(pairs):
            lanes = slice(pair * LANES, (pair + 1) * LANES)
            value = src[:, lanes]
            dst[pl.ds(place, size), lanes] = ((value * co + turned(value, low) * si) * scale).astype(bf16)

    chunk = step_of(extent, 384)

    def key_step(index):
        at = pl.multiple_of(index * chunk, chunk)
        here = pl.ds(at, chunk)
        part = (hat[here, :] * gains).astype(bf16)
        first[here, :] = part
        rotated(dot(part, key_w[...]), at, chunk, key, at, 1.0)
        value[here, :] = dot(part, value_w[...]).astype(bf16)

    loop(extent // chunk, key_step)
    size = step_of(rows, 256)

    def query_step(index):
        at = pl.multiple_of(index * size, size)
        start = pl.multiple_of(at + HALF, HALF)
        rotated(dot(first[pl.ds(start, size), :], query_w[...]), start, size, query, at, HEAD**-0.5)

    loop(rows // size, query_step)


def attend_kernel(chosen, last, bounds, query, key, value, *rest):
    if last:
        wide, done, shares, attended, branch = rest
        attended[...] = done[...]
    else:
        shares, attended = rest
    rows, local = query.shape
    count = len(chosen)
    key_at = lax.broadcasted_iota(jnp.int32, (KEYS, KEYS), 0)
    lane_at = lax.broadcasted_iota(jnp.int32, (1, KEYS), 1) % BLOCK

    def attend_step(index):
        at = pl.multiple_of(index * BLOCK, BLOCK)
        origin = bounds[NSEQ] + at - HALF
        own = lane_at + (origin + HALF)
        begin = jnp.zeros_like(own)
        end = jnp.zeros_like(own) + bounds[NSEQ - 1]
        for number in range(NSEQ - 1):
            begin = jnp.where(own >= bounds[number], bounds[number], begin)
        for number in reversed(range(NSEQ - 1)):
            end = jnp.where(own < bounds[number], bounds[number], end)
        least = jnp.maximum(lane_at, begin - origin)
        most = jnp.minimum(lane_at + WINDOW, end - 1 - origin)
        allowed = (key_at >= least) & (key_at <= most)
        for number, pair in enumerate(chosen):
            lanes = slice(pair * LANES, (pair + 1) * LANES)
            both = halves(query[pl.ds(at, BLOCK), lanes])
            scores = jnp.where(allowed, dot(key[pl.ds(at, KEYS), lanes], both, NT), -1e30)
            weight = jnp.exp(scores - jnp.max(scores, axis=0, keepdims=True))
            part = (weight * (1.0 / jnp.sum(weight, axis=0, keepdims=True))).astype(bf16)
            shares[index * count + number] = part
            mixed = dot(value[pl.ds(at, KEYS), lanes], part, TN)
            attended[pl.ds(at, BLOCK), lanes] = joined(mixed).astype(bf16)

    loop(rows // BLOCK, attend_step)
    if not last:
        return
    out_t = wide.at[:, 3 * local :]
    size = step_of(rows, 256)

    def out_step(index):
        here = pl.ds(pl.multiple_of(index * size, size), size)
        branch[here, :] = dot(attended[here, :], out_t[...], NT).astype(bf16)

    loop(rows // size, out_step)


def feed_kernel(slots, tokens, own, other, gain, cotangent, *rest):
    pieces, rest = rest[:-7], rest[-7:]
    middle, second, hidden, grad_gate, grad_upper, partial, whole = rest
    rows, width = tokens.shape
    groups = slots.shape[0]
    depth = width // groups
    for number, sources in enumerate(piece_plan(groups, [depth] * 3, 1)):
        place = pl.ds(pl.multiple_of(slots[number] * depth, depth), depth)
        for part, (piece, row) in enumerate(sources):
            whole[part, place, :] = pieces[piece][row : row + depth, :]
    gate_w, upper_w, down_t = (whole.at[number] for number in range(3))
    gains = gain[1:2, :]
    size = step_of(rows, 256)

    def step(index):
        here = pl.ds(pl.multiple_of(index * size, size), size)
        mid = tokens[here, :].astype(f32) + (own[here, :].astype(f32) + other[here, :].astype(f32))
        middle[here, :] = mid
        low = (normed(mid)[0] * gains).astype(bf16)
        second[here, :] = low
        gate = dot(low, gate_w[...])
        upper = dot(low, upper_w[...])
        grad = dot(cotangent[here, :], down_t[...])
        share = 0.5 * (1.0 + lax.erf(gate * (0.5**0.5)))
        smooth = gate * share
        slope = share + gate * (jnp.exp(gate * gate * -0.5) * ((2.0 * math.pi) ** -0.5))
        hidden[here, :] = (smooth * upper).astype(bf16)
        gate_low = (grad * upper * slope).astype(bf16)
        upper_low = (grad * smooth).astype(bf16)
        grad_gate[here, :] = gate_low
        grad_upper[here, :] = upper_low
        partial[here, :] = (dot(gate_low, gate_w[...], NT) + dot(upper_low, upper_w[...], NT)).astype(bf16)

    loop(rows // size, step)


def feed_out_kernel(hidden, whole, feed):
    rows = hidden.shape[0]
    size = step_of(rows, 256)

    def step(index):
        here = pl.ds(pl.multiple_of(index * size, size), size)
        feed[here, :] = dot(hidden[here, :], whole[2], NT).astype(bf16)

    loop(rows // size, step)


def weight_kernel(slots, second, hidden, grad_gate, grad_upper, cotangent, grads, total):
    rows, width = second.shape
    step_rows = step_of(width, 256)
    for number, (left, right) in enumerate(((second, grad_gate), (second, grad_upper), (cotangent, hidden))):
        for start in range(0, width, step_rows):
            here = slice(start, start + step_rows)
            total[number, here, :] = dot(left[:, here], right[...], TN).astype(bf16)
    depth = grads.shape[2]
    for number, slot in enumerate(hop_order(grads.shape[0])):
        grads[number] = total[:, pl.ds(pl.multiple_of(slots[slot] * depth, depth), depth), :]


def hop_order(count):
    middle = count // 2
    order = [middle]
    for hop in range(middle - 1, 0, -1):
        order += [hop, count - hop]
    return order + [0]


def middle_kernel(middle, own, other, gain, cotangent, wide, grad_middle, low_mid, grad_att):
    rows, width = middle.shape
    local = grad_att.shape[1]
    out_t = wide.at[:, 3 * local :]
    gains = gain[1:2, :]
    size = step_of(rows, 256)

    def norm_step(index):
        here = pl.ds(pl.multiple_of(index * size, size), size)
        hat, scale = normed(middle[here, :])
        grad = own[here, :].astype(f32) + other[here, :].astype(f32)
        mid = cotangent[here, :].astype(f32) + norm_back(grad, gains, hat, scale)
        grad_middle[here, :] = mid
        mid_low = mid.astype(bf16)
        low_mid[here, :] = mid_low
        grad_att[here, :] = dot(mid_low, out_t[...]).astype(bf16)

    loop(rows // size, norm_step)


def back_kernel(chosen, query, key, value, grad_att, cosine, sine, *rest):
    held, parts, (grad_key, grad_value) = rest[: len(chosen)], rest[len(chosen) : -2], rest[-2:]
    rows = query.shape[0]
    extent = key.shape[0]
    flat = [(part, number, len(group)) for part, group in zip(held, chosen) for number in range(len(group))]
    grad_key[...] = jnp.zeros_like(grad_key)
    grad_value[...] = jnp.zeros_like(grad_value)
    low = lax.broadcasted_iota(jnp.int32, (1, LANES), 1) % HEAD < HEAD // 2
    zero = jnp.zeros((HALF, LANES), bf16)
    for part in parts:
        part[:HALF, :LANES] = zero
        part[rows + HALF :, :LANES] = zero

    def attend_step(index):
        at = pl.multiple_of(index * BLOCK, BLOCK)
        start = pl.multiple_of(at + HALF, HALF)
        co, si = cosine[pl.ds(start, BLOCK), :], sine[pl.ds(start, BLOCK), :]
        for number, (shares, spot, count) in enumerate(flat):
            lanes = slice(number * LANES, (number + 1) * LANES)
            both = halves(query[pl.ds(at, BLOCK), lanes])
            grad = halves(grad_att[pl.ds(at, BLOCK), lanes])
            keys = key[pl.ds(at, KEYS), lanes]
            part = shares[index * count + spot]
            wide = part.astype(f32)
            grad_shares = dot(value[pl.ds(at, KEYS), lanes], grad, NT)
            delta = jnp.sum(wide * grad_shares, axis=0, keepdims=True)
            raw = (wide * (grad_shares - delta)).astype(bf16)
            grad_query = joined(dot(keys, raw, TN)) * HEAD**-0.5
            turn = (grad_query * co - turned(grad_query, low) * si).astype(bf16)
            parts[number][pl.ds(start, BLOCK), :LANES] = turn
            grad_key[pl.ds(at, KEYS), lanes] += dot(raw, both)
            grad_value[pl.ds(at, KEYS), lanes] += dot(part, grad)

    loop(rows // BLOCK, attend_step)

    def turn_step(index):
        here = pl.ds(pl.multiple_of(index * BLOCK, BLOCK), BLOCK)
        co, si = cosine[here, :], sine[here, :]
        for number, out in enumerate(parts):
            lanes = slice(number * LANES, (number + 1) * LANES)
            part = grad_key[here, lanes]
            out[here, LANES : 2 * LANES] = (part * co - turned(part, low) * si).astype(bf16)
            out[here, 2 * LANES :] = grad_value[here, lanes].astype(bf16)

    loop(extent // BLOCK, turn_step)


def grad_kernel_one(slots, first, *rest):
    parts, (grad_proj, grads, total) = rest[:-3], rest[-3:]
    local = len(parts) * LANES
    for pair, part in enumerate(parts):
        for number in range(3):
            lanes = slice(number * local + pair * LANES, number * local + (pair + 1) * LANES)
            grad_proj[:, lanes] = part[:, number * LANES : (number + 1) * LANES]
    weight_grads([(first, grad_proj.at[:, at * local : (at + 1) * local]) for at in range(2)], slots, grads, total)


def grad_kernel_two(slots, first, grad_proj, low_mid, attended, grads, total):
    local = attended.shape[1]
    weight_grads([(first, grad_proj.at[:, 2 * local :]), (low_mid, attended)], slots, grads, total)


def weight_grads(sides, slots, grads, total):
    width = total.shape[1]
    depth = grads.shape[2]
    step_rows = step_of(width, 256)
    for number, (left, right) in enumerate(sides):
        for start in range(0, width, step_rows):
            here = slice(start, start + step_rows)
            total[number, here, :] = dot(left[:, here], right[...], TN).astype(bf16)
    for number, slot in enumerate(hop_order(grads.shape[0])):
        grads[number] = total[:, pl.ds(pl.multiple_of(slots[slot] * depth, depth), depth), :]


def first_kernel(grad_proj, wide, partial):
    extent, inner = grad_proj.shape
    size = step_of(extent, 384)

    def step(index):
        here = pl.ds(pl.multiple_of(index * size, size), size)
        partial[here, :] = dot(grad_proj[here, :], wide[:, :inner], NT).astype(bf16)

    loop(extent // size, step)


def final_kernel(tokens, gain, grad_middle, own, other, before, after, middle, feed_own, feed_other, mixed, token_grad):
    rows, width = tokens.shape
    gains = gain[:1, :]
    size = BLOCK

    def back(here, grad):
        hat, scale = normed(tokens[here, :].astype(f32))
        return norm_back(grad, gains, hat, scale)

    def step(index):
        at = pl.multiple_of(index * size, size)
        here, wider = pl.ds(at, size), pl.ds(pl.multiple_of(at + HALF, HALF), size)
        grad = own[wider, :].astype(f32) + other[wider, :].astype(f32)
        token_grad[here, :] = grad_middle[here, :] + back(here, grad)
        feed = feed_own[here, :].astype(f32) + feed_other[here, :].astype(f32)
        mixed[here, :] = (middle[here, :] + feed).astype(bf16)

    loop(rows // size, step)
    for start, edge in ((0, before), (rows - HALF, after)):
        here = pl.ds(start, HALF)
        token_grad[here, :] += back(here, edge[...].astype(f32))


def exchange(initial, last):
    devices, spot = lax.axis_size("ctx"), lax.axis_index("ctx")
    if devices == 2:
        got = lax.ppermute(jnp.where(spot == 0, last, initial), "ctx", [(0, 1), (1, 0)])
        none = jnp.zeros_like(got)
        return jnp.where(spot == 1, got, none), jnp.where(spot == 0, got, none)
    up = [(i, i + 1) for i in range(devices - 1)]
    return lax.ppermute(last, "ctx", up), lax.ppermute(initial, "ctx", [(j, i) for i, j in up])


def over_ctx(array):
    if lax.axis_size("ctx") == 2:
        return array.astype(f32) + swap(array, "ctx").astype(f32)
    return lax.psum(array, "ctx").astype(f32)


def swap(array, axis="tensor"):
    return lax.ppermute(array, axis, [(0, 1), (1, 0)])


def ring():
    count = lax.axis_size("dp")
    order = [2 * i for i in range(count // 2)] + [2 * i + 1 for i in reversed(range(count // 2))]
    ahead = [(order[i], order[(i + 1) % count]) for i in range(count)]
    back = [(j, i) for i, j in ahead]
    index = lax.axis_index("dp")
    spot = jnp.where(index % 2 == 0, index // 2, count - 1 - index // 2)
    place = (spot + jnp.arange(count, dtype=jnp.int32)) % count
    slots = jnp.where(place < count // 2, 2 * place, 2 * (count - 1 - place) + 1)
    return count, ahead, back, slots.astype(jnp.int32)


def tied(values, others):
    held = lax.optimization_barrier((tuple(values), tuple(others)))
    return held[0]


def locked(values, chain):
    held = lax.optimization_barrier((tuple(values), tuple(chain.state)))
    chain.state = held[1]
    return held[0]


def alternate(first, second):
    if len(second.past) > 1:
        first.after(second.past[-2])
    first.hop()
    if len(first.past) > 1:
        second.after(first.past[-2])
    second.hop()


class RingGather:
    def __init__(self, block, cut):
        self.count, self.ahead, self.back, _ = ring()
        self.cut = cut
        self.pieces = {0: (block,)}
        self.state = (block, block)
        self.hops = 0
        self.past = []

    def hop(self):
        one, two = self.state
        middle = self.count // 2
        if self.hops + 1 == middle:
            one, two = one[: self.cut], two[self.cut :]
        one, two = lax.ppermute(one, "dp", self.ahead), lax.ppermute(two, "dp", self.back)
        self.hops += 1
        one, two = lax.optimization_barrier((one, two))
        self.state = (one, two)
        self.past.append(self.state)
        if self.hops == middle:
            self.pieces[middle] = (one, two)
        else:
            self.pieces[self.count - self.hops], self.pieces[self.hops] = (one,), (two,)

    def after(self, others):
        self.state = tied(self.state, others)


class RingScatter:
    def __init__(self, parts, axis):
        self.count, self.ahead, self.back, _ = ring()
        self.parts = parts
        self.axis = axis
        self.hops = 0
        self.state = ()
        self.past = []

    def part(self, at):
        total = self.parts[0][at]
        for part in self.parts[1:]:
            total = total + part[at]
        return total

    def hop(self):
        if self.hops == 0:
            one, two = jnp.split(self.part(0), 2, axis=self.axis)
        else:
            one, two = self.state
            if self.hops == 1:
                none = jnp.zeros_like(one)
                one = jnp.concatenate([one, none], axis=self.axis)
                two = jnp.concatenate([none, two], axis=self.axis)
            at = 2 * self.hops - 1
            one, two = self.part(at) + one, self.part(at + 1) + two
        one, two = lax.ppermute(one, "dp", self.ahead), lax.ppermute(two, "dp", self.back)
        self.state = lax.optimization_barrier((one, two))
        self.past.append(self.state)
        self.hops += 1

    def after(self, others):
        self.state = tied(self.state, others)

    def total(self):
        one, two = self.state
        return (self.part(self.count - 1).astype(f32) + one.astype(f32) + two.astype(f32)).astype(bf16)


def tables(lengths, rows):
    place = lax.axis_index("ctx") * rows
    ends = jnp.cumsum(lengths[0])
    starts = ends - lengths[0]
    span = place + jnp.arange(-HALF, rows + HALF, dtype=jnp.int32)
    inside = (span[:, None] >= starts[None, :]) & (span[:, None] < ends[None, :])
    position = span - jnp.sum(jnp.where(inside, starts[None, :], 0), axis=1)
    lane = jnp.arange(LANES, dtype=jnp.int32)
    number = (lane % (HEAD // 2)).astype(f32)
    freq = jnp.exp(number * (-2.0 * math.log(10000.0) / HEAD))
    angle = position.astype(f32)[:, None] * freq[None, :]
    sine = jnp.sin(angle)
    sine = jnp.where((lane % HEAD < HEAD // 2)[None, :], -sine, sine)
    bounds = jnp.concatenate([ends, place[None]]).astype(jnp.int32)
    return jnp.cos(angle), sine, bounds


def body(tokens, lengths, gain_one, w_qkv, w_out, gain_two, w_in, w_down, cotangent):
    rows, width = tokens.shape
    local, units = w_out.shape[0], w_down.shape[0]
    pairs, blocks, extent = local // LANES, rows // BLOCK, rows + WINDOW
    groups = lax.axis_size("dp")
    depth = width // groups
    middle_hop = groups // 2
    gains = jnp.pad(jnp.stack([gain_one, gain_two]), ((0, PAD - 2), (0, local - depth)))
    middle_hop = groups // 2
    now = [
        RingGather(w_qkv[:2].reshape(2 * depth, local), depth),
        RingGather(jnp.concatenate([w_qkv[2], w_out.T, gains]), depth),
    ]
    alternate(*now)
    before, after = exchange(tokens[:HALF], tokens[rows - HALF :])
    slots = ring()[-1]
    cosine, sine, bounds = tables(lengths, rows)
    while now[0].hops < middle_hop:
        alternate(*now)
    mine_two = jnp.concatenate([w_in.reshape(2 * depth, units), w_down.T])
    later = RingGather(tied([mine_two], [*now[0].state, *now[1].past[-2]])[0], depth)
    later.hop()
    hat, = call(
        norm_kernel, [shape((extent, width), f32)], (tokens, before, after), rows * width * 2000, "first_norm"
    )
    pieces = [piece for chain in now for slot in range(groups) for piece in chain.pieces[slot]]
    wide, gain, first, query, key, value = call(
        project_kernel,
        [
            shape((width, 4 * local), bf16),
            shape((PAD, width), f32),
            shape((extent, width), bf16),
            shape((rows, local), bf16),
            shape((extent, local), bf16),
            shape((extent, local), bf16),
        ],
        (hat, cosine, sine, *pieces),
        2 * rows * width * local * 8,
        "project",
        (slots,),
    )
    early, late = tuple(range(pairs - 1)), (pairs - 1,)

    query, key, value = locked([query, key, value], later)
    later.hop()
    shares_early, attended = call(
        functools.partial(attend_kernel, early, False),
        [shape((blocks * len(early), KEYS, KEYS), bf16), shape((rows, local), bf16)],
        (query, key, value),
        2 * rows * width * local * 10,
        "attend",
        (bounds,),
    )
    attended, = locked([attended], later)
    later.hop()
    shares_late, attended, branch = call(
        functools.partial(attend_kernel, late, True),
        [
            shape((blocks * len(late), KEYS, KEYS), bf16),
            shape((rows, local), bf16),
            shape((rows, width), bf16),
        ],
        (query, key, value, wide, attended),
        2 * rows * width * local * 7,
        "attend",
        (bounds,),
    )
    branch, = locked([branch], later)
    branch_other = swap(branch)
    while later.hops < middle_hop:
        later.hop()
    pieces = [piece for slot in range(groups) for piece in later.pieces[slot]]
    middle, second, hidden, grad_gate, grad_upper, partial, whole = call(
        feed_kernel,
        [
            shape((rows, width), f32),
            shape((rows, width), bf16),
            shape((rows, units), bf16),
            shape((rows, units), bf16),
            shape((rows, units), bf16),
            shape((rows, width), bf16),
            shape((3, width, units), bf16),
        ],
        (tokens, branch, branch_other, gain, cotangent, *pieces),
        2 * rows * width * units * 8,
        "feed_forward_and_back",
        (slots,),
    )
    partial_other = swap(partial)
    grads_two, = call(
        weight_kernel,
        [shape((groups, 3, depth, units), bf16)],
        (second, hidden, grad_gate, grad_upper, cotangent),
        2 * rows * width * units * 5,
        "feed_weight_grads",
        (slots,),
        [pltpu.VMEM((3, width, units), bf16)],
    )
    grads_two, = tied([grads_two], [partial_other])
    sums_two = RingScatter([grads_two], 1)
    sums_two.hop()
    grad_middle, low_mid, grad_att = call(
        middle_kernel,
        [shape((rows, width), f32), shape((rows, width), bf16), shape((rows, local), bf16)],
        (middle, partial, partial_other, gain, cotangent, wide),
        2 * rows * width * local * 4,
        "middle_grad",
    )
    grad_att, = locked([grad_att], sums_two)
    sums_two.hop()
    grad_parts = call(
        functools.partial(back_kernel, (early, late)),
        [shape((extent, 3 * LANES), bf16)] * pairs,
        (query, key, value, grad_att, cosine, sine, shares_early, shares_late),
        2 * rows * width * local * 15,
        "attention_back",
        (),
        [pltpu.VMEM((extent, local), f32)] * 2,
    )
    grad_parts = locked(grad_parts, sums_two)
    sums_two.hop()
    grad_proj, grads_a = call(
        grad_kernel_one,
        [shape((extent, 3 * local), bf16), shape((groups, 2, depth, local), bf16)],
        (first, *grad_parts),
        2 * rows * width * local * 3,
        "query_key_grads",
        (slots,),
        [pltpu.VMEM((2, width, local), bf16)],
    )
    first_part, = call(
        first_kernel,
        [shape((extent, width), bf16)],
        (grad_proj, wide),
        2 * rows * width * local * 3,
        "first_grad",
    )
    first_other = swap(first_part)
    low_mid, grad_value_proj = tied([low_mid, grad_proj], [first_part, *sums_two.state])
    grads_b, = call(
        grad_kernel_two,
        [shape((groups, 2, depth, local), bf16)],
        (first, grad_value_proj, low_mid, attended),
        2 * rows * width * local * 3,
        "value_out_grads",
        (slots,),
        [pltpu.VMEM((2, width, local), bf16)],
    )
    grads_one = [grads_a, grads_b]
    feed, = call(
        feed_out_kernel,
        [shape((rows, width), bf16)],
        (tied([hidden], grads_one)[0], whole),
        2 * rows * width * units,
        "feed_out",
    )
    feed_other = swap(feed)
    sums_one = [RingScatter([part], 0) for part in grads_one]
    alternate(*sums_one)
    sums_two.after(sums_one[0].state)
    while sums_two.hops < middle_hop:
        sums_two.hop()

    def edge_sum(at):
        here = slice(at, at + HALF)
        return (first_part[here].astype(f32) + first_other[here].astype(f32)).astype(bf16)

    from_before, from_after = exchange(edge_sum(0), edge_sum(rows + HALF))
    while sums_one[0].hops < middle_hop - 1:
        alternate(*sums_one)
    sums_one[1].after([from_before, from_after])
    tokens, = tied([tokens], sums_one[0].state)
    alternate(*sums_one)
    mixed, token_grad = call(
        final_kernel,
        [shape((rows, width), bf16), shape((rows, width), f32)],
        (tokens, gain, grad_middle, first_part, first_other, from_before, from_after, middle, feed, feed_other),
        rows * width * 2000,
        "token_grad",
    )
    two = over_ctx(sums_two.total())
    one = tied([chain.total() for chain in sums_one], [mixed, token_grad])
    one = jnp.concatenate([over_ctx(part) for part in one])
    gain_one_grad = jnp.sum(one[:3] * w_qkv.astype(f32), axis=(0, 2)) / gain_one.astype(f32)
    gain_two_grad = jnp.sum(two[:2] * w_in.astype(f32), axis=(0, 2)) / gain_two.astype(f32)
    both = jnp.stack([gain_one_grad, gain_two_grad])
    both = both + swap(both)
    return (mixed, token_grad, both[0], one[:3], one[3].T, both[1], two[:2], two[2].T)


def solution(mesh):
    in_specs = (
        P(("dp", "ctx"), None),
        P("dp", None),
        P("dp"),
        P(None, "dp", "tensor"),
        P("tensor", "dp"),
        P("dp"),
        P(None, "dp", "tensor"),
        P("tensor", "dp"),
        P(("dp", "ctx"), None),
    )
    out_specs = (
        P(("dp", "ctx"), None),
        P(("dp", "ctx"), None),
        P("dp"),
        P(None, "dp", "tensor"),
        P("tensor", "dp"),
        P("dp"),
        P(None, "dp", "tensor"),
        P("tensor", "dp"),
    )
    return jax.shard_map(body, mesh=mesh, in_specs=in_specs, out_specs=out_specs, check_vma=False)
```

```python
import functools
import math

import jax
import jax.numpy as jnp
from jax import lax
from jax.experimental import pallas as pl
from jax.experimental.pallas import tpu as pltpu
from jax.sharding import PartitionSpec as P

HEAD = 64
WINDOW = 128
NSEQ = 4
HALF = WINDOW // 2
PAD = 16
SPARE = 6
SHARE = 8
BLOCK = 128
LANES = 128
KEYS = BLOCK + WINDOW

norm_eps = 1e-05
f32 = jnp.float32
bf16 = jnp.bfloat16

NN = (((1,), (0,)), ((), ()))
NT = (((1,), (1,)), ((), ()))
TN = (((0,), (0,)), ((), ()))


def dot(a, b, dims=NN):
    return lax.dot_general(a, b, dims, preferred_element_type=f32)


def step_of(rows, most):
    best = LANES
    for size in range(LANES, most + 1, LANES):
        if rows % size == 0:
            best = size
    return best


def call(kernel, out_shape, args, flops, name, scalars=(), scratch=()):
    vmem = pl.BlockSpec(memory_space=pltpu.VMEM)
    smem = pl.BlockSpec(memory_space=pltpu.SMEM)
    moved = sum(x.size * x.dtype.itemsize for x in (*args, *out_shape))
    held = sum(math.prod(x.shape) * jnp.dtype(x.dtype).itemsize for x in scratch if x.dtype in (f32, bf16))
    limit = held + SPARE * 2**20
    return pl.pallas_call(
        kernel,
        out_shape=out_shape,
        in_specs=[smem] * len(scalars) + [vmem] * len(args),
        out_specs=[vmem] * len(out_shape),
        scratch_shapes=scratch,
        compiler_params=pltpu.CompilerParams(vmem_limit_bytes=limit),
        cost_estimate=pl.CostEstimate(flops=flops // SHARE, bytes_accessed=moved // SHARE, transcendentals=0),
        name=name,
    )(*scalars, *args)


def shape(dims, dtype):
    return jax.ShapeDtypeStruct(dims, dtype)


def normed(values):
    centered = values - jnp.mean(values, axis=-1, keepdims=True)
    spread = jnp.mean(centered * centered, axis=-1, keepdims=True)
    scale = lax.rsqrt(spread + norm_eps)
    return centered * scale, scale


def norm_back(grad, gain, hat, scale):
    inner = grad * gain
    one = jnp.mean(inner, axis=-1, keepdims=True)
    two = jnp.mean(inner * hat, axis=-1, keepdims=True)
    return scale * (inner - one - hat * two)


def turned(values, low):
    return jnp.where(low, pltpu.roll(values, LANES - HEAD // 2, 1), pltpu.roll(values, HEAD // 2, 1))


def halves(values):
    even = (lax.broadcasted_iota(jnp.int32, (1, LANES), 1) < HEAD).astype(f32).astype(bf16)
    return jnp.concatenate([values * even, values * (1 - even)], axis=0)


def joined(values):
    return jnp.concatenate([values[:HEAD, :BLOCK], values[HEAD:, BLOCK:]], axis=0).T


def loop(count, body):
    def run(index, carry):
        body(index)
        return carry

    lax.fori_loop(0, count, run, 0)


def norm_kernel(tokens, before, after, hat):
    rows, width = tokens.shape

    def norm_rows(src, dst, size):
        hat[pl.ds(dst, size), :] = normed(src.astype(f32))[0]

    norm_rows(before[...], 0, HALF)
    norm_rows(after[...], rows + HALF, HALF)

    def norm_step(index):
        at = pl.multiple_of(index * BLOCK, BLOCK)
        norm_rows(tokens[pl.ds(at, BLOCK), :], pl.multiple_of(at + HALF, HALF), BLOCK)

    loop(rows // BLOCK, norm_step)


def piece_plan(count, sizes, break_at):
    plan, used = [], 0
    for slot in range(count):
        row, sources = 0, []
        for number, size in enumerate(sizes):
            if slot == count // 2 and number == break_at:
                used, row = used + 1, 0
            sources.append((used, row))
            row += size
        plan.append(tuple(sources))
        used += 1
    return plan


def project_kernel(slots, hat, cosine, sine, *rest):
    pieces, (wide, gain, first, query, key, value) = rest[:-6], rest[-6:]
    extent, local = key.shape
    rows = query.shape[0]
    width = hat.shape[1]
    pairs = local // LANES
    groups = slots.shape[0]
    depth = width // groups
    half = piece_plan(groups, [depth] * 2, -1)
    later = piece_plan(groups, [depth] * 2 + [PAD], -1)
    plan = [one + tuple((piece + groups, row) for piece, row in two) for one, two in zip(half, later)]
    lane = lax.broadcasted_iota(jnp.int32, (LANES, width), 1) - lax.broadcasted_iota(jnp.int32, (LANES, width), 0)
    gain_sum = jnp.zeros((PAD, width), f32)
    for number, sources in enumerate(plan):
        start = pl.multiple_of(slots[number] * depth, depth)
        for part, (piece, row) in enumerate(sources[:4]):
            lanes = slice(part * local, (part + 1) * local)
            wide[pl.ds(start, depth), lanes] = pieces[piece][row : row + depth, :]
        piece, row = sources[4]
        spread = jnp.where(lane == start, 1.0, 0.0).astype(bf16)
        gain_sum += dot(pieces[piece][row : row + PAD, :LANES], spread)
    gain[...] = gain_sum
    gains = gain_sum[:1]
    query_w, key_w, value_w = (wide.at[:, at * local : (at + 1) * local] for at in range(3))
    low = lax.broadcasted_iota(jnp.int32, (1, LANES), 1) % HEAD < HEAD // 2

    def rotated(src, at, size, dst, place, scale):
        co, si = cosine[pl.ds(at, size), :], sine[pl.ds(at, size), :]
        for pair in range(pairs):
            lanes = slice(pair * LANES, (pair + 1) * LANES)
            value = src[:, lanes]
            dst[pl.ds(place, size), lanes] = ((value * co + turned(value, low) * si) * scale).astype(bf16)

    chunk = step_of(extent, 384)

    def key_step(index):
        at = pl.multiple_of(index * chunk, chunk)
        here = pl.ds(at, chunk)
        part = (hat[here, :] * gains).astype(bf16)
        first[here, :] = part
        rotated(dot(part, key_w[...]), at, chunk, key, at, 1.0)
        value[here, :] = dot(part, value_w[...]).astype(bf16)

    loop(extent // chunk, key_step)
    size = step_of(rows, 256)

    def query_step(index):
        at = pl.multiple_of(index * size, size)
        start = pl.multiple_of(at + HALF, HALF)
        rotated(dot(first[pl.ds(start, size), :], query_w[...]), start, size, query, at, HEAD**-0.5)

    loop(rows // size, query_step)


def attend_kernel(chosen, last, bounds, query, key, value, *rest):
    if last:
        wide, done, shares, attended, branch = rest
        attended[...] = done[...]
    else:
        shares, attended = rest
    rows, local = query.shape
    count = len(chosen)
    key_at = lax.broadcasted_iota(jnp.int32, (KEYS, KEYS), 0)
    lane_at = lax.broadcasted_iota(jnp.int32, (1, KEYS), 1) % BLOCK

    def attend_step(index):
        at = pl.multiple_of(index * BLOCK, BLOCK)
        origin = bounds[NSEQ] + at - HALF
        own = lane_at + (origin + HALF)
        begin = jnp.zeros_like(own)
        end = jnp.zeros_like(own) + bounds[NSEQ - 1]
        for number in range(NSEQ - 1):
            begin = jnp.where(own >= bounds[number], bounds[number], begin)
        for number in reversed(range(NSEQ - 1)):
            end = jnp.where(own < bounds[number], bounds[number], end)
        least = jnp.maximum(lane_at, begin - origin)
        most = jnp.minimum(lane_at + WINDOW, end - 1 - origin)
        allowed = (key_at >= least) & (key_at <= most)
        for number, pair in enumerate(chosen):
            lanes = slice(pair * LANES, (pair + 1) * LANES)
            both = halves(query[pl.ds(at, BLOCK), lanes])
            scores = jnp.where(allowed, dot(key[pl.ds(at, KEYS), lanes], both, NT), -1e30)
            weight = jnp.exp(scores - jnp.max(scores, axis=0, keepdims=True))
            part = (weight * (1.0 / jnp.sum(weight, axis=0, keepdims=True))).astype(bf16)
            shares[index * count + number] = part
            mixed = dot(value[pl.ds(at, KEYS), lanes], part, TN)
            attended[pl.ds(at, BLOCK), lanes] = joined(mixed).astype(bf16)

    loop(rows // BLOCK, attend_step)
    if not last:
        return
    out_t = wide.at[:, 3 * local :]
    size = step_of(rows, 256)

    def out_step(index):
        here = pl.ds(pl.multiple_of(index * size, size), size)
        branch[here, :] = dot(attended[here, :], out_t[...], NT).astype(bf16)

    loop(rows // size, out_step)


def feed_kernel(slots, tokens, own, other, gain, cotangent, *rest):
    pieces, rest = rest[:-7], rest[-7:]
    middle, second, hidden, grad_gate, grad_upper, partial, whole = rest
    rows, width = tokens.shape
    groups = slots.shape[0]
    depth = width // groups
    for number, sources in enumerate(piece_plan(groups, [depth] * 3, 1)):
        place = pl.ds(pl.multiple_of(slots[number] * depth, depth), depth)
        for part, (piece, row) in enumerate(sources):
            whole[part, place, :] = pieces[piece][row : row + depth, :]
    gate_w, upper_w, down_t = (whole.at[number] for number in range(3))
    gains = gain[1:2, :]
    size = step_of(rows, 256)

    def step(index):
        here = pl.ds(pl.multiple_of(index * size, size), size)
        mid = tokens[here, :].astype(f32) + (own[here, :].astype(f32) + other[here, :].astype(f32))
        middle[here, :] = mid
        low = (normed(mid)[0] * gains).astype(bf16)
        second[here, :] = low
        gate = dot(low, gate_w[...])
        upper = dot(low, upper_w[...])
        grad = dot(cotangent[here, :], down_t[...])
        share = 0.5 * (1.0 + lax.erf(gate * (0.5**0.5)))
        smooth = gate * share
        slope = share + gate * (jnp.exp(gate * gate * -0.5) * ((2.0 * math.pi) ** -0.5))
        hidden[here, :] = (smooth * upper).astype(bf16)
        gate_low = (grad * upper * slope).astype(bf16)
        upper_low = (grad * smooth).astype(bf16)
        grad_gate[here, :] = gate_low
        grad_upper[here, :] = upper_low
        partial[here, :] = (dot(gate_low, gate_w[...], NT) + dot(upper_low, upper_w[...], NT)).astype(bf16)

    loop(rows // size, step)


def feed_out_kernel(hidden, whole, feed):
    rows = hidden.shape[0]
    size = step_of(rows, 256)

    def step(index):
        here = pl.ds(pl.multiple_of(index * size, size), size)
        feed[here, :] = dot(hidden[here, :], whole[2], NT).astype(bf16)

    loop(rows // size, step)


def weight_kernel(slots, second, hidden, grad_gate, grad_upper, cotangent, grads, total):
    rows, width = second.shape
    step_rows = step_of(width, 256)
    for number, (left, right) in enumerate(((second, grad_gate), (second, grad_upper), (cotangent, hidden))):
        for start in range(0, width, step_rows):
            here = slice(start, start + step_rows)
            total[number, here, :] = dot(left[:, here], right[...], TN).astype(bf16)
    depth = grads.shape[2]
    for number, slot in enumerate(hop_order(grads.shape[0])):
        grads[number] = total[:, pl.ds(pl.multiple_of(slots[slot] * depth, depth), depth), :]


def hop_order(count):
    middle = count // 2
    order = [middle]
    for hop in range(middle - 1, 0, -1):
        order += [hop, count - hop]
    return order + [0]


def middle_kernel(middle, own, other, gain, cotangent, wide, grad_middle, low_mid, grad_att):
    rows, width = middle.shape
    local = grad_att.shape[1]
    out_t = wide.at[:, 3 * local :]
    gains = gain[1:2, :]
    size = step_of(rows, 256)

    def norm_step(index):
        here = pl.ds(pl.multiple_of(index * size, size), size)
        hat, scale = normed(middle[here, :])
        grad = own[here, :].astype(f32) + other[here, :].astype(f32)
        mid = cotangent[here, :].astype(f32) + norm_back(grad, gains, hat, scale)
        grad_middle[here, :] = mid
        mid_low = mid.astype(bf16)
        low_mid[here, :] = mid_low
        grad_att[here, :] = dot(mid_low, out_t[...]).astype(bf16)

    loop(rows // size, norm_step)


def back_kernel(chosen, query, key, value, grad_att, cosine, sine, *rest):
    held, parts, (grad_key, grad_value) = rest[: len(chosen)], rest[len(chosen) : -2], rest[-2:]
    rows = query.shape[0]
    extent = key.shape[0]
    flat = [(part, number, len(group)) for part, group in zip(held, chosen) for number in range(len(group))]
    grad_key[...] = jnp.zeros_like(grad_key)
    grad_value[...] = jnp.zeros_like(grad_value)
    low = lax.broadcasted_iota(jnp.int32, (1, LANES), 1) % HEAD < HEAD // 2
    zero = jnp.zeros((HALF, LANES), bf16)
    for part in parts:
        part[:HALF, :LANES] = zero
        part[rows + HALF :, :LANES] = zero

    def attend_step(index):
        at = pl.multiple_of(index * BLOCK, BLOCK)
        start = pl.multiple_of(at + HALF, HALF)
        co, si = cosine[pl.ds(start, BLOCK), :], sine[pl.ds(start, BLOCK), :]
        for number, (shares, spot, count) in enumerate(flat):
            lanes = slice(number * LANES, (number + 1) * LANES)
            both = halves(query[pl.ds(at, BLOCK), lanes])
            grad = halves(grad_att[pl.ds(at, BLOCK), lanes])
            keys = key[pl.ds(at, KEYS), lanes]
            part = shares[index * count + spot]
            wide = part.astype(f32)
            grad_shares = dot(value[pl.ds(at, KEYS), lanes], grad, NT)
            delta = jnp.sum(wide * grad_shares, axis=0, keepdims=True)
            raw = (wide * (grad_shares - delta)).astype(bf16)
            grad_query = joined(dot(keys, raw, TN)) * HEAD**-0.5
            turn = (grad_query * co - turned(grad_query, low) * si).astype(bf16)
            parts[number][pl.ds(start, BLOCK), :LANES] = turn
            grad_key[pl.ds(at, KEYS), lanes] += dot(raw, both)
            grad_value[pl.ds(at, KEYS), lanes] += dot(part, grad)

    loop(rows // BLOCK, attend_step)

    def turn_step(index):
        here = pl.ds(pl.multiple_of(index * BLOCK, BLOCK), BLOCK)
        co, si = cosine[here, :], sine[here, :]
        for number, out in enumerate(parts):
            lanes = slice(number * LANES, (number + 1) * LANES)
            part = grad_key[here, lanes]
            out[here, LANES : 2 * LANES] = (part * co - turned(part, low) * si).astype(bf16)
            out[here, 2 * LANES :] = grad_value[here, lanes].astype(bf16)

    loop(extent // BLOCK, turn_step)


def grad_kernel_one(slots, first, *rest):
    parts, (grad_proj, grads, total) = rest[:-3], rest[-3:]
    local = len(parts) * LANES
    for pair, part in enumerate(parts):
        for number in range(3):
            lanes = slice(number * local + pair * LANES, number * local + (pair + 1) * LANES)
            grad_proj[:, lanes] = part[:, number * LANES : (number + 1) * LANES]
    weight_grads([(first, grad_proj.at[:, at * local : (at + 1) * local]) for at in range(2)], slots, grads, total)


def grad_kernel_two(slots, first, grad_proj, low_mid, attended, grads, total):
    local = attended.shape[1]
    weight_grads([(first, grad_proj.at[:, 2 * local :]), (low_mid, attended)], slots, grads, total)


def weight_grads(sides, slots, grads, total):
    width = total.shape[1]
    depth = grads.shape[2]
    step_rows = step_of(width, 256)
    for number, (left, right) in enumerate(sides):
        for start in range(0, width, step_rows):
            here = slice(start, start + step_rows)
            total[number, here, :] = dot(left[:, here], right[...], TN).astype(bf16)
    for number, slot in enumerate(hop_order(grads.shape[0])):
        grads[number] = total[:, pl.ds(pl.multiple_of(slots[slot] * depth, depth), depth), :]


def first_kernel(grad_proj, wide, partial):
    extent, inner = grad_proj.shape
    size = step_of(extent, 384)

    def step(index):
        here = pl.ds(pl.multiple_of(index * size, size), size)
        partial[here, :] = dot(grad_proj[here, :], wide[:, :inner], NT).astype(bf16)

    loop(extent // size, step)


def final_kernel(tokens, gain, grad_middle, own, other, before, after, middle, feed_own, feed_other, mixed, token_grad):
    rows, width = tokens.shape
    gains = gain[:1, :]
    size = BLOCK

    def back(here, grad):
        hat, scale = normed(tokens[here, :].astype(f32))
        return norm_back(grad, gains, hat, scale)

    def step(index):
        at = pl.multiple_of(index * size, size)
        here, wider = pl.ds(at, size), pl.ds(pl.multiple_of(at + HALF, HALF), size)
        grad = own[wider, :].astype(f32) + other[wider, :].astype(f32)
        token_grad[here, :] = grad_middle[here, :] + back(here, grad)
        feed = feed_own[here, :].astype(f32) + feed_other[here, :].astype(f32)
        mixed[here, :] = (middle[here, :] + feed).astype(bf16)

    loop(rows // size, step)
    for start, edge in ((0, before), (rows - HALF, after)):
        here = pl.ds(start, HALF)
        token_grad[here, :] += back(here, edge[...].astype(f32))


def exchange(initial, last):
    devices, spot = lax.axis_size("ctx"), lax.axis_index("ctx")
    if devices == 2:
        got = lax.ppermute(jnp.where(spot == 0, last, initial), "ctx", [(0, 1), (1, 0)])
        none = jnp.zeros_like(got)
        return jnp.where(spot == 1, got, none), jnp.where(spot == 0, got, none)
    up = [(i, i + 1) for i in range(devices - 1)]
    return lax.ppermute(last, "ctx", up), lax.ppermute(initial, "ctx", [(j, i) for i, j in up])


def over_ctx(array):
    if lax.axis_size("ctx") == 2:
        return array.astype(f32) + swap(array, "ctx").astype(f32)
    return lax.psum(array, "ctx").astype(f32)


def swap(array, axis="tensor"):
    return lax.ppermute(array, axis, [(0, 1), (1, 0)])


def ring():
    count = lax.axis_size("dp")
    order = [2 * i for i in range(count // 2)] + [2 * i + 1 for i in reversed(range(count // 2))]
    ahead = [(order[i], order[(i + 1) % count]) for i in range(count)]
    back = [(j, i) for i, j in ahead]
    index = lax.axis_index("dp")
    spot = jnp.where(index % 2 == 0, index // 2, count - 1 - index // 2)
    place = (spot + jnp.arange(count, dtype=jnp.int32)) % count
    slots = jnp.where(place < count // 2, 2 * place, 2 * (count - 1 - place) + 1)
    return count, ahead, back, slots.astype(jnp.int32)


def tied(values, others):
    held = lax.optimization_barrier((tuple(values), tuple(others)))
    return held[0]


def locked(values, chain):
    held = lax.optimization_barrier((tuple(values), tuple(chain.state)))
    chain.state = held[1]
    return held[0]


def alternate(first, second):
    if len(second.past) > 1:
        first.after(second.past[-2])
    first.hop()
    if len(first.past) > 1:
        second.after(first.past[-2])
    second.hop()


class RingGather:
    def __init__(self, block, cut=0, way=None):
        self.count, self.ahead, self.back, _ = ring()
        self.cut = cut
        self.way = way
        self.pieces = {0: (block,)}
        self.state = (block, block)
        self.hops = 0
        self.past = []

    def hop(self):
        one, two = self.state
        middle = self.count // 2
        if self.hops + 1 == middle and self.way is not None:
            got = lax.ppermute((one, two)[self.way], "dp", (self.ahead, self.back)[self.way])
            self.hops += 1
            self.state = (got,)
            self.past.append(self.state)
            self.pieces[middle] = (got,)
            return
        if self.hops + 1 == middle:
            one, two = one[: self.cut], two[self.cut :]
        one, two = lax.ppermute(one, "dp", self.ahead), lax.ppermute(two, "dp", self.back)
        self.hops += 1
        one, two = lax.optimization_barrier((one, two))
        self.state = (one, two)
        self.past.append(self.state)
        if self.hops == middle:
            self.pieces[middle] = (one, two)
        else:
            self.pieces[self.count - self.hops], self.pieces[self.hops] = (one,), (two,)

    def after(self, others):
        self.state = tied(self.state, others)


class RingScatter:
    def __init__(self, parts, axis=0, way=None):
        self.count, self.ahead, self.back, _ = ring()
        self.parts = parts
        self.axis = axis
        self.way = way
        self.hops = 0
        self.state = ()
        self.past = []

    def part(self, at):
        total = self.parts[0][at]
        for part in self.parts[1:]:
            total = total + part[at]
        return total

    def hop(self):
        if self.hops == 0 and self.way is not None:
            got = lax.ppermute(self.part(0), "dp", (self.ahead, self.back)[self.way])
            self.state = (got,)
            self.past.append(self.state)
            self.hops += 1
            return
        if self.hops == 0:
            one, two = jnp.split(self.part(0), 2, axis=self.axis)
        else:
            sides = [self.part(2 * self.hops - 1), self.part(2 * self.hops)]
            if self.hops == 1 and self.way is not None:
                sides[self.way] = sides[self.way] + self.state[0]
            one, two = sides if self.hops == 1 and self.way is not None else self.state
            if self.hops == 1 and self.way is None:
                none = jnp.zeros_like(one)
                one = jnp.concatenate([one, none], axis=self.axis)
                two = jnp.concatenate([none, two], axis=self.axis)
            if self.hops > 1 or self.way is None:
                one, two = sides[0] + one, sides[1] + two
        one, two = lax.ppermute(one, "dp", self.ahead), lax.ppermute(two, "dp", self.back)
        self.state = lax.optimization_barrier((one, two))
        self.past.append(self.state)
        self.hops += 1

    def after(self, others):
        self.state = tied(self.state, others)

    def total(self):
        one, two = self.state
        return (self.part(self.count - 1).astype(f32) + one.astype(f32) + two.astype(f32)).astype(bf16)


def tables(lengths, rows):
    place = lax.axis_index("ctx") * rows
    ends = jnp.cumsum(lengths[0])
    starts = ends - lengths[0]
    span = place + jnp.arange(-HALF, rows + HALF, dtype=jnp.int32)
    inside = (span[:, None] >= starts[None, :]) & (span[:, None] < ends[None, :])
    position = span - jnp.sum(jnp.where(inside, starts[None, :], 0), axis=1)
    lane = jnp.arange(LANES, dtype=jnp.int32)
    number = (lane % (HEAD // 2)).astype(f32)
    freq = jnp.exp(number * (-2.0 * math.log(10000.0) / HEAD))
    angle = position.astype(f32)[:, None] * freq[None, :]
    sine = jnp.sin(angle)
    sine = jnp.where((lane % HEAD < HEAD // 2)[None, :], -sine, sine)
    bounds = jnp.concatenate([ends, place[None]]).astype(jnp.int32)
    return jnp.cos(angle), sine, bounds


def body(tokens, lengths, gain_one, w_qkv, w_out, gain_two, w_in, w_down, cotangent):
    rows, width = tokens.shape
    local, units = w_out.shape[0], w_down.shape[0]
    pairs, blocks, extent = local // LANES, rows // BLOCK, rows + WINDOW
    groups = lax.axis_size("dp")
    depth = width // groups
    middle_hop = groups // 2
    gains = jnp.pad(jnp.stack([gain_one, gain_two]), ((0, PAD - 2), (0, local - depth)))
    middle_hop = groups // 2
    now = [
        RingGather(w_qkv[:2].reshape(2 * depth, local), way=0),
        RingGather(jnp.concatenate([w_qkv[2], w_out.T, gains]), way=1),
    ]
    alternate(*now)
    before, after = exchange(tokens[:HALF], tokens[rows - HALF :])
    slots = ring()[-1]
    cosine, sine, bounds = tables(lengths, rows)
    hat, = call(
        norm_kernel, [shape((extent, width), f32)], (tokens, before, after), rows * width * 2000, "first_norm"
    )
    alternate(*now)
    now[1].after([hat])
    while now[0].hops < middle_hop:
        alternate(*now)
    mine_two = jnp.concatenate([w_in.reshape(2 * depth, units), w_down.T])
    later = RingGather(tied([mine_two], [*now[0].state, *now[1].state])[0], depth)
    later.hop()
    pieces = [piece for chain in now for slot in range(groups) for piece in chain.pieces[slot]]
    wide, gain, first, query, key, value = call(
        project_kernel,
        [
            shape((width, 4 * local), bf16),
            shape((PAD, width), f32),
            shape((extent, width), bf16),
            shape((rows, local), bf16),
            shape((extent, local), bf16),
            shape((extent, local), bf16),
        ],
        (hat, cosine, sine, *pieces),
        2 * rows * width * local * 8,
        "project",
        (slots,),
    )
    early, late = tuple(range(pairs - 1)), (pairs - 1,)

    query, key, value = locked([query, key, value], later)
    later.hop()
    shares_early, attended = call(
        functools.partial(attend_kernel, early, False),
        [shape((blocks * len(early), KEYS, KEYS), bf16), shape((rows, local), bf16)],
        (query, key, value),
        2 * rows * width * local * 10,
        "attend",
        (bounds,),
    )
    attended, = locked([attended], later)
    later.hop()
    shares_late, attended, branch = call(
        functools.partial(attend_kernel, late, True),
        [
            shape((blocks * len(late), KEYS, KEYS), bf16),
            shape((rows, local), bf16),
            shape((rows, width), bf16),
        ],
        (query, key, value, wide, attended),
        2 * rows * width * local * 7,
        "attend",
        (bounds,),
    )
    branch, = locked([branch], later)
    branch_other = swap(branch)
    while later.hops < middle_hop:
        later.hop()
    pieces = [piece for slot in range(groups) for piece in later.pieces[slot]]
    middle, second, hidden, grad_gate, grad_upper, partial, whole = call(
        feed_kernel,
        [
            shape((rows, width), f32),
            shape((rows, width), bf16),
            shape((rows, units), bf16),
            shape((rows, units), bf16),
            shape((rows, units), bf16),
            shape((rows, width), bf16),
            shape((3, width, units), bf16),
        ],
        (tokens, branch, branch_other, gain, cotangent, *pieces),
        2 * rows * width * units * 8,
        "feed_forward_and_back",
        (slots,),
    )
    partial_other = swap(partial)
    grads_two, = call(
        weight_kernel,
        [shape((groups, 3, depth, units), bf16)],
        (second, hidden, grad_gate, grad_upper, cotangent),
        2 * rows * width * units * 5,
        "feed_weight_grads",
        (slots,),
        [pltpu.VMEM((3, width, units), bf16)],
    )
    grads_two, = tied([grads_two], [partial_other])
    sums_two = RingScatter([grads_two], 1)
    sums_two.hop()
    grad_middle, low_mid, grad_att = call(
        middle_kernel,
        [shape((rows, width), f32), shape((rows, width), bf16), shape((rows, local), bf16)],
        (middle, partial, partial_other, gain, cotangent, wide),
        2 * rows * width * local * 4,
        "middle_grad",
    )
    grad_att, = locked([grad_att], sums_two)
    sums_two.hop()
    grad_parts = call(
        functools.partial(back_kernel, (early, late)),
        [shape((extent, 3 * LANES), bf16)] * pairs,
        (query, key, value, grad_att, cosine, sine, shares_early, shares_late),
        2 * rows * width * local * 15,
        "attention_back",
        (),
        [pltpu.VMEM((extent, local), f32)] * 2,
    )
    grad_parts = locked(grad_parts, sums_two)
    sums_two.hop()
    grad_proj, grads_a = call(
        grad_kernel_one,
        [shape((extent, 3 * local), bf16), shape((groups, 2, depth, local), bf16)],
        (first, *grad_parts),
        2 * rows * width * local * 3,
        "query_key_grads",
        (slots,),
        [pltpu.VMEM((2, width, local), bf16)],
    )
    first_part, = call(
        first_kernel,
        [shape((extent, width), bf16)],
        (grad_proj, wide),
        2 * rows * width * local * 3,
        "first_grad",
    )
    first_other = swap(first_part)
    def edge_sum(at):
        here = slice(at, at + HALF)
        return (first_part[here].astype(f32) + first_other[here].astype(f32)).astype(bf16)

    from_before, from_after = exchange(edge_sum(0), edge_sum(rows + HALF))
    low_mid, grad_value_proj = tied([low_mid, grad_proj], [first_part, *sums_two.state])
    grads_b, = call(
        grad_kernel_two,
        [shape((groups, 2, depth, local), bf16)],
        (first, grad_value_proj, low_mid, attended),
        2 * rows * width * local * 3,
        "value_out_grads",
        (slots,),
        [pltpu.VMEM((2, width, local), bf16)],
    )
    grads_one = [grads_a, grads_b]
    feed, = call(
        feed_out_kernel,
        [shape((rows, width), bf16)],
        (tied([hidden], [from_before, from_after])[0], whole),
        2 * rows * width * units,
        "feed_out",
    )
    feed_other = swap(feed)
    sums_one = [RingScatter([part], way=way) for way, part in enumerate(grads_one)]
    alternate(*sums_one)
    sums_two.after(sums_one[0].state)
    while sums_two.hops < middle_hop:
        sums_two.hop()

    while sums_one[0].hops < middle_hop - 1:
        if sums_one[0].hops == 2:
            sums_one[1].after(sums_two.state)
        alternate(*sums_one)
    tokens, = tied([tokens], sums_one[0].state)
    alternate(*sums_one)
    mixed, token_grad = call(
        final_kernel,
        [shape((rows, width), bf16), shape((rows, width), f32)],
        (tokens, gain, grad_middle, first_part, first_other, from_before, from_after, middle, feed, feed_other),
        rows * width * 2000,
        "token_grad",
    )
    two = over_ctx(sums_two.total())
    one = over_ctx(tied([sums_one[0].total()], [mixed, token_grad])[0])
    one = jnp.concatenate([one, over_ctx(sums_one[1].total())])
    gain_one_grad = jnp.sum(one[:3] * w_qkv.astype(f32), axis=(0, 2)) / gain_one.astype(f32)
    gain_two_grad = jnp.sum(two[:2] * w_in.astype(f32), axis=(0, 2)) / gain_two.astype(f32)
    both = jnp.stack([gain_one_grad, gain_two_grad])
    both = both + swap(both)
    return (mixed, token_grad, both[0], one[:3], one[3].T, both[1], two[:2], two[2].T)


def solution(mesh):
    in_specs = (
        P(("dp", "ctx"), None),
        P("dp", None),
        P("dp"),
        P(None, "dp", "tensor"),
        P("tensor", "dp"),
        P("dp"),
        P(None, "dp", "tensor"),
        P("tensor", "dp"),
        P(("dp", "ctx"), None),
    )
    out_specs = (
        P(("dp", "ctx"), None),
        P(("dp", "ctx"), None),
        P("dp"),
        P(None, "dp", "tensor"),
        P("tensor", "dp"),
        P("dp"),
        P(None, "dp", "tensor"),
        P("tensor", "dp"),
    )
    return jax.shard_map(body, mesh=mesh, in_specs=in_specs, out_specs=out_specs, check_vma=False)
```

```python
import functools
import math

import jax
import jax.numpy as jnp
import numpy as np
from jax import lax
from jax.experimental import pallas as pl
from jax.experimental.pallas import tpu as pltpu
from jax.sharding import PartitionSpec as P

HEAD = 64
WINDOW = 128
NSEQ = 4
HALF = WINDOW // 2
PAD = 16
SPARE = 6
SHARE = 8
BLOCK = 128
LANES = 128
KEYS = BLOCK + WINDOW

norm_eps = 1e-05
f32 = jnp.float32
bf16 = jnp.bfloat16

NN = (((1,), (0,)), ((), ()))
NT = (((1,), (1,)), ((), ()))
TN = (((0,), (0,)), ((), ()))


def dot(a, b, dims=NN):
    return lax.dot_general(a, b, dims, preferred_element_type=f32)


def step_of(rows, most):
    best = LANES
    for size in range(LANES, most + 1, LANES):
        if rows % size == 0:
            best = size
    return best


def call(kernel, out_shape, args, flops, name, scalars=(), scratch=()):
    vmem = pl.BlockSpec(memory_space=pltpu.VMEM)
    smem = pl.BlockSpec(memory_space=pltpu.SMEM)
    moved = sum(x.size * x.dtype.itemsize for x in (*args, *out_shape))
    held = sum(math.prod(x.shape) * jnp.dtype(x.dtype).itemsize for x in scratch if x.dtype in (f32, bf16))
    limit = held + SPARE * 2**20
    return pl.pallas_call(
        kernel,
        out_shape=out_shape,
        in_specs=[smem] * len(scalars) + [vmem] * len(args),
        out_specs=[vmem] * len(out_shape),
        scratch_shapes=scratch,
        compiler_params=pltpu.CompilerParams(vmem_limit_bytes=limit),
        cost_estimate=pl.CostEstimate(flops=flops // SHARE, bytes_accessed=moved // SHARE, transcendentals=0),
        name=name,
    )(*scalars, *args)


def shape(dims, dtype):
    return jax.ShapeDtypeStruct(dims, dtype)


def normed(values):
    centered = values - jnp.mean(values, axis=-1, keepdims=True)
    spread = jnp.mean(centered * centered, axis=-1, keepdims=True)
    scale = lax.rsqrt(spread + norm_eps)
    return centered * scale, scale


def norm_back(grad, gain, hat, scale):
    inner = grad * gain
    one = jnp.mean(inner, axis=-1, keepdims=True)
    two = jnp.mean(inner * hat, axis=-1, keepdims=True)
    return scale * (inner - one - hat * two)


def turned(values, low):
    return jnp.where(low, pltpu.roll(values, LANES - HEAD // 2, 1), pltpu.roll(values, HEAD // 2, 1))


def halves(values):
    even = (lax.broadcasted_iota(jnp.int32, (1, LANES), 1) < HEAD).astype(f32).astype(bf16)
    return jnp.concatenate([values * even, values * (1 - even)], axis=0)


def joined(values):
    return jnp.concatenate([values[:HEAD, :BLOCK], values[HEAD:, BLOCK:]], axis=0).T


def loop(count, body):
    def run(index, carry):
        body(index)
        return carry

    lax.fori_loop(0, count, run, 0)


def norm_kernel(tokens, before, after, hat):
    rows, width = tokens.shape

    def norm_rows(src, dst, size):
        hat[pl.ds(dst, size), :] = normed(src.astype(f32))[0]

    norm_rows(before[...], 0, HALF)
    norm_rows(after[...], rows + HALF, HALF)

    def norm_step(index):
        at = pl.multiple_of(index * BLOCK, BLOCK)
        norm_rows(tokens[pl.ds(at, BLOCK), :], pl.multiple_of(at + HALF, HALF), BLOCK)

    loop(rows // BLOCK, norm_step)


def piece_plan(count, sizes, break_at):
    plan, used = [], 0
    for slot in range(count):
        row, sources = 0, []
        for number, size in enumerate(sizes):
            if slot == count // 2 and number == break_at:
                used, row = used + 1, 0
            sources.append((used, row))
            row += size
        plan.append(tuple(sources))
        used += 1
    return plan


def project_kernel(slots, hat, cosine, sine, *rest):
    pieces, (wide, gain, first, query, key, value) = rest[:-6], rest[-6:]
    extent, local = key.shape
    rows = query.shape[0]
    width = hat.shape[1]
    pairs = local // LANES
    groups = slots.shape[0]
    depth = width // groups
    half = piece_plan(groups, [depth] * 2, -1)
    later = piece_plan(groups, [depth] * 2 + [PAD], -1)
    plan = [one + tuple((piece + groups, row) for piece, row in two) for one, two in zip(half, later)]
    lane = lax.broadcasted_iota(jnp.int32, (LANES, width), 1) - lax.broadcasted_iota(jnp.int32, (LANES, width), 0)
    gain_sum = jnp.zeros((PAD, width), f32)
    for number, sources in enumerate(plan):
        start = pl.multiple_of(slots[number] * depth, depth)
        for part, (piece, row) in enumerate(sources[:4]):
            lanes = slice(part * local, (part + 1) * local)
            wide[pl.ds(start, depth), lanes] = pieces[piece][row : row + depth, :]
        piece, row = sources[4]
        spread = jnp.where(lane == start, 1.0, 0.0).astype(bf16)
        gain_sum += dot(pieces[piece][row : row + PAD, :LANES], spread)
    gain[...] = gain_sum
    gains = gain_sum[:1]
    query_w, key_w, value_w = (wide.at[:, at * local : (at + 1) * local] for at in range(3))
    low = lax.broadcasted_iota(jnp.int32, (1, LANES), 1) % HEAD < HEAD // 2

    def rotated(src, at, size, dst, place, scale):
        co, si = cosine[pl.ds(at, size), :], sine[pl.ds(at, size), :]
        for pair in range(pairs):
            lanes = slice(pair * LANES, (pair + 1) * LANES)
            value = src[:, lanes]
            dst[pl.ds(place, size), lanes] = ((value * co + turned(value, low) * si) * scale).astype(bf16)

    chunk = step_of(extent, 384)

    def key_step(index):
        at = pl.multiple_of(index * chunk, chunk)
        here = pl.ds(at, chunk)
        part = (hat[here, :] * gains).astype(bf16)
        first[here, :] = part
        rotated(dot(part, key_w[...]), at, chunk, key, at, 1.0)
        value[here, :] = dot(part, value_w[...]).astype(bf16)

    loop(extent // chunk, key_step)
    size = step_of(rows, 256)

    def query_step(index):
        at = pl.multiple_of(index * size, size)
        start = pl.multiple_of(at + HALF, HALF)
        rotated(dot(first[pl.ds(start, size), :], query_w[...]), start, size, query, at, HEAD**-0.5)

    loop(rows // size, query_step)


def attend_kernel(chosen, last, bounds, query, key, value, *rest):
    if last:
        wide, done, shares, attended, branch = rest
        attended[...] = done[...]
    else:
        shares, attended = rest
    rows, local = query.shape
    count = len(chosen)
    key_at = lax.broadcasted_iota(jnp.int32, (KEYS, KEYS), 0)
    lane_at = lax.broadcasted_iota(jnp.int32, (1, KEYS), 1) % BLOCK

    def attend_step(index):
        at = pl.multiple_of(index * BLOCK, BLOCK)
        origin = bounds[NSEQ] + at - HALF
        own = lane_at + (origin + HALF)
        begin = jnp.zeros_like(own)
        end = jnp.zeros_like(own) + bounds[NSEQ - 1]
        for number in range(NSEQ - 1):
            begin = jnp.where(own >= bounds[number], bounds[number], begin)
        for number in reversed(range(NSEQ - 1)):
            end = jnp.where(own < bounds[number], bounds[number], end)
        least = jnp.maximum(lane_at, begin - origin)
        most = jnp.minimum(lane_at + WINDOW, end - 1 - origin)
        allowed = (key_at >= least) & (key_at <= most)
        for number, pair in enumerate(chosen):
            lanes = slice(pair * LANES, (pair + 1) * LANES)
            both = halves(query[pl.ds(at, BLOCK), lanes])
            scores = jnp.where(allowed, dot(key[pl.ds(at, KEYS), lanes], both, NT), -1e30)
            weight = jnp.exp(scores - jnp.max(scores, axis=0, keepdims=True))
            part = (weight * (1.0 / jnp.sum(weight, axis=0, keepdims=True))).astype(bf16)
            shares[index * count + number] = part
            mixed = dot(value[pl.ds(at, KEYS), lanes], part, TN)
            attended[pl.ds(at, BLOCK), lanes] = joined(mixed).astype(bf16)

    loop(rows // BLOCK, attend_step)
    if not last:
        return
    out_t = wide.at[:, 3 * local :]
    size = step_of(rows, 256)

    def out_step(index):
        here = pl.ds(pl.multiple_of(index * size, size), size)
        branch[here, :] = dot(attended[here, :], out_t[...], NT).astype(bf16)

    loop(rows // size, out_step)


def feed_kernel(slots, tokens, own, other, gain, cotangent, *rest):
    pieces, rest = rest[:-7], rest[-7:]
    middle, second, hidden, grad_gate, grad_upper, partial, whole = rest
    rows, width = tokens.shape
    groups = slots.shape[0]
    depth = width // groups
    for number, sources in enumerate(piece_plan(groups, [depth] * 3, 1)):
        place = pl.ds(pl.multiple_of(slots[number] * depth, depth), depth)
        for part, (piece, row) in enumerate(sources):
            whole[part, place, :] = pieces[piece][row : row + depth, :]
    gate_w, upper_w, down_t = (whole.at[number] for number in range(3))
    gains = gain[1:2, :]
    size = step_of(rows, 256)

    def step(index):
        here = pl.ds(pl.multiple_of(index * size, size), size)
        mid = tokens[here, :].astype(f32) + (own[here, :].astype(f32) + other[here, :].astype(f32))
        middle[here, :] = mid
        low = (normed(mid)[0] * gains).astype(bf16)
        second[here, :] = low
        gate = dot(low, gate_w[...])
        upper = dot(low, upper_w[...])
        grad = dot(cotangent[here, :], down_t[...])
        share = 0.5 * (1.0 + lax.erf(gate * (0.5**0.5)))
        smooth = gate * share
        slope = share + gate * (jnp.exp(gate * gate * -0.5) * ((2.0 * math.pi) ** -0.5))
        hidden[here, :] = (smooth * upper).astype(bf16)
        gate_low = (grad * upper * slope).astype(bf16)
        upper_low = (grad * smooth).astype(bf16)
        grad_gate[here, :] = gate_low
        grad_upper[here, :] = upper_low
        partial[here, :] = (dot(gate_low, gate_w[...], NT) + dot(upper_low, upper_w[...], NT)).astype(bf16)

    loop(rows // size, step)


def feed_out_kernel(hidden, whole, feed):
    rows = hidden.shape[0]
    size = step_of(rows, 256)

    def step(index):
        here = pl.ds(pl.multiple_of(index * size, size), size)
        feed[here, :] = dot(hidden[here, :], whole[2], NT).astype(bf16)

    loop(rows // size, step)


def weight_kernel(slots, second, hidden, grad_gate, grad_upper, cotangent, grads, total):
    rows, width = second.shape
    step_rows = step_of(width, 256)
    for number, (left, right) in enumerate(((second, grad_gate), (second, grad_upper), (cotangent, hidden))):
        for start in range(0, width, step_rows):
            here = slice(start, start + step_rows)
            total[number, here, :] = dot(left[:, here], right[...], TN).astype(bf16)
    depth = grads.shape[2]
    for number, slot in enumerate(hop_order(grads.shape[0])):
        grads[number] = total[:, pl.ds(pl.multiple_of(slots[slot] * depth, depth), depth), :]


def hop_order(count):
    middle = count // 2
    order = [middle]
    for hop in range(middle - 1, 0, -1):
        order += [hop, count - hop]
    return order + [0]


def middle_kernel(middle, own, other, gain, cotangent, wide, grad_middle, low_mid, grad_att):
    rows, width = middle.shape
    local = grad_att.shape[1]
    out_t = wide.at[:, 3 * local :]
    gains = gain[1:2, :]
    size = step_of(rows, 256)

    def norm_step(index):
        here = pl.ds(pl.multiple_of(index * size, size), size)
        hat, scale = normed(middle[here, :])
        grad = own[here, :].astype(f32) + other[here, :].astype(f32)
        mid = cotangent[here, :].astype(f32) + norm_back(grad, gains, hat, scale)
        grad_middle[here, :] = mid
        mid_low = mid.astype(bf16)
        low_mid[here, :] = mid_low
        grad_att[here, :] = dot(mid_low, out_t[...]).astype(bf16)

    loop(rows // size, norm_step)


def back_kernel(chosen, query, key, value, grad_att, cosine, sine, *rest):
    held, parts, (grad_key, grad_value) = rest[: len(chosen)], rest[len(chosen) : -2], rest[-2:]
    rows = query.shape[0]
    extent = key.shape[0]
    flat = [(part, number, len(group)) for part, group in zip(held, chosen) for number in range(len(group))]
    grad_key[...] = jnp.zeros_like(grad_key)
    grad_value[...] = jnp.zeros_like(grad_value)
    low = lax.broadcasted_iota(jnp.int32, (1, LANES), 1) % HEAD < HEAD // 2
    zero = jnp.zeros((HALF, LANES), bf16)
    for part in parts:
        part[:HALF, :LANES] = zero
        part[rows + HALF :, :LANES] = zero

    def attend_step(index):
        at = pl.multiple_of(index * BLOCK, BLOCK)
        start = pl.multiple_of(at + HALF, HALF)
        co, si = cosine[pl.ds(start, BLOCK), :], sine[pl.ds(start, BLOCK), :]
        for number, (shares, spot, count) in enumerate(flat):
            lanes = slice(number * LANES, (number + 1) * LANES)
            both = halves(query[pl.ds(at, BLOCK), lanes])
            grad = halves(grad_att[pl.ds(at, BLOCK), lanes])
            keys = key[pl.ds(at, KEYS), lanes]
            part = shares[index * count + spot]
            wide = part.astype(f32)
            grad_shares = dot(value[pl.ds(at, KEYS), lanes], grad, NT)
            delta = jnp.sum(wide * grad_shares, axis=0, keepdims=True)
            raw = (wide * (grad_shares - delta)).astype(bf16)
            grad_query = joined(dot(keys, raw, TN)) * HEAD**-0.5
            turn = (grad_query * co - turned(grad_query, low) * si).astype(bf16)
            parts[number][pl.ds(start, BLOCK), :LANES] = turn
            grad_key[pl.ds(at, KEYS), lanes] += dot(raw, both)
            grad_value[pl.ds(at, KEYS), lanes] += dot(part, grad)

    loop(rows // BLOCK, attend_step)

    def turn_step(index):
        here = pl.ds(pl.multiple_of(index * BLOCK, BLOCK), BLOCK)
        co, si = cosine[here, :], sine[here, :]
        for number, out in enumerate(parts):
            lanes = slice(number * LANES, (number + 1) * LANES)
            part = grad_key[here, lanes]
            out[here, LANES : 2 * LANES] = (part * co - turned(part, low) * si).astype(bf16)
            out[here, 2 * LANES :] = grad_value[here, lanes].astype(bf16)

    loop(extent // BLOCK, turn_step)


def grad_kernel_one(slots, first, *rest):
    parts, (grad_proj, grads, total) = rest[:-3], rest[-3:]
    local = len(parts) * LANES
    for pair, part in enumerate(parts):
        for number in range(3):
            lanes = slice(number * local + pair * LANES, number * local + (pair + 1) * LANES)
            grad_proj[:, lanes] = part[:, number * LANES : (number + 1) * LANES]
    weight_grads([(first, grad_proj.at[:, at * local : (at + 1) * local]) for at in range(2)], slots, grads, total)


def grad_kernel_two(slots, first, grad_proj, low_mid, attended, grads, total):
    local = attended.shape[1]
    weight_grads([(first, grad_proj.at[:, 2 * local :]), (low_mid, attended)], slots, grads, total)


def weight_grads(sides, slots, grads, total):
    width = total.shape[1]
    depth = grads.shape[2]
    step_rows = step_of(width, 256)
    for number, (left, right) in enumerate(sides):
        for start in range(0, width, step_rows):
            here = slice(start, start + step_rows)
            total[number, here, :] = dot(left[:, here], right[...], TN).astype(bf16)
    for number, slot in enumerate(hop_order(grads.shape[0])):
        grads[number] = total[:, pl.ds(pl.multiple_of(slots[slot] * depth, depth), depth), :]


def first_kernel(grad_proj, wide, partial):
    extent, inner = grad_proj.shape
    size = step_of(extent, 384)

    def step(index):
        here = pl.ds(pl.multiple_of(index * size, size), size)
        partial[here, :] = dot(grad_proj[here, :], wide[:, :inner], NT).astype(bf16)

    loop(extent // size, step)


def final_kernel(tokens, gain, grad_middle, own, other, before, after, middle, feed_own, feed_other, mixed, token_grad):
    rows, width = tokens.shape
    gains = gain[:1, :]
    size = BLOCK

    def back(here, grad):
        hat, scale = normed(tokens[here, :].astype(f32))
        return norm_back(grad, gains, hat, scale)

    def step(index):
        at = pl.multiple_of(index * size, size)
        here, wider = pl.ds(at, size), pl.ds(pl.multiple_of(at + HALF, HALF), size)
        grad = own[wider, :].astype(f32) + other[wider, :].astype(f32)
        token_grad[here, :] = grad_middle[here, :] + back(here, grad)
        feed = feed_own[here, :].astype(f32) + feed_other[here, :].astype(f32)
        mixed[here, :] = (middle[here, :] + feed).astype(bf16)

    loop(rows // size, step)
    for start, edge in ((0, before), (rows - HALF, after)):
        here = pl.ds(start, HALF)
        token_grad[here, :] += back(here, edge[...].astype(f32))


def exchange(initial, last):
    devices, spot = lax.axis_size("ctx"), lax.axis_index("ctx")
    if devices == 2:
        got = lax.ppermute(jnp.where(spot == 0, last, initial), "ctx", [(0, 1), (1, 0)])
        none = jnp.zeros_like(got)
        return jnp.where(spot == 1, got, none), jnp.where(spot == 0, got, none)
    up = [(i, i + 1) for i in range(devices - 1)]
    return lax.ppermute(last, "ctx", up), lax.ppermute(initial, "ctx", [(j, i) for i, j in up])


def over_ctx(array):
    if lax.axis_size("ctx") == 2:
        return array.astype(f32) + swap(array, "ctx").astype(f32)
    return lax.psum(array, "ctx").astype(f32)


def swap(array, axis="tensor"):
    return lax.ppermute(array, axis, [(0, 1), (1, 0)])


def ring():
    count = lax.axis_size("dp")
    order = [2 * i for i in range(count // 2)] + [2 * i + 1 for i in reversed(range(count // 2))]
    ahead = [(order[i], order[(i + 1) % count]) for i in range(count)]
    back = [(j, i) for i, j in ahead]
    places = {group: at for at, group in enumerate(order)}
    table = np.array([[order[(places[i] + j) % count] for j in range(count)] for i in range(count)], np.int32)
    slots = lax.dynamic_index_in_dim(jnp.asarray(table), lax.axis_index("dp"), keepdims=False)
    return count, ahead, back, slots


def tied(values, others):
    held = lax.optimization_barrier((tuple(values), tuple(others)))
    return held[0]


def locked(values, chain):
    held = lax.optimization_barrier((tuple(values), tuple(chain.state)))
    chain.state = held[1]
    return held[0]


def alternate(first, second):
    if len(second.past) > 1:
        first.after(second.past[-2])
    first.hop()
    if len(first.past) > 1:
        second.after(first.past[-2])
    second.hop()


class RingGather:
    def __init__(self, block, cut=0, way=None):
        self.count, self.ahead, self.back, _ = ring()
        self.cut = cut
        self.way = way
        self.pieces = {0: (block,)}
        self.state = (block, block)
        self.hops = 0
        self.past = []

    def hop(self):
        one, two = self.state
        middle = self.count // 2
        if self.hops + 1 == middle and self.way is not None:
            got = lax.ppermute((one, two)[self.way], "dp", (self.ahead, self.back)[self.way])
            self.hops += 1
            self.state = (got,)
            self.past.append(self.state)
            self.pieces[middle] = (got,)
            return
        if self.hops + 1 == middle:
            one, two = one[: self.cut], two[self.cut :]
        one, two = lax.ppermute(one, "dp", self.ahead), lax.ppermute(two, "dp", self.back)
        self.hops += 1
        one, two = lax.optimization_barrier((one, two))
        self.state = (one, two)
        self.past.append(self.state)
        if self.hops == middle:
            self.pieces[middle] = (one, two)
        else:
            self.pieces[self.count - self.hops], self.pieces[self.hops] = (one,), (two,)

    def after(self, others):
        self.state = tied(self.state, others)


class RingScatter:
    def __init__(self, parts, axis=0, way=None):
        self.count, self.ahead, self.back, _ = ring()
        self.parts = parts
        self.axis = axis
        self.way = way
        self.hops = 0
        self.state = ()
        self.past = []

    def part(self, at):
        total = self.parts[0][at]
        for part in self.parts[1:]:
            total = total + part[at]
        return total

    def hop(self):
        if self.hops == 0 and self.way is not None:
            got = lax.ppermute(self.part(0), "dp", (self.ahead, self.back)[self.way])
            self.state = (got,)
            self.past.append(self.state)
            self.hops += 1
            return
        if self.hops == 0:
            one, two = jnp.split(self.part(0), 2, axis=self.axis)
        else:
            sides = [self.part(2 * self.hops - 1), self.part(2 * self.hops)]
            if self.hops == 1 and self.way is not None:
                sides[self.way] = sides[self.way] + self.state[0]
            one, two = sides if self.hops == 1 and self.way is not None else self.state
            if self.hops == 1 and self.way is None:
                none = jnp.zeros_like(one)
                one = jnp.concatenate([one, none], axis=self.axis)
                two = jnp.concatenate([none, two], axis=self.axis)
            if self.hops > 1 or self.way is None:
                one, two = sides[0] + one, sides[1] + two
        one, two = lax.ppermute(one, "dp", self.ahead), lax.ppermute(two, "dp", self.back)
        self.state = lax.optimization_barrier((one, two))
        self.past.append(self.state)
        self.hops += 1

    def after(self, others):
        self.state = tied(self.state, others)

    def total(self):
        one, two = self.state
        return (self.part(self.count - 1).astype(f32) + one.astype(f32) + two.astype(f32)).astype(bf16)


def tables(lengths, rows):
    place = lax.axis_index("ctx") * rows
    spots = jnp.arange(NSEQ, dtype=jnp.int32)
    ends = jnp.sum(jnp.where(spots[None, :] <= spots[:, None], lengths[0][None, :], 0), axis=1)
    starts = ends - lengths[0]
    span = place + jnp.arange(-HALF, rows + HALF, dtype=jnp.int32)
    inside = (span[:, None] >= starts[None, :]) & (span[:, None] < ends[None, :])
    position = span - jnp.sum(jnp.where(inside, starts[None, :], 0), axis=1)
    lane = jnp.arange(LANES, dtype=jnp.int32)
    number = (lane % (HEAD // 2)).astype(f32)
    freq = jnp.exp(number * (-2.0 * math.log(10000.0) / HEAD))
    angle = position.astype(f32)[:, None] * freq[None, :]
    sine = jnp.sin(angle)
    sine = jnp.where((lane % HEAD < HEAD // 2)[None, :], -sine, sine)
    bounds = jnp.concatenate([ends, place[None]]).astype(jnp.int32)
    return jnp.cos(angle), sine, bounds


def body(tokens, lengths, gain_one, w_qkv, w_out, gain_two, w_in, w_down, cotangent):
    rows, width = tokens.shape
    local, units = w_out.shape[0], w_down.shape[0]
    pairs, blocks, extent = local // LANES, rows // BLOCK, rows + WINDOW
    groups = lax.axis_size("dp")
    depth = width // groups
    middle_hop = groups // 2
    gains = jnp.pad(jnp.stack([gain_one, gain_two]), ((0, PAD - 2), (0, local - depth)))
    middle_hop = groups // 2
    now = [
        RingGather(w_qkv[:2].reshape(2 * depth, local), way=0),
        RingGather(jnp.concatenate([w_qkv[2], w_out.T, gains]), way=1),
    ]
    alternate(*now)
    before, after = exchange(tokens[:HALF], tokens[rows - HALF :])
    slots = ring()[-1]
    cosine, sine, bounds = tables(lengths, rows)
    for chain in now:
        chain.after([cosine, sine, bounds, slots, before, after])
    hat, = call(
        norm_kernel, [shape((extent, width), f32)], (tokens, before, after), rows * width * 2000, "first_norm"
    )
    alternate(*now)
    now[1].after([hat])
    while now[0].hops < middle_hop:
        alternate(*now)
    mine_two = jnp.concatenate([w_in.reshape(2 * depth, units), w_down.T])
    later = RingGather(tied([mine_two], [*now[0].state, *now[1].state])[0], depth)
    later.hop()
    pieces = [piece for chain in now for slot in range(groups) for piece in chain.pieces[slot]]
    wide, gain, first, query, key, value = call(
        project_kernel,
        [
            shape((width, 4 * local), bf16),
            shape((PAD, width), f32),
            shape((extent, width), bf16),
            shape((rows, local), bf16),
            shape((extent, local), bf16),
            shape((extent, local), bf16),
        ],
        (hat, cosine, sine, *pieces),
        2 * rows * width * local * 8,
        "project",
        (slots,),
    )
    early, late = tuple(range(pairs - 1)), (pairs - 1,)

    query, key, value = locked([query, key, value], later)
    later.hop()
    shares_early, attended = call(
        functools.partial(attend_kernel, early, False),
        [shape((blocks * len(early), KEYS, KEYS), bf16), shape((rows, local), bf16)],
        (query, key, value),
        2 * rows * width * local * 10,
        "attend",
        (bounds,),
    )
    attended, = locked([attended], later)
    later.hop()
    shares_late, attended, branch = call(
        functools.partial(attend_kernel, late, True),
        [
            shape((blocks * len(late), KEYS, KEYS), bf16),
            shape((rows, local), bf16),
            shape((rows, width), bf16),
        ],
        (query, key, value, wide, attended),
        2 * rows * width * local * 7,
        "attend",
        (bounds,),
    )
    branch, = locked([branch], later)
    branch_other = swap(branch)
    while later.hops < middle_hop:
        later.hop()
    pieces = [piece for slot in range(groups) for piece in later.pieces[slot]]
    middle, second, hidden, grad_gate, grad_upper, partial, whole = call(
        feed_kernel,
        [
            shape((rows, width), f32),
            shape((rows, width), bf16),
            shape((rows, units), bf16),
            shape((rows, units), bf16),
            shape((rows, units), bf16),
            shape((rows, width), bf16),
            shape((3, width, units), bf16),
        ],
        (tokens, branch, branch_other, gain, cotangent, *pieces),
        2 * rows * width * units * 8,
        "feed_forward_and_back",
        (slots,),
    )
    partial_other = swap(partial)
    grads_two, = call(
        weight_kernel,
        [shape((groups, 3, depth, units), bf16)],
        (second, hidden, grad_gate, grad_upper, cotangent),
        2 * rows * width * units * 5,
        "feed_weight_grads",
        (slots,),
        [pltpu.VMEM((3, width, units), bf16)],
    )
    grads_two, = tied([grads_two], [partial_other])
    sums_two = RingScatter([grads_two], 1)
    sums_two.hop()
    grad_middle, low_mid, grad_att = call(
        middle_kernel,
        [shape((rows, width), f32), shape((rows, width), bf16), shape((rows, local), bf16)],
        (middle, partial, partial_other, gain, cotangent, wide),
        2 * rows * width * local * 4,
        "middle_grad",
    )
    feed, = call(
        feed_out_kernel,
        [shape((rows, width), bf16)],
        (tied([hidden], [grads_two])[0], whole),
        2 * rows * width * units,
        "feed_out",
    )
    grad_att, feed = locked([grad_att, feed], sums_two)
    feed_other = swap(feed)
    sums_two.hop()
    grad_parts = call(
        functools.partial(back_kernel, (early, late)),
        [shape((extent, 3 * LANES), bf16)] * pairs,
        (query, key, value, grad_att, cosine, sine, shares_early, shares_late),
        2 * rows * width * local * 15,
        "attention_back",
        (),
        [pltpu.VMEM((extent, local), f32)] * 2,
    )
    grad_parts = locked(grad_parts, sums_two)
    sums_two.hop()
    grad_proj, grads_a = call(
        grad_kernel_one,
        [shape((extent, 3 * local), bf16), shape((groups, 2, depth, local), bf16)],
        (first, *grad_parts),
        2 * rows * width * local * 3,
        "query_key_grads",
        (slots,),
        [pltpu.VMEM((2, width, local), bf16)],
    )
    first_part, = call(
        first_kernel,
        [shape((extent, width), bf16)],
        (grad_proj, wide),
        2 * rows * width * local * 3,
        "first_grad",
    )
    grads_b, = call(
        grad_kernel_two,
        [shape((groups, 2, depth, local), bf16)],
        (first, grad_proj, low_mid, attended),
        2 * rows * width * local * 3,
        "value_out_grads",
        (slots,),
        [pltpu.VMEM((2, width, local), bf16)],
    )
    *grads_one, first_part = locked([grads_a, grads_b, first_part], sums_two)
    first_other = swap(first_part)
    def edge_sum(at):
        here = slice(at, at + HALF)
        return (first_part[here].astype(f32) + first_other[here].astype(f32)).astype(bf16)

    from_before, from_after = exchange(edge_sum(0), edge_sum(rows + HALF))
    sums_one = [RingScatter([part], way=way) for way, part in enumerate(grads_one)]
    alternate(*sums_one)
    sums_two.after(sums_one[0].state)
    while sums_two.hops < middle_hop:
        sums_two.hop()

    sums_one[1].after([from_before, from_after])
    while sums_one[0].hops < middle_hop - 2:
        alternate(*sums_one)
    sums_one[1].after(sums_two.state)
    tokens, = tied([tokens], sums_one[0].state)
    alternate(*sums_one)
    mixed, token_grad = call(
        final_kernel,
        [shape((rows, width), bf16), shape((rows, width), f32)],
        (tokens, gain, grad_middle, first_part, first_other, from_before, from_after, middle, feed, feed_other),
        rows * width * 2000,
        "token_grad",
    )
    sums_one[0].after([mixed, token_grad])
    alternate(*sums_one)
    two = over_ctx(sums_two.total())
    one = over_ctx(sums_one[0].total())
    one = jnp.concatenate([one, over_ctx(sums_one[1].total())])
    gain_one_grad = jnp.sum(one[:3] * w_qkv.astype(f32), axis=(0, 2)) / gain_one.astype(f32)
    gain_two_grad = jnp.sum(two[:2] * w_in.astype(f32), axis=(0, 2)) / gain_two.astype(f32)
    both = jnp.stack([gain_one_grad, gain_two_grad])
    both = both + swap(both)
    return (mixed, token_grad, both[0], one[:3], one[3].T, both[1], two[:2], two[2].T)


def solution(mesh):
    in_specs = (
        P(("dp", "ctx"), None),
        P("dp", None),
        P("dp"),
        P(None, "dp", "tensor"),
        P("tensor", "dp"),
        P("dp"),
        P(None, "dp", "tensor"),
        P("tensor", "dp"),
        P(("dp", "ctx"), None),
    )
    out_specs = (
        P(("dp", "ctx"), None),
        P(("dp", "ctx"), None),
        P("dp"),
        P(None, "dp", "tensor"),
        P("tensor", "dp"),
        P("dp"),
        P(None, "dp", "tensor"),
        P("tensor", "dp"),
    )
    return jax.shard_map(body, mesh=mesh, in_specs=in_specs, out_specs=out_specs, check_vma=False)
```

```python
import functools
import math

import jax
import jax.numpy as jnp
import numpy as np
from jax import lax
from jax.experimental import pallas as pl
from jax.experimental.pallas import tpu as pltpu
from jax.sharding import PartitionSpec as P

HEAD = 64
WINDOW = 128
NSEQ = 4
HALF = WINDOW // 2
PAD = 16
SPARE = 6
SHARE = 8
BLOCK = 128
LANES = 128
KEYS = BLOCK + WINDOW

norm_eps = 1e-05
f32 = jnp.float32
bf16 = jnp.bfloat16

NN = (((1,), (0,)), ((), ()))
NT = (((1,), (1,)), ((), ()))
TN = (((0,), (0,)), ((), ()))


def dot(a, b, dims=NN):
    return lax.dot_general(a, b, dims, preferred_element_type=f32)


def step_of(rows, most):
    best = LANES
    for size in range(LANES, most + 1, LANES):
        if rows % size == 0:
            best = size
    return best


def call(kernel, out_shape, args, flops, name, scalars=(), scratch=()):
    vmem = pl.BlockSpec(memory_space=pltpu.VMEM)
    smem = pl.BlockSpec(memory_space=pltpu.SMEM)
    moved = sum(x.size * x.dtype.itemsize for x in (*args, *out_shape))
    held = sum(math.prod(x.shape) * jnp.dtype(x.dtype).itemsize for x in scratch if x.dtype in (f32, bf16))
    limit = held + SPARE * 2**20
    return pl.pallas_call(
        kernel,
        out_shape=out_shape,
        in_specs=[smem] * len(scalars) + [vmem] * len(args),
        out_specs=[vmem] * len(out_shape),
        scratch_shapes=scratch,
        compiler_params=pltpu.CompilerParams(vmem_limit_bytes=limit),
        cost_estimate=pl.CostEstimate(flops=flops // SHARE, bytes_accessed=moved // SHARE, transcendentals=0),
        name=name,
    )(*scalars, *args)


def shape(dims, dtype):
    return jax.ShapeDtypeStruct(dims, dtype)


def normed(values):
    centered = values - jnp.mean(values, axis=-1, keepdims=True)
    spread = jnp.mean(centered * centered, axis=-1, keepdims=True)
    scale = lax.rsqrt(spread + norm_eps)
    return centered * scale, scale


def norm_back(grad, gain, hat, scale):
    inner = grad * gain
    one = jnp.mean(inner, axis=-1, keepdims=True)
    two = jnp.mean(inner * hat, axis=-1, keepdims=True)
    return scale * (inner - one - hat * two)


def turned(values, low):
    return jnp.where(low, pltpu.roll(values, LANES - HEAD // 2, 1), pltpu.roll(values, HEAD // 2, 1))


def halves(values):
    even = (lax.broadcasted_iota(jnp.int32, (1, LANES), 1) < HEAD).astype(f32).astype(bf16)
    return jnp.concatenate([values * even, values * (1 - even)], axis=0)


def joined(values):
    return jnp.concatenate([values[:HEAD, :BLOCK], values[HEAD:, BLOCK:]], axis=0).T


def loop(count, body):
    def run(index, carry):
        body(index)
        return carry

    lax.fori_loop(0, count, run, 0)


def norm_kernel(tokens, before, after, hat):
    rows, width = tokens.shape

    def norm_rows(src, dst, size):
        hat[pl.ds(dst, size), :] = normed(src.astype(f32))[0]

    norm_rows(before[...], 0, HALF)
    norm_rows(after[...], rows + HALF, HALF)

    def norm_step(index):
        at = pl.multiple_of(index * BLOCK, BLOCK)
        norm_rows(tokens[pl.ds(at, BLOCK), :], pl.multiple_of(at + HALF, HALF), BLOCK)

    loop(rows // BLOCK, norm_step)


def piece_plan(count, sizes, break_at):
    plan, used = [], 0
    for slot in range(count):
        row, sources = 0, []
        for number, size in enumerate(sizes):
            if slot == count // 2 and number == break_at:
                used, row = used + 1, 0
            sources.append((used, row))
            row += size
        plan.append(tuple(sources))
        used += 1
    return plan


def project_kernel(slots, hat, cosine, sine, *rest):
    pieces, (wide, gain, first, query, key, value) = rest[:-6], rest[-6:]
    extent, local = key.shape
    rows = query.shape[0]
    width = hat.shape[1]
    pairs = local // LANES
    groups = slots.shape[0]
    depth = width // groups
    plan = piece_plan(groups, [depth] * 4 + [PAD], 2)
    lane = lax.broadcasted_iota(jnp.int32, (LANES, width), 1) - lax.broadcasted_iota(jnp.int32, (LANES, width), 0)
    gain_sum = jnp.zeros((PAD, width), f32)
    for number, sources in enumerate(plan):
        start = pl.multiple_of(slots[number] * depth, depth)
        for part, (piece, row) in enumerate(sources[:4]):
            lanes = slice(part * local, (part + 1) * local)
            wide[pl.ds(start, depth), lanes] = pieces[piece][row : row + depth, :]
        piece, row = sources[4]
        spread = jnp.where(lane == start, 1.0, 0.0).astype(bf16)
        gain_sum += dot(pieces[piece][row : row + PAD, :LANES], spread)
    gain[...] = gain_sum
    gains = gain_sum[:1]
    query_w, key_w, value_w = (wide.at[:, at * local : (at + 1) * local] for at in range(3))
    low = lax.broadcasted_iota(jnp.int32, (1, LANES), 1) % HEAD < HEAD // 2

    def rotated(src, at, size, dst, place, scale):
        co, si = cosine[pl.ds(at, size), :], sine[pl.ds(at, size), :]
        for pair in range(pairs):
            lanes = slice(pair * LANES, (pair + 1) * LANES)
            value = src[:, lanes]
            dst[pl.ds(place, size), lanes] = ((value * co + turned(value, low) * si) * scale).astype(bf16)

    chunk = step_of(extent, 384)

    def key_step(index):
        at = pl.multiple_of(index * chunk, chunk)
        here = pl.ds(at, chunk)
        part = (hat[here, :] * gains).astype(bf16)
        first[here, :] = part
        rotated(dot(part, key_w[...]), at, chunk, key, at, 1.0)
        value[here, :] = dot(part, value_w[...]).astype(bf16)

    loop(extent // chunk, key_step)
    size = step_of(rows, 256)

    def query_step(index):
        at = pl.multiple_of(index * size, size)
        start = pl.multiple_of(at + HALF, HALF)
        rotated(dot(first[pl.ds(start, size), :], query_w[...]), start, size, query, at, HEAD**-0.5)

    loop(rows // size, query_step)


def attend_kernel(chosen, last, bounds, query, key, value, *rest):
    if last:
        wide, done, shares, attended, branch = rest
        attended[...] = done[...]
    else:
        shares, attended = rest
    rows, local = query.shape
    count = len(chosen)
    key_at = lax.broadcasted_iota(jnp.int32, (KEYS, KEYS), 0)
    lane_at = lax.broadcasted_iota(jnp.int32, (1, KEYS), 1) % BLOCK

    def attend_step(index):
        at = pl.multiple_of(index * BLOCK, BLOCK)
        origin = bounds[NSEQ] + at - HALF
        own = lane_at + (origin + HALF)
        begin = jnp.zeros_like(own)
        end = jnp.zeros_like(own) + bounds[NSEQ - 1]
        for number in range(NSEQ - 1):
            begin = jnp.where(own >= bounds[number], bounds[number], begin)
        for number in reversed(range(NSEQ - 1)):
            end = jnp.where(own < bounds[number], bounds[number], end)
        least = jnp.maximum(lane_at, begin - origin)
        most = jnp.minimum(lane_at + WINDOW, end - 1 - origin)
        allowed = (key_at >= least) & (key_at <= most)
        for number, pair in enumerate(chosen):
            lanes = slice(pair * LANES, (pair + 1) * LANES)
            both = halves(query[pl.ds(at, BLOCK), lanes])
            scores = jnp.where(allowed, dot(key[pl.ds(at, KEYS), lanes], both, NT), -1e30)
            weight = jnp.exp(scores - jnp.max(scores, axis=0, keepdims=True))
            part = (weight * (1.0 / jnp.sum(weight, axis=0, keepdims=True))).astype(bf16)
            shares[index * count + number] = part
            mixed = dot(value[pl.ds(at, KEYS), lanes], part, TN)
            attended[pl.ds(at, BLOCK), lanes] = joined(mixed).astype(bf16)

    loop(rows // BLOCK, attend_step)
    if not last:
        return
    out_t = wide.at[:, 3 * local :]
    size = step_of(rows, 256)

    def out_step(index):
        here = pl.ds(pl.multiple_of(index * size, size), size)
        branch[here, :] = dot(attended[here, :], out_t[...], NT).astype(bf16)

    loop(rows // size, out_step)


def feed_kernel(slots, tokens, own, other, gain, cotangent, *rest):
    pieces, rest = rest[:-7], rest[-7:]
    middle, second, hidden, grad_gate, grad_upper, partial, whole = rest
    rows, width = tokens.shape
    groups = slots.shape[0]
    depth = width // groups
    for number, sources in enumerate(piece_plan(groups, [depth] * 3, 1)):
        place = pl.ds(pl.multiple_of(slots[number] * depth, depth), depth)
        for part, (piece, row) in enumerate(sources):
            whole[part, place, :] = pieces[piece][row : row + depth, :]
    gate_w, upper_w, down_t = (whole.at[number] for number in range(3))
    gains = gain[1:2, :]
    size = step_of(rows, 256)

    def step(index):
        here = pl.ds(pl.multiple_of(index * size, size), size)
        mid = tokens[here, :].astype(f32) + (own[here, :].astype(f32) + other[here, :].astype(f32))
        middle[here, :] = mid
        low = (normed(mid)[0] * gains).astype(bf16)
        second[here, :] = low
        gate = dot(low, gate_w[...])
        upper = dot(low, upper_w[...])
        grad = dot(cotangent[here, :], down_t[...])
        share = 0.5 * (1.0 + lax.erf(gate * (0.5**0.5)))
        smooth = gate * share
        slope = share + gate * (jnp.exp(gate * gate * -0.5) * ((2.0 * math.pi) ** -0.5))
        hidden[here, :] = (smooth * upper).astype(bf16)
        gate_low = (grad * upper * slope).astype(bf16)
        upper_low = (grad * smooth).astype(bf16)
        grad_gate[here, :] = gate_low
        grad_upper[here, :] = upper_low
        partial[here, :] = (dot(gate_low, gate_w[...], NT) + dot(upper_low, upper_w[...], NT)).astype(bf16)

    loop(rows // size, step)


def feed_out_kernel(hidden, whole, feed):
    rows = hidden.shape[0]
    size = step_of(rows, 256)

    def step(index):
        here = pl.ds(pl.multiple_of(index * size, size), size)
        feed[here, :] = dot(hidden[here, :], whole[2], NT).astype(bf16)

    loop(rows // size, step)


def weight_kernel(slots, second, hidden, grad_gate, grad_upper, cotangent, grads, total):
    rows, width = second.shape
    step_rows = step_of(width, 256)
    for number, (left, right) in enumerate(((second, grad_gate), (second, grad_upper), (cotangent, hidden))):
        for start in range(0, width, step_rows):
            here = slice(start, start + step_rows)
            total[number, here, :] = dot(left[:, here], right[...], TN).astype(bf16)
    depth = grads.shape[2]
    for number, slot in enumerate(hop_order(grads.shape[0])):
        grads[number] = total[:, pl.ds(pl.multiple_of(slots[slot] * depth, depth), depth), :]


def hop_order(count):
    middle = count // 2
    order = [middle]
    for hop in range(middle - 1, 0, -1):
        order += [hop, count - hop]
    return order + [0]


def middle_kernel(middle, own, other, gain, cotangent, wide, grad_middle, low_mid, grad_att):
    rows, width = middle.shape
    local = grad_att.shape[1]
    out_t = wide.at[:, 3 * local :]
    gains = gain[1:2, :]
    size = step_of(rows, 256)

    def norm_step(index):
        here = pl.ds(pl.multiple_of(index * size, size), size)
        hat, scale = normed(middle[here, :])
        grad = own[here, :].astype(f32) + other[here, :].astype(f32)
        mid = cotangent[here, :].astype(f32) + norm_back(grad, gains, hat, scale)
        grad_middle[here, :] = mid
        mid_low = mid.astype(bf16)
        low_mid[here, :] = mid_low
        grad_att[here, :] = dot(mid_low, out_t[...]).astype(bf16)

    loop(rows // size, norm_step)


def back_kernel(chosen, query, key, value, grad_att, cosine, sine, *rest):
    held, parts, (grad_key, grad_value) = rest[: len(chosen)], rest[len(chosen) : -2], rest[-2:]
    rows = query.shape[0]
    extent = key.shape[0]
    flat = [(part, number, len(group)) for part, group in zip(held, chosen) for number in range(len(group))]
    grad_key[...] = jnp.zeros_like(grad_key)
    grad_value[...] = jnp.zeros_like(grad_value)
    low = lax.broadcasted_iota(jnp.int32, (1, LANES), 1) % HEAD < HEAD // 2
    zero = jnp.zeros((HALF, LANES), bf16)
    for part in parts:
        part[:HALF, :LANES] = zero
        part[rows + HALF :, :LANES] = zero

    def attend_step(index):
        at = pl.multiple_of(index * BLOCK, BLOCK)
        start = pl.multiple_of(at + HALF, HALF)
        co, si = cosine[pl.ds(start, BLOCK), :], sine[pl.ds(start, BLOCK), :]
        for number, (shares, spot, count) in enumerate(flat):
            lanes = slice(number * LANES, (number + 1) * LANES)
            both = halves(query[pl.ds(at, BLOCK), lanes])
            grad = halves(grad_att[pl.ds(at, BLOCK), lanes])
            keys = key[pl.ds(at, KEYS), lanes]
            part = shares[index * count + spot]
            wide = part.astype(f32)
            grad_shares = dot(value[pl.ds(at, KEYS), lanes], grad, NT)
            delta = jnp.sum(wide * grad_shares, axis=0, keepdims=True)
            raw = (wide * (grad_shares - delta)).astype(bf16)
            grad_query = joined(dot(keys, raw, TN)) * HEAD**-0.5
            turn = (grad_query * co - turned(grad_query, low) * si).astype(bf16)
            parts[number][pl.ds(start, BLOCK), :LANES] = turn
            grad_key[pl.ds(at, KEYS), lanes] += dot(raw, both)
            grad_value[pl.ds(at, KEYS), lanes] += dot(part, grad)

    loop(rows // BLOCK, attend_step)

    def turn_step(index):
        here = pl.ds(pl.multiple_of(index * BLOCK, BLOCK), BLOCK)
        co, si = cosine[here, :], sine[here, :]
        for number, out in enumerate(parts):
            lanes = slice(number * LANES, (number + 1) * LANES)
            part = grad_key[here, lanes]
            out[here, LANES : 2 * LANES] = (part * co - turned(part, low) * si).astype(bf16)
            out[here, 2 * LANES :] = grad_value[here, lanes].astype(bf16)

    loop(extent // BLOCK, turn_step)


def grad_kernel_one(slots, first, wide, *rest):
    parts, (grad_proj, grads, edges, total) = rest[:-4], rest[-4:]
    local = len(parts) * LANES
    for pair, part in enumerate(parts):
        for number in range(3):
            lanes = slice(number * local + pair * LANES, number * local + (pair + 1) * LANES)
            grad_proj[:, lanes] = part[:, number * LANES : (number + 1) * LANES]
    extent = first.shape[0]
    for side, start in enumerate((0, extent - HALF)):
        outer = grad_proj[start : start + HALF, :]
        edges[side] = dot(outer, wide[:, : 3 * local], NT).astype(bf16)
    weight_grads([(first, grad_proj.at[:, at * local : (at + 1) * local]) for at in range(2)], slots, grads, total)


def grad_kernel_two(slots, first, grad_proj, low_mid, attended, grads, total):
    local = attended.shape[1]
    weight_grads([(first, grad_proj.at[:, 2 * local :]), (low_mid, attended)], slots, grads, total)


def weight_grads(sides, slots, grads, total):
    width = total.shape[1]
    depth = grads.shape[2]
    step_rows = step_of(width, 256)
    for number, (left, right) in enumerate(sides):
        for start in range(0, width, step_rows):
            here = slice(start, start + step_rows)
            total[number, here, :] = dot(left[:, here], right[...], TN).astype(bf16)
    for number, slot in enumerate(hop_order(grads.shape[0])):
        grads[number] = total[:, pl.ds(pl.multiple_of(slots[slot] * depth, depth), depth), :]


def first_kernel(grad_proj, wide, partial):
    rows = partial.shape[0]
    inner = grad_proj.shape[1]
    size = step_of(rows, 256)

    def step(index):
        at = pl.multiple_of(index * size, size)
        wider = pl.ds(pl.multiple_of(at + HALF, HALF), size)
        partial[pl.ds(at, size), :] = dot(grad_proj[wider, :], wide[:, :inner], NT).astype(bf16)

    loop(rows // size, step)


def token_kernel(tokens, gain, grad_middle, own, other, one, two, token_grad):
    rows, width = tokens.shape
    gains = gain[:1, :]
    size = BLOCK

    def back(here, grad):
        hat, scale = normed(tokens[here, :].astype(f32))
        return norm_back(grad, gains, hat, scale)

    def step(index):
        here = pl.ds(pl.multiple_of(index * size, size), size)
        grad = own[here, :].astype(f32) + other[here, :].astype(f32)
        token_grad[here, :] = grad_middle[here, :] + back(here, grad)

    loop(rows // size, step)
    for side, start in enumerate((0, rows - HALF)):
        here = pl.ds(start, HALF)
        token_grad[here, :] += back(here, one[side].astype(f32) + two[side].astype(f32))


def mixed_kernel(middle, own, other, mixed):
    rows = middle.shape[0]

    def step(index):
        here = pl.ds(pl.multiple_of(index * BLOCK, BLOCK), BLOCK)
        mixed[here, :] = (middle[here, :] + (own[here, :].astype(f32) + other[here, :].astype(f32))).astype(bf16)

    loop(rows // BLOCK, step)


def traded(edges, cross):
    devices, cores = lax.axis_size("ctx"), lax.axis_size("tensor")
    spot = lax.axis_index("ctx")

    def pairs(by, start, stop):
        return [(i * cores + c, (i + by) * cores + (c + cross) % cores) for i in range(start, stop) for c in range(cores)]

    axes = ("ctx", "tensor")
    if devices == 2:
        got = lax.ppermute(jnp.where(spot == 0, edges[1], edges[0]), axes, pairs(1, 0, 1) + pairs(-1, 1, 2))
        none = jnp.zeros_like(got)
        return jnp.stack([jnp.where(spot == 1, got, none), jnp.where(spot == 0, got, none)])
    return jnp.stack(
        [
            lax.ppermute(edges[1], axes, pairs(1, 0, devices - 1)),
            lax.ppermute(edges[0], axes, pairs(-1, 1, devices)),
        ]
    )


def exchange(initial, last):
    devices, spot = lax.axis_size("ctx"), lax.axis_index("ctx")
    if devices == 2:
        got = lax.ppermute(jnp.where(spot == 0, last, initial), "ctx", [(0, 1), (1, 0)])
        none = jnp.zeros_like(got)
        return jnp.where(spot == 1, got, none), jnp.where(spot == 0, got, none)
    up = [(i, i + 1) for i in range(devices - 1)]
    return lax.ppermute(last, "ctx", up), lax.ppermute(initial, "ctx", [(j, i) for i, j in up])


def over_ctx(array):
    if lax.axis_size("ctx") == 2:
        return array.astype(f32) + swap(array, "ctx").astype(f32)
    return lax.psum(array, "ctx").astype(f32)


def swap(array, axis="tensor"):
    return lax.ppermute(array, axis, [(0, 1), (1, 0)])


def ring():
    count = lax.axis_size("dp")
    order = [2 * i for i in range(count // 2)] + [2 * i + 1 for i in reversed(range(count // 2))]
    ahead = [(order[i], order[(i + 1) % count]) for i in range(count)]
    back = [(j, i) for i, j in ahead]
    places = {group: at for at, group in enumerate(order)}
    table = np.array([[order[(places[i] + j) % count] for j in range(count)] for i in range(count)], np.int32)
    slots = lax.dynamic_index_in_dim(jnp.asarray(table), lax.axis_index("dp"), keepdims=False)
    return count, ahead, back, slots


def tied(values, others):
    held = lax.optimization_barrier((tuple(values), tuple(others)))
    return held[0]


def locked(values, chain):
    held = lax.optimization_barrier((tuple(values), tuple(chain.state)))
    chain.state = held[1]
    return held[0]


def alternate(first, second):
    if len(second.past) > 1:
        first.after(second.past[-2])
    first.hop()
    if len(first.past) > 1:
        second.after(first.past[-2])
    second.hop()


class RingGather:
    def __init__(self, block, cut=0, way=None):
        self.count, self.ahead, self.back, _ = ring()
        self.cut = cut
        self.way = way
        self.pieces = {0: (block,)}
        self.state = (block, block)
        self.hops = 0
        self.past = []

    def hop(self):
        one, two = self.state
        middle = self.count // 2
        if self.hops + 1 == middle and self.way is not None:
            got = lax.ppermute((one, two)[self.way], "dp", (self.ahead, self.back)[self.way])
            self.hops += 1
            self.state = (got,)
            self.past.append(self.state)
            self.pieces[middle] = (got,)
            return
        if self.hops + 1 == middle:
            one, two = one[: self.cut], two[self.cut :]
        one, two = lax.ppermute(one, "dp", self.ahead), lax.ppermute(two, "dp", self.back)
        self.hops += 1
        one, two = lax.optimization_barrier((one, two))
        self.state = (one, two)
        self.past.append(self.state)
        if self.hops == middle:
            self.pieces[middle] = (one, two)
        else:
            self.pieces[self.count - self.hops], self.pieces[self.hops] = (one,), (two,)

    def after(self, others):
        self.state = tied(self.state, others)


class RingScatter:
    def __init__(self, parts, axis=0, way=None):
        self.count, self.ahead, self.back, _ = ring()
        self.parts = parts
        self.axis = axis
        self.way = way
        self.hops = 0
        self.state = ()
        self.past = []

    def part(self, at):
        total = self.parts[0][at]
        for part in self.parts[1:]:
            total = total + part[at]
        return total

    def hop(self):
        if self.hops == 0 and self.way is not None:
            got = lax.ppermute(self.part(0), "dp", (self.ahead, self.back)[self.way])
            self.state = (got,)
            self.past.append(self.state)
            self.hops += 1
            return
        if self.hops == 0:
            one, two = jnp.split(self.part(0), 2, axis=self.axis)
        else:
            sides = [self.part(2 * self.hops - 1), self.part(2 * self.hops)]
            if self.hops == 1 and self.way is not None:
                sides[self.way] = sides[self.way] + self.state[0]
            one, two = sides if self.hops == 1 and self.way is not None else self.state
            if self.hops == 1 and self.way is None:
                none = jnp.zeros_like(one)
                one = jnp.concatenate([one, none], axis=self.axis)
                two = jnp.concatenate([none, two], axis=self.axis)
            if self.hops > 1 or self.way is None:
                one, two = sides[0] + one, sides[1] + two
        one, two = lax.ppermute(one, "dp", self.ahead), lax.ppermute(two, "dp", self.back)
        self.state = lax.optimization_barrier((one, two))
        self.past.append(self.state)
        self.hops += 1

    def after(self, others):
        self.state = tied(self.state, others)

    def total(self):
        one, two = self.state
        return (self.part(self.count - 1).astype(f32) + one.astype(f32) + two.astype(f32)).astype(bf16)


def tables(lengths, rows):
    place = lax.axis_index("ctx") * rows
    spots = jnp.arange(NSEQ, dtype=jnp.int32)
    ends = jnp.sum(jnp.where(spots[None, :] <= spots[:, None], lengths[0][None, :], 0), axis=1)
    starts = ends - lengths[0]
    span = place + jnp.arange(-HALF, rows + HALF, dtype=jnp.int32)
    inside = (span[:, None] >= starts[None, :]) & (span[:, None] < ends[None, :])
    position = span - jnp.sum(jnp.where(inside, starts[None, :], 0), axis=1)
    lane = jnp.arange(LANES, dtype=jnp.int32)
    number = (lane % (HEAD // 2)).astype(f32)
    freq = jnp.exp(number * (-2.0 * math.log(10000.0) / HEAD))
    angle = position.astype(f32)[:, None] * freq[None, :]
    sine = jnp.sin(angle)
    sine = jnp.where((lane % HEAD < HEAD // 2)[None, :], -sine, sine)
    bounds = jnp.concatenate([ends, place[None]]).astype(jnp.int32)
    return jnp.cos(angle), sine, bounds


def body(tokens, lengths, gain_one, w_qkv, w_out, gain_two, w_in, w_down, cotangent):
    rows, width = tokens.shape
    local, units = w_out.shape[0], w_down.shape[0]
    pairs, blocks, extent = local // LANES, rows // BLOCK, rows + WINDOW
    groups = lax.axis_size("dp")
    depth = width // groups
    middle_hop = groups // 2
    gains = jnp.pad(jnp.stack([gain_one, gain_two]), ((0, PAD - 2), (0, local - depth)))
    middle_hop = groups // 2
    now = RingGather(jnp.concatenate([w_qkv.reshape(3 * depth, local), w_out.T, gains]), 2 * depth)
    now.hop()
    before, after = exchange(tokens[:HALF], tokens[rows - HALF :])
    slots = ring()[-1]
    cosine, sine, bounds = tables(lengths, rows)
    now.hop()
    now.after([cosine, sine, bounds, slots, before, after])
    hat, = call(
        norm_kernel, [shape((extent, width), f32)], (tokens, before, after), rows * width * 2000, "first_norm"
    )
    while now.hops < middle_hop:
        if now.hops + 1 == middle_hop:
            now.after([hat])
        now.hop()
    mine_two = jnp.concatenate([w_in.reshape(2 * depth, units), w_down.T])
    later = RingGather(tied([mine_two], now.state)[0], depth)
    later.hop()
    pieces = [piece for slot in range(groups) for piece in now.pieces[slot]]
    wide, gain, first, query, key, value = call(
        project_kernel,
        [
            shape((width, 4 * local), bf16),
            shape((PAD, width), f32),
            shape((extent, width), bf16),
            shape((rows, local), bf16),
            shape((extent, local), bf16),
            shape((extent, local), bf16),
        ],
        (hat, cosine, sine, *pieces),
        2 * rows * width * local * 8,
        "project",
        (slots,),
    )
    early, late = tuple(range(pairs - 1)), (pairs - 1,)

    query, key, value = locked([query, key, value], later)
    later.hop()
    shares_early, attended = call(
        functools.partial(attend_kernel, early, False),
        [shape((blocks * len(early), KEYS, KEYS), bf16), shape((rows, local), bf16)],
        (query, key, value),
        2 * rows * width * local * 10,
        "attend",
        (bounds,),
    )
    attended, = locked([attended], later)
    later.hop()
    shares_late, attended, branch = call(
        functools.partial(attend_kernel, late, True),
        [
            shape((blocks * len(late), KEYS, KEYS), bf16),
            shape((rows, local), bf16),
            shape((rows, width), bf16),
        ],
        (query, key, value, wide, attended),
        2 * rows * width * local * 7,
        "attend",
        (bounds,),
    )
    branch, = locked([branch], later)
    branch_other = swap(branch)
    while later.hops < middle_hop:
        later.hop()
    pieces = [piece for slot in range(groups) for piece in later.pieces[slot]]
    middle, second, hidden, grad_gate, grad_upper, partial, whole = call(
        feed_kernel,
        [
            shape((rows, width), f32),
            shape((rows, width), bf16),
            shape((rows, units), bf16),
            shape((rows, units), bf16),
            shape((rows, units), bf16),
            shape((rows, width), bf16),
            shape((3, width, units), bf16),
        ],
        (tokens, branch, branch_other, gain, cotangent, *pieces),
        2 * rows * width * units * 8,
        "feed_forward_and_back",
        (slots,),
    )
    partial_other = swap(partial)
    grads_two, = call(
        weight_kernel,
        [shape((groups, 3, depth, units), bf16)],
        (second, hidden, grad_gate, grad_upper, cotangent),
        2 * rows * width * units * 5,
        "feed_weight_grads",
        (slots,),
        [pltpu.VMEM((3, width, units), bf16)],
    )
    grads_two, = tied([grads_two], [partial_other])
    sums_two = RingScatter([grads_two], 1)
    sums_two.hop()
    grad_middle, low_mid, grad_att = call(
        middle_kernel,
        [shape((rows, width), f32), shape((rows, width), bf16), shape((rows, local), bf16)],
        (middle, partial, partial_other, gain, cotangent, wide),
        2 * rows * width * local * 4,
        "middle_grad",
    )
    feed, = call(
        feed_out_kernel,
        [shape((rows, width), bf16)],
        (tied([hidden], [grads_two])[0], whole),
        2 * rows * width * units,
        "feed_out",
    )
    grad_att, feed = locked([grad_att, feed], sums_two)
    feed_other = swap(feed)
    sums_two.hop()
    grad_parts = call(
        functools.partial(back_kernel, (early, late)),
        [shape((extent, 3 * LANES), bf16)] * pairs,
        (query, key, value, grad_att, cosine, sine, shares_early, shares_late),
        2 * rows * width * local * 15,
        "attention_back",
        (),
        [pltpu.VMEM((extent, local), f32)] * 2,
    )
    grad_parts = locked(grad_parts, sums_two)
    sums_two.hop()
    grad_proj, grads_a, edges = call(
        grad_kernel_one,
        [
            shape((extent, 3 * local), bf16),
            shape((groups, 2, depth, local), bf16),
            shape((2, HALF, width), bf16),
        ],
        (first, wide, *grad_parts),
        2 * rows * width * local * 3,
        "query_key_grads",
        (slots,),
        [pltpu.VMEM((2, width, local), bf16)],
    )
    first_part, = call(
        first_kernel,
        [shape((rows, width), bf16)],
        (grad_proj, wide),
        2 * rows * width * local * 3,
        "first_grad",
    )
    grads_b, = call(
        grad_kernel_two,
        [shape((groups, 2, depth, local), bf16)],
        (first, grad_proj, low_mid, attended),
        2 * rows * width * local * 3,
        "value_out_grads",
        (slots,),
        [pltpu.VMEM((2, width, local), bf16)],
    )
    sent = [traded(edges, 0), traded(edges, 1)]
    *grads_one, first_part, same, cross = locked([grads_a, grads_b, first_part, *sent], sums_two)
    first_other = swap(first_part)
    sums_one = [RingScatter([part], way=way) for way, part in enumerate(grads_one)]
    alternate(*sums_one)
    sums_two.after(sums_one[0].state)
    while sums_two.hops < middle_hop:
        sums_two.hop()

    while sums_one[0].hops < middle_hop - 2:
        alternate(*sums_one)
    sums_one[1].after(sums_two.state)
    alternate(*sums_one)
    alternate(*sums_one)
    tokens, middle = tied([tokens, middle], sums_one[1].past[-2])
    token_grad, = call(
        token_kernel,
        [shape((rows, width), f32)],
        (tokens, gain, grad_middle, first_part, first_other, same, cross),
        rows * width * 200,
        "token_grad",
    )
    two = over_ctx(sums_two.total())
    two, = locked([two], sums_one[1])
    mixed, = call(
        mixed_kernel,
        [shape((rows, width), bf16)],
        (middle, feed, feed_other),
        rows * width * 100,
        "mixed",
    )
    one = [chain.total() for chain in sums_one]
    if lax.axis_size("ctx") == 2:
        mixed, token_grad, *got = lax.optimization_barrier((mixed, token_grad, *[swap(part, "ctx") for part in one]))
        one = [part.astype(f32) + more.astype(f32) for part, more in zip(one, got)]
    else:
        one = [lax.psum(part, "ctx").astype(f32) for part in one]
    one = jnp.concatenate(one)
    gain_one_grad = jnp.sum(one[:3] * w_qkv.astype(f32), axis=(0, 2)) / gain_one.astype(f32)
    gain_two_grad = jnp.sum(two[:2] * w_in.astype(f32), axis=(0, 2)) / gain_two.astype(f32)
    both = jnp.stack([gain_one_grad, gain_two_grad])
    both = both + swap(both)
    return (mixed, token_grad, both[0], one[:3], one[3].T, both[1], two[:2], two[2].T)


def solution(mesh):
    in_specs = (
        P(("dp", "ctx"), None),
        P("dp", None),
        P("dp"),
        P(None, "dp", "tensor"),
        P("tensor", "dp"),
        P("dp"),
        P(None, "dp", "tensor"),
        P("tensor", "dp"),
        P(("dp", "ctx"), None),
    )
    out_specs = (
        P(("dp", "ctx"), None),
        P(("dp", "ctx"), None),
        P("dp"),
        P(None, "dp", "tensor"),
        P("tensor", "dp"),
        P("dp"),
        P(None, "dp", "tensor"),
        P("tensor", "dp"),
    )
    return jax.shard_map(body, mesh=mesh, in_specs=in_specs, out_specs=out_specs, check_vma=False)
```

```python
import functools
import math

import jax
import jax.numpy as jnp
import numpy as np
from jax import lax
from jax.experimental import pallas as pl
from jax.experimental.pallas import tpu as pltpu
from jax.sharding import PartitionSpec as P

HEAD = 64
WINDOW = 128
NSEQ = 4
HALF = WINDOW // 2
PAD = 16
SPARE = 6
SHARE = 8
BLOCK = 128
LANES = 128
KEYS = BLOCK + WINDOW

norm_eps = 1e-05
f32 = jnp.float32
bf16 = jnp.bfloat16

NN = (((1,), (0,)), ((), ()))
NT = (((1,), (1,)), ((), ()))
TN = (((0,), (0,)), ((), ()))


def dot(a, b, dims=NN):
    return lax.dot_general(a, b, dims, preferred_element_type=f32)


def step_of(rows, most):
    best = LANES
    for size in range(LANES, most + 1, LANES):
        if rows % size == 0:
            best = size
    return best


def call(kernel, out_shape, args, flops, name, scalars=(), scratch=()):
    vmem = pl.BlockSpec(memory_space=pltpu.VMEM)
    smem = pl.BlockSpec(memory_space=pltpu.SMEM)
    moved = sum(x.size * x.dtype.itemsize for x in (*args, *out_shape))
    held = sum(math.prod(x.shape) * jnp.dtype(x.dtype).itemsize for x in scratch if x.dtype in (f32, bf16))
    limit = held + SPARE * 2**20
    return pl.pallas_call(
        kernel,
        out_shape=out_shape,
        in_specs=[smem] * len(scalars) + [vmem] * len(args),
        out_specs=[vmem] * len(out_shape),
        scratch_shapes=scratch,
        compiler_params=pltpu.CompilerParams(vmem_limit_bytes=limit),
        cost_estimate=pl.CostEstimate(flops=flops // SHARE, bytes_accessed=moved // SHARE, transcendentals=0),
        name=name,
    )(*scalars, *args)


def shape(dims, dtype):
    return jax.ShapeDtypeStruct(dims, dtype)


def normed(values):
    centered = values - jnp.mean(values, axis=-1, keepdims=True)
    spread = jnp.mean(centered * centered, axis=-1, keepdims=True)
    scale = lax.rsqrt(spread + norm_eps)
    return centered * scale, scale


def norm_back(grad, gain, hat, scale):
    inner = grad * gain
    one = jnp.mean(inner, axis=-1, keepdims=True)
    two = jnp.mean(inner * hat, axis=-1, keepdims=True)
    return scale * (inner - one - hat * two)


def turned(values, low):
    return jnp.where(low, pltpu.roll(values, LANES - HEAD // 2, 1), pltpu.roll(values, HEAD // 2, 1))


def halves(values):
    even = (lax.broadcasted_iota(jnp.int32, (1, LANES), 1) < HEAD).astype(f32).astype(bf16)
    return jnp.concatenate([values * even, values * (1 - even)], axis=0)


def joined(values):
    return jnp.concatenate([values[:HEAD, :BLOCK], values[HEAD:, BLOCK:]], axis=0).T


def loop(count, body):
    def run(index, carry):
        body(index)
        return carry

    lax.fori_loop(0, count, run, 0)


def norm_kernel(tokens, before, after, hat):
    rows, width = tokens.shape

    def norm_rows(src, dst, size):
        hat[pl.ds(dst, size), :] = normed(src.astype(f32))[0]

    norm_rows(before[...], 0, HALF)
    norm_rows(after[...], rows + HALF, HALF)

    def norm_step(index):
        at = pl.multiple_of(index * BLOCK, BLOCK)
        norm_rows(tokens[pl.ds(at, BLOCK), :], pl.multiple_of(at + HALF, HALF), BLOCK)

    loop(rows // BLOCK, norm_step)


def piece_plan(count, sizes, break_at):
    plan, used = [], 0
    for slot in range(count):
        row, sources = 0, []
        for number, size in enumerate(sizes):
            if slot == count // 2 and number == break_at:
                used, row = used + 1, 0
            sources.append((used, row))
            row += size
        plan.append(tuple(sources))
        used += 1
    return plan


def project_kernel(slots, hat, cosine, sine, *rest):
    pieces, (wide, gain, first, query, key, value) = rest[:-6], rest[-6:]
    extent, local = key.shape
    rows = query.shape[0]
    width = hat.shape[1]
    pairs = local // LANES
    groups = slots.shape[0]
    depth = width // groups
    plan = piece_plan(groups, [depth] * 4 + [PAD], 2)
    lane = lax.broadcasted_iota(jnp.int32, (LANES, width), 1) - lax.broadcasted_iota(jnp.int32, (LANES, width), 0)
    gain_sum = jnp.zeros((PAD, width), f32)
    for number, sources in enumerate(plan):
        start = pl.multiple_of(slots[number] * depth, depth)
        for part, (piece, row) in enumerate(sources[:4]):
            lanes = slice(part * local, (part + 1) * local)
            wide[pl.ds(start, depth), lanes] = pieces[piece][row : row + depth, :]
        piece, row = sources[4]
        spread = jnp.where(lane == start, 1.0, 0.0).astype(bf16)
        gain_sum += dot(pieces[piece][row : row + PAD, :LANES], spread)
    gain[...] = gain_sum
    gains = gain_sum[:1]
    query_w, key_w, value_w = (wide.at[:, at * local : (at + 1) * local] for at in range(3))
    low = lax.broadcasted_iota(jnp.int32, (1, LANES), 1) % HEAD < HEAD // 2

    def rotated(src, at, size, dst, place, scale):
        co, si = cosine[pl.ds(at, size), :], sine[pl.ds(at, size), :]
        for pair in range(pairs):
            lanes = slice(pair * LANES, (pair + 1) * LANES)
            value = src[:, lanes]
            dst[pl.ds(place, size), lanes] = ((value * co + turned(value, low) * si) * scale).astype(bf16)

    chunk = step_of(extent, 384)

    def key_step(index):
        at = pl.multiple_of(index * chunk, chunk)
        here = pl.ds(at, chunk)
        part = (hat[here, :] * gains).astype(bf16)
        first[here, :] = part
        rotated(dot(part, key_w[...]), at, chunk, key, at, 1.0)
        value[here, :] = dot(part, value_w[...]).astype(bf16)

    loop(extent // chunk, key_step)
    size = step_of(rows, 256)

    def query_step(index):
        at = pl.multiple_of(index * size, size)
        start = pl.multiple_of(at + HALF, HALF)
        rotated(dot(first[pl.ds(start, size), :], query_w[...]), start, size, query, at, HEAD**-0.5)

    loop(rows // size, query_step)


def attend_kernel(chosen, last, bounds, query, key, value, *rest):
    if last:
        wide, shares, attended, branch = rest
    else:
        shares, attended = rest
    rows, local = query.shape
    count = len(chosen)
    key_at = lax.broadcasted_iota(jnp.int32, (KEYS, KEYS), 0)
    lane_at = lax.broadcasted_iota(jnp.int32, (1, KEYS), 1) % BLOCK

    def attend_step(index):
        at = pl.multiple_of(index * BLOCK, BLOCK)
        origin = bounds[NSEQ] + at - HALF
        own = lane_at + (origin + HALF)
        begin = jnp.zeros_like(own)
        end = jnp.zeros_like(own) + bounds[NSEQ - 1]
        for number in range(NSEQ - 1):
            begin = jnp.where(own >= bounds[number], bounds[number], begin)
        for number in reversed(range(NSEQ - 1)):
            end = jnp.where(own < bounds[number], bounds[number], end)
        least = jnp.maximum(lane_at, begin - origin)
        most = jnp.minimum(lane_at + WINDOW, end - 1 - origin)
        allowed = (key_at >= least) & (key_at <= most)
        for number, pair in enumerate(chosen):
            lanes = slice(pair * LANES, (pair + 1) * LANES)
            both = halves(query[pl.ds(at, BLOCK), lanes])
            scores = jnp.where(allowed, dot(key[pl.ds(at, KEYS), lanes], both, NT), -1e30)
            weight = jnp.exp(scores - jnp.max(scores, axis=0, keepdims=True))
            part = (weight * (1.0 / jnp.sum(weight, axis=0, keepdims=True))).astype(bf16)
            shares[index * count + number] = part
            mixed = dot(value[pl.ds(at, KEYS), lanes], part, TN)
            attended[pl.ds(at, BLOCK), lanes] = joined(mixed).astype(bf16)

    loop(rows // BLOCK, attend_step)
    if not last:
        return
    out_t = wide.at[:, 3 * local :]
    size = step_of(rows, 256)

    def out_step(index):
        here = pl.ds(pl.multiple_of(index * size, size), size)
        branch[here, :] = dot(attended[here, :], out_t[...], NT).astype(bf16)

    loop(rows // size, out_step)


def feed_kernel(slots, tokens, own, other, gain, cotangent, *rest):
    pieces, rest = rest[:-7], rest[-7:]
    middle, second, hidden, grad_gate, grad_upper, partial, whole = rest
    rows, width = tokens.shape
    groups = slots.shape[0]
    depth = width // groups
    for number, sources in enumerate(piece_plan(groups, [depth] * 3, 1)):
        place = pl.ds(pl.multiple_of(slots[number] * depth, depth), depth)
        for part, (piece, row) in enumerate(sources):
            whole[part, place, :] = pieces[piece][row : row + depth, :]
    gate_w, upper_w, down_t = (whole.at[number] for number in range(3))
    gains = gain[1:2, :]
    size = step_of(rows, 256)

    def step(index):
        here = pl.ds(pl.multiple_of(index * size, size), size)
        mid = tokens[here, :].astype(f32) + (own[here, :].astype(f32) + other[here, :].astype(f32))
        middle[here, :] = mid
        low = (normed(mid)[0] * gains).astype(bf16)
        second[here, :] = low
        gate = dot(low, gate_w[...])
        upper = dot(low, upper_w[...])
        grad = dot(cotangent[here, :], down_t[...])
        share = 0.5 * (1.0 + lax.erf(gate * (0.5**0.5)))
        smooth = gate * share
        slope = share + gate * (jnp.exp(gate * gate * -0.5) * ((2.0 * math.pi) ** -0.5))
        hidden[here, :] = (smooth * upper).astype(bf16)
        gate_low = (grad * upper * slope).astype(bf16)
        upper_low = (grad * smooth).astype(bf16)
        grad_gate[here, :] = gate_low
        grad_upper[here, :] = upper_low
        partial[here, :] = (dot(gate_low, gate_w[...], NT) + dot(upper_low, upper_w[...], NT)).astype(bf16)

    loop(rows // size, step)


def feed_out_kernel(hidden, whole, feed):
    rows = hidden.shape[0]
    size = step_of(rows, 256)

    def step(index):
        here = pl.ds(pl.multiple_of(index * size, size), size)
        feed[here, :] = dot(hidden[here, :], whole[2], NT).astype(bf16)

    loop(rows // size, step)


def weight_kernel(slots, second, hidden, grad_gate, grad_upper, cotangent, grads, total):
    rows, width = second.shape
    step_rows = step_of(width, 256)
    for number, (left, right) in enumerate(((second, grad_gate), (second, grad_upper), (cotangent, hidden))):
        for start in range(0, width, step_rows):
            here = slice(start, start + step_rows)
            total[number, here, :] = dot(left[:, here], right[...], TN).astype(bf16)
    depth = grads.shape[2]
    for number, slot in enumerate(hop_order(grads.shape[0])):
        grads[number] = total[:, pl.ds(pl.multiple_of(slots[slot] * depth, depth), depth), :]


def hop_order(count):
    middle = count // 2
    order = [middle]
    for hop in range(middle - 1, 0, -1):
        order += [hop, count - hop]
    return order + [0]


def middle_kernel(middle, own, other, gain, cotangent, wide, grad_middle, low_mid, grad_att):
    rows, width = middle.shape
    local = grad_att.shape[1]
    out_t = wide.at[:, 3 * local :]
    gains = gain[1:2, :]
    size = step_of(rows, 256)

    def norm_step(index):
        here = pl.ds(pl.multiple_of(index * size, size), size)
        hat, scale = normed(middle[here, :])
        grad = own[here, :].astype(f32) + other[here, :].astype(f32)
        mid = cotangent[here, :].astype(f32) + norm_back(grad, gains, hat, scale)
        grad_middle[here, :] = mid
        mid_low = mid.astype(bf16)
        low_mid[here, :] = mid_low
        grad_att[here, :] = dot(mid_low, out_t[...]).astype(bf16)

    loop(rows // size, norm_step)


def back_kernel(chosen, query, key, value, grad_att, cosine, sine, *rest):
    held, parts, (grad_key, grad_value) = rest[: len(chosen)], rest[len(chosen) : -2], rest[-2:]
    rows = query.shape[0]
    extent = key.shape[0]
    flat = [(part, number, len(group)) for part, group in zip(held, chosen) for number in range(len(group))]
    grad_key[...] = jnp.zeros_like(grad_key)
    grad_value[...] = jnp.zeros_like(grad_value)
    low = lax.broadcasted_iota(jnp.int32, (1, LANES), 1) % HEAD < HEAD // 2
    zero = jnp.zeros((HALF, LANES), bf16)
    for part in parts:
        part[:HALF, :LANES] = zero
        part[rows + HALF :, :LANES] = zero

    def attend_step(index):
        at = pl.multiple_of(index * BLOCK, BLOCK)
        start = pl.multiple_of(at + HALF, HALF)
        co, si = cosine[pl.ds(start, BLOCK), :], sine[pl.ds(start, BLOCK), :]
        for number, (shares, spot, count) in enumerate(flat):
            lanes = slice(number * LANES, (number + 1) * LANES)
            both = halves(query[pl.ds(at, BLOCK), lanes])
            grad = halves(grad_att[pl.ds(at, BLOCK), lanes])
            keys = key[pl.ds(at, KEYS), lanes]
            part = shares[index * count + spot]
            wide = part.astype(f32)
            grad_shares = dot(value[pl.ds(at, KEYS), lanes], grad, NT)
            delta = jnp.sum(wide * grad_shares, axis=0, keepdims=True)
            raw = (wide * (grad_shares - delta)).astype(bf16)
            grad_query = joined(dot(keys, raw, TN)) * HEAD**-0.5
            turn = (grad_query * co - turned(grad_query, low) * si).astype(bf16)
            parts[number][pl.ds(start, BLOCK), :LANES] = turn
            grad_key[pl.ds(at, KEYS), lanes] += dot(raw, both)
            grad_value[pl.ds(at, KEYS), lanes] += dot(part, grad)

    loop(rows // BLOCK, attend_step)

    def turn_step(index):
        here = pl.ds(pl.multiple_of(index * BLOCK, BLOCK), BLOCK)
        co, si = cosine[here, :], sine[here, :]
        for number, out in enumerate(parts):
            lanes = slice(number * LANES, (number + 1) * LANES)
            part = grad_key[here, lanes]
            out[here, LANES : 2 * LANES] = (part * co - turned(part, low) * si).astype(bf16)
            out[here, 2 * LANES :] = grad_value[here, lanes].astype(bf16)

    loop(extent // BLOCK, turn_step)


def grad_kernel_one(slots, first, *rest):
    parts, (grad_proj, grads, total) = rest[:-3], rest[-3:]
    local = len(parts) * LANES
    for pair, part in enumerate(parts):
        for number in range(3):
            lanes = slice(number * local + pair * LANES, number * local + (pair + 1) * LANES)
            grad_proj[:, lanes] = part[:, number * LANES : (number + 1) * LANES]
    weight_grads([(first, grad_proj.at[:, at * local : (at + 1) * local]) for at in range(2)], slots, grads, total)


def grad_kernel_two(slots, first, grad_proj, low_mid, attended, grads, total):
    local = attended.shape[1]
    weight_grads([(first, grad_proj.at[:, 2 * local :]), (low_mid, attended)], slots, grads, total)


def weight_grads(sides, slots, grads, total):
    width = total.shape[1]
    depth = grads.shape[2]
    step_rows = step_of(width, 256)
    for number, (left, right) in enumerate(sides):
        for start in range(0, width, step_rows):
            here = slice(start, start + step_rows)
            total[number, here, :] = dot(left[:, here], right[...], TN).astype(bf16)
    for number, slot in enumerate(hop_order(grads.shape[0])):
        grads[number] = total[:, pl.ds(pl.multiple_of(slots[slot] * depth, depth), depth), :]


def first_kernel(grad_proj, wide, partial, edges):
    rows = partial.shape[0]
    for side, start in enumerate((0, rows + HALF)):
        outer = grad_proj[start : start + HALF, :]
        edges[side] = dot(outer, wide[:, : outer.shape[1]], NT).astype(bf16)
    inner = grad_proj.shape[1]
    size = step_of(rows, 256)

    def step(index):
        at = pl.multiple_of(index * size, size)
        wider = pl.ds(pl.multiple_of(at + HALF, HALF), size)
        partial[pl.ds(at, size), :] = dot(grad_proj[wider, :], wide[:, :inner], NT).astype(bf16)

    loop(rows // size, step)


def token_kernel(tokens, gain, grad_middle, own, other, one, two, token_grad):
    rows, width = tokens.shape
    gains = gain[:1, :]
    size = BLOCK

    def back(here, grad):
        hat, scale = normed(tokens[here, :].astype(f32))
        return norm_back(grad, gains, hat, scale)

    def step(index):
        here = pl.ds(pl.multiple_of(index * size, size), size)
        grad = own[here, :].astype(f32) + other[here, :].astype(f32)
        token_grad[here, :] = grad_middle[here, :] + back(here, grad)

    loop(rows // size, step)
    for side, start in enumerate((0, rows - HALF)):
        here = pl.ds(start, HALF)
        token_grad[here, :] += back(here, one[side].astype(f32) + two[side].astype(f32))


def mixed_kernel(middle, own, other, mixed):
    rows = middle.shape[0]

    def step(index):
        here = pl.ds(pl.multiple_of(index * BLOCK, BLOCK), BLOCK)
        mixed[here, :] = (middle[here, :] + (own[here, :].astype(f32) + other[here, :].astype(f32))).astype(bf16)

    loop(rows // BLOCK, step)


def traded(edges, cross):
    devices, cores = lax.axis_size("ctx"), lax.axis_size("tensor")
    spot = lax.axis_index("ctx")

    def pairs(by, start, stop):
        return [(i * cores + c, (i + by) * cores + (c + cross) % cores) for i in range(start, stop) for c in range(cores)]

    axes = ("ctx", "tensor")
    if devices == 2:
        got = lax.ppermute(jnp.where(spot == 0, edges[1], edges[0]), axes, pairs(1, 0, 1) + pairs(-1, 1, 2))
        none = jnp.zeros_like(got)
        return jnp.stack([jnp.where(spot == 1, got, none), jnp.where(spot == 0, got, none)])
    return jnp.stack(
        [
            lax.ppermute(edges[1], axes, pairs(1, 0, devices - 1)),
            lax.ppermute(edges[0], axes, pairs(-1, 1, devices)),
        ]
    )


def exchange(initial, last):
    devices, spot = lax.axis_size("ctx"), lax.axis_index("ctx")
    if devices == 2:
        got = lax.ppermute(jnp.where(spot == 0, last, initial), "ctx", [(0, 1), (1, 0)])
        none = jnp.zeros_like(got)
        return jnp.where(spot == 1, got, none), jnp.where(spot == 0, got, none)
    up = [(i, i + 1) for i in range(devices - 1)]
    return lax.ppermute(last, "ctx", up), lax.ppermute(initial, "ctx", [(j, i) for i, j in up])


def over_ctx(array):
    if lax.axis_size("ctx") == 2:
        return array.astype(f32) + swap(array, "ctx").astype(f32)
    return lax.psum(array, "ctx").astype(f32)


def swap(array, axis="tensor"):
    return lax.ppermute(array, axis, [(0, 1), (1, 0)])


def ring():
    count = lax.axis_size("dp")
    order = [2 * i for i in range(count // 2)] + [2 * i + 1 for i in reversed(range(count // 2))]
    ahead = [(order[i], order[(i + 1) % count]) for i in range(count)]
    back = [(j, i) for i, j in ahead]
    places = {group: at for at, group in enumerate(order)}
    table = np.array([[order[(places[i] + j) % count] for j in range(count)] for i in range(count)], np.int32)
    slots = lax.dynamic_index_in_dim(jnp.asarray(table), lax.axis_index("dp"), keepdims=False)
    return count, ahead, back, slots


def tied(values, others):
    held = lax.optimization_barrier((tuple(values), tuple(others)))
    return held[0]


def locked(values, chain):
    held = lax.optimization_barrier((tuple(values), tuple(chain.state)))
    chain.state = held[1]
    return held[0]


def alternate(first, second):
    if len(second.past) > 1:
        first.after(second.past[-2])
    first.hop()
    if len(first.past) > 1:
        second.after(first.past[-2])
    second.hop()


class RingGather:
    def __init__(self, block, cut=0, way=None):
        self.count, self.ahead, self.back, _ = ring()
        self.cut = cut
        self.way = way
        self.pieces = {0: (block,)}
        self.state = (block, block)
        self.hops = 0
        self.past = []

    def hop(self):
        one, two = self.state
        middle = self.count // 2
        if self.hops + 1 == middle and self.way is not None:
            got = lax.ppermute((one, two)[self.way], "dp", (self.ahead, self.back)[self.way])
            self.hops += 1
            self.state = (got,)
            self.past.append(self.state)
            self.pieces[middle] = (got,)
            return
        if self.hops + 1 == middle:
            one, two = one[: self.cut], two[self.cut :]
        one, two = lax.ppermute(one, "dp", self.ahead), lax.ppermute(two, "dp", self.back)
        self.hops += 1
        one, two = lax.optimization_barrier((one, two))
        self.state = (one, two)
        self.past.append(self.state)
        if self.hops == middle:
            self.pieces[middle] = (one, two)
        else:
            self.pieces[self.count - self.hops], self.pieces[self.hops] = (one,), (two,)

    def after(self, others):
        self.state = tied(self.state, others)


class RingScatter:
    def __init__(self, parts, axis=0, way=None):
        self.count, self.ahead, self.back, _ = ring()
        self.parts = parts
        self.axis = axis
        self.way = way
        self.hops = 0
        self.state = ()
        self.past = []

    def part(self, at):
        total = self.parts[0][at]
        for part in self.parts[1:]:
            total = total + part[at]
        return total

    def hop(self):
        if self.hops == 0 and self.way is not None:
            got = lax.ppermute(self.part(0), "dp", (self.ahead, self.back)[self.way])
            self.state = (got,)
            self.past.append(self.state)
            self.hops += 1
            return
        if self.hops == 0:
            one, two = jnp.split(self.part(0), 2, axis=self.axis)
        else:
            sides = [self.part(2 * self.hops - 1), self.part(2 * self.hops)]
            if self.hops == 1 and self.way is not None:
                sides[self.way] = sides[self.way] + self.state[0]
            one, two = sides if self.hops == 1 and self.way is not None else self.state
            if self.hops == 1 and self.way is None:
                none = jnp.zeros_like(one)
                one = jnp.concatenate([one, none], axis=self.axis)
                two = jnp.concatenate([none, two], axis=self.axis)
            if self.hops > 1 or self.way is None:
                one, two = sides[0] + one, sides[1] + two
        one, two = lax.ppermute(one, "dp", self.ahead), lax.ppermute(two, "dp", self.back)
        self.state = lax.optimization_barrier((one, two))
        self.past.append(self.state)
        self.hops += 1

    def after(self, others):
        self.state = tied(self.state, others)

    def total(self):
        one, two = self.state
        return (self.part(self.count - 1).astype(f32) + one.astype(f32) + two.astype(f32)).astype(bf16)


def tables(lengths, rows):
    place = lax.axis_index("ctx") * rows
    spots = jnp.arange(NSEQ, dtype=jnp.int32)
    ends = jnp.sum(jnp.where(spots[None, :] <= spots[:, None], lengths[0][None, :], 0), axis=1)
    starts = ends - lengths[0]
    span = place + jnp.arange(-HALF, rows + HALF, dtype=jnp.int32)
    inside = (span[:, None] >= starts[None, :]) & (span[:, None] < ends[None, :])
    position = span - jnp.sum(jnp.where(inside, starts[None, :], 0), axis=1)
    lane = jnp.arange(LANES, dtype=jnp.int32)
    number = (lane % (HEAD // 2)).astype(f32)
    freq = jnp.exp(number * (-2.0 * math.log(10000.0) / HEAD))
    angle = position.astype(f32)[:, None] * freq[None, :]
    sine = jnp.sin(angle)
    sine = jnp.where((lane % HEAD < HEAD // 2)[None, :], -sine, sine)
    bounds = jnp.concatenate([ends, place[None]]).astype(jnp.int32)
    return jnp.cos(angle), sine, bounds


def body(tokens, lengths, gain_one, w_qkv, w_out, gain_two, w_in, w_down, cotangent):
    rows, width = tokens.shape
    local, units = w_out.shape[0], w_down.shape[0]
    pairs, blocks, extent = local // LANES, rows // BLOCK, rows + WINDOW
    groups = lax.axis_size("dp")
    depth = width // groups
    middle_hop = groups // 2
    gains = jnp.pad(jnp.stack([gain_one, gain_two]), ((0, PAD - 2), (0, local - depth)))
    middle_hop = groups // 2
    now = RingGather(jnp.concatenate([w_qkv.reshape(3 * depth, local), w_out.T, gains]), 2 * depth)
    now.hop()
    before, after = exchange(tokens[:HALF], tokens[rows - HALF :])
    slots = ring()[-1]
    cosine, sine, bounds = tables(lengths, rows)
    mine_two = jnp.concatenate([w_in.reshape(2 * depth, units), w_down.T])
    later = RingGather(tied([mine_two], now.state)[0], depth)
    now.hop()
    later.hop()
    now.after([cosine, sine, bounds, slots, before, after])
    hat, = call(
        norm_kernel, [shape((extent, width), f32)], (tokens, before, after), rows * width * 2000, "first_norm"
    )
    while now.hops < middle_hop:
        if now.hops + 1 == middle_hop:
            now.after([hat])
        now.hop()
        later.after(now.past[-2])
        later.hop()
    later.after(now.state)
    while later.hops < middle_hop:
        later.hop()
    pieces = [piece for slot in range(groups) for piece in now.pieces[slot]]
    wide, gain, first, query, key, value = call(
        project_kernel,
        [
            shape((width, 4 * local), bf16),
            shape((PAD, width), f32),
            shape((extent, width), bf16),
            shape((rows, local), bf16),
            shape((extent, local), bf16),
            shape((extent, local), bf16),
        ],
        (hat, cosine, sine, *pieces),
        2 * rows * width * local * 8,
        "project",
        (slots,),
    )
    query, key, value = tied([query, key, value], later.state)
    everything = tuple(range(pairs))
    shares, attended, branch = call(
        functools.partial(attend_kernel, everything, True),
        [
            shape((blocks * pairs, KEYS, KEYS), bf16),
            shape((rows, local), bf16),
            shape((rows, width), bf16),
        ],
        (query, key, value, wide),
        2 * rows * width * local * 16,
        "attend",
        (bounds,),
    )
    branch_other = swap(branch)
    pieces = [piece for slot in range(groups) for piece in later.pieces[slot]]
    middle, second, hidden, grad_gate, grad_upper, partial, whole = call(
        feed_kernel,
        [
            shape((rows, width), f32),
            shape((rows, width), bf16),
            shape((rows, units), bf16),
            shape((rows, units), bf16),
            shape((rows, units), bf16),
            shape((rows, width), bf16),
            shape((3, width, units), bf16),
        ],
        (tokens, branch, branch_other, gain, cotangent, *pieces),
        2 * rows * width * units * 8,
        "feed_forward_and_back",
        (slots,),
    )
    partial_other = swap(partial)
    grads_two, = call(
        weight_kernel,
        [shape((groups, 3, depth, units), bf16)],
        (second, hidden, grad_gate, grad_upper, cotangent),
        2 * rows * width * units * 5,
        "feed_weight_grads",
        (slots,),
        [pltpu.VMEM((3, width, units), bf16)],
    )
    grads_two, = tied([grads_two], [partial_other])
    sums_two = RingScatter([grads_two], 1)
    sums_two.hop()
    grad_middle, low_mid, grad_att = call(
        middle_kernel,
        [shape((rows, width), f32), shape((rows, width), bf16), shape((rows, local), bf16)],
        (middle, partial, partial_other, gain, cotangent, wide),
        2 * rows * width * local * 4,
        "middle_grad",
    )
    feed, = call(
        feed_out_kernel,
        [shape((rows, width), bf16)],
        (tied([hidden], [grads_two])[0], whole),
        2 * rows * width * units,
        "feed_out",
    )
    grad_att, feed = locked([grad_att, feed], sums_two)
    feed_other = swap(feed)
    sums_two.hop()
    grad_parts = call(
        functools.partial(back_kernel, (everything,)),
        [shape((extent, 3 * LANES), bf16)] * pairs,
        (query, key, value, grad_att, cosine, sine, shares),
        2 * rows * width * local * 15,
        "attention_back",
        (),
        [pltpu.VMEM((extent, local), f32)] * 2,
    )
    grad_parts = locked(grad_parts, sums_two)
    sums_two.hop()
    grad_proj, grads_a = call(
        grad_kernel_one,
        [
            shape((extent, 3 * local), bf16),
            shape((groups, 2, depth, local), bf16),
        ],
        (first, *grad_parts),
        2 * rows * width * local * 3,
        "query_key_grads",
        (slots,),
        [pltpu.VMEM((2, width, local), bf16)],
    )
    first_part, edges = call(
        first_kernel,
        [shape((rows, width), bf16), shape((2, HALF, width), bf16)],
        (grad_proj, wide),
        2 * rows * width * local * 3,
        "first_grad",
    )
    grads_b, = call(
        grad_kernel_two,
        [shape((groups, 2, depth, local), bf16)],
        (first, grad_proj, low_mid, attended),
        2 * rows * width * local * 3,
        "value_out_grads",
        (slots,),
        [pltpu.VMEM((2, width, local), bf16)],
    )
    *grads_one, first_part, edges = locked([grads_a, grads_b, first_part, edges], sums_two)
    same, cross = traded(edges, 0), traded(edges, 1)
    first_other = swap(first_part)
    sums_one = [RingScatter([part], way=way) for way, part in enumerate(grads_one)]
    alternate(*sums_one)
    while sums_two.hops < middle_hop:
        sums_two.hop()

    for chain in sums_one:
        chain.after(sums_two.state)
    while sums_one[0].hops < middle_hop - 2:
        alternate(*sums_one)
    mixed, = call(
        mixed_kernel,
        [shape((rows, width), bf16)],
        (middle, feed, feed_other),
        rows * width * 100,
        "mixed",
    )
    sums_one[1].after([mixed])
    alternate(*sums_one)
    alternate(*sums_one)
    tokens, middle = tied([tokens, middle], sums_one[1].past[-2])
    two = sums_two.total()
    gain_two_grad = jnp.sum(two[:2].astype(f32) * w_in.astype(f32), axis=(0, 2)) / gain_two.astype(f32)
    two = over_ctx(two)
    two, gain_two_grad, same, cross = locked([two, gain_two_grad, same, cross], sums_one[1])
    token_grad, = call(
        token_kernel,
        [shape((rows, width), f32)],
        (tokens, gain, grad_middle, first_part, first_other, same, cross),
        rows * width * 200,
        "token_grad",
    )
    one = [chain.total() for chain in sums_one]
    weights = w_qkv.astype(f32)
    gain_one_grad = jnp.sum(one[0].astype(f32) * weights[:2], axis=(0, 2)) + jnp.sum(one[1][0].astype(f32) * weights[2], axis=1)
    both = jnp.stack([gain_one_grad / gain_one.astype(f32), gain_two_grad])
    both = both + swap(both)
    if lax.axis_size("ctx") == 2:
        both = both + swap(both, "ctx")
        got = [swap(part, "ctx") for part in one]
        token_grad, both, *got = lax.optimization_barrier((token_grad, both, *got))
        one = [part.astype(f32) + more.astype(f32) for part, more in zip(one, got)]
    else:
        both = lax.psum(both, "ctx")
        one = [lax.psum(part, "ctx").astype(f32) for part in one]
    one = jnp.concatenate(one)
    return (mixed, token_grad, both[0], one[:3], one[3].T, both[1], two[:2], two[2].T)


def solution(mesh):
    in_specs = (
        P(("dp", "ctx"), None),
        P("dp", None),
        P("dp"),
        P(None, "dp", "tensor"),
        P("tensor", "dp"),
        P("dp"),
        P(None, "dp", "tensor"),
        P("tensor", "dp"),
        P(("dp", "ctx"), None),
    )
    out_specs = (
        P(("dp", "ctx"), None),
        P(("dp", "ctx"), None),
        P("dp"),
        P(None, "dp", "tensor"),
        P("tensor", "dp"),
        P("dp"),
        P(None, "dp", "tensor"),
        P("tensor", "dp"),
    )
    return jax.shard_map(body, mesh=mesh, in_specs=in_specs, out_specs=out_specs, check_vma=False)
```

```python
import functools
import math

import jax
import jax.numpy as jnp
import numpy as np
from jax import lax
from jax.experimental import pallas as pl
from jax.experimental.pallas import tpu as pltpu
from jax.sharding import PartitionSpec as P

HEAD = 64
WINDOW = 128
NSEQ = 4
HALF = WINDOW // 2
PAD = 16
SPARE = 6
SHARE = 8
BLOCK = 128
LANES = 128
KEYS = BLOCK + WINDOW

norm_eps = 1e-05
f32 = jnp.float32
bf16 = jnp.bfloat16

NN = (((1,), (0,)), ((), ()))
NT = (((1,), (1,)), ((), ()))
TN = (((0,), (0,)), ((), ()))


def dot(a, b, dims=NN):
    return lax.dot_general(a, b, dims, preferred_element_type=f32)


def step_of(rows, most):
    best = LANES
    for size in range(LANES, most + 1, LANES):
        if rows % size == 0:
            best = size
    return best


def call(kernel, out_shape, args, flops, name, scalars=(), scratch=()):
    vmem = pl.BlockSpec(memory_space=pltpu.VMEM)
    smem = pl.BlockSpec(memory_space=pltpu.SMEM)
    moved = sum(x.size * x.dtype.itemsize for x in (*args, *out_shape))
    held = sum(math.prod(x.shape) * jnp.dtype(x.dtype).itemsize for x in scratch if x.dtype in (f32, bf16))
    limit = held + SPARE * 2**20
    return pl.pallas_call(
        kernel,
        out_shape=out_shape,
        in_specs=[smem] * len(scalars) + [vmem] * len(args),
        out_specs=[vmem] * len(out_shape),
        scratch_shapes=scratch,
        compiler_params=pltpu.CompilerParams(vmem_limit_bytes=limit),
        cost_estimate=pl.CostEstimate(flops=flops // SHARE, bytes_accessed=moved // SHARE, transcendentals=0),
        name=name,
    )(*scalars, *args)


def shape(dims, dtype):
    return jax.ShapeDtypeStruct(dims, dtype)


def normed(values):
    centered = values - jnp.mean(values, axis=-1, keepdims=True)
    spread = jnp.mean(centered * centered, axis=-1, keepdims=True)
    scale = lax.rsqrt(spread + norm_eps)
    return centered * scale, scale


def norm_back(grad, gain, hat, scale):
    inner = grad * gain
    one = jnp.mean(inner, axis=-1, keepdims=True)
    two = jnp.mean(inner * hat, axis=-1, keepdims=True)
    return scale * (inner - one - hat * two)


def turned(values, low):
    return jnp.where(low, pltpu.roll(values, LANES - HEAD // 2, 1), pltpu.roll(values, HEAD // 2, 1))


def halves(values):
    even = (lax.broadcasted_iota(jnp.int32, (1, LANES), 1) < HEAD).astype(f32).astype(bf16)
    return jnp.concatenate([values * even, values * (1 - even)], axis=0)


def joined(values):
    return jnp.concatenate([values[:HEAD, :BLOCK], values[HEAD:, BLOCK:]], axis=0).T


def loop(count, body):
    def run(index, carry):
        body(index)
        return carry

    lax.fori_loop(0, count, run, 0)


def norm_kernel(tokens, before, after, hat):
    rows, width = tokens.shape

    def norm_rows(src, dst, size):
        hat[pl.ds(dst, size), :] = normed(src.astype(f32))[0]

    norm_rows(before[...], 0, HALF)
    norm_rows(after[...], rows + HALF, HALF)

    def norm_step(index):
        at = pl.multiple_of(index * BLOCK, BLOCK)
        norm_rows(tokens[pl.ds(at, BLOCK), :], pl.multiple_of(at + HALF, HALF), BLOCK)

    loop(rows // BLOCK, norm_step)


def piece_plan(count, sizes, break_at):
    plan, used = [], 0
    for slot in range(count):
        row, sources = 0, []
        for number, size in enumerate(sizes):
            if slot == count // 2 and number == break_at:
                used, row = used + 1, 0
            sources.append((used, row))
            row += size
        plan.append(tuple(sources))
        used += 1
    return plan


def project_kernel(slots, hat, cosine, sine, *rest):
    pieces, (wide, gain, first, query, key, value) = rest[:-6], rest[-6:]
    extent, local = key.shape
    rows = query.shape[0]
    width = hat.shape[1]
    pairs = local // LANES
    groups = slots.shape[0]
    depth = width // groups
    plan = piece_plan(groups, [depth] * 4 + [PAD], 2)
    lane = lax.broadcasted_iota(jnp.int32, (LANES, width), 1) - lax.broadcasted_iota(jnp.int32, (LANES, width), 0)
    gain_sum = jnp.zeros((PAD, width), f32)
    for number, sources in enumerate(plan):
        start = pl.multiple_of(slots[number] * depth, depth)
        for part, (piece, row) in enumerate(sources[:4]):
            lanes = slice(part * local, (part + 1) * local)
            wide[pl.ds(start, depth), lanes] = pieces[piece][row : row + depth, :]
        piece, row = sources[4]
        spread = jnp.where(lane == start, 1.0, 0.0).astype(bf16)
        gain_sum += dot(pieces[piece][row : row + PAD, :LANES], spread)
    gain[...] = gain_sum
    gains = gain_sum[:1]
    query_w, key_w, value_w = (wide.at[:, at * local : (at + 1) * local] for at in range(3))
    low = lax.broadcasted_iota(jnp.int32, (1, LANES), 1) % HEAD < HEAD // 2

    def rotated(src, at, size, dst, place, scale):
        co, si = cosine[pl.ds(at, size), :], sine[pl.ds(at, size), :]
        for pair in range(pairs):
            lanes = slice(pair * LANES, (pair + 1) * LANES)
            value = src[:, lanes]
            dst[pl.ds(place, size), lanes] = ((value * co + turned(value, low) * si) * scale).astype(bf16)

    chunk = step_of(extent, 384)

    def key_step(index):
        at = pl.multiple_of(index * chunk, chunk)
        here = pl.ds(at, chunk)
        part = (hat[here, :] * gains).astype(bf16)
        first[here, :] = part
        rotated(dot(part, key_w[...]), at, chunk, key, at, 1.0)
        value[here, :] = dot(part, value_w[...]).astype(bf16)

    loop(extent // chunk, key_step)
    size = step_of(rows, 256)

    def query_step(index):
        at = pl.multiple_of(index * size, size)
        start = pl.multiple_of(at + HALF, HALF)
        rotated(dot(first[pl.ds(start, size), :], query_w[...]), start, size, query, at, HEAD**-0.5)

    loop(rows // size, query_step)


def attend_kernel(chosen, last, bounds, query, key, value, *rest):
    if last:
        wide, done, shares, attended, branch = rest
        attended[...] = done[...]
    else:
        shares, attended = rest
    rows, local = query.shape
    count = len(chosen)
    key_at = lax.broadcasted_iota(jnp.int32, (KEYS, KEYS), 0)
    lane_at = lax.broadcasted_iota(jnp.int32, (1, KEYS), 1) % BLOCK

    def attend_step(index):
        at = pl.multiple_of(index * BLOCK, BLOCK)
        origin = bounds[NSEQ] + at - HALF
        own = lane_at + (origin + HALF)
        begin = jnp.zeros_like(own)
        end = jnp.zeros_like(own) + bounds[NSEQ - 1]
        for number in range(NSEQ - 1):
            begin = jnp.where(own >= bounds[number], bounds[number], begin)
        for number in reversed(range(NSEQ - 1)):
            end = jnp.where(own < bounds[number], bounds[number], end)
        least = jnp.maximum(lane_at, begin - origin)
        most = jnp.minimum(lane_at + WINDOW, end - 1 - origin)
        allowed = (key_at >= least) & (key_at <= most)
        for number, pair in enumerate(chosen):
            lanes = slice(pair * LANES, (pair + 1) * LANES)
            both = halves(query[pl.ds(at, BLOCK), lanes])
            scores = jnp.where(allowed, dot(key[pl.ds(at, KEYS), lanes], both, NT), -1e30)
            weight = jnp.exp(scores - jnp.max(scores, axis=0, keepdims=True))
            part = (weight * (1.0 / jnp.sum(weight, axis=0, keepdims=True))).astype(bf16)
            shares[index * count + number] = part
            mixed = dot(value[pl.ds(at, KEYS), lanes], part, TN)
            attended[pl.ds(at, BLOCK), lanes] = joined(mixed).astype(bf16)

    loop(rows // BLOCK, attend_step)
    if not last:
        return
    out_t = wide.at[:, 3 * local :]
    size = step_of(rows, 256)

    def out_step(index):
        here = pl.ds(pl.multiple_of(index * size, size), size)
        branch[here, :] = dot(attended[here, :], out_t[...], NT).astype(bf16)

    loop(rows // size, out_step)


def feed_kernel(slots, tokens, own, other, gain, cotangent, *rest):
    pieces, rest = rest[:-7], rest[-7:]
    middle, second, hidden, grad_gate, grad_upper, partial, whole = rest
    rows, width = tokens.shape
    groups = slots.shape[0]
    depth = width // groups
    for number, sources in enumerate(piece_plan(groups, [depth] * 3, 1)):
        place = pl.ds(pl.multiple_of(slots[number] * depth, depth), depth)
        for part, (piece, row) in enumerate(sources):
            whole[part, place, :] = pieces[piece][row : row + depth, :]
    gate_w, upper_w, down_t = (whole.at[number] for number in range(3))
    gains = gain[1:2, :]
    size = step_of(rows, 256)

    def step(index):
        here = pl.ds(pl.multiple_of(index * size, size), size)
        mid = tokens[here, :].astype(f32) + (own[here, :].astype(f32) + other[here, :].astype(f32))
        middle[here, :] = mid
        low = (normed(mid)[0] * gains).astype(bf16)
        second[here, :] = low
        gate = dot(low, gate_w[...])
        upper = dot(low, upper_w[...])
        grad = dot(cotangent[here, :], down_t[...])
        share = 0.5 * (1.0 + lax.erf(gate * (0.5**0.5)))
        smooth = gate * share
        slope = share + gate * (jnp.exp(gate * gate * -0.5) * ((2.0 * math.pi) ** -0.5))
        hidden[here, :] = (smooth * upper).astype(bf16)
        gate_low = (grad * upper * slope).astype(bf16)
        upper_low = (grad * smooth).astype(bf16)
        grad_gate[here, :] = gate_low
        grad_upper[here, :] = upper_low
        partial[here, :] = (dot(gate_low, gate_w[...], NT) + dot(upper_low, upper_w[...], NT)).astype(bf16)

    loop(rows // size, step)


def feed_out_kernel(hidden, whole, feed):
    rows = hidden.shape[0]
    size = step_of(rows, 256)

    def step(index):
        here = pl.ds(pl.multiple_of(index * size, size), size)
        feed[here, :] = dot(hidden[here, :], whole[2], NT).astype(bf16)

    loop(rows // size, step)


def weight_kernel(slots, second, hidden, grad_gate, grad_upper, cotangent, grads, total):
    rows, width = second.shape
    step_rows = step_of(width, 256)
    for number, (left, right) in enumerate(((second, grad_gate), (second, grad_upper), (cotangent, hidden))):
        for start in range(0, width, step_rows):
            here = slice(start, start + step_rows)
            total[number, here, :] = dot(left[:, here], right[...], TN).astype(bf16)
    depth = grads.shape[2]
    for number, slot in enumerate(hop_order(grads.shape[0])):
        grads[number] = total[:, pl.ds(pl.multiple_of(slots[slot] * depth, depth), depth), :]


def hop_order(count):
    middle = count // 2
    order = [middle]
    for hop in range(middle - 1, 0, -1):
        order += [hop, count - hop]
    return order + [0]


def middle_kernel(middle, own, other, gain, cotangent, wide, grad_middle, low_mid, grad_att):
    rows, width = middle.shape
    local = grad_att.shape[1]
    out_t = wide.at[:, 3 * local :]
    gains = gain[1:2, :]
    size = step_of(rows, 256)

    def norm_step(index):
        here = pl.ds(pl.multiple_of(index * size, size), size)
        hat, scale = normed(middle[here, :])
        grad = own[here, :].astype(f32) + other[here, :].astype(f32)
        mid = cotangent[here, :].astype(f32) + norm_back(grad, gains, hat, scale)
        grad_middle[here, :] = mid
        mid_low = mid.astype(bf16)
        low_mid[here, :] = mid_low
        grad_att[here, :] = dot(mid_low, out_t[...]).astype(bf16)

    loop(rows // size, norm_step)


def back_kernel(chosen, query, key, value, grad_att, cosine, sine, *rest):
    held, parts, (grad_key, grad_value) = rest[: len(chosen)], rest[len(chosen) : -2], rest[-2:]
    rows = query.shape[0]
    extent = key.shape[0]
    flat = [(part, number, len(group)) for part, group in zip(held, chosen) for number in range(len(group))]
    grad_key[...] = jnp.zeros_like(grad_key)
    grad_value[...] = jnp.zeros_like(grad_value)
    low = lax.broadcasted_iota(jnp.int32, (1, LANES), 1) % HEAD < HEAD // 2
    zero = jnp.zeros((HALF, LANES), bf16)
    for part in parts:
        part[:HALF, :LANES] = zero
        part[rows + HALF :, :LANES] = zero

    def attend_step(index):
        at = pl.multiple_of(index * BLOCK, BLOCK)
        start = pl.multiple_of(at + HALF, HALF)
        co, si = cosine[pl.ds(start, BLOCK), :], sine[pl.ds(start, BLOCK), :]
        for number, (shares, spot, count) in enumerate(flat):
            lanes = slice(number * LANES, (number + 1) * LANES)
            both = halves(query[pl.ds(at, BLOCK), lanes])
            grad = halves(grad_att[pl.ds(at, BLOCK), lanes])
            keys = key[pl.ds(at, KEYS), lanes]
            part = shares[index * count + spot]
            wide = part.astype(f32)
            grad_shares = dot(value[pl.ds(at, KEYS), lanes], grad, NT)
            delta = jnp.sum(wide * grad_shares, axis=0, keepdims=True)
            raw = (wide * (grad_shares - delta)).astype(bf16)
            grad_query = joined(dot(keys, raw, TN)) * HEAD**-0.5
            turn = (grad_query * co - turned(grad_query, low) * si).astype(bf16)
            parts[number][pl.ds(start, BLOCK), :LANES] = turn
            grad_key[pl.ds(at, KEYS), lanes] += dot(raw, both)
            grad_value[pl.ds(at, KEYS), lanes] += dot(part, grad)

    loop(rows // BLOCK, attend_step)

    def turn_step(index):
        here = pl.ds(pl.multiple_of(index * BLOCK, BLOCK), BLOCK)
        co, si = cosine[here, :], sine[here, :]
        for number, out in enumerate(parts):
            lanes = slice(number * LANES, (number + 1) * LANES)
            part = grad_key[here, lanes]
            out[here, LANES : 2 * LANES] = (part * co - turned(part, low) * si).astype(bf16)
            out[here, 2 * LANES :] = grad_value[here, lanes].astype(bf16)

    loop(extent // BLOCK, turn_step)


def grad_kernel_one(slots, first, *rest):
    parts, (grad_proj, grads, total) = rest[:-3], rest[-3:]
    local = len(parts) * LANES
    for pair, part in enumerate(parts):
        for number in range(3):
            lanes = slice(number * local + pair * LANES, number * local + (pair + 1) * LANES)
            grad_proj[:, lanes] = part[:, number * LANES : (number + 1) * LANES]
    weight_grads([(first, grad_proj.at[:, at * local : (at + 1) * local]) for at in range(2)], slots, grads, total)


def grad_kernel_two(slots, first, grad_proj, low_mid, attended, grads, total):
    local = attended.shape[1]
    weight_grads([(first, grad_proj.at[:, 2 * local :]), (low_mid, attended)], slots, grads, total)


def weight_grads(sides, slots, grads, total):
    width = total.shape[1]
    depth = grads.shape[2]
    step_rows = step_of(width, 256)
    for number, (left, right) in enumerate(sides):
        for start in range(0, width, step_rows):
            here = slice(start, start + step_rows)
            total[number, here, :] = dot(left[:, here], right[...], TN).astype(bf16)
    for number, slot in enumerate(hop_order(grads.shape[0])):
        grads[number] = total[:, pl.ds(pl.multiple_of(slots[slot] * depth, depth), depth), :]


def first_kernel(grad_proj, wide, partial, edges):
    rows = partial.shape[0]
    for side, start in enumerate((0, rows + HALF)):
        outer = grad_proj[start : start + HALF, :]
        edges[side] = dot(outer, wide[:, : outer.shape[1]], NT).astype(bf16)
    inner = grad_proj.shape[1]
    size = step_of(rows, 256)

    def step(index):
        at = pl.multiple_of(index * size, size)
        wider = pl.ds(pl.multiple_of(at + HALF, HALF), size)
        partial[pl.ds(at, size), :] = dot(grad_proj[wider, :], wide[:, :inner], NT).astype(bf16)

    loop(rows // size, step)


def token_kernel(tokens, gain, grad_middle, own, other, one, two, token_grad):
    rows, width = tokens.shape
    gains = gain[:1, :]
    size = BLOCK

    def back(here, grad):
        hat, scale = normed(tokens[here, :].astype(f32))
        return norm_back(grad, gains, hat, scale)

    def step(index):
        here = pl.ds(pl.multiple_of(index * size, size), size)
        grad = own[here, :].astype(f32) + other[here, :].astype(f32)
        token_grad[here, :] = grad_middle[here, :] + back(here, grad)

    loop(rows // size, step)
    for side, start in enumerate((0, rows - HALF)):
        here = pl.ds(start, HALF)
        token_grad[here, :] += back(here, one[side].astype(f32) + two[side].astype(f32))


def mixed_kernel(middle, own, other, mixed):
    rows = middle.shape[0]

    def step(index):
        here = pl.ds(pl.multiple_of(index * BLOCK, BLOCK), BLOCK)
        mixed[here, :] = (middle[here, :] + (own[here, :].astype(f32) + other[here, :].astype(f32))).astype(bf16)

    loop(rows // BLOCK, step)


def traded(edges, cross):
    devices, cores = lax.axis_size("ctx"), lax.axis_size("tensor")
    spot = lax.axis_index("ctx")

    def pairs(by, start, stop):
        return [(i * cores + c, (i + by) * cores + (c + cross) % cores) for i in range(start, stop) for c in range(cores)]

    axes = ("ctx", "tensor")
    if devices == 2:
        got = lax.ppermute(jnp.where(spot == 0, edges[1], edges[0]), axes, pairs(1, 0, 1) + pairs(-1, 1, 2))
        none = jnp.zeros_like(got)
        return jnp.stack([jnp.where(spot == 1, got, none), jnp.where(spot == 0, got, none)])
    return jnp.stack(
        [
            lax.ppermute(edges[1], axes, pairs(1, 0, devices - 1)),
            lax.ppermute(edges[0], axes, pairs(-1, 1, devices)),
        ]
    )


def exchange(initial, last):
    devices, spot = lax.axis_size("ctx"), lax.axis_index("ctx")
    if devices == 2:
        got = lax.ppermute(jnp.where(spot == 0, last, initial), "ctx", [(0, 1), (1, 0)])
        none = jnp.zeros_like(got)
        return jnp.where(spot == 1, got, none), jnp.where(spot == 0, got, none)
    up = [(i, i + 1) for i in range(devices - 1)]
    return lax.ppermute(last, "ctx", up), lax.ppermute(initial, "ctx", [(j, i) for i, j in up])


def over_ctx(array):
    if lax.axis_size("ctx") == 2:
        return array.astype(f32) + swap(array, "ctx").astype(f32)
    return lax.psum(array, "ctx").astype(f32)


def swap(array, axis="tensor"):
    return lax.ppermute(array, axis, [(0, 1), (1, 0)])


def ring():
    count = lax.axis_size("dp")
    order = [2 * i for i in range(count // 2)] + [2 * i + 1 for i in reversed(range(count // 2))]
    ahead = [(order[i], order[(i + 1) % count]) for i in range(count)]
    back = [(j, i) for i, j in ahead]
    places = {group: at for at, group in enumerate(order)}
    table = np.array([[order[(places[i] + j) % count] for j in range(count)] for i in range(count)], np.int32)
    slots = lax.dynamic_index_in_dim(jnp.asarray(table), lax.axis_index("dp"), keepdims=False)
    return count, ahead, back, slots


def tied(values, others):
    held = lax.optimization_barrier((tuple(values), tuple(others)))
    return held[0]


def locked(values, chain):
    held = lax.optimization_barrier((tuple(values), tuple(chain.state)))
    chain.state = held[1]
    return held[0]


def alternate(first, second):
    if len(second.past) > 1:
        first.after(second.past[-2])
    first.hop()
    if len(first.past) > 1:
        second.after(first.past[-2])
    second.hop()


class RingGather:
    def __init__(self, block, cut=0, way=None):
        self.count, self.ahead, self.back, _ = ring()
        self.cut = cut
        self.way = way
        self.pieces = {0: (block,)}
        self.state = (block, block)
        self.hops = 0
        self.past = []

    def hop(self):
        one, two = self.state
        middle = self.count // 2
        if self.hops + 1 == middle and self.way is not None:
            got = lax.ppermute((one, two)[self.way], "dp", (self.ahead, self.back)[self.way])
            self.hops += 1
            self.state = (got,)
            self.past.append(self.state)
            self.pieces[middle] = (got,)
            return
        if self.hops + 1 == middle:
            one, two = one[: self.cut], two[self.cut :]
        one, two = lax.ppermute(one, "dp", self.ahead), lax.ppermute(two, "dp", self.back)
        self.hops += 1
        one, two = lax.optimization_barrier((one, two))
        self.state = (one, two)
        self.past.append(self.state)
        if self.hops == middle:
            self.pieces[middle] = (one, two)
        else:
            self.pieces[self.count - self.hops], self.pieces[self.hops] = (one,), (two,)

    def after(self, others):
        self.state = tied(self.state, others)


class RingScatter:
    def __init__(self, parts, axis=0, way=None):
        self.count, self.ahead, self.back, _ = ring()
        self.parts = parts
        self.axis = axis
        self.way = way
        self.hops = 0
        self.state = ()
        self.past = []

    def part(self, at):
        total = self.parts[0][at]
        for part in self.parts[1:]:
            total = total + part[at]
        return total

    def hop(self):
        if self.hops == 0 and self.way is not None:
            got = lax.ppermute(self.part(0), "dp", (self.ahead, self.back)[self.way])
            self.state = (got,)
            self.past.append(self.state)
            self.hops += 1
            return
        if self.hops == 0:
            one, two = jnp.split(self.part(0), 2, axis=self.axis)
        else:
            sides = [self.part(2 * self.hops - 1), self.part(2 * self.hops)]
            if self.hops == 1 and self.way is not None:
                sides[self.way] = sides[self.way] + self.state[0]
            one, two = sides if self.hops == 1 and self.way is not None else self.state
            if self.hops == 1 and self.way is None:
                none = jnp.zeros_like(one)
                one = jnp.concatenate([one, none], axis=self.axis)
                two = jnp.concatenate([none, two], axis=self.axis)
            if self.hops > 1 or self.way is None:
                one, two = sides[0] + one, sides[1] + two
        one, two = lax.ppermute(one, "dp", self.ahead), lax.ppermute(two, "dp", self.back)
        self.state = lax.optimization_barrier((one, two))
        self.past.append(self.state)
        self.hops += 1

    def after(self, others):
        self.state = tied(self.state, others)

    def total(self):
        one, two = self.state
        return (self.part(self.count - 1).astype(f32) + one.astype(f32) + two.astype(f32)).astype(bf16)


def tables(lengths, rows):
    place = lax.axis_index("ctx") * rows
    spots = jnp.arange(NSEQ, dtype=jnp.int32)
    ends = jnp.sum(jnp.where(spots[None, :] <= spots[:, None], lengths[0][None, :], 0), axis=1)
    starts = ends - lengths[0]
    span = place + jnp.arange(-HALF, rows + HALF, dtype=jnp.int32)
    inside = (span[:, None] >= starts[None, :]) & (span[:, None] < ends[None, :])
    position = span - jnp.sum(jnp.where(inside, starts[None, :], 0), axis=1)
    lane = jnp.arange(LANES, dtype=jnp.int32)
    number = (lane % (HEAD // 2)).astype(f32)
    freq = jnp.exp(number * (-2.0 * math.log(10000.0) / HEAD))
    angle = position.astype(f32)[:, None] * freq[None, :]
    sine = jnp.sin(angle)
    sine = jnp.where((lane % HEAD < HEAD // 2)[None, :], -sine, sine)
    bounds = jnp.concatenate([ends, place[None]]).astype(jnp.int32)
    return jnp.cos(angle), sine, bounds


def body(tokens, lengths, gain_one, w_qkv, w_out, gain_two, w_in, w_down, cotangent):
    rows, width = tokens.shape
    local, units = w_out.shape[0], w_down.shape[0]
    pairs, blocks, extent = local // LANES, rows // BLOCK, rows + WINDOW
    groups = lax.axis_size("dp")
    depth = width // groups
    middle_hop = groups // 2
    gains = jnp.pad(jnp.stack([gain_one, gain_two]), ((0, PAD - 2), (0, local - depth)))
    middle_hop = groups // 2
    now = RingGather(jnp.concatenate([w_qkv.reshape(3 * depth, local), w_out.T, gains]), 2 * depth)
    now.hop()
    before, after = exchange(tokens[:HALF], tokens[rows - HALF :])
    slots = ring()[-1]
    cosine, sine, bounds = tables(lengths, rows)
    now.hop()
    now.after([cosine, sine, bounds, slots, before, after])
    hat, = call(
        norm_kernel, [shape((extent, width), f32)], (tokens, before, after), rows * width * 2000, "first_norm"
    )
    while now.hops < middle_hop:
        if now.hops + 1 == middle_hop:
            now.after([hat])
        now.hop()
    mine_two = jnp.concatenate([w_in.reshape(2 * depth, units), w_down.T])
    later = RingGather(tied([mine_two], now.state)[0], depth)
    later.hop()
    pieces = [piece for slot in range(groups) for piece in now.pieces[slot]]
    wide, gain, first, query, key, value = call(
        project_kernel,
        [
            shape((width, 4 * local), bf16),
            shape((PAD, width), f32),
            shape((extent, width), bf16),
            shape((rows, local), bf16),
            shape((extent, local), bf16),
            shape((extent, local), bf16),
        ],
        (hat, cosine, sine, *pieces),
        2 * rows * width * local * 8,
        "project",
        (slots,),
    )
    early, late = tuple(range(pairs - 1)), (pairs - 1,)

    query, key, value = locked([query, key, value], later)
    later.hop()
    shares_early, attended = call(
        functools.partial(attend_kernel, early, False),
        [shape((blocks * len(early), KEYS, KEYS), bf16), shape((rows, local), bf16)],
        (query, key, value),
        2 * rows * width * local * 10,
        "attend",
        (bounds,),
    )
    attended, = locked([attended], later)
    later.hop()
    shares_late, attended, branch = call(
        functools.partial(attend_kernel, late, True),
        [
            shape((blocks * len(late), KEYS, KEYS), bf16),
            shape((rows, local), bf16),
            shape((rows, width), bf16),
        ],
        (query, key, value, wide, attended),
        2 * rows * width * local * 7,
        "attend",
        (bounds,),
    )
    branch, = locked([branch], later)
    branch_other = swap(branch)
    while later.hops < middle_hop:
        later.hop()
    pieces = [piece for slot in range(groups) for piece in later.pieces[slot]]
    middle, second, hidden, grad_gate, grad_upper, partial, whole = call(
        feed_kernel,
        [
            shape((rows, width), f32),
            shape((rows, width), bf16),
            shape((rows, units), bf16),
            shape((rows, units), bf16),
            shape((rows, units), bf16),
            shape((rows, width), bf16),
            shape((3, width, units), bf16),
        ],
        (tokens, branch, branch_other, gain, cotangent, *pieces),
        2 * rows * width * units * 8,
        "feed_forward_and_back",
        (slots,),
    )
    partial_other = swap(partial)
    grads_two, = call(
        weight_kernel,
        [shape((groups, 3, depth, units), bf16)],
        (second, hidden, grad_gate, grad_upper, cotangent),
        2 * rows * width * units * 5,
        "feed_weight_grads",
        (slots,),
        [pltpu.VMEM((3, width, units), bf16)],
    )
    grads_two, = tied([grads_two], [partial_other])
    sums_two = RingScatter([grads_two], 1)
    sums_two.hop()
    grad_middle, low_mid, grad_att = call(
        middle_kernel,
        [shape((rows, width), f32), shape((rows, width), bf16), shape((rows, local), bf16)],
        (middle, partial, partial_other, gain, cotangent, wide),
        2 * rows * width * local * 4,
        "middle_grad",
    )
    feed, = call(
        feed_out_kernel,
        [shape((rows, width), bf16)],
        (tied([hidden], [grads_two])[0], whole),
        2 * rows * width * units,
        "feed_out",
    )
    grad_att, feed = locked([grad_att, feed], sums_two)
    feed_other = swap(feed)
    sums_two.hop()
    grad_parts = call(
        functools.partial(back_kernel, (early, late)),
        [shape((extent, 3 * LANES), bf16)] * pairs,
        (query, key, value, grad_att, cosine, sine, shares_early, shares_late),
        2 * rows * width * local * 15,
        "attention_back",
        (),
        [pltpu.VMEM((extent, local), f32)] * 2,
    )
    grad_parts = locked(grad_parts, sums_two)
    sums_two.hop()
    grad_proj, grads_a = call(
        grad_kernel_one,
        [
            shape((extent, 3 * local), bf16),
            shape((groups, 2, depth, local), bf16),
        ],
        (first, *grad_parts),
        2 * rows * width * local * 3,
        "query_key_grads",
        (slots,),
        [pltpu.VMEM((2, width, local), bf16)],
    )
    first_part, edges = call(
        first_kernel,
        [shape((rows, width), bf16), shape((2, HALF, width), bf16)],
        (grad_proj, wide),
        2 * rows * width * local * 3,
        "first_grad",
    )
    grads_b, = call(
        grad_kernel_two,
        [shape((groups, 2, depth, local), bf16)],
        (first, grad_proj, low_mid, attended),
        2 * rows * width * local * 3,
        "value_out_grads",
        (slots,),
        [pltpu.VMEM((2, width, local), bf16)],
    )
    *grads_one, first_part, edges = locked([grads_a, grads_b, first_part, edges], sums_two)
    first_other = swap(first_part)
    sums_one = [RingScatter([part], way=way) for way, part in enumerate(grads_one)]
    alternate(*sums_one)
    sums_two.after(sums_one[0].state)
    while sums_two.hops < middle_hop:
        sums_two.hop()

    while sums_one[0].hops < middle_hop - 2:
        alternate(*sums_one)
    edges, = tied([edges], sums_one[0].past[0])
    same, cross = traded(edges, 0), traded(edges, 1)
    sums_one[1].after([*sums_two.state, same, cross])
    alternate(*sums_one)
    alternate(*sums_one)
    tokens, middle = tied([tokens, middle], sums_one[1].past[-2])
    token_grad, = call(
        token_kernel,
        [shape((rows, width), f32)],
        (tokens, gain, grad_middle, first_part, first_other, same, cross),
        rows * width * 200,
        "token_grad",
    )
    two = over_ctx(sums_two.total())
    two, = locked([two], sums_one[1])
    mixed, = call(
        mixed_kernel,
        [shape((rows, width), bf16)],
        (middle, feed, feed_other),
        rows * width * 100,
        "mixed",
    )
    one = [chain.total() for chain in sums_one]
    if lax.axis_size("ctx") == 2:
        mixed, token_grad, *got = lax.optimization_barrier((mixed, token_grad, *[swap(part, "ctx") for part in one]))
        one = [part.astype(f32) + more.astype(f32) for part, more in zip(one, got)]
    else:
        one = [lax.psum(part, "ctx").astype(f32) for part in one]
    one = jnp.concatenate(one)
    gain_one_grad = jnp.sum(one[:3] * w_qkv.astype(f32), axis=(0, 2)) / gain_one.astype(f32)
    gain_two_grad = jnp.sum(two[:2] * w_in.astype(f32), axis=(0, 2)) / gain_two.astype(f32)
    both = jnp.stack([gain_one_grad, gain_two_grad])
    both = both + swap(both)
    return (mixed, token_grad, both[0], one[:3], one[3].T, both[1], two[:2], two[2].T)


def solution(mesh):
    in_specs = (
        P(("dp", "ctx"), None),
        P("dp", None),
        P("dp"),
        P(None, "dp", "tensor"),
        P("tensor", "dp"),
        P("dp"),
        P(None, "dp", "tensor"),
        P("tensor", "dp"),
        P(("dp", "ctx"), None),
    )
    out_specs = (
        P(("dp", "ctx"), None),
        P(("dp", "ctx"), None),
        P("dp"),
        P(None, "dp", "tensor"),
        P("tensor", "dp"),
        P("dp"),
        P(None, "dp", "tensor"),
        P("tensor", "dp"),
    )
    return jax.shard_map(body, mesh=mesh, in_specs=in_specs, out_specs=out_specs, check_vma=False)
```

```python
import functools
import math

import jax
import jax.numpy as jnp
import numpy as np
from jax import lax
from jax.experimental import pallas as pl
from jax.experimental.pallas import tpu as pltpu
from jax.sharding import PartitionSpec as P

HEAD = 64
WINDOW = 128
NSEQ = 4
HALF = WINDOW // 2
PAD = 16
SPARE = 6
SHARE = 8
BLOCK = 128
LANES = 128
KEYS = BLOCK + WINDOW

norm_eps = 1e-05
f32 = jnp.float32
bf16 = jnp.bfloat16

NN = (((1,), (0,)), ((), ()))
NT = (((1,), (1,)), ((), ()))
TN = (((0,), (0,)), ((), ()))


def dot(a, b, dims=NN):
    return lax.dot_general(a, b, dims, preferred_element_type=f32)


def step_of(rows, most):
    best = LANES
    for size in range(LANES, most + 1, LANES):
        if rows % size == 0:
            best = size
    return best


def call(kernel, out_shape, args, flops, name, scalars=(), scratch=()):
    vmem = pl.BlockSpec(memory_space=pltpu.VMEM)
    smem = pl.BlockSpec(memory_space=pltpu.SMEM)
    moved = sum(x.size * x.dtype.itemsize for x in (*args, *out_shape))
    held = sum(math.prod(x.shape) * jnp.dtype(x.dtype).itemsize for x in scratch if x.dtype in (f32, bf16))
    limit = held + SPARE * 2**20
    return pl.pallas_call(
        kernel,
        out_shape=out_shape,
        in_specs=[smem] * len(scalars) + [vmem] * len(args),
        out_specs=[vmem] * len(out_shape),
        scratch_shapes=scratch,
        compiler_params=pltpu.CompilerParams(vmem_limit_bytes=limit),
        cost_estimate=pl.CostEstimate(flops=flops // SHARE, bytes_accessed=moved // SHARE, transcendentals=0),
        name=name,
    )(*scalars, *args)


def shape(dims, dtype):
    return jax.ShapeDtypeStruct(dims, dtype)


def normed(values):
    centered = values - jnp.mean(values, axis=-1, keepdims=True)
    spread = jnp.mean(centered * centered, axis=-1, keepdims=True)
    scale = lax.rsqrt(spread + norm_eps)
    return centered * scale, scale


def norm_back(grad, gain, hat, scale):
    inner = grad * gain
    one = jnp.mean(inner, axis=-1, keepdims=True)
    two = jnp.mean(inner * hat, axis=-1, keepdims=True)
    return scale * (inner - one - hat * two)


def turned(values, low):
    return jnp.where(low, pltpu.roll(values, LANES - HEAD // 2, 1), pltpu.roll(values, HEAD // 2, 1))


def halves(values):
    even = (lax.broadcasted_iota(jnp.int32, (1, LANES), 1) < HEAD).astype(f32).astype(bf16)
    return jnp.concatenate([values * even, values * (1 - even)], axis=0)


def joined(values):
    return jnp.concatenate([values[:HEAD, :BLOCK], values[HEAD:, BLOCK:]], axis=0).T


def loop(count, body):
    def run(index, carry):
        body(index)
        return carry

    lax.fori_loop(0, count, run, 0)


def norm_kernel(tokens, before, after, hat):
    rows, width = tokens.shape

    def norm_rows(src, dst, size):
        hat[pl.ds(dst, size), :] = normed(src.astype(f32))[0]

    norm_rows(before[...], 0, HALF)
    norm_rows(after[...], rows + HALF, HALF)

    def norm_step(index):
        at = pl.multiple_of(index * BLOCK, BLOCK)
        norm_rows(tokens[pl.ds(at, BLOCK), :], pl.multiple_of(at + HALF, HALF), BLOCK)

    loop(rows // BLOCK, norm_step)


def piece_plan(count, sizes, break_at):
    plan, used = [], 0
    for slot in range(count):
        row, sources = 0, []
        for number, size in enumerate(sizes):
            if slot == count // 2 and number == break_at:
                used, row = used + 1, 0
            sources.append((used, row))
            row += size
        plan.append(tuple(sources))
        used += 1
    return plan


def project_kernel(slots, hat, cosine, sine, *rest):
    pieces, (wide, gain, first, query, key, value) = rest[:-6], rest[-6:]
    extent, local = key.shape
    rows = query.shape[0]
    width = hat.shape[1]
    pairs = local // LANES
    groups = slots.shape[0]
    depth = width // groups
    plan = piece_plan(groups, [depth] * 4 + [PAD], 2)
    lane = lax.broadcasted_iota(jnp.int32, (LANES, width), 1) - lax.broadcasted_iota(jnp.int32, (LANES, width), 0)
    gain_sum = jnp.zeros((PAD, width), f32)
    for number, sources in enumerate(plan):
        start = pl.multiple_of(slots[number] * depth, depth)
        for part, (piece, row) in enumerate(sources[:4]):
            lanes = slice(part * local, (part + 1) * local)
            wide[pl.ds(start, depth), lanes] = pieces[piece][row : row + depth, :]
        piece, row = sources[4]
        spread = jnp.where(lane == start, 1.0, 0.0).astype(bf16)
        gain_sum += dot(pieces[piece][row : row + PAD, :LANES], spread)
    gain[...] = gain_sum
    gains = gain_sum[:1]
    query_w, key_w, value_w = (wide.at[:, at * local : (at + 1) * local] for at in range(3))
    low = lax.broadcasted_iota(jnp.int32, (1, LANES), 1) % HEAD < HEAD // 2

    def rotated(src, at, size, dst, place, scale):
        co, si = cosine[pl.ds(at, size), :], sine[pl.ds(at, size), :]
        for pair in range(pairs):
            lanes = slice(pair * LANES, (pair + 1) * LANES)
            value = src[:, lanes]
            dst[pl.ds(place, size), lanes] = ((value * co + turned(value, low) * si) * scale).astype(bf16)

    chunk = step_of(extent, 384)

    def key_step(index):
        at = pl.multiple_of(index * chunk, chunk)
        here = pl.ds(at, chunk)
        part = (hat[here, :] * gains).astype(bf16)
        first[here, :] = part
        rotated(dot(part, key_w[...]), at, chunk, key, at, 1.0)
        value[here, :] = dot(part, value_w[...]).astype(bf16)

    loop(extent // chunk, key_step)
    size = step_of(rows, 256)

    def query_step(index):
        at = pl.multiple_of(index * size, size)
        start = pl.multiple_of(at + HALF, HALF)
        rotated(dot(first[pl.ds(start, size), :], query_w[...]), start, size, query, at, HEAD**-0.5)

    loop(rows // size, query_step)


def attend_kernel(chosen, last, bounds, query, key, value, *rest):
    if last:
        wide, done, shares, attended, branch = rest
        attended[...] = done[...]
    else:
        shares, attended = rest
    rows, local = query.shape
    count = len(chosen)
    key_at = lax.broadcasted_iota(jnp.int32, (KEYS, KEYS), 0)
    lane_at = lax.broadcasted_iota(jnp.int32, (1, KEYS), 1) % BLOCK

    def attend_step(index):
        at = pl.multiple_of(index * BLOCK, BLOCK)
        origin = bounds[NSEQ] + at - HALF
        own = lane_at + (origin + HALF)
        begin = jnp.zeros_like(own)
        end = jnp.zeros_like(own) + bounds[NSEQ - 1]
        for number in range(NSEQ - 1):
            begin = jnp.where(own >= bounds[number], bounds[number], begin)
        for number in reversed(range(NSEQ - 1)):
            end = jnp.where(own < bounds[number], bounds[number], end)
        least = jnp.maximum(lane_at, begin - origin)
        most = jnp.minimum(lane_at + WINDOW, end - 1 - origin)
        allowed = (key_at >= least) & (key_at <= most)
        for number, pair in enumerate(chosen):
            lanes = slice(pair * LANES, (pair + 1) * LANES)
            both = halves(query[pl.ds(at, BLOCK), lanes])
            scores = jnp.where(allowed, dot(key[pl.ds(at, KEYS), lanes], both, NT), -1e30)
            weight = jnp.exp(scores - jnp.max(scores, axis=0, keepdims=True))
            part = (weight * (1.0 / jnp.sum(weight, axis=0, keepdims=True))).astype(bf16)
            shares[index * count + number] = part
            mixed = dot(value[pl.ds(at, KEYS), lanes], part, TN)
            attended[pl.ds(at, BLOCK), lanes] = joined(mixed).astype(bf16)

    loop(rows // BLOCK, attend_step)
    if not last:
        return
    out_t = wide.at[:, 3 * local :]
    size = step_of(rows, 256)

    def out_step(index):
        here = pl.ds(pl.multiple_of(index * size, size), size)
        branch[here, :] = dot(attended[here, :], out_t[...], NT).astype(bf16)

    loop(rows // size, out_step)


def feed_kernel(slots, tokens, own, other, gain, cotangent, *rest):
    pieces, rest = rest[:-7], rest[-7:]
    middle, second, hidden, grad_gate, grad_upper, partial, whole = rest
    rows, width = tokens.shape
    groups = slots.shape[0]
    depth = width // groups
    for number, sources in enumerate(piece_plan(groups, [depth] * 3, 1)):
        place = pl.ds(pl.multiple_of(slots[number] * depth, depth), depth)
        for part, (piece, row) in enumerate(sources):
            whole[part, place, :] = pieces[piece][row : row + depth, :]
    gate_w, upper_w, down_t = (whole.at[number] for number in range(3))
    gains = gain[1:2, :]
    size = step_of(rows, 256)

    def step(index):
        here = pl.ds(pl.multiple_of(index * size, size), size)
        mid = tokens[here, :].astype(f32) + (own[here, :].astype(f32) + other[here, :].astype(f32))
        middle[here, :] = mid
        low = (normed(mid)[0] * gains).astype(bf16)
        second[here, :] = low
        gate = dot(low, gate_w[...])
        upper = dot(low, upper_w[...])
        grad = dot(cotangent[here, :], down_t[...])
        share = 0.5 * (1.0 + lax.erf(gate * (0.5**0.5)))
        smooth = gate * share
        slope = share + gate * (jnp.exp(gate * gate * -0.5) * ((2.0 * math.pi) ** -0.5))
        hidden[here, :] = (smooth * upper).astype(bf16)
        gate_low = (grad * upper * slope).astype(bf16)
        upper_low = (grad * smooth).astype(bf16)
        grad_gate[here, :] = gate_low
        grad_upper[here, :] = upper_low
        partial[here, :] = (dot(gate_low, gate_w[...], NT) + dot(upper_low, upper_w[...], NT)).astype(bf16)

    loop(rows // size, step)


def feed_out_kernel(hidden, whole, feed):
    rows = hidden.shape[0]
    size = step_of(rows, 256)

    def step(index):
        here = pl.ds(pl.multiple_of(index * size, size), size)
        feed[here, :] = dot(hidden[here, :], whole[2], NT).astype(bf16)

    loop(rows // size, step)


def weight_kernel(slots, second, hidden, grad_gate, grad_upper, cotangent, grads, total):
    rows, width = second.shape
    step_rows = step_of(width, 256)
    for number, (left, right) in enumerate(((second, grad_gate), (second, grad_upper), (cotangent, hidden))):
        for start in range(0, width, step_rows):
            here = slice(start, start + step_rows)
            total[number, here, :] = dot(left[:, here], right[...], TN).astype(bf16)
    depth = grads.shape[2]
    for number, slot in enumerate(hop_order(grads.shape[0])):
        grads[number] = total[:, pl.ds(pl.multiple_of(slots[slot] * depth, depth), depth), :]


def hop_order(count):
    middle = count // 2
    order = [middle]
    for hop in range(middle - 1, 0, -1):
        order += [hop, count - hop]
    return order + [0]


def middle_kernel(middle, own, other, gain, cotangent, wide, grad_middle, low_mid, grad_att):
    rows, width = middle.shape
    local = grad_att.shape[1]
    out_t = wide.at[:, 3 * local :]
    gains = gain[1:2, :]
    size = step_of(rows, 256)

    def norm_step(index):
        here = pl.ds(pl.multiple_of(index * size, size), size)
        hat, scale = normed(middle[here, :])
        grad = own[here, :].astype(f32) + other[here, :].astype(f32)
        mid = cotangent[here, :].astype(f32) + norm_back(grad, gains, hat, scale)
        grad_middle[here, :] = mid
        mid_low = mid.astype(bf16)
        low_mid[here, :] = mid_low
        grad_att[here, :] = dot(mid_low, out_t[...]).astype(bf16)

    loop(rows // size, norm_step)


def back_kernel(chosen, query, key, value, grad_att, cosine, sine, *rest):
    held, parts, (grad_key, grad_value) = rest[: len(chosen)], rest[len(chosen) : -2], rest[-2:]
    rows = query.shape[0]
    extent = key.shape[0]
    flat = [(part, number, len(group)) for part, group in zip(held, chosen) for number in range(len(group))]
    grad_key[...] = jnp.zeros_like(grad_key)
    grad_value[...] = jnp.zeros_like(grad_value)
    low = lax.broadcasted_iota(jnp.int32, (1, LANES), 1) % HEAD < HEAD // 2
    zero = jnp.zeros((HALF, LANES), bf16)
    for part in parts:
        part[:HALF, :LANES] = zero
        part[rows + HALF :, :LANES] = zero

    def attend_step(index):
        at = pl.multiple_of(index * BLOCK, BLOCK)
        start = pl.multiple_of(at + HALF, HALF)
        co, si = cosine[pl.ds(start, BLOCK), :], sine[pl.ds(start, BLOCK), :]
        for number, (shares, spot, count) in enumerate(flat):
            lanes = slice(number * LANES, (number + 1) * LANES)
            both = halves(query[pl.ds(at, BLOCK), lanes])
            grad = halves(grad_att[pl.ds(at, BLOCK), lanes])
            keys = key[pl.ds(at, KEYS), lanes]
            part = shares[index * count + spot]
            wide = part.astype(f32)
            grad_shares = dot(value[pl.ds(at, KEYS), lanes], grad, NT)
            delta = jnp.sum(wide * grad_shares, axis=0, keepdims=True)
            raw = (wide * (grad_shares - delta)).astype(bf16)
            grad_query = joined(dot(keys, raw, TN)) * HEAD**-0.5
            turn = (grad_query * co - turned(grad_query, low) * si).astype(bf16)
            parts[number][pl.ds(start, BLOCK), :LANES] = turn
            grad_key[pl.ds(at, KEYS), lanes] += dot(raw, both)
            grad_value[pl.ds(at, KEYS), lanes] += dot(part, grad)

    loop(rows // BLOCK, attend_step)

    def turn_step(index):
        here = pl.ds(pl.multiple_of(index * BLOCK, BLOCK), BLOCK)
        co, si = cosine[here, :], sine[here, :]
        for number, out in enumerate(parts):
            lanes = slice(number * LANES, (number + 1) * LANES)
            part = grad_key[here, lanes]
            out[here, LANES : 2 * LANES] = (part * co - turned(part, low) * si).astype(bf16)
            out[here, 2 * LANES :] = grad_value[here, lanes].astype(bf16)

    loop(extent // BLOCK, turn_step)


def grad_kernel_one(slots, first, *rest):
    parts, (grad_proj, grads, total) = rest[:-3], rest[-3:]
    local = len(parts) * LANES
    for pair, part in enumerate(parts):
        for number in range(3):
            lanes = slice(number * local + pair * LANES, number * local + (pair + 1) * LANES)
            grad_proj[:, lanes] = part[:, number * LANES : (number + 1) * LANES]
    weight_grads([(first, grad_proj.at[:, at * local : (at + 1) * local]) for at in range(2)], slots, grads, total)


def grad_kernel_two(slots, first, grad_proj, low_mid, attended, grads, total):
    local = attended.shape[1]
    weight_grads([(first, grad_proj.at[:, 2 * local :]), (low_mid, attended)], slots, grads, total)


def weight_grads(sides, slots, grads, total):
    width = total.shape[1]
    depth = grads.shape[2]
    step_rows = step_of(width, 256)
    for number, (left, right) in enumerate(sides):
        for start in range(0, width, step_rows):
            here = slice(start, start + step_rows)
            total[number, here, :] = dot(left[:, here], right[...], TN).astype(bf16)
    for number, slot in enumerate(hop_order(grads.shape[0])):
        grads[number] = total[:, pl.ds(pl.multiple_of(slots[slot] * depth, depth), depth), :]


def first_kernel(grad_proj, wide, partial, edges):
    rows = partial.shape[0]
    for side, start in enumerate((0, rows + HALF)):
        outer = grad_proj[start : start + HALF, :]
        edges[side] = dot(outer, wide[:, : outer.shape[1]], NT).astype(bf16)
    inner = grad_proj.shape[1]
    size = step_of(rows, 256)

    def step(index):
        at = pl.multiple_of(index * size, size)
        wider = pl.ds(pl.multiple_of(at + HALF, HALF), size)
        partial[pl.ds(at, size), :] = dot(grad_proj[wider, :], wide[:, :inner], NT).astype(bf16)

    loop(rows // size, step)


def token_kernel(tokens, gain, grad_middle, own, other, one, two, token_grad):
    rows, width = tokens.shape
    gains = gain[:1, :]
    size = BLOCK

    def back(here, grad):
        hat, scale = normed(tokens[here, :].astype(f32))
        return norm_back(grad, gains, hat, scale)

    def step(index):
        here = pl.ds(pl.multiple_of(index * size, size), size)
        grad = own[here, :].astype(f32) + other[here, :].astype(f32)
        token_grad[here, :] = grad_middle[here, :] + back(here, grad)

    loop(rows // size, step)
    for side, start in enumerate((0, rows - HALF)):
        here = pl.ds(start, HALF)
        token_grad[here, :] += back(here, one[side].astype(f32) + two[side].astype(f32))


def mixed_kernel(middle, own, other, mixed):
    rows = middle.shape[0]

    def step(index):
        here = pl.ds(pl.multiple_of(index * BLOCK, BLOCK), BLOCK)
        mixed[here, :] = (middle[here, :] + (own[here, :].astype(f32) + other[here, :].astype(f32))).astype(bf16)

    loop(rows // BLOCK, step)


def traded(edges, cross):
    devices, cores = lax.axis_size("ctx"), lax.axis_size("tensor")
    spot = lax.axis_index("ctx")

    def pairs(by, start, stop):
        return [(i * cores + c, (i + by) * cores + (c + cross) % cores) for i in range(start, stop) for c in range(cores)]

    axes = ("ctx", "tensor")
    if devices == 2:
        got = lax.ppermute(jnp.where(spot == 0, edges[1], edges[0]), axes, pairs(1, 0, 1) + pairs(-1, 1, 2))
        none = jnp.zeros_like(got)
        return jnp.stack([jnp.where(spot == 1, got, none), jnp.where(spot == 0, got, none)])
    return jnp.stack(
        [
            lax.ppermute(edges[1], axes, pairs(1, 0, devices - 1)),
            lax.ppermute(edges[0], axes, pairs(-1, 1, devices)),
        ]
    )


def exchange(initial, last):
    devices, spot = lax.axis_size("ctx"), lax.axis_index("ctx")
    if devices == 2:
        got = lax.ppermute(jnp.where(spot == 0, last, initial), "ctx", [(0, 1), (1, 0)])
        none = jnp.zeros_like(got)
        return jnp.where(spot == 1, got, none), jnp.where(spot == 0, got, none)
    up = [(i, i + 1) for i in range(devices - 1)]
    return lax.ppermute(last, "ctx", up), lax.ppermute(initial, "ctx", [(j, i) for i, j in up])


def over_ctx(array):
    if lax.axis_size("ctx") == 2:
        return array.astype(f32) + swap(array, "ctx").astype(f32)
    return lax.psum(array, "ctx").astype(f32)


def swap(array, axis="tensor"):
    return lax.ppermute(array, axis, [(0, 1), (1, 0)])


def ring():
    count = lax.axis_size("dp")
    order = [2 * i for i in range(count // 2)] + [2 * i + 1 for i in reversed(range(count // 2))]
    ahead = [(order[i], order[(i + 1) % count]) for i in range(count)]
    back = [(j, i) for i, j in ahead]
    places = {group: at for at, group in enumerate(order)}
    table = np.array([[order[(places[i] + j) % count] for j in range(count)] for i in range(count)], np.int32)
    slots = lax.dynamic_index_in_dim(jnp.asarray(table), lax.axis_index("dp"), keepdims=False)
    return count, ahead, back, slots


def tied(values, others):
    held = lax.optimization_barrier((tuple(values), tuple(others)))
    return held[0]


def locked(values, chain):
    held = lax.optimization_barrier((tuple(values), tuple(chain.state)))
    chain.state = held[1]
    return held[0]


def alternate(first, second):
    if len(second.past) > 1:
        first.after(second.past[-2])
    first.hop()
    if len(first.past) > 1:
        second.after(first.past[-2])
    second.hop()


class RingGather:
    def __init__(self, block, cut=0, way=None):
        self.count, self.ahead, self.back, _ = ring()
        self.cut = cut
        self.way = way
        self.pieces = {0: (block,)}
        self.state = (block, block)
        self.hops = 0
        self.past = []

    def hop(self):
        one, two = self.state
        middle = self.count // 2
        if self.hops + 1 == middle and self.way is not None:
            got = lax.ppermute((one, two)[self.way], "dp", (self.ahead, self.back)[self.way])
            self.hops += 1
            self.state = (got,)
            self.past.append(self.state)
            self.pieces[middle] = (got,)
            return
        if self.hops + 1 == middle:
            one, two = one[: self.cut], two[self.cut :]
        one, two = lax.ppermute(one, "dp", self.ahead), lax.ppermute(two, "dp", self.back)
        self.hops += 1
        one, two = lax.optimization_barrier((one, two))
        self.state = (one, two)
        self.past.append(self.state)
        if self.hops == middle:
            self.pieces[middle] = (one, two)
        else:
            self.pieces[self.count - self.hops], self.pieces[self.hops] = (one,), (two,)

    def after(self, others):
        self.state = tied(self.state, others)


class RingScatter:
    def __init__(self, parts, axis=0, way=None):
        self.count, self.ahead, self.back, _ = ring()
        self.parts = parts
        self.axis = axis
        self.way = way
        self.hops = 0
        self.state = ()
        self.past = []

    def part(self, at):
        total = self.parts[0][at]
        for part in self.parts[1:]:
            total = total + part[at]
        return total

    def hop(self):
        if self.hops == 0 and self.way is not None:
            got = lax.ppermute(self.part(0), "dp", (self.ahead, self.back)[self.way])
            self.state = (got,)
            self.past.append(self.state)
            self.hops += 1
            return
        if self.hops == 0:
            one, two = jnp.split(self.part(0), 2, axis=self.axis)
        else:
            sides = [self.part(2 * self.hops - 1), self.part(2 * self.hops)]
            if self.hops == 1 and self.way is not None:
                sides[self.way] = sides[self.way] + self.state[0]
            one, two = sides if self.hops == 1 and self.way is not None else self.state
            if self.hops == 1 and self.way is None:
                none = jnp.zeros_like(one)
                one = jnp.concatenate([one, none], axis=self.axis)
                two = jnp.concatenate([none, two], axis=self.axis)
            if self.hops > 1 or self.way is None:
                one, two = sides[0] + one, sides[1] + two
        one, two = lax.ppermute(one, "dp", self.ahead), lax.ppermute(two, "dp", self.back)
        self.state = lax.optimization_barrier((one, two))
        self.past.append(self.state)
        self.hops += 1

    def after(self, others):
        self.state = tied(self.state, others)

    def total(self):
        one, two = self.state
        return (self.part(self.count - 1).astype(f32) + one.astype(f32) + two.astype(f32)).astype(bf16)


def tables(lengths, rows):
    place = lax.axis_index("ctx") * rows
    spots = jnp.arange(NSEQ, dtype=jnp.int32)
    ends = jnp.sum(jnp.where(spots[None, :] <= spots[:, None], lengths[0][None, :], 0), axis=1)
    starts = ends - lengths[0]
    span = place + jnp.arange(-HALF, rows + HALF, dtype=jnp.int32)
    inside = (span[:, None] >= starts[None, :]) & (span[:, None] < ends[None, :])
    position = span - jnp.sum(jnp.where(inside, starts[None, :], 0), axis=1)
    lane = jnp.arange(LANES, dtype=jnp.int32)
    number = (lane % (HEAD // 2)).astype(f32)
    freq = jnp.exp(number * (-2.0 * math.log(10000.0) / HEAD))
    angle = position.astype(f32)[:, None] * freq[None, :]
    sine = jnp.sin(angle)
    sine = jnp.where((lane % HEAD < HEAD // 2)[None, :], -sine, sine)
    bounds = jnp.concatenate([ends, place[None]]).astype(jnp.int32)
    return jnp.cos(angle), sine, bounds


def body(tokens, lengths, gain_one, w_qkv, w_out, gain_two, w_in, w_down, cotangent):
    rows, width = tokens.shape
    local, units = w_out.shape[0], w_down.shape[0]
    pairs, blocks, extent = local // LANES, rows // BLOCK, rows + WINDOW
    groups = lax.axis_size("dp")
    depth = width // groups
    middle_hop = groups // 2
    gains = jnp.pad(jnp.stack([gain_one, gain_two]), ((0, PAD - 2), (0, local - depth)))
    middle_hop = groups // 2
    now = RingGather(jnp.concatenate([w_qkv.reshape(3 * depth, local), w_out.T, gains]), 2 * depth)
    now.hop()
    before, after = exchange(tokens[:HALF], tokens[rows - HALF :])
    slots = ring()[-1]
    cosine, sine, bounds = tables(lengths, rows)
    now.hop()
    now.after([cosine, sine, bounds, slots, before, after])
    hat, = call(
        norm_kernel, [shape((extent, width), f32)], (tokens, before, after), rows * width * 2000, "first_norm"
    )
    while now.hops < middle_hop:
        if now.hops + 1 == middle_hop:
            now.after([hat])
        now.hop()
    mine_two = jnp.concatenate([w_in.reshape(2 * depth, units), w_down.T])
    later = RingGather(tied([mine_two], now.state)[0], depth)
    later.hop()
    pieces = [piece for slot in range(groups) for piece in now.pieces[slot]]
    wide, gain, first, query, key, value = call(
        project_kernel,
        [
            shape((width, 4 * local), bf16),
            shape((PAD, width), f32),
            shape((extent, width), bf16),
            shape((rows, local), bf16),
            shape((extent, local), bf16),
            shape((extent, local), bf16),
        ],
        (hat, cosine, sine, *pieces),
        2 * rows * width * local * 8,
        "project",
        (slots,),
    )
    early, late = tuple(range(pairs - 1)), (pairs - 1,)

    query, key, value = locked([query, key, value], later)
    later.hop()
    shares_early, attended = call(
        functools.partial(attend_kernel, early, False),
        [shape((blocks * len(early), KEYS, KEYS), bf16), shape((rows, local), bf16)],
        (query, key, value),
        2 * rows * width * local * 10,
        "attend",
        (bounds,),
    )
    attended, = locked([attended], later)
    later.hop()
    shares_late, attended, branch = call(
        functools.partial(attend_kernel, late, True),
        [
            shape((blocks * len(late), KEYS, KEYS), bf16),
            shape((rows, local), bf16),
            shape((rows, width), bf16),
        ],
        (query, key, value, wide, attended),
        2 * rows * width * local * 7,
        "attend",
        (bounds,),
    )
    branch, = locked([branch], later)
    branch_other = swap(branch)
    while later.hops < middle_hop:
        later.hop()
    pieces = [piece for slot in range(groups) for piece in later.pieces[slot]]
    middle, second, hidden, grad_gate, grad_upper, partial, whole = call(
        feed_kernel,
        [
            shape((rows, width), f32),
            shape((rows, width), bf16),
            shape((rows, units), bf16),
            shape((rows, units), bf16),
            shape((rows, units), bf16),
            shape((rows, width), bf16),
            shape((3, width, units), bf16),
        ],
        (tokens, branch, branch_other, gain, cotangent, *pieces),
        2 * rows * width * units * 8,
        "feed_forward_and_back",
        (slots,),
    )
    partial_other = swap(partial)
    grads_two, = call(
        weight_kernel,
        [shape((groups, 3, depth, units), bf16)],
        (second, hidden, grad_gate, grad_upper, cotangent),
        2 * rows * width * units * 5,
        "feed_weight_grads",
        (slots,),
        [pltpu.VMEM((3, width, units), bf16)],
    )
    grads_two, = tied([grads_two], [partial_other])
    sums_two = RingScatter([grads_two], 1)
    sums_two.hop()
    grad_middle, low_mid, grad_att = call(
        middle_kernel,
        [shape((rows, width), f32), shape((rows, width), bf16), shape((rows, local), bf16)],
        (middle, partial, partial_other, gain, cotangent, wide),
        2 * rows * width * local * 4,
        "middle_grad",
    )
    feed, = call(
        feed_out_kernel,
        [shape((rows, width), bf16)],
        (tied([hidden], [grads_two])[0], whole),
        2 * rows * width * units,
        "feed_out",
    )
    grad_att, feed = locked([grad_att, feed], sums_two)
    feed_other = swap(feed)
    sums_two.hop()
    grad_parts = call(
        functools.partial(back_kernel, (early, late)),
        [shape((extent, 3 * LANES), bf16)] * pairs,
        (query, key, value, grad_att, cosine, sine, shares_early, shares_late),
        2 * rows * width * local * 15,
        "attention_back",
        (),
        [pltpu.VMEM((extent, local), f32)] * 2,
    )
    grad_parts = locked(grad_parts, sums_two)
    sums_two.hop()
    grad_proj, grads_a = call(
        grad_kernel_one,
        [
            shape((extent, 3 * local), bf16),
            shape((groups, 2, depth, local), bf16),
        ],
        (first, *grad_parts),
        2 * rows * width * local * 3,
        "query_key_grads",
        (slots,),
        [pltpu.VMEM((2, width, local), bf16)],
    )
    first_part, edges = call(
        first_kernel,
        [shape((rows, width), bf16), shape((2, HALF, width), bf16)],
        (grad_proj, wide),
        2 * rows * width * local * 3,
        "first_grad",
    )
    grads_b, = call(
        grad_kernel_two,
        [shape((groups, 2, depth, local), bf16)],
        (first, grad_proj, low_mid, attended),
        2 * rows * width * local * 3,
        "value_out_grads",
        (slots,),
        [pltpu.VMEM((2, width, local), bf16)],
    )
    *grads_one, first_part, edges = locked([grads_a, grads_b, first_part, edges], sums_two)
    first_other = swap(first_part)
    sums_one = [RingScatter([part], way=way) for way, part in enumerate(grads_one)]
    alternate(*sums_one)
    sums_two.after(sums_one[0].state)
    while sums_two.hops < middle_hop:
        sums_two.hop()

    while sums_one[0].hops < middle_hop - 2:
        alternate(*sums_one)
    edges, = tied([edges], sums_one[0].past[0])
    same, cross = traded(edges, 0), traded(edges, 1)
    sums_one[1].after([*sums_two.state, same, cross])
    alternate(*sums_one)
    alternate(*sums_one)
    tokens, middle = tied([tokens, middle], sums_one[1].past[-2])
    token_grad, = call(
        token_kernel,
        [shape((rows, width), f32)],
        (tokens, gain, grad_middle, first_part, first_other, same, cross),
        rows * width * 200,
        "token_grad",
    )
    mixed, = call(
        mixed_kernel,
        [shape((rows, width), bf16)],
        (middle, feed, feed_other),
        rows * width * 100,
        "mixed",
    )
    one = [chain.total() for chain in sums_one]
    two = sums_two.total()
    if lax.axis_size("ctx") == 2:
        got_two, = tied([swap(two, "ctx")], [one[1]])
        mixed, token_grad, *got = lax.optimization_barrier((mixed, token_grad, *[swap(part, "ctx") for part in one]))
        one = [part.astype(f32) + more.astype(f32) for part, more in zip(one, got)]
        two = two.astype(f32) + got_two.astype(f32)
    else:
        one = [lax.psum(part, "ctx").astype(f32) for part in one]
        two = lax.psum(two, "ctx").astype(f32)
    one = jnp.concatenate(one)
    gain_one_grad = jnp.sum(one[:3] * w_qkv.astype(f32), axis=(0, 2)) / gain_one.astype(f32)
    gain_two_grad = jnp.sum(two[:2] * w_in.astype(f32), axis=(0, 2)) / gain_two.astype(f32)
    both = jnp.stack([gain_one_grad, gain_two_grad])
    both = both + swap(both)
    return (mixed, token_grad, both[0], one[:3], one[3].T, both[1], two[:2], two[2].T)


def solution(mesh):
    in_specs = (
        P(("dp", "ctx"), None),
        P("dp", None),
        P("dp"),
        P(None, "dp", "tensor"),
        P("tensor", "dp"),
        P("dp"),
        P(None, "dp", "tensor"),
        P("tensor", "dp"),
        P(("dp", "ctx"), None),
    )
    out_specs = (
        P(("dp", "ctx"), None),
        P(("dp", "ctx"), None),
        P("dp"),
        P(None, "dp", "tensor"),
        P("tensor", "dp"),
        P("dp"),
        P(None, "dp", "tensor"),
        P("tensor", "dp"),
    )
    return jax.shard_map(body, mesh=mesh, in_specs=in_specs, out_specs=out_specs, check_vma=False)
```

```python
import functools
import math

import jax
import jax.numpy as jnp
import numpy as np
from jax import lax
from jax.experimental import pallas as pl
from jax.experimental.pallas import tpu as pltpu
from jax.sharding import PartitionSpec as P

HEAD = 64
WINDOW = 128
NSEQ = 4
HALF = WINDOW // 2
PAD = 16
SPARE = 6
SHARE = 8
BLOCK = 128
LANES = 128
KEYS = BLOCK + WINDOW

norm_eps = 1e-05
f32 = jnp.float32
bf16 = jnp.bfloat16

NN = (((1,), (0,)), ((), ()))
NT = (((1,), (1,)), ((), ()))
TN = (((0,), (0,)), ((), ()))


def dot(a, b, dims=NN):
    return lax.dot_general(a, b, dims, preferred_element_type=f32)


def step_of(rows, most):
    best = LANES
    for size in range(LANES, most + 1, LANES):
        if rows % size == 0:
            best = size
    return best


def call(kernel, out_shape, args, flops, name, scalars=(), scratch=()):
    vmem = pl.BlockSpec(memory_space=pltpu.VMEM)
    smem = pl.BlockSpec(memory_space=pltpu.SMEM)
    moved = sum(x.size * x.dtype.itemsize for x in (*args, *out_shape))
    held = sum(math.prod(x.shape) * jnp.dtype(x.dtype).itemsize for x in scratch if x.dtype in (f32, bf16))
    limit = held + SPARE * 2**20
    return pl.pallas_call(
        kernel,
        out_shape=out_shape,
        in_specs=[smem] * len(scalars) + [vmem] * len(args),
        out_specs=[vmem] * len(out_shape),
        scratch_shapes=scratch,
        compiler_params=pltpu.CompilerParams(vmem_limit_bytes=limit),
        cost_estimate=pl.CostEstimate(flops=flops // SHARE, bytes_accessed=moved // SHARE, transcendentals=0),
        name=name,
    )(*scalars, *args)


def shape(dims, dtype):
    return jax.ShapeDtypeStruct(dims, dtype)


def normed(values):
    centered = values - jnp.mean(values, axis=-1, keepdims=True)
    spread = jnp.mean(centered * centered, axis=-1, keepdims=True)
    scale = lax.rsqrt(spread + norm_eps)
    return centered * scale, scale


def norm_back(grad, gain, hat, scale):
    inner = grad * gain
    one = jnp.mean(inner, axis=-1, keepdims=True)
    two = jnp.mean(inner * hat, axis=-1, keepdims=True)
    return scale * (inner - one - hat * two)


def turned(values, low):
    return jnp.where(low, pltpu.roll(values, LANES - HEAD // 2, 1), pltpu.roll(values, HEAD // 2, 1))


def halves(values):
    even = (lax.broadcasted_iota(jnp.int32, (1, LANES), 1) < HEAD).astype(f32).astype(bf16)
    return jnp.concatenate([values * even, values * (1 - even)], axis=0)


def joined(values):
    return jnp.concatenate([values[:HEAD, :BLOCK], values[HEAD:, BLOCK:]], axis=0).T


def loop(count, body):
    def run(index, carry):
        body(index)
        return carry

    lax.fori_loop(0, count, run, 0)


def norm_kernel(tokens, before, after, hat):
    rows, width = tokens.shape

    def norm_rows(src, dst, size):
        hat[pl.ds(dst, size), :] = normed(src.astype(f32))[0]

    norm_rows(before[...], 0, HALF)
    norm_rows(after[...], rows + HALF, HALF)

    def norm_step(index):
        at = pl.multiple_of(index * BLOCK, BLOCK)
        norm_rows(tokens[pl.ds(at, BLOCK), :], pl.multiple_of(at + HALF, HALF), BLOCK)

    loop(rows // BLOCK, norm_step)


def piece_plan(count, sizes, break_at):
    plan, used = [], 0
    for slot in range(count):
        row, sources = 0, []
        for number, size in enumerate(sizes):
            if slot == count // 2 and number == break_at:
                used, row = used + 1, 0
            sources.append((used, row))
            row += size
        plan.append(tuple(sources))
        used += 1
    return plan


def project_kernel(slots, hat, cosine, sine, *rest):
    pieces, (wide, gain, first, query, key, value) = rest[:-6], rest[-6:]
    extent, local = key.shape
    rows = query.shape[0]
    width = hat.shape[1]
    pairs = local // LANES
    groups = slots.shape[0]
    depth = width // groups
    plan = piece_plan(groups, [depth] * 4 + [PAD], 2)
    lane = lax.broadcasted_iota(jnp.int32, (LANES, width), 1) - lax.broadcasted_iota(jnp.int32, (LANES, width), 0)
    gain_sum = jnp.zeros((PAD, width), f32)
    for number, sources in enumerate(plan):
        start = pl.multiple_of(slots[number] * depth, depth)
        for part, (piece, row) in enumerate(sources[:4]):
            lanes = slice(part * local, (part + 1) * local)
            wide[pl.ds(start, depth), lanes] = pieces[piece][row : row + depth, :]
        piece, row = sources[4]
        spread = jnp.where(lane == start, 1.0, 0.0).astype(bf16)
        gain_sum += dot(pieces[piece][row : row + PAD, :LANES], spread)
    gain[...] = gain_sum
    gains = gain_sum[:1]
    query_w, key_w, value_w = (wide.at[:, at * local : (at + 1) * local] for at in range(3))
    low = lax.broadcasted_iota(jnp.int32, (1, LANES), 1) % HEAD < HEAD // 2

    def rotated(src, at, size, dst, place, scale):
        co, si = cosine[pl.ds(at, size), :], sine[pl.ds(at, size), :]
        for pair in range(pairs):
            lanes = slice(pair * LANES, (pair + 1) * LANES)
            value = src[:, lanes]
            dst[pl.ds(place, size), lanes] = ((value * co + turned(value, low) * si) * scale).astype(bf16)

    chunk = step_of(extent, 384)

    def key_step(index):
        at = pl.multiple_of(index * chunk, chunk)
        here = pl.ds(at, chunk)
        part = (hat[here, :] * gains).astype(bf16)
        first[here, :] = part
        rotated(dot(part, key_w[...]), at, chunk, key, at, 1.0)
        value[here, :] = dot(part, value_w[...]).astype(bf16)

    loop(extent // chunk, key_step)
    size = step_of(rows, 256)

    def query_step(index):
        at = pl.multiple_of(index * size, size)
        start = pl.multiple_of(at + HALF, HALF)
        rotated(dot(first[pl.ds(start, size), :], query_w[...]), start, size, query, at, HEAD**-0.5)

    loop(rows // size, query_step)


def attend_kernel(chosen, last, bounds, query, key, value, *rest):
    if last:
        wide, done, shares, attended, branch = rest
        attended[...] = done[...]
    else:
        shares, attended = rest
    rows, local = query.shape
    count = len(chosen)
    key_at = lax.broadcasted_iota(jnp.int32, (KEYS, KEYS), 0)
    lane_at = lax.broadcasted_iota(jnp.int32, (1, KEYS), 1) % BLOCK

    def attend_step(index):
        at = pl.multiple_of(index * BLOCK, BLOCK)
        origin = bounds[NSEQ] + at - HALF
        own = lane_at + (origin + HALF)
        begin = jnp.zeros_like(own)
        end = jnp.zeros_like(own) + bounds[NSEQ - 1]
        for number in range(NSEQ - 1):
            begin = jnp.where(own >= bounds[number], bounds[number], begin)
        for number in reversed(range(NSEQ - 1)):
            end = jnp.where(own < bounds[number], bounds[number], end)
        least = jnp.maximum(lane_at, begin - origin)
        most = jnp.minimum(lane_at + WINDOW, end - 1 - origin)
        allowed = (key_at >= least) & (key_at <= most)
        for number, pair in enumerate(chosen):
            lanes = slice(pair * LANES, (pair + 1) * LANES)
            both = halves(query[pl.ds(at, BLOCK), lanes])
            scores = jnp.where(allowed, dot(key[pl.ds(at, KEYS), lanes], both, NT), -1e30)
            weight = jnp.exp(scores - jnp.max(scores, axis=0, keepdims=True))
            part = (weight * (1.0 / jnp.sum(weight, axis=0, keepdims=True))).astype(bf16)
            shares[index * count + number] = part
            mixed = dot(value[pl.ds(at, KEYS), lanes], part, TN)
            attended[pl.ds(at, BLOCK), lanes] = joined(mixed).astype(bf16)

    loop(rows // BLOCK, attend_step)
    if not last:
        return
    out_t = wide.at[:, 3 * local :]
    size = step_of(rows, 256)

    def out_step(index):
        here = pl.ds(pl.multiple_of(index * size, size), size)
        branch[here, :] = dot(attended[here, :], out_t[...], NT).astype(bf16)

    loop(rows // size, out_step)


def feed_kernel(slots, tokens, own, other, gain, cotangent, *rest):
    pieces, rest = rest[:-7], rest[-7:]
    middle, second, hidden, grad_gate, grad_upper, partial, whole = rest
    rows, width = tokens.shape
    groups = slots.shape[0]
    depth = width // groups
    for number, sources in enumerate(piece_plan(groups, [depth] * 3, 1)):
        place = pl.ds(pl.multiple_of(slots[number] * depth, depth), depth)
        for part, (piece, row) in enumerate(sources):
            whole[part, place, :] = pieces[piece][row : row + depth, :]
    gate_w, upper_w, down_t = (whole.at[number] for number in range(3))
    gains = gain[1:2, :]
    size = step_of(rows, 256)

    def step(index):
        here = pl.ds(pl.multiple_of(index * size, size), size)
        mid = tokens[here, :].astype(f32) + (own[here, :].astype(f32) + other[here, :].astype(f32))
        middle[here, :] = mid
        low = (normed(mid)[0] * gains).astype(bf16)
        second[here, :] = low
        gate = dot(low, gate_w[...])
        upper = dot(low, upper_w[...])
        grad = dot(cotangent[here, :], down_t[...])
        share = 0.5 * (1.0 + lax.erf(gate * (0.5**0.5)))
        smooth = gate * share
        slope = share + gate * (jnp.exp(gate * gate * -0.5) * ((2.0 * math.pi) ** -0.5))
        hidden[here, :] = (smooth * upper).astype(bf16)
        gate_low = (grad * upper * slope).astype(bf16)
        upper_low = (grad * smooth).astype(bf16)
        grad_gate[here, :] = gate_low
        grad_upper[here, :] = upper_low
        partial[here, :] = (dot(gate_low, gate_w[...], NT) + dot(upper_low, upper_w[...], NT)).astype(bf16)

    loop(rows // size, step)


def feed_out_kernel(hidden, whole, feed):
    rows = hidden.shape[0]
    size = step_of(rows, 256)

    def step(index):
        here = pl.ds(pl.multiple_of(index * size, size), size)
        feed[here, :] = dot(hidden[here, :], whole[2], NT).astype(bf16)

    loop(rows // size, step)


def weight_kernel(slots, second, hidden, grad_gate, grad_upper, cotangent, grads, total):
    rows, width = second.shape
    step_rows = step_of(width, 256)
    for number, (left, right) in enumerate(((second, grad_gate), (second, grad_upper), (cotangent, hidden))):
        for start in range(0, width, step_rows):
            here = slice(start, start + step_rows)
            total[number, here, :] = dot(left[:, here], right[...], TN).astype(bf16)
    depth = grads.shape[2]
    for number, slot in enumerate(hop_order(grads.shape[0])):
        grads[number] = total[:, pl.ds(pl.multiple_of(slots[slot] * depth, depth), depth), :]


def hop_order(count):
    middle = count // 2
    order = [middle]
    for hop in range(middle - 1, 0, -1):
        order += [hop, count - hop]
    return order + [0]


def middle_kernel(middle, own, other, gain, cotangent, wide, grad_middle, low_mid, grad_att):
    rows, width = middle.shape
    local = grad_att.shape[1]
    out_t = wide.at[:, 3 * local :]
    gains = gain[1:2, :]
    size = step_of(rows, 256)

    def norm_step(index):
        here = pl.ds(pl.multiple_of(index * size, size), size)
        hat, scale = normed(middle[here, :])
        grad = own[here, :].astype(f32) + other[here, :].astype(f32)
        mid = cotangent[here, :].astype(f32) + norm_back(grad, gains, hat, scale)
        grad_middle[here, :] = mid
        mid_low = mid.astype(bf16)
        low_mid[here, :] = mid_low
        grad_att[here, :] = dot(mid_low, out_t[...]).astype(bf16)

    loop(rows // size, norm_step)


def back_kernel(chosen, query, key, value, grad_att, cosine, sine, *rest):
    held, parts, (grad_key, grad_value) = rest[: len(chosen)], rest[len(chosen) : -2], rest[-2:]
    rows = query.shape[0]
    extent = key.shape[0]
    flat = [(part, number, len(group)) for part, group in zip(held, chosen) for number in range(len(group))]
    grad_key[...] = jnp.zeros_like(grad_key)
    grad_value[...] = jnp.zeros_like(grad_value)
    low = lax.broadcasted_iota(jnp.int32, (1, LANES), 1) % HEAD < HEAD // 2
    zero = jnp.zeros((HALF, LANES), bf16)
    for part in parts:
        part[:HALF, :LANES] = zero
        part[rows + HALF :, :LANES] = zero

    def attend_step(index):
        at = pl.multiple_of(index * BLOCK, BLOCK)
        start = pl.multiple_of(at + HALF, HALF)
        co, si = cosine[pl.ds(start, BLOCK), :], sine[pl.ds(start, BLOCK), :]
        for number, (shares, spot, count) in enumerate(flat):
            lanes = slice(number * LANES, (number + 1) * LANES)
            both = halves(query[pl.ds(at, BLOCK), lanes])
            grad = halves(grad_att[pl.ds(at, BLOCK), lanes])
            keys = key[pl.ds(at, KEYS), lanes]
            part = shares[index * count + spot]
            wide = part.astype(f32)
            grad_shares = dot(value[pl.ds(at, KEYS), lanes], grad, NT)
            delta = jnp.sum(wide * grad_shares, axis=0, keepdims=True)
            raw = (wide * (grad_shares - delta)).astype(bf16)
            grad_query = joined(dot(keys, raw, TN)) * HEAD**-0.5
            turn = (grad_query * co - turned(grad_query, low) * si).astype(bf16)
            parts[number][pl.ds(start, BLOCK), :LANES] = turn
            grad_key[pl.ds(at, KEYS), lanes] += dot(raw, both)
            grad_value[pl.ds(at, KEYS), lanes] += dot(part, grad)

    loop(rows // BLOCK, attend_step)

    def turn_step(index):
        here = pl.ds(pl.multiple_of(index * BLOCK, BLOCK), BLOCK)
        co, si = cosine[here, :], sine[here, :]
        for number, out in enumerate(parts):
            lanes = slice(number * LANES, (number + 1) * LANES)
            part = grad_key[here, lanes]
            out[here, LANES : 2 * LANES] = (part * co - turned(part, low) * si).astype(bf16)
            out[here, 2 * LANES :] = grad_value[here, lanes].astype(bf16)

    loop(extent // BLOCK, turn_step)


def grad_kernel_one(slots, first, *rest):
    parts, (grad_proj, grads, total) = rest[:-3], rest[-3:]
    local = len(parts) * LANES
    for pair, part in enumerate(parts):
        for number in range(3):
            lanes = slice(number * local + pair * LANES, number * local + (pair + 1) * LANES)
            grad_proj[:, lanes] = part[:, number * LANES : (number + 1) * LANES]
    weight_grads([(first, grad_proj.at[:, at * local : (at + 1) * local]) for at in range(2)], slots, grads, total)


def grad_kernel_two(slots, first, grad_proj, low_mid, attended, grads, total):
    local = attended.shape[1]
    weight_grads([(first, grad_proj.at[:, 2 * local :]), (low_mid, attended)], slots, grads, total)


def weight_grads(sides, slots, grads, total):
    width = total.shape[1]
    depth = grads.shape[2]
    step_rows = step_of(width, 256)
    for number, (left, right) in enumerate(sides):
        for start in range(0, width, step_rows):
            here = slice(start, start + step_rows)
            total[number, here, :] = dot(left[:, here], right[...], TN).astype(bf16)
    for number, slot in enumerate(hop_order(grads.shape[0])):
        grads[number] = total[:, pl.ds(pl.multiple_of(slots[slot] * depth, depth), depth), :]


def first_kernel(grad_proj, wide, partial, edges):
    rows = partial.shape[0]
    for side, start in enumerate((0, rows + HALF)):
        outer = grad_proj[start : start + HALF, :]
        edges[side] = dot(outer, wide[:, : outer.shape[1]], NT).astype(bf16)
    inner = grad_proj.shape[1]
    size = step_of(rows, 256)

    def step(index):
        at = pl.multiple_of(index * size, size)
        wider = pl.ds(pl.multiple_of(at + HALF, HALF), size)
        partial[pl.ds(at, size), :] = dot(grad_proj[wider, :], wide[:, :inner], NT).astype(bf16)

    loop(rows // size, step)


def token_kernel(tokens, gain, grad_middle, own, other, one, two, token_grad):
    rows, width = tokens.shape
    gains = gain[:1, :]
    size = BLOCK

    def back(here, grad):
        hat, scale = normed(tokens[here, :].astype(f32))
        return norm_back(grad, gains, hat, scale)

    def step(index):
        here = pl.ds(pl.multiple_of(index * size, size), size)
        grad = own[here, :].astype(f32) + other[here, :].astype(f32)
        token_grad[here, :] = grad_middle[here, :] + back(here, grad)

    loop(rows // size, step)
    for side, start in enumerate((0, rows - HALF)):
        here = pl.ds(start, HALF)
        token_grad[here, :] += back(here, one[side].astype(f32) + two[side].astype(f32))


def mixed_kernel(middle, own, other, mixed):
    rows = middle.shape[0]

    def step(index):
        here = pl.ds(pl.multiple_of(index * BLOCK, BLOCK), BLOCK)
        mixed[here, :] = (middle[here, :] + (own[here, :].astype(f32) + other[here, :].astype(f32))).astype(bf16)

    loop(rows // BLOCK, step)


def traded(edges, cross):
    devices, cores = lax.axis_size("ctx"), lax.axis_size("tensor")
    spot = lax.axis_index("ctx")

    def pairs(by, start, stop):
        return [(i * cores + c, (i + by) * cores + (c + cross) % cores) for i in range(start, stop) for c in range(cores)]

    axes = ("ctx", "tensor")
    if devices == 2:
        got = lax.ppermute(jnp.where(spot == 0, edges[1], edges[0]), axes, pairs(1, 0, 1) + pairs(-1, 1, 2))
        none = jnp.zeros_like(got)
        return jnp.stack([jnp.where(spot == 1, got, none), jnp.where(spot == 0, got, none)])
    return jnp.stack(
        [
            lax.ppermute(edges[1], axes, pairs(1, 0, devices - 1)),
            lax.ppermute(edges[0], axes, pairs(-1, 1, devices)),
        ]
    )


def exchange(initial, last):
    devices, spot = lax.axis_size("ctx"), lax.axis_index("ctx")
    if devices == 2:
        got = lax.ppermute(jnp.where(spot == 0, last, initial), "ctx", [(0, 1), (1, 0)])
        none = jnp.zeros_like(got)
        return jnp.where(spot == 1, got, none), jnp.where(spot == 0, got, none)
    up = [(i, i + 1) for i in range(devices - 1)]
    return lax.ppermute(last, "ctx", up), lax.ppermute(initial, "ctx", [(j, i) for i, j in up])


def over_ctx(array):
    if lax.axis_size("ctx") == 2:
        return array.astype(f32) + swap(array, "ctx").astype(f32)
    return lax.psum(array, "ctx").astype(f32)


def swap(array, axis="tensor"):
    return lax.ppermute(array, axis, [(0, 1), (1, 0)])


def ring():
    count = lax.axis_size("dp")
    order = [2 * i for i in range(count // 2)] + [2 * i + 1 for i in reversed(range(count // 2))]
    ahead = [(order[i], order[(i + 1) % count]) for i in range(count)]
    back = [(j, i) for i, j in ahead]
    places = {group: at for at, group in enumerate(order)}
    table = np.array([[order[(places[i] + j) % count] for j in range(count)] for i in range(count)], np.int32)
    slots = lax.dynamic_index_in_dim(jnp.asarray(table), lax.axis_index("dp"), keepdims=False)
    return count, ahead, back, slots


def tied(values, others):
    held = lax.optimization_barrier((tuple(values), tuple(others)))
    return held[0]


def locked(values, chain):
    held = lax.optimization_barrier((tuple(values), tuple(chain.state)))
    chain.state = held[1]
    return held[0]


def alternate(first, second):
    if len(second.past) > 1:
        first.after(second.past[-2])
    first.hop()
    if len(first.past) > 1:
        second.after(first.past[-2])
    second.hop()


class RingGather:
    def __init__(self, block, cut=0, way=None):
        self.count, self.ahead, self.back, _ = ring()
        self.cut = cut
        self.way = way
        self.pieces = {0: (block,)}
        self.state = (block, block)
        self.hops = 0
        self.past = []

    def hop(self):
        one, two = self.state
        middle = self.count // 2
        if self.hops + 1 == middle and self.way is not None:
            got = lax.ppermute((one, two)[self.way], "dp", (self.ahead, self.back)[self.way])
            self.hops += 1
            self.state = (got,)
            self.past.append(self.state)
            self.pieces[middle] = (got,)
            return
        if self.hops + 1 == middle:
            one, two = one[: self.cut], two[self.cut :]
        one, two = lax.ppermute(one, "dp", self.ahead), lax.ppermute(two, "dp", self.back)
        self.hops += 1
        one, two = lax.optimization_barrier((one, two))
        self.state = (one, two)
        self.past.append(self.state)
        if self.hops == middle:
            self.pieces[middle] = (one, two)
        else:
            self.pieces[self.count - self.hops], self.pieces[self.hops] = (one,), (two,)

    def after(self, others):
        self.state = tied(self.state, others)


class RingScatter:
    def __init__(self, parts, axis=0, way=None):
        self.count, self.ahead, self.back, _ = ring()
        self.parts = parts
        self.axis = axis
        self.way = way
        self.hops = 0
        self.state = ()
        self.past = []

    def part(self, at):
        total = self.parts[0][at]
        for part in self.parts[1:]:
            total = total + part[at]
        return total

    def hop(self):
        if self.hops == 0 and self.way is not None:
            got = lax.ppermute(self.part(0), "dp", (self.ahead, self.back)[self.way])
            self.state = (got,)
            self.past.append(self.state)
            self.hops += 1
            return
        if self.hops == 0:
            one, two = jnp.split(self.part(0), 2, axis=self.axis)
        else:
            sides = [self.part(2 * self.hops - 1), self.part(2 * self.hops)]
            if self.hops == 1 and self.way is not None:
                sides[self.way] = sides[self.way] + self.state[0]
            one, two = sides if self.hops == 1 and self.way is not None else self.state
            if self.hops == 1 and self.way is None:
                none = jnp.zeros_like(one)
                one = jnp.concatenate([one, none], axis=self.axis)
                two = jnp.concatenate([none, two], axis=self.axis)
            if self.hops > 1 or self.way is None:
                one, two = sides[0] + one, sides[1] + two
        one, two = lax.ppermute(one, "dp", self.ahead), lax.ppermute(two, "dp", self.back)
        self.state = lax.optimization_barrier((one, two))
        self.past.append(self.state)
        self.hops += 1

    def after(self, others):
        self.state = tied(self.state, others)

    def total(self):
        one, two = self.state
        return (self.part(self.count - 1).astype(f32) + one.astype(f32) + two.astype(f32)).astype(bf16)


def tables(lengths, rows):
    place = lax.axis_index("ctx") * rows
    spots = jnp.arange(NSEQ, dtype=jnp.int32)
    ends = jnp.sum(jnp.where(spots[None, :] <= spots[:, None], lengths[0][None, :], 0), axis=1)
    starts = ends - lengths[0]
    span = place + jnp.arange(-HALF, rows + HALF, dtype=jnp.int32)
    inside = (span[:, None] >= starts[None, :]) & (span[:, None] < ends[None, :])
    position = span - jnp.sum(jnp.where(inside, starts[None, :], 0), axis=1)
    lane = jnp.arange(LANES, dtype=jnp.int32)
    number = (lane % (HEAD // 2)).astype(f32)
    freq = jnp.exp(number * (-2.0 * math.log(10000.0) / HEAD))
    angle = position.astype(f32)[:, None] * freq[None, :]
    sine = jnp.sin(angle)
    sine = jnp.where((lane % HEAD < HEAD // 2)[None, :], -sine, sine)
    bounds = jnp.concatenate([ends, place[None]]).astype(jnp.int32)
    return jnp.cos(angle), sine, bounds


def body(tokens, lengths, gain_one, w_qkv, w_out, gain_two, w_in, w_down, cotangent):
    rows, width = tokens.shape
    local, units = w_out.shape[0], w_down.shape[0]
    pairs, blocks, extent = local // LANES, rows // BLOCK, rows + WINDOW
    groups = lax.axis_size("dp")
    depth = width // groups
    middle_hop = groups // 2
    gains = jnp.pad(jnp.stack([gain_one, gain_two]), ((0, PAD - 2), (0, local - depth)))
    middle_hop = groups // 2
    now = RingGather(jnp.concatenate([w_qkv.reshape(3 * depth, local), w_out.T, gains]), 2 * depth)
    now.hop()
    before, after = exchange(tokens[:HALF], tokens[rows - HALF :])
    slots = ring()[-1]
    cosine, sine, bounds = tables(lengths, rows)
    now.hop()
    now.after([cosine, sine, bounds, slots, before, after])
    hat, = call(
        norm_kernel, [shape((extent, width), f32)], (tokens, before, after), rows * width * 2000, "first_norm"
    )
    while now.hops < middle_hop:
        if now.hops + 1 == middle_hop:
            now.after([hat])
        now.hop()
    mine_two = jnp.concatenate([w_in.reshape(2 * depth, units), w_down.T])
    later = RingGather(tied([mine_two], now.state)[0], depth)
    later.hop()
    pieces = [piece for slot in range(groups) for piece in now.pieces[slot]]
    wide, gain, first, query, key, value = call(
        project_kernel,
        [
            shape((width, 4 * local), bf16),
            shape((PAD, width), f32),
            shape((extent, width), bf16),
            shape((rows, local), bf16),
            shape((extent, local), bf16),
            shape((extent, local), bf16),
        ],
        (hat, cosine, sine, *pieces),
        2 * rows * width * local * 8,
        "project",
        (slots,),
    )
    early, late = tuple(range(pairs - 1)), (pairs - 1,)

    query, key, value = locked([query, key, value], later)
    later.hop()
    shares_early, attended = call(
        functools.partial(attend_kernel, early, False),
        [shape((blocks * len(early), KEYS, KEYS), bf16), shape((rows, local), bf16)],
        (query, key, value),
        2 * rows * width * local * 10,
        "attend",
        (bounds,),
    )
    attended, = locked([attended], later)
    later.hop()
    shares_late, attended, branch = call(
        functools.partial(attend_kernel, late, True),
        [
            shape((blocks * len(late), KEYS, KEYS), bf16),
            shape((rows, local), bf16),
            shape((rows, width), bf16),
        ],
        (query, key, value, wide, attended),
        2 * rows * width * local * 7,
        "attend",
        (bounds,),
    )
    branch, = locked([branch], later)
    branch_other = swap(branch)
    while later.hops < middle_hop:
        later.hop()
    pieces = [piece for slot in range(groups) for piece in later.pieces[slot]]
    middle, second, hidden, grad_gate, grad_upper, partial, whole = call(
        feed_kernel,
        [
            shape((rows, width), f32),
            shape((rows, width), bf16),
            shape((rows, units), bf16),
            shape((rows, units), bf16),
            shape((rows, units), bf16),
            shape((rows, width), bf16),
            shape((3, width, units), bf16),
        ],
        (tokens, branch, branch_other, gain, cotangent, *pieces),
        2 * rows * width * units * 8,
        "feed_forward_and_back",
        (slots,),
    )
    partial_other = swap(partial)
    grads_two, = call(
        weight_kernel,
        [shape((groups, 3, depth, units), bf16)],
        (second, hidden, grad_gate, grad_upper, cotangent),
        2 * rows * width * units * 5,
        "feed_weight_grads",
        (slots,),
        [pltpu.VMEM((3, width, units), bf16)],
    )
    grads_two, = tied([grads_two], [partial_other])
    sums_two = RingScatter([grads_two], 1)
    sums_two.hop()
    grad_middle, low_mid, grad_att = call(
        middle_kernel,
        [shape((rows, width), f32), shape((rows, width), bf16), shape((rows, local), bf16)],
        (middle, partial, partial_other, gain, cotangent, wide),
        2 * rows * width * local * 4,
        "middle_grad",
    )
    feed, = call(
        feed_out_kernel,
        [shape((rows, width), bf16)],
        (tied([hidden], [grads_two])[0], whole),
        2 * rows * width * units,
        "feed_out",
    )
    grad_att, feed = locked([grad_att, feed], sums_two)
    feed_other = swap(feed)
    sums_two.hop()
    grad_parts = call(
        functools.partial(back_kernel, (early, late)),
        [shape((extent, 3 * LANES), bf16)] * pairs,
        (query, key, value, grad_att, cosine, sine, shares_early, shares_late),
        2 * rows * width * local * 15,
        "attention_back",
        (),
        [pltpu.VMEM((extent, local), f32)] * 2,
    )
    grad_parts = locked(grad_parts, sums_two)
    sums_two.hop()
    grad_proj, grads_a = call(
        grad_kernel_one,
        [
            shape((extent, 3 * local), bf16),
            shape((groups, 2, depth, local), bf16),
        ],
        (first, *grad_parts),
        2 * rows * width * local * 3,
        "query_key_grads",
        (slots,),
        [pltpu.VMEM((2, width, local), bf16)],
    )
    first_part, edges = call(
        first_kernel,
        [shape((rows, width), bf16), shape((2, HALF, width), bf16)],
        (grad_proj, wide),
        2 * rows * width * local * 3,
        "first_grad",
    )
    grads_b, = call(
        grad_kernel_two,
        [shape((groups, 2, depth, local), bf16)],
        (first, grad_proj, low_mid, attended),
        2 * rows * width * local * 3,
        "value_out_grads",
        (slots,),
        [pltpu.VMEM((2, width, local), bf16)],
    )
    *grads_one, first_part, edges = locked([grads_a, grads_b, first_part, edges], sums_two)
    first_other = swap(first_part)
    sums_one = [RingScatter([part], way=way) for way, part in enumerate(grads_one)]
    alternate(*sums_one)
    sums_two.after(sums_one[0].state)
    while sums_two.hops < middle_hop:
        sums_two.hop()

    while sums_one[0].hops < middle_hop - 2:
        alternate(*sums_one)
    edges, = tied([edges], sums_one[0].past[0])
    same, cross = traded(edges, 0), traded(edges, 1)
    sums_one[1].after([*sums_two.state, same, cross])
    alternate(*sums_one)
    alternate(*sums_one)
    tokens, middle = tied([tokens, middle], sums_one[1].past[-2])
    token_grad, = call(
        token_kernel,
        [shape((rows, width), f32)],
        (tokens, gain, grad_middle, first_part, first_other, same, cross),
        rows * width * 200,
        "token_grad",
    )
    mixed, = call(
        mixed_kernel,
        [shape((rows, width), bf16)],
        (middle, feed, feed_other),
        rows * width * 100,
        "mixed",
    )
    one = [chain.total() for chain in sums_one]
    two = sums_two.total()
    if lax.axis_size("ctx") == 2:
        got_two, = tied([swap(two, "ctx")], [one[1], mixed, token_grad])
        mixed, token_grad, *got = lax.optimization_barrier((mixed, token_grad, *[swap(part, "ctx") for part in one]))
        one = [part.astype(f32) + more.astype(f32) for part, more in zip(one, got)]
        two = two.astype(f32) + got_two.astype(f32)
    else:
        one = [lax.psum(part, "ctx").astype(f32) for part in one]
        two = lax.psum(two, "ctx").astype(f32)
    one = jnp.concatenate(one)
    gain_one_grad = jnp.sum(one[:3] * w_qkv.astype(f32), axis=(0, 2)) / gain_one.astype(f32)
    gain_two_grad = jnp.sum(two[:2] * w_in.astype(f32), axis=(0, 2)) / gain_two.astype(f32)
    both = jnp.stack([gain_one_grad, gain_two_grad])
    both = both + swap(both)
    return (mixed, token_grad, both[0], one[:3], one[3].T, both[1], two[:2], two[2].T)


def solution(mesh):
    in_specs = (
        P(("dp", "ctx"), None),
        P("dp", None),
        P("dp"),
        P(None, "dp", "tensor"),
        P("tensor", "dp"),
        P("dp"),
        P(None, "dp", "tensor"),
        P("tensor", "dp"),
        P(("dp", "ctx"), None),
    )
    out_specs = (
        P(("dp", "ctx"), None),
        P(("dp", "ctx"), None),
        P("dp"),
        P(None, "dp", "tensor"),
        P("tensor", "dp"),
        P("dp"),
        P(None, "dp", "tensor"),
        P("tensor", "dp"),
    )
    return jax.shard_map(body, mesh=mesh, in_specs=in_specs, out_specs=out_specs, check_vma=False)
```
